32 devices in a mesh: outer: 4 (over z), inner: 8 (over y, x, core).
Axes of the slice: x: 2, y: 2, z: 4, core: 2. Of those that a mesh axis runs over, the one named last changes fastest.
Arguments:
- queries: bfloat16 [4096, 2048], P(('outer', 'inner')), may hold values from -6 to 6
- keys: bfloat16 [4096, 2048], P(('outer', 'inner')), may hold values from -6 to 6
- values: bfloat16 [4096, 2048], P(('outer', 'inner')), may hold values from -6 to 6
- cotangent: bfloat16 [4096, 2048], P(('outer', 'inner')), may hold values from -6 to 6
Outputs:
- attended: bfloat16 [4096, 2048], P(('outer', 'inner'))
- grad_queries: bfloat16 [4096, 2048], P(('outer', 'inner'))
- grad_keys: bfloat16 [4096, 2048], P(('outer', 'inner'))
- grad_values: bfloat16 [4096, 2048], P(('outer', 'inner'))
The draws below stay inside these ranges and needn't reach their ends.
All inputs are finite; a program needn't handle non-finite values.
Results may differ from the reference program's by a relative error of at most 0.013.
Values may be sent and summed in bfloat16 or wider, within the bound.
No kernel may reach another device: no remote copies, remote signals or barrier semaphores. Data moves between devices by JAX's collectives and lax.ppermute only.
A program may use at most 64 MiB of HBM per device.

```python
import jax
import jax.numpy as jnp
from jax import lax

HEADS = 16
HEAD = 128
BLOCK = 512
HALF = 64
TOKENS = 4096


def level_of(rng, extent, split, least, high):
    loudness, own = 1.0, jax.random.fold_in(rng, 6)
    for axis_at, shards_of in split:
        draws = jnp.exp(jax.random.uniform(jax.random.fold_in(own, axis_at), (shards_of,), jnp.float32, least / len(split), high / len(split)))
        loudness = loudness * jnp.repeat(draws, extent[axis_at] // shards_of).reshape([-1 if axis == axis_at else 1 for axis in range(len(extent))])
    return loudness


def centred(own_key, shape, scale, limit, pieces=(), kind=jnp.bfloat16):
    array = scale * jax.random.normal(own_key, shape, jnp.float32)
    if pieces:
        array = array * level_of(own_key, shape, pieces, -0.22, 0.18)
    return jnp.clip(array, -limit, limit).astype(kind)


def setup_inputs(seed: int = 0) -> dict:
    arg_keys = jax.random.split(jax.random.key(seed), 5)
    queries = centred(arg_keys[0], (TOKENS, HEADS * HEAD), 1.0, 6.0, ((0, 32),))
    keys = centred(arg_keys[1], (TOKENS, HEADS * HEAD), 1.0, 6.0, ((0, 32),))
    values = centred(arg_keys[2], (TOKENS, HEADS * HEAD), 1.0, 6.0, ((0, 32),))
    cotangent = centred(arg_keys[3], (TOKENS, HEADS * HEAD), 1.0, 6.0, ((0, 32),))
    return {"queries": queries, "keys": keys, "values": values, "cotangent": cotangent}


def round_keep(x):
    return lax.optimization_barrier(x.astype(jnp.bfloat16)).astype(jnp.float32)


def reference(queries, keys, values, cotangent):
    scale = float(HEAD * TOKENS) ** -0.5
    nblocks = TOKENS // BLOCK
    qs = queries.reshape(nblocks, BLOCK, HEADS, HEAD)
    ks = keys.reshape(nblocks, BLOCK, HEADS, HEAD)
    vs = values.reshape(nblocks, BLOCK, HEADS, 2, HALF)
    ds = cotangent.reshape(nblocks, BLOCK, HEADS, 2, HALF)

    def totals(parts):
        qq, kk, vv, dd = [x.astype(jnp.float32) for x in parts]
        kv_sum = jnp.einsum('shk,shpv->hpkv', kk, vv)
        qd_sum = jnp.einsum('thk,thpv->hpkv', qq, dd)
        return kv_sum, qd_sum

    kv_blocks, qd_blocks = lax.map(totals, (qs, ks, vs, ds))
    s_before = jnp.cumsum(kv_blocks, 0) - kv_blocks
    g_after = jnp.sum(qd_blocks, 0)[None] - jnp.cumsum(qd_blocks, 0)
    lower = jnp.arange(BLOCK)[:, None] >= jnp.arange(BLOCK)[None, :]

    def one_block(parts):
        qq, kk, vv, dd, state, adjoint = parts
        qq = qq.astype(jnp.float32)
        kk = kk.astype(jnp.float32)
        vv = vv.astype(jnp.float32)
        dd = dd.astype(jnp.float32)
        s_round = round_keep(state)
        g_round = round_keep(adjoint)
        scores = jnp.einsum('thk,shk->hts', qq, kk)
        a_round = round_keep(jnp.where(lower[None], scores, 0.0))
        back = jnp.einsum('thpv,shpv->hpts', dd, vv)
        b_round = round_keep(jnp.where(lower[None, None], back, 0.0))
        attended = scale * (jnp.einsum('thk,hpkv->thpv', qq, s_round) + jnp.einsum('hts,shpv->thpv', a_round, vv))
        grad_q = scale * (jnp.einsum('thpv,hpkv->thk', dd, s_round) + jnp.einsum('hpts,shk->thk', b_round, kk))
        grad_k = scale * (jnp.einsum('shpv,hpkv->shk', vv, g_round) + jnp.einsum('hpts,thk->shk', b_round, qq))
        grad_v = scale * (jnp.einsum('shk,hpkv->shpv', kk, g_round) + jnp.einsum('hts,thpv->shpv', a_round, dd))
        return (attended.astype(jnp.bfloat16), grad_q.astype(jnp.bfloat16),
                grad_k.astype(jnp.bfloat16), grad_v.astype(jnp.bfloat16))

    attended, grad_q, grad_k, grad_v = lax.map(one_block, (qs, ks, vs, ds, s_before, g_after))
    width = HEADS * HEAD
    return (attended.reshape(TOKENS, width), grad_q.reshape(TOKENS, width),
            grad_k.reshape(TOKENS, width), grad_v.reshape(TOKENS, width))
```

```python
import functools

import jax
import jax.numpy as jnp
from jax import lax
from jax.experimental import pallas as pl
from jax.experimental.pallas import tpu as pltpu
from jax.sharding import PartitionSpec as P

HEAD = 128
GROUP = 4
MIB = 1024 * 1024


def dot(a, b, over_a, over_b):
    return lax.dot_general(
        a, b, (((over_a,), (over_b,)), ((), ())), preferred_element_type=jnp.float32
    )


def own_states_kernel(q_ref, k_ref, v_ref, d_ref, states_ref):
    slices, _, depth, _ = states_ref.shape
    kv, qd = [], []
    for h in range(q_ref.shape[1] // HEAD):
        cols = slice(h * HEAD, (h + 1) * HEAD)
        kv.append(dot(k_ref[:, cols], v_ref[:, cols], 0, 0).astype(jnp.bfloat16))
        qd.append(dot(q_ref[:, cols], d_ref[:, cols], 0, 0).astype(jnp.bfloat16))
    kv = jnp.concatenate(kv, axis=0)
    qd = jnp.concatenate(qd, axis=0)
    for j in range(slices):
        states_ref[j, 0] = kv[j * depth : (j + 1) * depth]
        states_ref[j, 1] = qd[j * depth : (j + 1) * depth]


def own_states(queries, keys, values, cotangent, count):
    rows, width = queries.shape
    depth = width // count
    steps = width // (HEAD * GROUP)
    tokens = pl.BlockSpec((rows, GROUP * HEAD), lambda g: (0, g))
    return pl.pallas_call(
        own_states_kernel,
        grid=(steps,),
        in_specs=[tokens] * 4,
        out_specs=pl.BlockSpec((count // steps, 2, depth, HEAD), lambda g: (g, 0, 0, 0)),
        out_shape=jax.ShapeDtypeStruct((count, 2, depth, HEAD), jnp.bfloat16),
        cost_estimate=pl.CostEstimate(
            flops=4 * rows * width * HEAD, bytes_accessed=12 * rows * width, transcendentals=0
        ),
        compiler_params=pltpu.CompilerParams(vmem_limit_bytes=32 * MIB),
    )(queries, keys, values, cotangent)


def scan_kernel(place_ref, arrived_ref, groups_ref, out_ref):
    count = arrived_ref.shape[0]
    outer_count = groups_ref.shape[0]
    place = place_ref[0]
    before = jnp.zeros(arrived_ref.shape[2:], jnp.float32)
    after = before
    for z in range(outer_count):
        before += jnp.where(z < place, groups_ref[z, 0], 0.0)
        after += jnp.where(z > place, groups_ref[z, 1], 0.0)
    for i in range(count):
        out_ref[i, 0] = before.astype(jnp.bfloat16)
        before += arrived_ref[i, 0].astype(jnp.float32)
    for i in reversed(range(count)):
        out_ref[i, 1] = after.astype(jnp.bfloat16)
        after += arrived_ref[i, 1].astype(jnp.float32)


def scan_states(arrived, groups, place):
    return pl.pallas_call(
        scan_kernel,
        in_specs=[
            pl.BlockSpec(memory_space=pltpu.SMEM),
            pl.BlockSpec(memory_space=pltpu.VMEM),
            pl.BlockSpec(memory_space=pltpu.VMEM),
        ],
        out_specs=pl.BlockSpec(memory_space=pltpu.VMEM),
        out_shape=jax.ShapeDtypeStruct(arrived.shape, jnp.bfloat16),
        compiler_params=pltpu.CompilerParams(vmem_limit_bytes=32 * MIB),
    )(place, arrived, groups)


def finish_kernel(scale, q_ref, k_ref, v_ref, d_ref, states_ref, att_ref, gq_ref, gk_ref, gv_ref):
    rows = q_ref.shape[0]
    at = lax.broadcasted_iota(jnp.int32, (rows, rows), 0)
    to = lax.broadcasted_iota(jnp.int32, (rows, rows), 1)
    lower, upper = at >= to, at <= to
    slices, _, depth, _ = states_ref.shape
    s_all = jnp.concatenate([states_ref[j, 0] for j in range(slices)], axis=0)
    g_all = jnp.concatenate([states_ref[j, 1] for j in range(slices)], axis=0)

    def masked(mask, a, b):
        return jnp.where(mask, dot(a, b, 1, 1), 0.0).astype(jnp.bfloat16)

    for h in range(q_ref.shape[1] // HEAD):
        cols = slice(h * HEAD, (h + 1) * HEAD)
        q, k, v, d = (ref[:, cols] for ref in (q_ref, k_ref, v_ref, d_ref))
        s, g = s_all[cols], g_all[cols]
        a, a_t = masked(lower, q, k), masked(upper, k, q)
        b, b_t = masked(lower, d, v), masked(upper, v, d)
        att = dot(q, s, 1, 0) + dot(a, v, 1, 0)
        gq = dot(d, s, 1, 1) + dot(b, k, 1, 0)
        gk = dot(v, g, 1, 1) + dot(b_t, q, 1, 0)
        gv = dot(k, g, 1, 0) + dot(a_t, d, 1, 0)
        att_ref[:, cols] = (scale * att).astype(jnp.bfloat16)
        gq_ref[:, cols] = (scale * gq).astype(jnp.bfloat16)
        gk_ref[:, cols] = (scale * gk).astype(jnp.bfloat16)
        gv_ref[:, cols] = (scale * gv).astype(jnp.bfloat16)


def finish(queries, keys, values, cotangent, states, scale):
    rows, width = queries.shape
    count, _, depth, _ = states.shape
    steps = width // (HEAD * GROUP)
    tokens = pl.BlockSpec((rows, GROUP * HEAD), lambda g: (0, g))
    out = jax.ShapeDtypeStruct((rows, width), jnp.bfloat16)
    return pl.pallas_call(
        functools.partial(finish_kernel, scale),
        grid=(steps,),
        in_specs=[tokens] * 4
        + [pl.BlockSpec((count // steps, 2, depth, HEAD), lambda g: (g, 0, 0, 0))],
        out_specs=[tokens] * 4,
        out_shape=[out] * 4,
        cost_estimate=pl.CostEstimate(
            flops=24 * rows * width * HEAD, bytes_accessed=20 * rows * width, transcendentals=0
        ),
        compiler_params=pltpu.CompilerParams(vmem_limit_bytes=32 * MIB),
    )(queries, keys, values, cotangent, states)


def body(queries, keys, values, cotangent):
    rows = queries.shape[0]
    count = lax.axis_size("inner")
    outer_count = lax.axis_size("outer")
    scale = float(HEAD * rows * count * outer_count) ** (-0.5)
    own = own_states(queries, keys, values, cotangent, count)
    arrived = lax.all_to_all(own, "inner", split_axis=0, concat_axis=0, tiled=True)
    total = jnp.sum(arrived.astype(jnp.float32), 0)
    groups = lax.all_gather(total, "outer")
    place = lax.axis_index("outer").astype(jnp.int32).reshape(1)
    scanned = scan_states(arrived, groups, place)
    states = lax.all_to_all(scanned, "inner", split_axis=0, concat_axis=0, tiled=True)
    return tuple(finish(queries, keys, values, cotangent, states, scale))


def solution(mesh):
    spec = P(("outer", "inner"), None)
    return jax.shard_map(
        body, mesh=mesh, in_specs=(spec,) * 4, out_specs=(spec,) * 4, check_vma=False
    )
```

```python
import functools

import jax
import jax.numpy as jnp
from jax import lax
from jax.experimental import pallas as pl
from jax.experimental.pallas import tpu as pltpu
from jax.sharding import PartitionSpec as P

HEAD = 128
GROUP = 4
MIB = 1024 * 1024
ANY = pl.BlockSpec(memory_space=pl.ANY)
SMEM = pl.BlockSpec(memory_space=pltpu.SMEM)
VMEM = pl.BlockSpec(memory_space=pltpu.VMEM)


def dot(a, b, over_a, over_b):
    return lax.dot_general(
        a, b, (((over_a,), (over_b,)), ((), ())), preferred_element_type=jnp.float32
    )


def own_states_kernel(place_ref, q_ref, k_ref, v_ref, d_ref, *refs):
    count = len(refs) - 1
    slots, whole = refs[:count], refs[count]
    depth = slots[0].shape[1]
    wide = max(depth, HEAD)
    inner = place_ref[1]
    for s, slot in enumerate(slots):
        row = (inner ^ s) * depth
        first = pl.multiple_of(row // HEAD * HEAD, HEAD)
        for h in range(wide // HEAD):
            cols = pl.ds(pl.multiple_of(first + h * HEAD, HEAD), HEAD)
            into = slice(h * HEAD, (h + 1) * HEAD)
            kv = dot(k_ref[:, cols], v_ref[:, cols], 0, 0)
            qd = dot(q_ref[:, cols], d_ref[:, cols], 0, 0)
            if depth >= HEAD:
                slot[0, into] = kv.astype(jnp.bfloat16)
                slot[1, into] = qd.astype(jnp.bfloat16)
            else:
                whole[0], whole[1] = kv, qd
                part = pl.ds(pl.multiple_of(row - first, depth), depth)
                slot[0] = whole[0, part].astype(jnp.bfloat16)
                slot[1] = whole[1, part].astype(jnp.bfloat16)


def own_states(place, queries, keys, values, cotangent, count):
    rows, width = queries.shape
    depth = width // count
    slot = jax.ShapeDtypeStruct((2, depth, HEAD), jnp.bfloat16)
    return pl.pallas_call(
        own_states_kernel,
        in_specs=[SMEM] + [VMEM] * 4,
        out_specs=[VMEM] * count,
        out_shape=[slot] * count,
        scratch_shapes=[pltpu.VMEM((2, HEAD, HEAD), jnp.float32)],
        cost_estimate=pl.CostEstimate(
            flops=4 * rows * width * HEAD, bytes_accessed=12 * rows * width, transcendentals=0
        ),
        compiler_params=pltpu.CompilerParams(vmem_limit_bytes=60 * MIB),
    )(place, queries, keys, values, cotangent)


def fetch(slots, held, sems, inner):
    copies = [
        pltpu.make_async_copy(slot, held.at[inner ^ s], sems.at[s]) for s, slot in enumerate(slots)
    ]
    for copy in copies:
        copy.start()
    for copy in copies:
        copy.wait()


def totals_kernel(count, outer_count, place_ref, *refs):
    slots, sends = refs[:count], refs[count : count + outer_count - 1]
    held, sems = refs[-2:]
    outer = place_ref[0]
    fetch(slots, held, sems, place_ref[1])
    totals = []
    for which in range(2):
        total = held[0, which].astype(jnp.float32)
        for i in range(1, count):
            total += held[i, which].astype(jnp.float32)
        totals.append(total.astype(jnp.bfloat16))
    for s, send in enumerate(sends):
        upward = outer + s + 1 < outer_count

        @pl.when(upward)
        def _():
            send[...] = totals[0]

        @pl.when(jnp.logical_not(upward))
        def _():
            send[...] = totals[1]


def totals(place, slots, outer_count):
    count, shape = len(slots), slots[0].shape
    return pl.pallas_call(
        functools.partial(totals_kernel, count, outer_count),
        in_specs=[SMEM] + [ANY] * count,
        out_specs=[VMEM] * (outer_count - 1),
        out_shape=[jax.ShapeDtypeStruct(shape[1:], jnp.bfloat16)] * (outer_count - 1),
        scratch_shapes=[
            pltpu.VMEM((count, *shape), jnp.bfloat16),
            pltpu.SemaphoreType.DMA((count,)),
        ],
        compiler_params=pltpu.CompilerParams(vmem_limit_bytes=32 * MIB),
    )(place, *slots)


def scan_kernel(count, place_ref, *refs):
    slots, refs = refs[:count], refs[count:]
    outs, held, scanned, sems = refs[-count - 3 : -3], *refs[-3:]
    others = refs[: -count - 3]
    outer_count = len(others) + 1
    outer, inner = place_ref[0], place_ref[1]
    fetch(slots, held, sems, inner)
    before = jnp.zeros(held.shape[2:], jnp.float32)
    after = before
    for s, other in enumerate(others):
        term = other[...].astype(jnp.float32)
        lower = outer >= s + 1
        before += jnp.where(lower, term, 0.0)
        after += jnp.where(lower, 0.0, term)
    for i in range(count):
        scanned[i, 0] = before.astype(jnp.bfloat16)
        before += held[i, 0].astype(jnp.float32)
    for i in reversed(range(count)):
        scanned[i, 1] = after.astype(jnp.bfloat16)
        after += held[i, 1].astype(jnp.float32)
    for s, out in enumerate(outs):
        out[...] = scanned[inner ^ s]


def scan_states(place, slots, others):
    count, slot = len(slots), jax.ShapeDtypeStruct(slots[0].shape, jnp.bfloat16)
    held = pltpu.VMEM((count, *slot.shape), jnp.bfloat16)
    return pl.pallas_call(
        functools.partial(scan_kernel, count),
        in_specs=[SMEM] + [ANY] * count + [VMEM] * len(others),
        out_specs=[VMEM] * count,
        out_shape=[slot] * count,
        scratch_shapes=[held, held, pltpu.SemaphoreType.DMA((count,))],
        compiler_params=pltpu.CompilerParams(vmem_limit_bytes=32 * MIB),
    )(place, *slots, *others)


def finish_kernel(scale, count, place_ref, q_ref, k_ref, v_ref, d_ref, *refs):
    slots, (att_ref, gq_ref, gk_ref, gv_ref, held, sems) = refs[:count], refs[count:]
    rows, width = q_ref.shape
    depth = held.shape[2]
    step = pl.program_id(0)

    @pl.when(step == 0)
    def _():
        fetch(slots, held, sems, place_ref[1])

    at = lax.broadcasted_iota(jnp.int32, (rows, rows), 0)
    to = lax.broadcasted_iota(jnp.int32, (rows, rows), 1)
    lower, upper = at >= to, at <= to

    def state(which, h):
        row = (step * (width // HEAD) + h) * HEAD
        if depth >= HEAD:
            return held[row // depth, which, pl.ds(pl.multiple_of(row % depth, HEAD), HEAD)]
        parts = range(HEAD // depth)
        return jnp.concatenate([held[row // depth + p, which] for p in parts], axis=0)

    def masked(mask, a, b):
        return jnp.where(mask, dot(a, b, 1, 1), 0.0).astype(jnp.bfloat16)

    for h in range(width // HEAD):
        cols = slice(h * HEAD, (h + 1) * HEAD)
        q, k, v, d = (ref[:, cols] for ref in (q_ref, k_ref, v_ref, d_ref))
        s, g = state(0, h), state(1, h)
        a, a_t = masked(lower, q, k), masked(upper, k, q)
        b, b_t = masked(lower, d, v), masked(upper, v, d)
        att = dot(q, s, 1, 0) + dot(a, v, 1, 0)
        gq = dot(d, s, 1, 1) + dot(b, k, 1, 0)
        gk = dot(v, g, 1, 1) + dot(b_t, q, 1, 0)
        gv = dot(k, g, 1, 0) + dot(a_t, d, 1, 0)
        att_ref[:, cols] = (scale * att).astype(jnp.bfloat16)
        gq_ref[:, cols] = (scale * gq).astype(jnp.bfloat16)
        gk_ref[:, cols] = (scale * gk).astype(jnp.bfloat16)
        gv_ref[:, cols] = (scale * gv).astype(jnp.bfloat16)


def finish(place, queries, keys, values, cotangent, slots, scale):
    rows, width = queries.shape
    count = len(slots)
    tokens = pl.BlockSpec((rows, GROUP * HEAD), lambda g: (0, g))
    out = jax.ShapeDtypeStruct((rows, width), jnp.bfloat16)
    return pl.pallas_call(
        functools.partial(finish_kernel, scale, count),
        grid=(width // (HEAD * GROUP),),
        in_specs=[SMEM] + [tokens] * 4 + [ANY] * count,
        out_specs=[tokens] * 4,
        out_shape=[out] * 4,
        scratch_shapes=[
            pltpu.VMEM((count, *slots[0].shape), jnp.bfloat16),
            pltpu.SemaphoreType.DMA((count,)),
        ],
        cost_estimate=pl.CostEstimate(
            flops=24 * rows * width * HEAD, bytes_accessed=20 * rows * width, transcendentals=0
        ),
        compiler_params=pltpu.CompilerParams(vmem_limit_bytes=32 * MIB),
    )(place, queries, keys, values, cotangent, *slots)


def swap(slots):
    count = len(slots)
    return [slots[0]] + [
        lax.ppermute(slots[s], "inner", [(i, i ^ s) for i in range(count)])
        for s in range(1, count)
    ]


def body(queries, keys, values, cotangent):
    rows = queries.shape[0]
    count = lax.axis_size("inner")
    outer_count = lax.axis_size("outer")
    scale = float(HEAD * rows * count * outer_count) ** (-0.5)
    place = jnp.stack([lax.axis_index("outer"), lax.axis_index("inner")]).astype(jnp.int32)
    slots = swap(own_states(place, queries, keys, values, cotangent, count))
    sends = totals(place, slots, outer_count)
    others = [
        lax.ppermute(send, "outer", [(z, (z + s + 1) % outer_count) for z in range(outer_count)])
        for s, send in enumerate(sends)
    ]
    slots = swap(scan_states(place, slots, others))
    return tuple(finish(place, queries, keys, values, cotangent, slots, scale))


def solution(mesh):
    spec = P(("outer", "inner"), None)
    return jax.shard_map(
        body, mesh=mesh, in_specs=(spec,) * 4, out_specs=(spec,) * 4, check_vma=False
    )
```

```python
import functools

import jax
import jax.numpy as jnp
from jax import lax
from jax.experimental import pallas as pl
from jax.experimental.pallas import tpu as pltpu
from jax.sharding import PartitionSpec as P

HEAD = 128
GROUP = 4
PIECES = 2
MIB = 1024 * 1024
ANY = pl.BlockSpec(memory_space=pl.ANY)
HBM = pl.BlockSpec(memory_space=pltpu.HBM)
VMEM = pl.BlockSpec(memory_space=pltpu.VMEM)
BF16 = jnp.bfloat16
F32 = jnp.float32


def dot(a, b, over_a, over_b):
    return lax.dot_general(
        a, b, (((over_a,), (over_b,)), ((), ())), preferred_element_type=F32
    )


def near_far():
    inner = lax.axis_index("inner")
    return lax.rem(inner, 2), lax.div(inner, 2)


def states_kernel(other, *refs):
    tokens, (out, held, sems) = refs[:4], refs[4:]
    half = out.shape[1]
    piece = half // PIECES
    near, _ = near_far()
    side = 1 - near if other else near
    copies = [
        [
            pltpu.make_async_copy(
                ref.at[:, pl.ds(pl.multiple_of(side * half + p * piece, piece), piece)],
                held.at[i, :, pl.ds(p * piece, piece)],
                sems.at[i, p],
            )
            for i, ref in enumerate(tokens)
        ]
        for p in range(PIECES)
    ]
    for group in copies:
        for copy in group:
            copy.start()
    for p, group in enumerate(copies):
        for copy in group:
            copy.wait()
        for h in range(p * piece // HEAD, (p + 1) * piece // HEAD):
            cols = slice(h * HEAD, (h + 1) * HEAD)
            out[0, cols] = dot(held[1, :, cols], held[2, :, cols], 0, 0).astype(BF16)
            out[1, cols] = dot(held[0, :, cols], held[3, :, cols], 0, 0).astype(BF16)


def half_states(tokens, other):
    rows, width = tokens[0].shape
    half = width // 2
    return pl.pallas_call(
        functools.partial(states_kernel, other),
        in_specs=[HBM] * 4,
        out_specs=VMEM,
        out_shape=jax.ShapeDtypeStruct((2, half, HEAD), BF16),
        scratch_shapes=[
            pltpu.VMEM((4, rows, half), BF16),
            pltpu.SemaphoreType.DMA((4, PIECES)),
        ],
        cost_estimate=pl.CostEstimate(
            flops=4 * rows * half * HEAD, bytes_accessed=12 * rows * half, transcendentals=0
        ),
        compiler_params=pltpu.CompilerParams(vmem_limit_bytes=(60 if other else 16) * MIB),
    )(*tokens)


def pair_kernel(keep_ref, got_ref, *slots):
    depth = slots[0].shape[1]
    _, far = near_far()
    for s, slot in enumerate(slots):
        part = pl.ds(pl.multiple_of((far ^ s) * depth, depth), depth)
        for which in range(2):
            both = keep_ref[which, part].astype(F32) + got_ref[which, part].astype(F32)
            slot[which] = both.astype(BF16)


def pair_slots(keep, got, far_count):
    slot = jax.ShapeDtypeStruct((2, keep.shape[1] // far_count, HEAD), BF16)
    return pl.pallas_call(
        pair_kernel,
        in_specs=[VMEM] * 2,
        out_specs=[VMEM] * far_count,
        out_shape=[slot] * far_count,
        compiler_params=pltpu.CompilerParams(vmem_limit_bytes=32 * MIB),
    )(keep, got)


def totals_kernel(far_count, *refs):
    slots, sends = refs[:far_count], refs[far_count:]
    outer = lax.axis_index("outer")
    totals = []
    for which in range(2):
        total = slots[0][which].astype(F32)
        for slot in slots[1:]:
            total += slot[which].astype(F32)
        totals.append(total.astype(BF16))
    for s, send in enumerate(sends):
        upward = (outer ^ (s + 1)) > outer
        send[...] = jnp.where(upward, totals[0], totals[1])


def group_sends(slots, outer_count):
    send = jax.ShapeDtypeStruct(slots[0].shape[1:], BF16)
    return pl.pallas_call(
        functools.partial(totals_kernel, len(slots)),
        in_specs=[VMEM] * len(slots),
        out_specs=[VMEM] * (outer_count - 1),
        out_shape=[send] * (outer_count - 1),
        compiler_params=pltpu.CompilerParams(vmem_limit_bytes=32 * MIB),
    )(*slots)


def scan_kernel(far_count, *refs):
    slots, others, outs = refs[:far_count], refs[far_count:-far_count], refs[-far_count:]
    outer = lax.axis_index("outer")
    _, far = near_far()
    for which in range(2):
        base = jnp.zeros(slots[0].shape[1:], F32)
        for s, other in enumerate(others):
            below = (outer ^ (s + 1)) < outer
            wanted = below if which == 0 else jnp.logical_not(below)
            base += jnp.where(wanted, other[...].astype(F32), 0.0)
        terms = [slot[which].astype(F32) for slot in slots]
        for s, out in enumerate(outs):
            total = base
            for t, term in enumerate(terms):
                if s != t:
                    below = (far ^ t) < (far ^ s)
                    wanted = below if which == 0 else jnp.logical_not(below)
                    total += jnp.where(wanted, term, 0.0)
            out[which] = total.astype(BF16)


def scan_slots(slots, others):
    far_count, slot = len(slots), jax.ShapeDtypeStruct(slots[0].shape, BF16)
    return pl.pallas_call(
        functools.partial(scan_kernel, far_count),
        in_specs=[VMEM] * (far_count + len(others)),
        out_specs=[VMEM] * far_count,
        out_shape=[slot] * far_count,
        compiler_params=pltpu.CompilerParams(vmem_limit_bytes=32 * MIB),
    )(*slots, *others)


def expand_kernel(far_count, *refs):
    slots, (keep, got, mine, theirs) = refs[:far_count], refs[far_count:]
    depth = slots[0].shape[1]
    near, far = near_far()
    for s, slot in enumerate(slots):
        part = pl.ds(pl.multiple_of((far ^ s) * depth, depth), depth)
        for which in range(2):
            base = slot[which].astype(F32)
            for_me = near == 1 - which
            own, others = keep[which, part].astype(F32), got[which, part].astype(F32)
            mine[which, part] = (base + jnp.where(for_me, others, 0.0)).astype(BF16)
            theirs[which, part] = (base + jnp.where(for_me, 0.0, own)).astype(BF16)


def expand(slots, keep, got):
    state = jax.ShapeDtypeStruct(keep.shape, BF16)
    return pl.pallas_call(
        functools.partial(expand_kernel, len(slots)),
        in_specs=[VMEM] * (len(slots) + 2),
        out_specs=[VMEM] * 2,
        out_shape=[state] * 2,
        compiler_params=pltpu.CompilerParams(vmem_limit_bytes=32 * MIB),
    )(*slots, keep, got)


def local_kernel(q_ref, k_ref, v_ref, d_ref, att_ref, gq_ref, gk_ref, gv_ref):
    rows = q_ref.shape[0]
    at = lax.broadcasted_iota(jnp.int32, (rows, rows), 0)
    to = lax.broadcasted_iota(jnp.int32, (rows, rows), 1)
    lower, upper = at >= to, at <= to

    def masked(mask, a, b):
        return jnp.where(mask, dot(a, b, 1, 1), 0.0).astype(BF16)

    for h in range(q_ref.shape[1] // HEAD):
        cols = slice(h * HEAD, (h + 1) * HEAD)
        q, k, v, d = (ref[:, cols] for ref in (q_ref, k_ref, v_ref, d_ref))
        att_ref[:, cols] = dot(masked(lower, q, k), v, 1, 0)
        gq_ref[:, cols] = dot(masked(lower, d, v), k, 1, 0)
        gk_ref[:, cols] = dot(masked(upper, v, d), q, 1, 0)
        gv_ref[:, cols] = dot(masked(upper, k, q), d, 1, 0)


def local_part(tokens):
    rows, width = tokens[0].shape
    block = pl.BlockSpec((rows, GROUP * HEAD), lambda g: (0, g))
    return pl.pallas_call(
        local_kernel,
        grid=(width // (HEAD * GROUP),),
        in_specs=[block] * 4,
        out_specs=[block] * 4,
        out_shape=[jax.ShapeDtypeStruct((rows, width), F32)] * 4,
        cost_estimate=pl.CostEstimate(
            flops=16 * rows * width * HEAD, bytes_accessed=24 * rows * width, transcendentals=0
        ),
        compiler_params=pltpu.CompilerParams(vmem_limit_bytes=32 * MIB),
    )(*tokens)


def finish_kernel(scale, side_ref, *refs):
    tokens, local, states, outs = refs[:4], refs[4:8], refs[8], refs[-4:]
    for h in range(tokens[0].shape[1] // HEAD):
        cols = slice(h * HEAD, (h + 1) * HEAD)
        q, k, v, d = (ref[:, cols] for ref in tokens)
        s, g = states[0, cols], states[1, cols]
        parts = (dot(q, s, 1, 0), dot(d, s, 1, 1), dot(v, g, 1, 1), dot(k, g, 1, 0))
        for part, near, out in zip(parts, local, outs):
            out[:, cols] = (scale * (part + near[:, cols])).astype(BF16)


def finish(side, tokens, local, states, scale, before=()):
    rows, width = tokens[0].shape
    steps = width // 2 // (HEAD * GROUP)
    block = pl.BlockSpec((rows, GROUP * HEAD), lambda g, side: (0, side[0] * steps + g))
    out = jax.ShapeDtypeStruct((rows, width), BF16)
    return pl.pallas_call(
        functools.partial(finish_kernel, scale),
        grid_spec=pltpu.PrefetchScalarGridSpec(
            num_scalar_prefetch=1,
            grid=(steps,),
            in_specs=[block] * 8
            + [pl.BlockSpec((2, GROUP * HEAD, HEAD), lambda g, side: (0, g, 0))]
            + [ANY] * len(before),
            out_specs=[block] * 4,
        ),
        out_shape=[out] * 4,
        input_output_aliases={10 + i: i for i in range(len(before))},
        cost_estimate=pl.CostEstimate(
            flops=4 * rows * width * HEAD, bytes_accessed=17 * rows * width, transcendentals=0
        ),
        compiler_params=pltpu.CompilerParams(vmem_limit_bytes=32 * MIB),
    )(side, *tokens, *local, states, *before)


def swap(x, axis, bits):
    return lax.ppermute(x, axis, [(i, i ^ bits) for i in range(lax.axis_size(axis))])


def swap_far(slots):
    sent = {s: swap(slots[s], "inner", 2 * s) for s in reversed(range(1, len(slots)))}
    return [slots[0]] + [sent[s] for s in range(1, len(slots))]


def body(queries, keys, values, cotangent):
    tokens = (queries, keys, values, cotangent)
    count = lax.axis_size("inner")
    outer_count = lax.axis_size("outer")
    scale = float(HEAD * queries.shape[0] * count * outer_count) ** (-0.5)
    got = swap(half_states(tokens, True), "inner", 1)
    keep = half_states(tokens, False)
    slots = swap_far(pair_slots(keep, got, count // 2))
    slots, local = lax.optimization_barrier((slots, local_part(tokens)))
    sends = group_sends(slots, outer_count)
    others = [swap(send, "outer", s + 1) for s, send in enumerate(sends)]
    slots = swap_far(scan_slots(slots, others))
    mine, theirs = expand(slots, keep, got)
    arrived = swap(theirs, "inner", 1)
    side = lax.rem(lax.axis_index("inner"), 2).astype(jnp.int32).reshape(1)
    outs = finish(side, tokens, local, mine, scale)
    return tuple(finish(1 - side, tokens, local, arrived, scale, outs))


def solution(mesh):
    spec = P(("outer", "inner"), None)
    return jax.shard_map(
        body, mesh=mesh, in_specs=(spec,) * 4, out_specs=(spec,) * 4, check_vma=False
    )
```

```python
import functools

import jax
import jax.numpy as jnp
from jax import lax
from jax.experimental import pallas as pl
from jax.experimental.pallas import tpu as pltpu
from jax.sharding import PartitionSpec as P

HEAD = 128
PIECES = 4
MIB = 1024 * 1024
ANY = pl.BlockSpec(memory_space=pl.ANY)
VMEM = pl.BlockSpec(memory_space=pltpu.VMEM)
BF16 = jnp.bfloat16
F32 = jnp.float32


def dot(a, b, over_a, over_b):
    return lax.dot_general(
        a, b, (((over_a,), (over_b,)), ((), ())), preferred_element_type=F32
    )


def near_far():
    inner = lax.axis_index("inner")
    return lax.rem(inner, 2), lax.div(inner, 2)


def states_kernel(other, *refs):
    tokens, (out_ref, held, out, in_sems, out_sems) = refs[:4], refs[4:]
    half = held.shape[2]
    piece = half // PIECES
    near, _ = near_far()
    side = 1 - near if other else near
    copies = [
        [
            pltpu.make_async_copy(
                ref.at[:, pl.ds(pl.multiple_of(side * half + p * piece, piece), piece)],
                held.at[i, :, pl.ds(p * piece, piece)],
                in_sems.at[i, p],
            )
            for i, ref in enumerate(tokens)
        ]
        for p in range(PIECES)
    ]
    backs = [
        pltpu.make_async_copy(out.at[:, part], out_ref.at[:, part], out_sems.at[p])
        for p in range(PIECES)
        for part in [pl.ds(p * piece, piece)]
    ]
    for group in copies:
        for copy in group:
            copy.start()
    for p, group in enumerate(copies):
        for copy in group:
            copy.wait()
        for h in range(p * piece // HEAD, (p + 1) * piece // HEAD):
            cols = slice(h * HEAD, (h + 1) * HEAD)
            out[0, cols] = dot(held[1, :, cols], held[2, :, cols], 0, 0).astype(BF16)
            out[1, cols] = dot(held[0, :, cols], held[3, :, cols], 0, 0).astype(BF16)
        backs[p].start()
    for back in backs:
        back.wait()


def resident_states_kernel(q_ref, k_ref, v_ref, d_ref, out):
    half = out.shape[1]
    near, _ = near_far()
    for h in range(half // HEAD):
        cols = pl.ds(pl.multiple_of(near * half + h * HEAD, HEAD), HEAD)
        into = slice(h * HEAD, (h + 1) * HEAD)
        out[0, into] = dot(k_ref[:, cols], v_ref[:, cols], 0, 0).astype(BF16)
        out[1, into] = dot(q_ref[:, cols], d_ref[:, cols], 0, 0).astype(BF16)


def half_states(tokens, other):
    rows, width = tokens[0].shape
    half = width // 2
    cost = pl.CostEstimate(
        flops=4 * rows * half * HEAD, bytes_accessed=12 * rows * half, transcendentals=0
    )
    out = jax.ShapeDtypeStruct((2, half, HEAD), BF16)
    if not other:
        return pl.pallas_call(
            resident_states_kernel,
            in_specs=[VMEM] * 4,
            out_specs=VMEM,
            out_shape=out,
            cost_estimate=cost,
            compiler_params=pltpu.CompilerParams(vmem_limit_bytes=4 * MIB),
        )(*tokens)
    return pl.pallas_call(
        functools.partial(states_kernel, other),
        in_specs=[ANY] * 4,
        out_specs=ANY,
        out_shape=out,
        scratch_shapes=[
            pltpu.VMEM((4, rows, half), BF16),
            pltpu.VMEM(out.shape, BF16),
            pltpu.SemaphoreType.DMA((4, PIECES)),
            pltpu.SemaphoreType.DMA((PIECES,)),
        ],
        cost_estimate=cost,
        compiler_params=pltpu.CompilerParams(vmem_limit_bytes=60 * MIB),
    )(*tokens)


def pair_kernel(keep_ref, got_ref, *slots):
    depth = slots[0].shape[1]
    _, far = near_far()
    for s, slot in enumerate(slots):
        part = pl.ds(pl.multiple_of((far ^ s) * depth, depth), depth)
        for which in range(2):
            both = keep_ref[which, part].astype(F32) + got_ref[which, part].astype(F32)
            slot[which] = both.astype(BF16)


def pair_slots(keep, got, far_count):
    slot = jax.ShapeDtypeStruct((2, keep.shape[1] // far_count, HEAD), BF16)
    return pl.pallas_call(
        pair_kernel,
        in_specs=[VMEM] * 2,
        out_specs=[VMEM] * far_count,
        out_shape=[slot] * far_count,
        compiler_params=pltpu.CompilerParams(vmem_limit_bytes=4 * MIB),
    )(keep, got)


def totals_kernel(far_count, *refs):
    slots, sends = refs[:far_count], refs[far_count:]
    outer = lax.axis_index("outer")
    totals = []
    for which in range(2):
        total = slots[0][which].astype(F32)
        for slot in slots[1:]:
            total += slot[which].astype(F32)
        totals.append(total.astype(BF16))
    for s, send in enumerate(sends):
        upward = (outer ^ (s + 1)) > outer
        send[...] = jnp.where(upward, totals[0], totals[1])


def group_sends(slots, outer_count):
    send = jax.ShapeDtypeStruct(slots[0].shape[1:], BF16)
    return pl.pallas_call(
        functools.partial(totals_kernel, len(slots)),
        in_specs=[VMEM] * len(slots),
        out_specs=[VMEM] * (outer_count - 1),
        out_shape=[send] * (outer_count - 1),
        compiler_params=pltpu.CompilerParams(vmem_limit_bytes=4 * MIB),
    )(*slots)


def scan_kernel(far_count, *refs):
    slots, others, outs = refs[:far_count], refs[far_count:-far_count], refs[-far_count:]
    outer = lax.axis_index("outer")
    _, far = near_far()
    for which in range(2):
        base = jnp.zeros(slots[0].shape[1:], F32)
        for s, other in enumerate(others):
            below = (outer ^ (s + 1)) < outer
            wanted = below if which == 0 else jnp.logical_not(below)
            base += jnp.where(wanted, other[...].astype(F32), 0.0)
        terms = [slot[which].astype(F32) for slot in slots]
        for s, out in enumerate(outs):
            total = base
            for t, term in enumerate(terms):
                if s != t:
                    below = (far ^ t) < (far ^ s)
                    wanted = below if which == 0 else jnp.logical_not(below)
                    total += jnp.where(wanted, term, 0.0)
            out[which] = total.astype(BF16)


def scan_slots(slots, others):
    far_count, slot = len(slots), jax.ShapeDtypeStruct(slots[0].shape, BF16)
    return pl.pallas_call(
        functools.partial(scan_kernel, far_count),
        in_specs=[VMEM] * (far_count + len(others)),
        out_specs=[VMEM] * far_count,
        out_shape=[slot] * far_count,
        compiler_params=pltpu.CompilerParams(vmem_limit_bytes=4 * MIB),
    )(*slots, *others)


def expand(slots, out, extras, extra_which):
    depth = slots[0].shape[1]
    _, far = near_far()
    for s, slot in enumerate(slots):
        part = pl.ds(pl.multiple_of((far ^ s) * depth, depth), depth)
        for which in range(2):
            @pl.when(extra_which == which)
            def _():
                out[which, part] = (slot[which].astype(F32) + extras[which, part].astype(F32)).astype(BF16)

            @pl.when(extra_which != which)
            def _():
                out[which, part] = slot[which]


def theirs_kernel(*refs):
    slots, (keep, out) = refs[:-2], refs[-2:]
    near, _ = near_far()
    expand(slots, out, keep, near)


def state_for_neighbour(slots, keep):
    return pl.pallas_call(
        theirs_kernel,
        in_specs=[VMEM] * (len(slots) + 1),
        out_specs=VMEM,
        out_shape=jax.ShapeDtypeStruct(keep.shape, BF16),
        compiler_params=pltpu.CompilerParams(vmem_limit_bytes=4 * MIB),
    )(*slots, keep)


def local_kernel(q_ref, k_ref, v_ref, d_ref, att_ref, gq_ref, gk_ref, gv_ref):
    rows = q_ref.shape[0]
    at = lax.broadcasted_iota(jnp.int32, (rows, rows), 0)
    to = lax.broadcasted_iota(jnp.int32, (rows, rows), 1)
    lower, upper = at >= to, at <= to

    def masked(mask, a, b):
        return jnp.where(mask, dot(a, b, 1, 1), 0.0).astype(BF16)

    for h in range(q_ref.shape[1] // HEAD):
        cols = slice(h * HEAD, (h + 1) * HEAD)
        q, k, v, d = (ref[:, cols] for ref in (q_ref, k_ref, v_ref, d_ref))
        att_ref[:, cols] = dot(masked(lower, q, k), v, 1, 0)
        gq_ref[:, cols] = dot(masked(lower, d, v), k, 1, 0)
        gk_ref[:, cols] = dot(masked(upper, v, d), q, 1, 0)
        gv_ref[:, cols] = dot(masked(upper, k, q), d, 1, 0)


def local_part(tokens):
    rows, width = tokens[0].shape
    return pl.pallas_call(
        local_kernel,
        in_specs=[VMEM] * 4,
        out_specs=[VMEM] * 4,
        out_shape=[jax.ShapeDtypeStruct((rows, width), F32)] * 4,
        cost_estimate=pl.CostEstimate(
            flops=16 * rows * width * HEAD, bytes_accessed=24 * rows * width, transcendentals=0
        ),
        compiler_params=pltpu.CompilerParams(vmem_limit_bytes=4 * MIB),
    )(*tokens)


def finish_kernel(scale, slot_count, *refs):
    tokens, local, refs = refs[:4], refs[4:8], refs[8:]
    held, sems = refs[-2:]
    near, _ = near_far()
    if slot_count:
        outs, states = refs[-7:-3], refs[-3]
        expand(refs[:slot_count], states, refs[slot_count], 1 - near)
        side = near
    else:
        outs, states, side = refs[-6:-2], refs[0], 1 - near
    half = held.shape[2]
    piece = half // PIECES
    copies = []
    for p in range(PIECES):
        for h in range(p * piece // HEAD, (p + 1) * piece // HEAD):
            into = slice(h * HEAD, (h + 1) * HEAD)
            cols = pl.ds(pl.multiple_of(side * half + h * HEAD, HEAD), HEAD)
            q, k, v, d = (ref[:, cols] for ref in tokens)
            s, g = states[0, into], states[1, into]
            parts = (dot(q, s, 1, 0), dot(d, s, 1, 1), dot(v, g, 1, 1), dot(k, g, 1, 0))
            for i, part in enumerate(parts):
                held[i, :, into] = (scale * (part + local[i][:, cols])).astype(BF16)
        for i, out in enumerate(outs):
            there = pl.ds(pl.multiple_of(side * half + p * piece, piece), piece)
            copy = pltpu.make_async_copy(
                held.at[i, :, pl.ds(p * piece, piece)], out.at[:, there], sems.at[i, p]
            )
            copy.start()
            copies.append(copy)
    for copy in copies:
        copy.wait()


def finish(tokens, local, states, scale, before=()):
    rows, width = tokens[0].shape
    half = width // 2
    slot_count = 0 if before else len(states) - 1
    out = jax.ShapeDtypeStruct((rows, width), BF16)
    scratch = [pltpu.VMEM((2, half, HEAD), BF16)] if slot_count else []
    return pl.pallas_call(
        functools.partial(finish_kernel, scale, slot_count),
        in_specs=[VMEM] * (8 + len(states)) + [ANY] * len(before),
        out_specs=[ANY] * 4,
        out_shape=[out] * 4,
        scratch_shapes=scratch
        + [pltpu.VMEM((4, rows, half), BF16), pltpu.SemaphoreType.DMA((4, PIECES))],
        input_output_aliases={8 + len(states) + i: i for i in range(len(before))},
        cost_estimate=pl.CostEstimate(
            flops=4 * rows * width * HEAD, bytes_accessed=17 * rows * width, transcendentals=0
        ),
        compiler_params=pltpu.CompilerParams(vmem_limit_bytes=8 * MIB),
    )(*tokens, *local, *states, *before)


def swap(x, axis, bits):
    return lax.ppermute(x, axis, [(i, i ^ bits) for i in range(lax.axis_size(axis))])


def swap_far(slots):
    sent = {s: swap(slots[s], "inner", 2 * s) for s in reversed(range(1, len(slots)))}
    return [slots[0]] + [sent[s] for s in range(1, len(slots))]


def body(queries, keys, values, cotangent):
    tokens = (queries, keys, values, cotangent)
    count = lax.axis_size("inner")
    outer_count = lax.axis_size("outer")
    scale = float(HEAD * queries.shape[0] * count * outer_count) ** (-0.5)
    got = swap(half_states(tokens, True), "inner", 1)
    keep = half_states(tokens, False)
    slots = swap_far(pair_slots(keep, got, count // 2))
    slots, local = lax.optimization_barrier((slots, local_part(tokens)))
    sends = group_sends(slots, outer_count)
    others = [swap(send, "outer", s + 1) for s, send in enumerate(sends)]
    slots = swap_far(scan_slots(slots, others))
    arrived = swap(state_for_neighbour(slots, keep), "inner", 1)
    outs = finish(tokens, local, (*slots, got), scale)
    return tuple(finish(tokens, local, (arrived,), scale, outs))


def solution(mesh):
    spec = P(("outer", "inner"), None)
    return jax.shard_map(
        body, mesh=mesh, in_specs=(spec,) * 4, out_specs=(spec,) * 4, check_vma=False
    )
```

```python
import functools

import jax
import jax.numpy as jnp
from jax import lax
from jax.experimental import pallas as pl
from jax.experimental.pallas import tpu as pltpu
from jax.sharding import PartitionSpec as P

HEAD = 128
PIECES = 4
MIB = 1024 * 1024
ANY = pl.BlockSpec(memory_space=pl.ANY)
VMEM = pl.BlockSpec(memory_space=pltpu.VMEM)
BF16 = jnp.bfloat16
F32 = jnp.float32


def dot(a, b, over_a, over_b):
    return lax.dot_general(
        a, b, (((over_a,), (over_b,)), ((), ())), preferred_element_type=F32
    )


def near_far():
    inner = lax.axis_index("inner")
    return lax.rem(inner, 2), lax.div(inner, 2)


def states_of(tokens, out, into, cols):
    q, k, v, d = (ref[:, cols] for ref in tokens)
    out[0, into] = dot(k, v, 0, 0).astype(BF16)
    out[1, into] = dot(q, d, 0, 0).astype(BF16)


def load_kernel(*refs):
    tokens, held, (out, sems) = refs[:4], refs[4:8], refs[8:]
    half = out.shape[1]
    piece = half // PIECES
    near, _ = near_far()

    def columns(side, p):
        return pl.ds(pl.multiple_of(side * half + p * piece, piece), piece)

    copies = [
        [
            pltpu.make_async_copy(
                ref.at[:, columns(side, p)], to.at[:, columns(side, p)], sems.at[turn, p, i]
            )
            for i, (ref, to) in enumerate(zip(tokens, held))
        ]
        for turn, side in enumerate((1 - near, near))
        for p in range(PIECES)
    ]
    for group in copies:
        for copy in group:
            copy.start()
    for p, group in enumerate(copies):
        for copy in group:
            copy.wait()
        if p < PIECES:
            for h in range(p * piece // HEAD, (p + 1) * piece // HEAD):
                cols = pl.ds(pl.multiple_of((1 - near) * half + h * HEAD, HEAD), HEAD)
                states_of(held, out, slice(h * HEAD, (h + 1) * HEAD), cols)


def load(tokens):
    rows, width = tokens[0].shape
    half = width // 2
    *held, give = pl.pallas_call(
        load_kernel,
        in_specs=[ANY] * 4,
        out_specs=[VMEM] * 5,
        out_shape=[pltpu.VMEM((rows, width), BF16)] * 4 + [pltpu.VMEM((2, half, HEAD), BF16)],
        scratch_shapes=[pltpu.SemaphoreType.DMA((2, PIECES, 4))],
        cost_estimate=pl.CostEstimate(
            flops=4 * rows * half * HEAD, bytes_accessed=20 * rows * half, transcendentals=0
        ),
        compiler_params=pltpu.CompilerParams(vmem_limit_bytes=4 * MIB),
    )(*(pltpu.with_memory_space_constraint(x, pltpu.HBM) for x in tokens))
    return tuple(held), give


def keep_kernel(*refs):
    tokens, out = refs[:4], refs[4]
    half = out.shape[1]
    near, _ = near_far()
    for h in range(half // HEAD):
        cols = pl.ds(pl.multiple_of(near * half + h * HEAD, HEAD), HEAD)
        states_of(tokens, out, slice(h * HEAD, (h + 1) * HEAD), cols)


def keep_states(tokens):
    rows, width = tokens[0].shape
    half = width // 2
    return pl.pallas_call(
        keep_kernel,
        in_specs=[VMEM] * 4,
        out_specs=VMEM,
        out_shape=jax.ShapeDtypeStruct((2, half, HEAD), BF16),
        cost_estimate=pl.CostEstimate(
            flops=4 * rows * half * HEAD, bytes_accessed=12 * rows * half, transcendentals=0
        ),
        compiler_params=pltpu.CompilerParams(vmem_limit_bytes=4 * MIB),
    )(*tokens)


def pair_kernel(keep_ref, got_ref, *slots):
    depth = slots[0].shape[1]
    _, far = near_far()
    for s, slot in enumerate(slots):
        part = pl.ds(pl.multiple_of((far ^ s) * depth, depth), depth)
        for which in range(2):
            both = keep_ref[which, part].astype(F32) + got_ref[which, part].astype(F32)
            slot[which] = both.astype(BF16)


def pair_slots(keep, got, far_count):
    slot = jax.ShapeDtypeStruct((2, keep.shape[1] // far_count, HEAD), BF16)
    return pl.pallas_call(
        pair_kernel,
        in_specs=[VMEM] * 2,
        out_specs=[VMEM] * far_count,
        out_shape=[slot] * far_count,
        compiler_params=pltpu.CompilerParams(vmem_limit_bytes=4 * MIB),
    )(keep, got)


def totals_kernel(far_count, *refs):
    slots, sends = refs[:far_count], refs[far_count:]
    outer = lax.axis_index("outer")
    totals = []
    for which in range(2):
        total = slots[0][which].astype(F32)
        for slot in slots[1:]:
            total += slot[which].astype(F32)
        totals.append(total.astype(BF16))
    for s, send in enumerate(sends):
        upward = (outer ^ (s + 1)) > outer
        send[...] = jnp.where(upward, totals[0], totals[1])


def group_sends(slots, outer_count):
    send = jax.ShapeDtypeStruct(slots[0].shape[1:], BF16)
    return pl.pallas_call(
        functools.partial(totals_kernel, len(slots)),
        in_specs=[VMEM] * len(slots),
        out_specs=[VMEM] * (outer_count - 1),
        out_shape=[send] * (outer_count - 1),
        compiler_params=pltpu.CompilerParams(vmem_limit_bytes=4 * MIB),
    )(*slots)


def scan_kernel(far_count, *refs):
    slots, others, outs = refs[:far_count], refs[far_count:-far_count], refs[-far_count:]
    outer = lax.axis_index("outer")
    _, far = near_far()
    for which in range(2):
        base = jnp.zeros(slots[0].shape[1:], F32)
        for s, other in enumerate(others):
            below = (outer ^ (s + 1)) < outer
            wanted = below if which == 0 else jnp.logical_not(below)
            base += jnp.where(wanted, other[...].astype(F32), 0.0)
        terms = [slot[which].astype(F32) for slot in slots]
        for s, out in enumerate(outs):
            total = base
            for t, term in enumerate(terms):
                if s != t:
                    below = (far ^ t) < (far ^ s)
                    wanted = below if which == 0 else jnp.logical_not(below)
                    total += jnp.where(wanted, term, 0.0)
            out[which] = total.astype(BF16)


def scan_slots(slots, others):
    far_count, slot = len(slots), jax.ShapeDtypeStruct(slots[0].shape, BF16)
    return pl.pallas_call(
        functools.partial(scan_kernel, far_count),
        in_specs=[VMEM] * (far_count + len(others)),
        out_specs=[VMEM] * far_count,
        out_shape=[slot] * far_count,
        compiler_params=pltpu.CompilerParams(vmem_limit_bytes=4 * MIB),
    )(*slots, *others)


def expand(slots, out, extras, extra_which):
    depth = slots[0].shape[1]
    _, far = near_far()
    for s, slot in enumerate(slots):
        part = pl.ds(pl.multiple_of((far ^ s) * depth, depth), depth)
        for which in range(2):
            @pl.when(extra_which == which)
            def _():
                out[which, part] = (slot[which].astype(F32) + extras[which, part].astype(F32)).astype(BF16)

            @pl.when(extra_which != which)
            def _():
                out[which, part] = slot[which]


def theirs_kernel(*refs):
    slots, (keep, out) = refs[:-2], refs[-2:]
    near, _ = near_far()
    expand(slots, out, keep, near)


def state_for_neighbour(slots, keep):
    return pl.pallas_call(
        theirs_kernel,
        in_specs=[VMEM] * (len(slots) + 1),
        out_specs=VMEM,
        out_shape=jax.ShapeDtypeStruct(keep.shape, BF16),
        compiler_params=pltpu.CompilerParams(vmem_limit_bytes=4 * MIB),
    )(*slots, keep)


def local_kernel(q_ref, k_ref, v_ref, d_ref, att_ref, gq_ref, gk_ref, gv_ref):
    rows, width = q_ref.shape
    at = lax.broadcasted_iota(jnp.int32, (rows, rows), 0)
    to = lax.broadcasted_iota(jnp.int32, (rows, rows), 1)
    lower = at >= to

    def masked(a, b):
        return jnp.where(lower, dot(a, b, 1, 1), 0.0).astype(BF16)

    def second(cols, a, b):
        att_ref[:, cols] = dot(a, v_ref[:, cols], 1, 0)
        gq_ref[:, cols] = dot(b, k_ref[:, cols], 1, 0)
        gk_ref[:, cols] = dot(b, q_ref[:, cols], 0, 0)
        gv_ref[:, cols] = dot(a, d_ref[:, cols], 0, 0)

    last = None
    for h in range(width // HEAD):
        cols = slice(h * HEAD, (h + 1) * HEAD)
        a, b = masked(q_ref[:, cols], k_ref[:, cols]), masked(d_ref[:, cols], v_ref[:, cols])
        if last:
            second(*last)
        last = (cols, a, b)
    second(*last)


def local_part(tokens):
    rows, width = tokens[0].shape
    return pl.pallas_call(
        local_kernel,
        in_specs=[VMEM] * 4,
        out_specs=[VMEM] * 4,
        out_shape=[jax.ShapeDtypeStruct((rows, width), F32)] * 4,
        cost_estimate=pl.CostEstimate(
            flops=16 * rows * width * HEAD, bytes_accessed=24 * rows * width, transcendentals=0
        ),
        compiler_params=pltpu.CompilerParams(vmem_limit_bytes=4 * MIB),
    )(*tokens)


def finish_kernel(scale, slot_count, *refs):
    tokens, local, refs = refs[:4], refs[4:8], refs[8:]
    held, sems = refs[-2:]
    near, _ = near_far()
    if slot_count:
        outs, states = refs[-7:-3], refs[-3]
        expand(refs[:slot_count], states, refs[slot_count], 1 - near)
        side = near
    else:
        outs, states, side = refs[-6:-2], refs[0], 1 - near
    half = held.shape[2]
    piece = half // PIECES
    copies = []
    for p in range(PIECES):
        for h in range(p * piece // HEAD, (p + 1) * piece // HEAD):
            into = slice(h * HEAD, (h + 1) * HEAD)
            cols = pl.ds(pl.multiple_of(side * half + h * HEAD, HEAD), HEAD)
            q, k, v, d = (ref[:, cols] for ref in tokens)
            s, g = states[0, into], states[1, into]
            parts = (dot(q, s, 1, 0), dot(d, s, 1, 1), dot(v, g, 1, 1), dot(k, g, 1, 0))
            for i, part in enumerate(parts):
                held[i, :, into] = (scale * (part + local[i][:, cols])).astype(BF16)
        for i, out in enumerate(outs):
            there = pl.ds(pl.multiple_of(side * half + p * piece, piece), piece)
            copy = pltpu.make_async_copy(
                held.at[i, :, pl.ds(p * piece, piece)], out.at[:, there], sems.at[i, p]
            )
            copy.start()
            copies.append(copy)
    for copy in copies:
        copy.wait()


def finish(tokens, local, states, scale, before=()):
    rows, width = tokens[0].shape
    half = width // 2
    slot_count = 0 if before else len(states) - 1
    out = jax.ShapeDtypeStruct((rows, width), BF16)
    scratch = [pltpu.VMEM((2, half, HEAD), BF16)] if slot_count else []
    return pl.pallas_call(
        functools.partial(finish_kernel, scale, slot_count),
        in_specs=[VMEM] * (8 + len(states)) + [ANY] * len(before),
        out_specs=[ANY] * 4,
        out_shape=[out] * 4,
        scratch_shapes=scratch
        + [pltpu.VMEM((4, rows, half), BF16), pltpu.SemaphoreType.DMA((4, PIECES))],
        input_output_aliases={8 + len(states) + i: i for i in range(len(before))},
        cost_estimate=pl.CostEstimate(
            flops=4 * rows * width * HEAD, bytes_accessed=17 * rows * width, transcendentals=0
        ),
        compiler_params=pltpu.CompilerParams(vmem_limit_bytes=8 * MIB),
    )(*tokens, *local, *states, *before)


def swap(x, axis, bits):
    return lax.ppermute(x, axis, [(i, i ^ bits) for i in range(lax.axis_size(axis))])


def swap_far(slots):
    sent = {s: swap(slots[s], "inner", 2 * s) for s in reversed(range(1, len(slots)))}
    return [slots[0]] + [sent[s] for s in range(1, len(slots))]


def body(queries, keys, values, cotangent):
    tokens = (queries, keys, values, cotangent)
    count = lax.axis_size("inner")
    outer_count = lax.axis_size("outer")
    scale = float(HEAD * queries.shape[0] * count * outer_count) ** (-0.5)
    tokens, give = load(tokens)
    got = swap(give, "inner", 1)
    keep = keep_states(tokens)
    slots = swap_far(pair_slots(keep, got, count // 2))
    slots, local = lax.optimization_barrier((slots, local_part(tokens)))
    sends = group_sends(slots, outer_count)
    others = [swap(sends[s], "outer", s + 1) for s in reversed(range(outer_count - 1))][::-1]
    slots = swap_far(scan_slots(slots, others))
    arrived = swap(state_for_neighbour(slots, keep), "inner", 1)
    outs = finish(tokens, local, (*slots, got), scale)
    return tuple(finish(tokens, local, (arrived,), scale, outs))


def solution(mesh):
    spec = P(("outer", "inner"), None)
    return jax.shard_map(
        body, mesh=mesh, in_specs=(spec,) * 4, out_specs=(spec,) * 4, check_vma=False
    )
```

```python
import functools

import jax
import jax.numpy as jnp
from jax import lax
from jax.experimental import pallas as pl
from jax.experimental.pallas import tpu as pltpu
from jax.sharding import PartitionSpec as P

HEAD = 128
PIECES = 4
MIB = 1024 * 1024
ANY = pl.BlockSpec(memory_space=pl.ANY)
VMEM = pl.BlockSpec(memory_space=pltpu.VMEM)
BF16 = jnp.bfloat16
F32 = jnp.float32
SMALL = pltpu.CompilerParams(vmem_limit_bytes=4 * MIB)


def dot(a, b, over_a, over_b):
    return lax.dot_general(
        a, b, (((over_a,), (over_b,)), ((), ())), preferred_element_type=F32
    )


def near_far():
    inner = lax.axis_index("inner")
    return lax.rem(inner, 2), lax.div(inner, 2)


def outer_product(a, b, cols):
    return dot(a[:, cols], b[:, cols], 0, 0).astype(BF16)


def head_columns(side, half, h):
    return pl.ds(pl.multiple_of(side * half + h * HEAD, HEAD), HEAD)


def load_kernel(*refs):
    tokens, held, (out, sems) = refs[:4], refs[4:8], refs[8:]
    half = out.shape[0]
    piece = half // PIECES
    near, _ = near_far()
    other = 1 - near

    def copy(i, side, p):
        cols = pl.ds(pl.multiple_of(side * half + p * piece, piece), piece)
        return pltpu.make_async_copy(
            tokens[i].at[:, cols], held[i].at[:, cols], sems.at[i, int(side is near), p]
        )

    first = [[copy(i, other, p) for i in (1, 2)] for p in range(PIECES)]
    rest = [copy(i, other, p) for i in (0, 3) for p in range(PIECES)]
    rest += [copy(i, near, p) for i in range(4) for p in range(PIECES)]
    for c in sum(first, []) + rest:
        c.start()
    for p, group in enumerate(first):
        for c in group:
            c.wait()
        for h in range(p * piece // HEAD, (p + 1) * piece // HEAD):
            out[h * HEAD : (h + 1) * HEAD] = outer_product(
                held[1], held[2], head_columns(other, half, h)
            )
    for c in rest:
        c.wait()


def load(tokens):
    rows, width = tokens[0].shape
    half = width // 2
    *held, give = pl.pallas_call(
        load_kernel,
        name="load",
        in_specs=[ANY] * 4,
        out_specs=[VMEM] * 5,
        out_shape=[pltpu.VMEM((rows, width), BF16)] * 4 + [pltpu.VMEM((half, HEAD), BF16)],
        scratch_shapes=[pltpu.SemaphoreType.DMA((4, 2, PIECES))],
        cost_estimate=pl.CostEstimate(
            flops=2 * rows * half * HEAD, bytes_accessed=20 * rows * half, transcendentals=0
        ),
        compiler_params=SMALL,
    )(*(pltpu.with_memory_space_constraint(x, pltpu.HBM) for x in tokens))
    return tuple(held), give


def states_kernel(own, *refs):
    half = refs[-1].shape[0]
    near, _ = near_far()
    side = near if own else 1 - near
    outs = refs[len(refs) * 2 // 3 :]
    for n, out in enumerate(outs):
        for h in range(half // HEAD):
            out[h * HEAD : (h + 1) * HEAD] = outer_product(
                refs[2 * n], refs[2 * n + 1], head_columns(side, half, h)
            )


def states(own, *pairs):
    rows, width = pairs[0][0].shape
    half = width // 2
    return pl.pallas_call(
        functools.partial(states_kernel, own),
        name="states",
        in_specs=[VMEM] * (2 * len(pairs)),
        out_specs=[VMEM] * len(pairs),
        out_shape=[jax.ShapeDtypeStruct((half, HEAD), BF16)] * len(pairs),
        cost_estimate=pl.CostEstimate(
            flops=2 * rows * half * HEAD * len(pairs),
            bytes_accessed=6 * rows * half * len(pairs),
            transcendentals=0,
        ),
        compiler_params=SMALL,
    )(*(x for pair in pairs for x in pair))


def pair_kernel(keep_ref, got_ref, *slots):
    depth = slots[0].shape[0]
    _, far = near_far()
    for s, slot in enumerate(slots):
        part = pl.ds(pl.multiple_of((far ^ s) * depth, depth), depth)
        slot[...] = (keep_ref[part].astype(F32) + got_ref[part].astype(F32)).astype(BF16)


def pair_slots(keep, got, far_count):
    slot = jax.ShapeDtypeStruct((keep.shape[0] // far_count, HEAD), BF16)
    return pl.pallas_call(
        pair_kernel,
        name="pair",
        in_specs=[VMEM] * 2,
        out_specs=[VMEM] * far_count,
        out_shape=[slot] * far_count,
        compiler_params=SMALL,
    )(keep, got)


def total_kernel(*refs):
    total = refs[0][...].astype(F32)
    for slot in refs[1:-1]:
        total += slot[...].astype(F32)
    refs[-1][...] = total.astype(BF16)


def total_of(slots):
    return pl.pallas_call(
        total_kernel,
        name="total",
        in_specs=[VMEM] * len(slots),
        out_specs=VMEM,
        out_shape=jax.ShapeDtypeStruct(slots[0].shape, BF16),
        compiler_params=SMALL,
    )(*slots)


def scan_kernel(later, far_count, *refs):
    slots, others, outs = refs[:far_count], refs[far_count:-far_count], refs[-far_count:]
    _, far = near_far()
    base = jnp.zeros(slots[0].shape, F32)
    for other in others:
        base += other[...].astype(F32)
    terms = [slot[...].astype(F32) for slot in slots]
    for s, out in enumerate(outs):
        total = base
        for t, term in enumerate(terms):
            if s != t:
                wanted = (far ^ t) > (far ^ s) if later else (far ^ t) < (far ^ s)
                total += jnp.where(wanted, term, 0.0)
        out[...] = total.astype(BF16)


def scan_slots(later, slots, others):
    far_count, slot = len(slots), jax.ShapeDtypeStruct(slots[0].shape, BF16)
    return pl.pallas_call(
        functools.partial(scan_kernel, later, far_count),
        name="scan",
        in_specs=[VMEM] * (far_count + len(others)),
        out_specs=[VMEM] * far_count,
        out_shape=[slot] * far_count,
        compiler_params=SMALL,
    )(*slots, *others)


def expand(slots, out, extra, wanted):
    depth = slots[0].shape[0]
    _, far = near_far()
    for s, slot in enumerate(slots):
        part = pl.ds(pl.multiple_of((far ^ s) * depth, depth), depth)

        @pl.when(wanted)
        def _():
            out[part] = (slot[...].astype(F32) + extra[part].astype(F32)).astype(BF16)

        @pl.when(jnp.logical_not(wanted))
        def _():
            out[part] = slot[...]


def theirs_kernel(later, *refs):
    slots, (keep, out) = refs[:-2], refs[-2:]
    near, _ = near_far()
    expand(slots, out, keep, near == int(later))


def state_for_neighbour(later, slots, keep):
    return pl.pallas_call(
        functools.partial(theirs_kernel, later),
        name="theirs",
        in_specs=[VMEM] * (len(slots) + 1),
        out_specs=VMEM,
        out_shape=jax.ShapeDtypeStruct(keep.shape, BF16),
        compiler_params=SMALL,
    )(*slots, keep)


def local_kernel(q_ref, k_ref, v_ref, d_ref, att_ref, gq_ref, gv_ref, gk_ref):
    rows, width = q_ref.shape
    at = lax.broadcasted_iota(jnp.int32, (rows, rows), 0)
    to = lax.broadcasted_iota(jnp.int32, (rows, rows), 1)
    lower = at >= to

    def masked(a, b):
        return jnp.where(lower, dot(a, b, 1, 1), 0.0).astype(BF16)

    def second(cols, a, b):
        att_ref[:, cols] = dot(a, v_ref[:, cols], 1, 0)
        gq_ref[:, cols] = dot(b, k_ref[:, cols], 1, 0)
        gv_ref[:, cols] = dot(a, d_ref[:, cols], 0, 0)
        gk_ref[:, cols] = dot(b, q_ref[:, cols], 0, 0)

    last = None
    for h in range(width // HEAD):
        cols = slice(h * HEAD, (h + 1) * HEAD)
        a, b = masked(q_ref[:, cols], k_ref[:, cols]), masked(d_ref[:, cols], v_ref[:, cols])
        if last:
            second(*last)
        last = (cols, a, b)
    second(*last)


def local_part(tokens):
    rows, width = tokens[0].shape
    return pl.pallas_call(
        local_kernel,
        name="local",
        in_specs=[VMEM] * 4,
        out_specs=[VMEM] * 4,
        out_shape=[jax.ShapeDtypeStruct((rows, width), F32)] * 4,
        cost_estimate=pl.CostEstimate(
            flops=16 * rows * width * HEAD, bytes_accessed=24 * rows * width, transcendentals=0
        ),
        compiler_params=SMALL,
    )(*tokens)


def finish_kernel(scale, later, slot_count, *refs):
    a_ref, b_ref, *local = refs[:4]
    refs = refs[4:]
    held, sems = refs[-2:]
    near, _ = near_far()
    if slot_count:
        outs, state, side = refs[-5:-3], refs[-3], near
        expand(refs[:slot_count], state, refs[slot_count], near == 1 - int(later))
    else:
        outs, state, side = refs[-4:-2], refs[0], 1 - near
    half = held.shape[2]
    piece = half // PIECES
    copies = []
    for p in range(PIECES):
        for h in range(p * piece // HEAD, (p + 1) * piece // HEAD):
            into, cols = slice(h * HEAD, (h + 1) * HEAD), head_columns(side, half, h)
            x = state[into]
            parts = dot(a_ref[:, cols], x, 1, 0), dot(b_ref[:, cols], x, 1, 1)
            for i, part in enumerate(parts):
                held[i, :, into] = (scale * (part + local[i][:, cols])).astype(BF16)
        for i, out in enumerate(outs):
            there = pl.ds(pl.multiple_of(side * half + p * piece, piece), piece)
            copy = pltpu.make_async_copy(
                held.at[i, :, pl.ds(p * piece, piece)], out.at[:, there], sems.at[i, p]
            )
            copy.start()
            copies.append(copy)
    for copy in copies:
        copy.wait()


def finish(later, tokens, local, states, scale, before=()):
    rows, width = tokens[0].shape
    half = width // 2
    slot_count = 0 if before else len(states) - 1
    out = jax.ShapeDtypeStruct((rows, width), BF16)
    scratch = [pltpu.VMEM((half, HEAD), BF16)] if slot_count else []
    return pl.pallas_call(
        functools.partial(finish_kernel, scale, later, slot_count),
        name="finish",
        in_specs=[VMEM] * (4 + len(states)) + [ANY] * len(before),
        out_specs=[ANY] * 2,
        out_shape=[out] * 2,
        scratch_shapes=scratch
        + [pltpu.VMEM((2, rows, half), BF16), pltpu.SemaphoreType.DMA((2, PIECES))],
        input_output_aliases={4 + len(states) + i: i for i in range(len(before))},
        cost_estimate=pl.CostEstimate(
            flops=2 * rows * width * HEAD, bytes_accessed=9 * rows * width, transcendentals=0
        ),
        compiler_params=SMALL,
    )(*tokens, *local, *states, *before)


def swap(x, axis, bits):
    return lax.ppermute(x, axis, [(i, i ^ bits) for i in range(lax.axis_size(axis))])


def swap_far(slots):
    return [slots[0]] + [swap(slots[s], "inner", 2 * s) for s in range(1, len(slots))]


def from_groups(later, total):
    count = lax.axis_size("outer")
    pairs = [[(z, z ^ s) for z in range(count) if (z ^ s < z) == later] for s in range(1, count)]
    return [lax.ppermute(total, "outer", p) for p in pairs]


def body(queries, keys, values, cotangent):
    count = lax.axis_size("inner")
    outer_count = lax.axis_size("outer")
    scale = float(HEAD * queries.shape[0] * count * outer_count) ** (-0.5)
    tokens, give_s = load((queries, keys, values, cotangent))
    q, k, v, d = tokens
    got_s = swap(give_s, "inner", 1)
    got_g = swap(*states(False, (q, d)), "inner", 1)
    keep_s, keep_g = states(True, (k, v), (q, d))
    slots_s = swap_far(pair_slots(keep_s, got_s, count // 2))
    slots_g = swap_far(pair_slots(keep_g, got_g, count // 2))
    others_s = from_groups(False, total_of(slots_s))
    others_g = from_groups(True, total_of(slots_g))
    others_s, local = lax.optimization_barrier((others_s, local_part(tokens)))
    slots_s = swap_far(scan_slots(False, slots_s, others_s))
    slots_g = swap_far(scan_slots(True, slots_g, others_g))
    arrived_s = swap(state_for_neighbour(False, slots_s, keep_s), "inner", 1)
    outs_s = finish(False, (q, d), local[:2], (*slots_s, got_s), scale)
    outs_s = finish(False, (q, d), local[:2], (arrived_s,), scale, outs_s)
    slots_g, (att, gq) = lax.optimization_barrier((slots_g, tuple(outs_s)))
    arrived_g = swap(state_for_neighbour(True, slots_g, keep_g), "inner", 1)
    outs_g = finish(True, (k, v), local[2:], (*slots_g, got_g), scale)
    gv, gk = finish(True, (k, v), local[2:], (arrived_g,), scale, outs_g)
    return att, gq, gk, gv


def solution(mesh):
    spec = P(("outer", "inner"), None)
    return jax.shard_map(
        body, mesh=mesh, in_specs=(spec,) * 4, out_specs=(spec,) * 4, check_vma=False
    )
```

```python
import functools

import jax
import jax.numpy as jnp
from jax import lax
from jax.experimental import pallas as pl
from jax.experimental.pallas import tpu as pltpu
from jax.sharding import PartitionSpec as P

HEAD = 128
PIECES = 4
MIB = 1024 * 1024
ANY = pl.BlockSpec(memory_space=pl.ANY)
VMEM = pl.BlockSpec(memory_space=pltpu.VMEM)
BF16 = jnp.bfloat16
F32 = jnp.float32
SMALL = pltpu.CompilerParams(vmem_limit_bytes=4 * MIB)


def dot(a, b, over_a, over_b):
    return lax.dot_general(
        a, b, (((over_a,), (over_b,)), ((), ())), preferred_element_type=F32
    )


def near_far():
    inner = lax.axis_index("inner")
    return lax.rem(inner, 2), lax.div(inner, 2)


def partner(s, far_count):
    return (s & ~3) | (0, 3, 1, 2)[s & 3] if far_count >= 4 else s


def slot_rows(s, far, far_count, depth):
    low, high = far & 1, (far >> 1) & 1
    place = (far - low - 2 * high) + 2 * (low ^ high) + high if far_count >= 4 else far
    return pl.ds(pl.multiple_of((place ^ s) * depth, depth), depth)


def distances(outer_count):
    return range(outer_count - 1, 0, -1)


def load_kernel(own, *refs):
    tokens, held, (out, sems) = refs[:4], refs[4:8], refs[8:]
    half = out.shape[1]
    piece = half // PIECES
    near, _ = near_far()
    side = near if own else 1 - near
    copies = [
        [
            pltpu.make_async_copy(
                ref.at[:, pl.ds(pl.multiple_of(side * half + p * piece, piece), piece)],
                to.at[:, pl.ds(p * piece, piece)],
                sems.at[p, i],
            )
            for i, (ref, to) in enumerate(zip(tokens, held))
        ]
        for p in range(PIECES)
    ]
    for group in copies:
        for copy in group:
            copy.start()
    for p, group in enumerate(copies):
        for copy in group:
            copy.wait()
        for h in range(p * piece // HEAD, (p + 1) * piece // HEAD):
            cols = slice(h * HEAD, (h + 1) * HEAD)
            q, k, v, d = (ref[:, cols] for ref in held)
            out[0, cols] = dot(k, v, 0, 0).astype(BF16)
            out[1, cols] = dot(q, d, 0, 0).astype(BF16)


def load(tokens, own):
    rows, width = tokens[0].shape
    half = width // 2
    *held, sums = pl.pallas_call(
        functools.partial(load_kernel, own),
        name="load",
        in_specs=[ANY] * 4,
        out_specs=[VMEM] * 5,
        out_shape=[pltpu.VMEM((rows, half), BF16)] * 4 + [pltpu.VMEM((2, half, HEAD), BF16)],
        scratch_shapes=[pltpu.SemaphoreType.DMA((PIECES, 4))],
        cost_estimate=pl.CostEstimate(
            flops=4 * rows * half * HEAD, bytes_accessed=20 * rows * half, transcendentals=0
        ),
        compiler_params=SMALL,
    )(*(pltpu.with_memory_space_constraint(x, pltpu.HBM) for x in tokens))
    return tuple(held), sums


def pair_kernel(keep_ref, got_ref, *slots):
    depth = slots[0].shape[1]
    _, far = near_far()
    for s, slot in enumerate(slots):
        part = slot_rows(s, far, len(slots), depth)
        for which in range(2):
            both = keep_ref[which, part].astype(F32) + got_ref[which, part].astype(F32)
            slot[which] = both.astype(BF16)


def pair_slots(keep, got, far_count):
    slot = jax.ShapeDtypeStruct((2, keep.shape[1] // far_count, HEAD), BF16)
    return pl.pallas_call(
        pair_kernel,
        name="pair",
        in_specs=[VMEM] * 2,
        out_specs=[VMEM] * far_count,
        out_shape=[slot] * far_count,
        compiler_params=SMALL,
    )(keep, got)


def totals_kernel(far_count, *refs):
    slots, sends = refs[:far_count], refs[far_count:]
    outer = lax.axis_index("outer")
    totals = []
    for which in range(2):
        total = slots[0][which].astype(F32)
        for slot in slots[1:]:
            total += slot[which].astype(F32)
        totals.append(total.astype(BF16))
    for s, send in zip(distances(len(sends) + 1), sends):
        upward = (outer ^ s) > outer
        send[...] = jnp.where(upward, totals[0], totals[1])


def group_sends(slots, outer_count):
    send = jax.ShapeDtypeStruct(slots[0].shape[1:], BF16)
    return pl.pallas_call(
        functools.partial(totals_kernel, len(slots)),
        name="totals",
        in_specs=[VMEM] * len(slots),
        out_specs=[VMEM] * (outer_count - 1),
        out_shape=[send] * (outer_count - 1),
        compiler_params=SMALL,
    )(*slots)


def scan_kernel(far_count, *refs):
    slots, others, outs = refs[:far_count], refs[far_count:-far_count], refs[-far_count:]
    outer = lax.axis_index("outer")
    _, far = near_far()
    for which in range(2):
        base = jnp.zeros(slots[0].shape[1:], F32)
        for s, other in zip(distances(len(others) + 1), others):
            below = (outer ^ s) < outer
            wanted = below if which == 0 else jnp.logical_not(below)
            base += jnp.where(wanted, other[...].astype(F32), 0.0)
        terms = [slot[which].astype(F32) for slot in slots]
        for s, out in enumerate(outs):
            total = base
            for t, term in enumerate(terms):
                if s != t:
                    below = (far ^ partner(t, far_count)) < (far ^ partner(s, far_count))
                    wanted = below if which == 0 else jnp.logical_not(below)
                    total += jnp.where(wanted, term, 0.0)
            out[which] = total.astype(BF16)


def scan_slots(slots, others):
    far_count, slot = len(slots), jax.ShapeDtypeStruct(slots[0].shape, BF16)
    return pl.pallas_call(
        functools.partial(scan_kernel, far_count),
        name="scan",
        in_specs=[VMEM] * (far_count + len(others)),
        out_specs=[VMEM] * far_count,
        out_shape=[slot] * far_count,
        compiler_params=SMALL,
    )(*slots, *others)


def expand(slots, out, extras, extra_which):
    depth = slots[0].shape[1]
    _, far = near_far()
    for s, slot in enumerate(slots):
        part = slot_rows(s, far, len(slots), depth)
        for which in range(2):
            @pl.when(extra_which == which)
            def _():
                out[which, part] = (slot[which].astype(F32) + extras[which, part].astype(F32)).astype(BF16)

            @pl.when(extra_which != which)
            def _():
                out[which, part] = slot[which]


def theirs_kernel(*refs):
    slots, (keep, out) = refs[:-2], refs[-2:]
    near, _ = near_far()
    expand(slots, out, keep, near)


def state_for_neighbour(slots, keep):
    return pl.pallas_call(
        theirs_kernel,
        name="theirs",
        in_specs=[VMEM] * (len(slots) + 1),
        out_specs=VMEM,
        out_shape=jax.ShapeDtypeStruct(keep.shape, BF16),
        compiler_params=SMALL,
    )(*slots, keep)


def local_kernel(*refs):
    rows, half = refs[0].shape
    at = lax.broadcasted_iota(jnp.int32, (rows, rows), 0)
    to = lax.broadcasted_iota(jnp.int32, (rows, rows), 1)
    lower = at >= to

    def masked(a, b):
        return jnp.where(lower, dot(a, b, 1, 1), 0.0).astype(BF16)

    def second(at, cols, a, b):
        q, k, v, d = (ref[:, cols] for ref in refs[at : at + 4])
        att, gq, gk, gv = refs[8 + at : 12 + at]
        att[:, cols] = dot(a, v, 1, 0)
        gq[:, cols] = dot(b, k, 1, 0)
        gk[:, cols] = dot(b, q, 0, 0)
        gv[:, cols] = dot(a, d, 0, 0)

    last = None
    for at in (0, 4):
        for h in range(half // HEAD):
            cols = slice(h * HEAD, (h + 1) * HEAD)
            q, k, v, d = (ref[:, cols] for ref in refs[at : at + 4])
            a, b = masked(q, k), masked(d, v)
            if last:
                second(*last)
            last = (at, cols, a, b)
    second(*last)


def local_part(own, other):
    rows, half = own[0].shape
    outs = pl.pallas_call(
        local_kernel,
        name="local",
        in_specs=[VMEM] * 8,
        out_specs=[VMEM] * 8,
        out_shape=[jax.ShapeDtypeStruct((rows, half), F32)] * 8,
        cost_estimate=pl.CostEstimate(
            flops=24 * rows * half * HEAD, bytes_accessed=48 * rows * half, transcendentals=0
        ),
        compiler_params=SMALL,
    )(*own, *other)
    return outs[:4], outs[4:]


def finish_kernel(scale, slot_count, *refs):
    tokens, local, refs = refs[:4], refs[4:8], refs[8:]
    held, sems = refs[-2:]
    near, _ = near_far()
    if slot_count:
        outs, states = refs[-7:-3], refs[-3]
        expand(refs[:slot_count], states, refs[slot_count], 1 - near)
        side = near
    else:
        outs, states, side = refs[-6:-2], refs[0], 1 - near
    half = held.shape[2]
    piece = half // PIECES
    copies = []
    for p in range(PIECES):
        for h in range(p * piece // HEAD, (p + 1) * piece // HEAD):
            into = slice(h * HEAD, (h + 1) * HEAD)
            q, k, v, d = (ref[:, into] for ref in tokens)
            s, g = states[0, into], states[1, into]
            parts = (dot(q, s, 1, 0), dot(d, s, 1, 1), dot(v, g, 1, 1), dot(k, g, 1, 0))
            for i, part in enumerate(parts):
                held[i, :, into] = (scale * (part + local[i][:, into])).astype(BF16)
        for i, out in enumerate(outs):
            there = pl.ds(pl.multiple_of(side * half + p * piece, piece), piece)
            copy = pltpu.make_async_copy(
                held.at[i, :, pl.ds(p * piece, piece)], out.at[:, there], sems.at[i, p]
            )
            copy.start()
            copies.append(copy)
    for copy in copies:
        copy.wait()


def finish(tokens, local, states, scale, before=()):
    rows, half = tokens[0].shape
    width = 2 * half
    slot_count = 0 if before else len(states) - 1
    out = jax.ShapeDtypeStruct((rows, width), BF16)
    scratch = [pltpu.VMEM((2, half, HEAD), BF16)] if slot_count else []
    return pl.pallas_call(
        functools.partial(finish_kernel, scale, slot_count),
        name="finish",
        in_specs=[VMEM] * (8 + len(states)) + [ANY] * len(before),
        out_specs=[ANY] * 4,
        out_shape=[out] * 4,
        scratch_shapes=scratch
        + [pltpu.VMEM((4, rows, half), BF16), pltpu.SemaphoreType.DMA((4, PIECES))],
        input_output_aliases={8 + len(states) + i: i for i in range(len(before))},
        cost_estimate=pl.CostEstimate(
            flops=4 * rows * width * HEAD, bytes_accessed=17 * rows * width, transcendentals=0
        ),
        compiler_params=SMALL,
    )(*tokens, *local, *states, *before)


def swap(x, axis, bits):
    return lax.ppermute(x, axis, [(i, i ^ bits) for i in range(lax.axis_size(axis))])


def swap_far(slots):
    count = len(slots)
    return [slots[0]] + [swap(slots[s], "inner", 2 * partner(s, count)) for s in range(1, count)]


def body(queries, keys, values, cotangent):
    tokens = (queries, keys, values, cotangent)
    count = lax.axis_size("inner")
    outer_count = lax.axis_size("outer")
    scale = float(HEAD * queries.shape[0] * count * outer_count) ** (-0.5)
    other, give = load(tokens, False)
    got = swap(give, "inner", 1)
    own, keep = load(tokens, True)
    slots = swap_far(pair_slots(keep, got, count // 2))
    slots, local = lax.optimization_barrier((slots, local_part(own, other)))
    sends = group_sends(slots, outer_count)
    others = [swap(send, "outer", s) for s, send in zip(distances(outer_count), sends)]
    slots = swap_far(scan_slots(slots, others))
    arrived = swap(state_for_neighbour(slots, keep), "inner", 1)
    outs = finish(own, local[0], (*slots, got), scale)
    return tuple(finish(other, local[1], (arrived,), scale, outs))


def solution(mesh):
    spec = P(("outer", "inner"), None)
    return jax.shard_map(
        body, mesh=mesh, in_specs=(spec,) * 4, out_specs=(spec,) * 4, check_vma=False
    )
```

```python
import functools

import jax
import jax.numpy as jnp
from jax import lax
from jax.experimental import pallas as pl
from jax.experimental.pallas import tpu as pltpu
from jax.sharding import PartitionSpec as P

HEAD = 128
LOADS = 2
MIB = 1024 * 1024
ANY = pl.BlockSpec(memory_space=pl.ANY)
VMEM = pl.BlockSpec(memory_space=pltpu.VMEM)
BF16 = jnp.bfloat16
F32 = jnp.float32
SMALL = pltpu.CompilerParams(vmem_limit_bytes=4 * MIB)


def dot(a, b, over_a, over_b):
    return lax.dot_general(
        a, b, (((over_a,), (over_b,)), ((), ())), preferred_element_type=F32
    )


def near_far():
    inner = lax.axis_index("inner")
    return lax.rem(inner, 2), lax.div(inner, 2)


def slot_rows(s, far, depth):
    return pl.ds(pl.multiple_of((far ^ s) * depth, depth), depth)


def distances(outer_count):
    return range(outer_count - 1, 0, -1)


def sums_of(tokens, out, heads):
    for h in heads:
        cols = slice(h * HEAD, (h + 1) * HEAD)
        q, k, v, d = (ref[:, cols] for ref in tokens)
        out[0, cols] = dot(k, v, 0, 0).astype(BF16)
        out[1, cols] = dot(q, d, 0, 0).astype(BF16)


def load_kernel(*refs):
    tokens, other, own, (out, sems) = refs[:4], refs[4:8], refs[8:12], refs[12:]
    half = out.shape[1]
    piece = half // LOADS
    near, _ = near_far()

    def copy(i, to, side, p):
        there = pl.ds(pl.multiple_of(side * half + p * piece, piece), piece)
        here = pl.ds(p * piece, piece)
        sem = sems.at[0 if to is other else 1, p, i]
        return pltpu.make_async_copy(tokens[i].at[:, there], to[i].at[:, here], sem)

    first = [[copy(i, other, 1 - near, p) for i in range(4)] for p in range(LOADS)]
    rest = [copy(i, own, near, p) for p in range(LOADS) for i in range(4)]
    for c in sum(first, []) + rest:
        c.start()
    for p, group in enumerate(first):
        for c in group:
            c.wait()
        sums_of(other, out, range(p * piece // HEAD, (p + 1) * piece // HEAD))
    for c in rest:
        c.wait()


def load(tokens):
    rows, width = tokens[0].shape
    half = width // 2
    *held, sums = pl.pallas_call(
        load_kernel,
        name="load",
        in_specs=[ANY] * 4,
        out_specs=[VMEM] * 9,
        out_shape=[pltpu.VMEM((rows, half), BF16)] * 8 + [pltpu.VMEM((2, half, HEAD), BF16)],
        scratch_shapes=[pltpu.SemaphoreType.DMA((2, LOADS, 4))],
        cost_estimate=pl.CostEstimate(
            flops=4 * rows * half * HEAD, bytes_accessed=40 * rows * half, transcendentals=0
        ),
        compiler_params=SMALL,
    )(*(pltpu.with_memory_space_constraint(x, pltpu.HBM) for x in tokens))
    return tuple(held[:4]), tuple(held[4:]), sums


def keep_kernel(*refs):
    sums_of(refs[:4], refs[4], range(refs[0].shape[1] // HEAD))


def keep_sums(own):
    rows, half = own[0].shape
    return pl.pallas_call(
        keep_kernel,
        name="keep",
        in_specs=[VMEM] * 4,
        out_specs=VMEM,
        out_shape=jax.ShapeDtypeStruct((2, half, HEAD), BF16),
        cost_estimate=pl.CostEstimate(
            flops=4 * rows * half * HEAD, bytes_accessed=12 * rows * half, transcendentals=0
        ),
        compiler_params=SMALL,
    )(*own)


def pair_kernel(keep_ref, got_ref, *slots):
    depth = slots[0].shape[1]
    _, far = near_far()
    for s, slot in enumerate(slots):
        part = slot_rows(s, far, depth)
        for which in range(2):
            both = keep_ref[which, part].astype(F32) + got_ref[which, part].astype(F32)
            slot[which] = both.astype(BF16)


def pair_slots(keep, got, far_count):
    slot = jax.ShapeDtypeStruct((2, keep.shape[1] // far_count, HEAD), BF16)
    return pl.pallas_call(
        pair_kernel,
        name="pair",
        in_specs=[VMEM] * 2,
        out_specs=[VMEM] * far_count,
        out_shape=[slot] * far_count,
        compiler_params=SMALL,
    )(keep, got)


def totals_kernel(far_count, *refs):
    slots, sends = refs[:far_count], refs[far_count:]
    outer = lax.axis_index("outer")
    totals = []
    for which in range(2):
        total = slots[0][which].astype(F32)
        for slot in slots[1:]:
            total += slot[which].astype(F32)
        totals.append(total.astype(BF16))
    for s, send in zip(distances(len(sends) + 1), sends):
        upward = (outer ^ s) > outer
        send[...] = jnp.where(upward, totals[0], totals[1])


def group_sends(slots, outer_count):
    send = jax.ShapeDtypeStruct(slots[0].shape[1:], BF16)
    return pl.pallas_call(
        functools.partial(totals_kernel, len(slots)),
        name="totals",
        in_specs=[VMEM] * len(slots),
        out_specs=[VMEM] * (outer_count - 1),
        out_shape=[send] * (outer_count - 1),
        compiler_params=SMALL,
    )(*slots)


def scan_kernel(far_count, *refs):
    slots, others, outs = refs[:far_count], refs[far_count:-far_count], refs[-far_count:]
    outer = lax.axis_index("outer")
    _, far = near_far()
    for which in range(2):
        base = jnp.zeros(slots[0].shape[1:], F32)
        for s, other in zip(distances(len(others) + 1), others):
            below = (outer ^ s) < outer
            wanted = below if which == 0 else jnp.logical_not(below)
            base += jnp.where(wanted, other[...].astype(F32), 0.0)
        terms = [slot[which].astype(F32) for slot in slots]
        for s, out in enumerate(outs):
            total = base
            for t, term in enumerate(terms):
                if s != t:
                    below = (far ^ t) < (far ^ s)
                    wanted = below if which == 0 else jnp.logical_not(below)
                    total += jnp.where(wanted, term, 0.0)
            out[which] = total.astype(BF16)


def scan_slots(slots, others):
    far_count, slot = len(slots), jax.ShapeDtypeStruct(slots[0].shape, BF16)
    return pl.pallas_call(
        functools.partial(scan_kernel, far_count),
        name="scan",
        in_specs=[VMEM] * (far_count + len(others)),
        out_specs=[VMEM] * far_count,
        out_shape=[slot] * far_count,
        compiler_params=SMALL,
    )(*slots, *others)


def expand(blocks, slots, out, extras, extra_which):
    depth = slots[0].shape[1]
    size = len(slots) // len(blocks)
    _, far = near_far()
    rows = []
    for n, block in enumerate(blocks):
        row = lax.div(far, size) ^ block
        rows.append(pl.multiple_of(row * size * depth, size * depth))
        for s in range(size):
            at = lax.rem(far ^ s, size) * depth
            into = pl.ds(pl.multiple_of(n * size * depth + at, depth), depth)
            there = pl.ds(pl.multiple_of(rows[n] + at, depth), depth)
            slot = slots[n * size + s]
            for which in range(2):

                @pl.when(extra_which == which)
                def _():
                    total = slot[which].astype(F32) + extras[which, there].astype(F32)
                    out[which, into] = total.astype(BF16)

                @pl.when(extra_which != which)
                def _():
                    out[which, into] = slot[which]

    return rows


def theirs_kernel(blocks, *refs):
    slots, (keep, out) = refs[:-2], refs[-2:]
    near, _ = near_far()
    expand(blocks, slots, out, keep, near)


def state_for_neighbour(blocks, slots, keep):
    rows = len(slots) * slots[0].shape[1]
    return pl.pallas_call(
        functools.partial(theirs_kernel, blocks),
        name="theirs",
        in_specs=[VMEM] * (len(slots) + 1),
        out_specs=VMEM,
        out_shape=jax.ShapeDtypeStruct((2, rows, HEAD), BF16),
        compiler_params=SMALL,
    )(*slots, keep)


def local_kernel(*refs):
    rows, half = refs[0].shape
    at = lax.broadcasted_iota(jnp.int32, (rows, rows), 0)
    to = lax.broadcasted_iota(jnp.int32, (rows, rows), 1)
    lower = at >= to

    def masked(a, b):
        return jnp.where(lower, dot(a, b, 1, 1), 0.0).astype(BF16)

    def second(at, cols, a, b):
        q, k, v, d = (ref[:, cols] for ref in refs[at : at + 4])
        att, gq, gk, gv = refs[8 + at : 12 + at]
        att[:, cols] = dot(a, v, 1, 0)
        gq[:, cols] = dot(b, k, 1, 0)
        gk[:, cols] = dot(b, q, 0, 0)
        gv[:, cols] = dot(a, d, 0, 0)

    last = None
    for at in (0, 4):
        for h in range(half // HEAD):
            cols = slice(h * HEAD, (h + 1) * HEAD)
            q, k, v, d = (ref[:, cols] for ref in refs[at : at + 4])
            a, b = masked(q, k), masked(d, v)
            if last:
                second(*last)
            last = (at, cols, a, b)
    second(*last)


def local_part(own, other):
    rows, half = own[0].shape
    outs = pl.pallas_call(
        local_kernel,
        name="local",
        in_specs=[VMEM] * 8,
        out_specs=[VMEM] * 8,
        out_shape=[jax.ShapeDtypeStruct((rows, half), F32)] * 8,
        cost_estimate=pl.CostEstimate(
            flops=24 * rows * half * HEAD, bytes_accessed=48 * rows * half, transcendentals=0
        ),
        compiler_params=SMALL,
    )(*own, *other)
    return outs[:4], outs[4:]


def finish_kernel(scale, blocks, size, before_count, *refs):
    tokens, local, refs = refs[:4], refs[4:8], refs[8:]
    held, sems = refs[-2:]
    half = tokens[0].shape[1]
    width = held.shape[2] // len(blocks)
    near, far = near_far()
    if size:
        slot_count = len(blocks) * size
        states, side = refs[-3], near
        rows = expand(blocks, refs[:slot_count], states, refs[slot_count], 1 - near)
        outs = refs[slot_count + 1 + before_count : -3]
    else:
        states, side = refs[0], 1 - near
        count = half // width
        share = lax.axis_size("inner") // 2 // count
        rows = [pl.multiple_of((lax.div(far, share) ^ b) * width, width) for b in blocks]
        outs = refs[1 + before_count : -2]
    copies = []
    for n, row in enumerate(rows):
        for h in range(width // HEAD):
            into = slice(n * width + h * HEAD, n * width + (h + 1) * HEAD)
            cols = pl.ds(pl.multiple_of(row + h * HEAD, HEAD), HEAD)
            q, k, v, d = (ref[:, cols] for ref in tokens)
            s, g = states[0, into], states[1, into]
            parts = (dot(q, s, 1, 0), dot(d, s, 1, 1), dot(v, g, 1, 1), dot(k, g, 1, 0))
            for i, part in enumerate(parts):
                held[i, :, into] = (scale * (part + local[i][:, cols])).astype(BF16)
        for i, out in enumerate(outs):
            there = pl.ds(pl.multiple_of(side * half + row, width), width)
            copy = pltpu.make_async_copy(
                held.at[i, :, pl.ds(n * width, width)], out.at[:, there], sems.at[i, n]
            )
            copy.start()
            copies.append(copy)
    for copy in copies:
        copy.wait()


def finish(blocks, tokens, local, states, scale, before=()):
    rows, half = tokens[0].shape
    slots = states[:-1]
    held = len(slots) * slots[0].shape[1] if slots else states[0].shape[1]
    out = jax.ShapeDtypeStruct((rows, 2 * half), BF16)
    scratch = [pltpu.VMEM((2, held, HEAD), BF16)] if slots else []
    return pl.pallas_call(
        functools.partial(finish_kernel, scale, blocks, len(slots) // len(blocks), len(before)),
        name="finish",
        in_specs=[VMEM] * (8 + len(states)) + [ANY] * len(before),
        out_specs=[ANY] * 4,
        out_shape=[out] * 4,
        scratch_shapes=scratch
        + [pltpu.VMEM((4, rows, held), BF16), pltpu.SemaphoreType.DMA((4, len(blocks)))],
        input_output_aliases={8 + len(states) + i: i for i in range(len(before))},
        cost_estimate=pl.CostEstimate(
            flops=8 * rows * held * HEAD, bytes_accessed=34 * rows * held, transcendentals=0
        ),
        compiler_params=SMALL,
    )(*tokens, *local, *states, *before)


def swap(x, axis, bits):
    return lax.ppermute(x, axis, [(i, i ^ bits) for i in range(lax.axis_size(axis))])


def swap_far(slots):
    return [slots[0]] + [swap(slots[s], "inner", 2 * s) for s in range(1, len(slots))]


def body(queries, keys, values, cotangent):
    tokens = (queries, keys, values, cotangent)
    count = lax.axis_size("inner")
    outer_count = lax.axis_size("outer")
    scale = float(HEAD * queries.shape[0] * count * outer_count) ** (-0.5)
    other, own, give = load(tokens)
    got = swap(give, "inner", 1)
    keep = keep_sums(own)
    slots = swap_far(pair_slots(keep, got, count // 2))
    slots, local = lax.optimization_barrier((slots, local_part(own, other)))
    sends = group_sends(slots, outer_count)
    others = [swap(send, "outer", s) for s, send in zip(distances(outer_count), sends)]
    slots = swap_far(scan_slots(slots, others))
    size = max(1, HEAD // slots[0].shape[1])
    blocks = len(slots) // size
    outs = ()
    for chosen in (range(1), range(1, blocks)):
        part = slots[chosen[0] * size : (chosen[-1] + 1) * size]
        if outs:
            part, outs = lax.optimization_barrier((part, outs))
        arrived = swap(state_for_neighbour(chosen, part, keep), "inner", 1)
        outs = finish(chosen, own, local[0], (*part, got), scale, outs)
        outs = finish(chosen, other, local[1], (arrived,), scale, outs)
    return tuple(outs)


def solution(mesh):
    spec = P(("outer", "inner"), None)
    return jax.shard_map(
        body, mesh=mesh, in_specs=(spec,) * 4, out_specs=(spec,) * 4, check_vma=False
    )
```

```python
import functools

import jax
import jax.numpy as jnp
from jax import lax
from jax.experimental import pallas as pl
from jax.experimental.pallas import tpu as pltpu
from jax.sharding import PartitionSpec as P

HEAD = 128
PIECES = 2
MIB = 1024 * 1024
ANY = pl.BlockSpec(memory_space=pl.ANY)
VMEM = pl.BlockSpec(memory_space=pltpu.VMEM)
BF16 = jnp.bfloat16
F32 = jnp.float32
SMALL = pltpu.CompilerParams(vmem_limit_bytes=4 * MIB)


def dot(a, b, over_a, over_b):
    return lax.dot_general(
        a, b, (((over_a,), (over_b,)), ((), ())), preferred_element_type=F32
    )


def near_far():
    inner = lax.axis_index("inner")
    return lax.rem(inner, 2), lax.div(inner, 2)


def slot_rows(s, far, depth):
    return pl.ds(pl.multiple_of((far ^ s) * depth, depth), depth)


def distances(outer_count):
    return range(outer_count - 1, 0, -1)


def sums_of(tokens, out):
    q, k, v, d = tokens
    for h in range(out.shape[1] // HEAD):
        cols = slice(h * HEAD, (h + 1) * HEAD)
        out[0, cols] = dot(k[:, cols], v[:, cols], 0, 0).astype(BF16)
        out[1, cols] = dot(q[:, cols], d[:, cols], 0, 0).astype(BF16)


def load_kernel(*refs):
    tokens, held, (out, sems) = refs[:4], refs[4:20], refs[20:]
    part = out.shape[1]
    near, _ = near_far()
    copies = []
    for n in range(16):
        side = 1 - near if n < 8 else near
        there = pl.ds(pl.multiple_of((side * 2 + n // 4 % 2) * part, part), part)
        copies.append(pltpu.make_async_copy(tokens[n % 4].at[:, there], held[n], sems.at[n]))
    for copy in copies:
        copy.start()
    for copy in copies[:4]:
        copy.wait()
    sums_of(held[:4], out)
    for copy in copies[4:]:
        copy.wait()


def load(tokens):
    rows, width = tokens[0].shape
    part = width // 4
    *held, sums = pl.pallas_call(
        load_kernel,
        name="load",
        in_specs=[ANY] * 4,
        out_specs=[VMEM] * 17,
        out_shape=[pltpu.VMEM((rows, part), BF16)] * 16 + [pltpu.VMEM((2, part, HEAD), BF16)],
        scratch_shapes=[pltpu.SemaphoreType.DMA((16,))],
        cost_estimate=pl.CostEstimate(
            flops=4 * rows * part * HEAD, bytes_accessed=40 * rows * part, transcendentals=0
        ),
        compiler_params=SMALL,
    )(*(pltpu.with_memory_space_constraint(x, pltpu.HBM) for x in tokens))
    return (held[:4], held[4:8]), (held[8:12], held[12:]), sums


def sums_kernel(*refs):
    outs = refs[len(refs) * 4 // 5 :]
    for n, out in enumerate(outs):
        sums_of(refs[4 * n : 4 * n + 4], out)


def sums(*parts):
    rows, part = parts[0][0].shape
    return pl.pallas_call(
        sums_kernel,
        name="sums",
        in_specs=[VMEM] * (4 * len(parts)),
        out_specs=[VMEM] * len(parts),
        out_shape=[jax.ShapeDtypeStruct((2, part, HEAD), BF16)] * len(parts),
        cost_estimate=pl.CostEstimate(
            flops=4 * rows * part * HEAD, bytes_accessed=12 * rows * part, transcendentals=0
        ),
        compiler_params=SMALL,
    )(*(x for tokens in parts for x in tokens))


def pair_kernel(after, keep_ref, got_ref, *refs):
    slots = refs[after:]
    depth = slots[0].shape[1]
    _, far = near_far()
    for s, slot in enumerate(slots):
        part = slot_rows(s, far, depth)
        for which in range(2):
            both = keep_ref[which, part].astype(F32) + got_ref[which, part].astype(F32)
            slot[which] = both.astype(BF16)


def pair_slots(keep, got, far_count, after):
    slot = jax.ShapeDtypeStruct((2, keep.shape[1] // far_count, HEAD), BF16)
    return pl.pallas_call(
        functools.partial(pair_kernel, len(after)),
        name="pair",
        in_specs=[VMEM] * 2 + [ANY] * len(after),
        out_specs=[VMEM] * far_count,
        out_shape=[slot] * far_count,
        compiler_params=SMALL,
    )(keep, got, *after)


def totals_kernel(far_count, after, *refs):
    slots, sends = refs[:far_count], refs[far_count + after :]
    outer = lax.axis_index("outer")
    totals = []
    for which in range(2):
        total = slots[0][which].astype(F32)
        for slot in slots[1:]:
            total += slot[which].astype(F32)
        totals.append(total.astype(BF16))
    for s, send in zip(distances(len(sends) + 1), sends):
        upward = (outer ^ s) > outer
        send[...] = jnp.where(upward, totals[0], totals[1])


def group_sends(slots, outer_count, after):
    send = jax.ShapeDtypeStruct(slots[0].shape[1:], BF16)
    return pl.pallas_call(
        functools.partial(totals_kernel, len(slots), len(after)),
        name="totals",
        in_specs=[VMEM] * len(slots) + [ANY] * len(after),
        out_specs=[VMEM] * (outer_count - 1),
        out_shape=[send] * (outer_count - 1),
        compiler_params=SMALL,
    )(*slots, *after)


def scan_kernel(far_count, others_count, *refs):
    slots, outs = refs[:far_count], refs[-far_count:]
    others = refs[far_count : far_count + others_count]
    outer = lax.axis_index("outer")
    _, far = near_far()
    for which in range(2):
        base = jnp.zeros(slots[0].shape[1:], F32)
        for s, other in zip(distances(len(others) + 1), others):
            below = (outer ^ s) < outer
            wanted = below if which == 0 else jnp.logical_not(below)
            base += jnp.where(wanted, other[...].astype(F32), 0.0)
        terms = [slot[which].astype(F32) for slot in slots]
        for s, out in enumerate(outs):
            total = base
            for t, term in enumerate(terms):
                if s != t:
                    below = (far ^ t) < (far ^ s)
                    wanted = below if which == 0 else jnp.logical_not(below)
                    total += jnp.where(wanted, term, 0.0)
            out[which] = total.astype(BF16)


def scan_slots(slots, others, after):
    far_count, slot = len(slots), jax.ShapeDtypeStruct(slots[0].shape, BF16)
    return pl.pallas_call(
        functools.partial(scan_kernel, far_count, len(others)),
        name="scan",
        in_specs=[VMEM] * (far_count + len(others)) + [ANY] * len(after),
        out_specs=[VMEM] * far_count,
        out_shape=[slot] * far_count,
        compiler_params=SMALL,
    )(*slots, *others, *after)


def expand(slots, out, extras, extra_which):
    depth = slots[0].shape[1]
    _, far = near_far()
    for s, slot in enumerate(slots):
        part = slot_rows(s, far, depth)
        for which in range(2):

            @pl.when(extra_which == which)
            def _():
                total = slot[which].astype(F32) + extras[which, part].astype(F32)
                out[which, part] = total.astype(BF16)

            @pl.when(extra_which != which)
            def _():
                out[which, part] = slot[which]


def theirs_kernel(far_count, *refs):
    near, _ = near_far()
    expand(refs[:far_count], refs[-1], refs[far_count], near)


def state_for_neighbour(slots, keep, after):
    return pl.pallas_call(
        functools.partial(theirs_kernel, len(slots)),
        name="theirs",
        in_specs=[VMEM] * (len(slots) + 1) + [ANY] * len(after),
        out_specs=VMEM,
        out_shape=jax.ShapeDtypeStruct(keep.shape, BF16),
        compiler_params=SMALL,
    )(*slots, keep, *after)


def local_kernel(*refs):
    count = len(refs) // 2
    rows, part = refs[0].shape
    at = lax.broadcasted_iota(jnp.int32, (rows, rows), 0)
    to = lax.broadcasted_iota(jnp.int32, (rows, rows), 1)
    lower = at >= to

    def masked(a, b):
        return jnp.where(lower, dot(a, b, 1, 1), 0.0).astype(BF16)

    def second(at, cols, a, b):
        q, k, v, d = (ref[:, cols] for ref in refs[at : at + 4])
        att, gq, gk, gv = refs[count + at : count + at + 4]
        att[:, cols] = dot(a, v, 1, 0)
        gq[:, cols] = dot(b, k, 1, 0)
        gk[:, cols] = dot(b, q, 0, 0)
        gv[:, cols] = dot(a, d, 0, 0)

    last = None
    for at in range(0, count, 4):
        for h in range(part // HEAD):
            cols = slice(h * HEAD, (h + 1) * HEAD)
            q, k, v, d = (ref[:, cols] for ref in refs[at : at + 4])
            a, b = masked(q, k), masked(d, v)
            if last:
                second(*last)
            last = (at, cols, a, b)
    second(*last)


def local_part(*parts):
    rows, part = parts[0][0].shape
    count = 4 * len(parts)
    outs = pl.pallas_call(
        local_kernel,
        name="local",
        in_specs=[VMEM] * count,
        out_specs=[VMEM] * count,
        out_shape=[jax.ShapeDtypeStruct((rows, part), F32)] * count,
        cost_estimate=pl.CostEstimate(
            flops=3 * count * rows * part * HEAD,
            bytes_accessed=6 * count * rows * part,
            transcendentals=0,
        ),
        compiler_params=SMALL,
    )(*(x for tokens in parts for x in tokens))
    return [outs[n : n + 4] for n in range(0, count, 4)]


def finish_kernel(scale, at, slot_count, *refs):
    tokens, local, refs = refs[:4], refs[4:8], refs[8:]
    held, sems = refs[-2:]
    near, _ = near_far()
    if slot_count:
        outs, done, states, side = refs[-8:-4], refs[-4], refs[-3], near
        expand(refs[:slot_count], states, refs[slot_count], 1 - near)
    else:
        outs, done, states, side = refs[-7:-3], refs[-3], refs[0], 1 - near
    done[...] = jnp.zeros_like(done)
    part = held.shape[2]
    piece = part // PIECES
    copies = []
    for p in range(PIECES):
        for h in range(p * piece // HEAD, (p + 1) * piece // HEAD):
            cols = slice(h * HEAD, (h + 1) * HEAD)
            q, k, v, d = (ref[:, cols] for ref in tokens)
            s, g = states[0, cols], states[1, cols]
            parts = (dot(q, s, 1, 0), dot(d, s, 1, 1), dot(v, g, 1, 1), dot(k, g, 1, 0))
            for i, x in enumerate(parts):
                held[i, :, cols] = (scale * (x + local[i][:, cols])).astype(BF16)
        for i, out in enumerate(outs):
            first = (side * 2 + at) * part + p * piece
            copy = pltpu.make_async_copy(
                held.at[i, :, pl.ds(p * piece, piece)],
                out.at[:, pl.ds(pl.multiple_of(first, piece), piece)],
                sems.at[i, p],
            )
            copy.start()
            copies.append(copy)
    for copy in copies:
        copy.wait()


def finish(at, tokens, local, states, scale, before):
    rows, part = tokens[0].shape
    slot_count = len(states) - 1
    out = jax.ShapeDtypeStruct((rows, 4 * part), BF16)
    scratch = [pltpu.VMEM((2, part, HEAD), BF16)] if slot_count else []
    return pl.pallas_call(
        functools.partial(finish_kernel, scale, at, slot_count),
        name="finish",
        in_specs=[VMEM] * (8 + len(states)) + [ANY] * len(before),
        out_specs=[ANY] * 4 + [VMEM],
        out_shape=[out] * 4 + [pltpu.VMEM((8, HEAD), F32)],
        scratch_shapes=scratch
        + [pltpu.VMEM((4, rows, part), BF16), pltpu.SemaphoreType.DMA((4, PIECES))],
        input_output_aliases={8 + len(states) + i: i for i in range(len(before))},
        cost_estimate=pl.CostEstimate(
            flops=8 * rows * part * HEAD, bytes_accessed=34 * rows * part, transcendentals=0
        ),
        compiler_params=SMALL,
    )(*tokens, *local, *states, *before)


def swap(x, axis, bits):
    return lax.ppermute(x, axis, [(i, i ^ bits) for i in range(lax.axis_size(axis))])


def swap_far(slots):
    return [slots[0]] + [swap(slots[s], "inner", 2 * s) for s in range(1, len(slots))]


def body(queries, keys, values, cotangent):
    tokens = (queries, keys, values, cotangent)
    far_count = lax.axis_size("inner") // 2
    outer_count = lax.axis_size("outer")
    scale = float(HEAD * queries.shape[0] * 2 * far_count * outer_count) ** (-0.5)
    other, own, give = load(tokens)
    got = [swap(give, "inner", 1), swap(*sums(other[1]), "inner", 1)]
    keep = sums(*own)
    after, slots, sends = [], [], []
    for at in range(2):
        slots.append(pair_slots(keep[at], got[at], far_count, after))
        after = slots[at][:1]
    slots = [swap_far(x) for x in slots]
    for at in range(2):
        sends.append(group_sends(slots[at], outer_count, after))
        after = sends[at][:1]
    for at in range(2):
        others = [swap(x, "outer", s) for s, x in zip(distances(outer_count), sends[at])]
        slots[at] = scan_slots(slots[at], others, after)
        after = slots[at][:1]
    slots = [swap_far(x) for x in slots]
    local = local_part(*own, *other)
    outs = ()
    for at in range(2):
        arrived = swap(state_for_neighbour(slots[at], keep[at], after), "inner", 1)
        *outs, _ = finish(at, own[at], local[at], (*slots[at], got[at]), scale, outs)
        *outs, done = finish(at, other[at], local[2 + at], (arrived,), scale, outs)
        after = [done]
    return tuple(outs)


def solution(mesh):
    spec = P(("outer", "inner"), None)
    return jax.shard_map(
        body, mesh=mesh, in_specs=(spec,) * 4, out_specs=(spec,) * 4, check_vma=False
    )
```

```python
import functools

import jax
import jax.numpy as jnp
from jax import lax
from jax.experimental import pallas as pl
from jax.experimental.pallas import tpu as pltpu
from jax.sharding import PartitionSpec as P

HEAD = 128
PIECES = 4
MIB = 1024 * 1024
ANY = pl.BlockSpec(memory_space=pl.ANY)
VMEM = pl.BlockSpec(memory_space=pltpu.VMEM)
BF16 = jnp.bfloat16
F32 = jnp.float32
SMALL = pltpu.CompilerParams(vmem_limit_bytes=4 * MIB)


def dot(a, b, over_a, over_b):
    return lax.dot_general(
        a, b, (((over_a,), (over_b,)), ((), ())), preferred_element_type=F32
    )


def near_far():
    inner = lax.axis_index("inner")
    return lax.rem(inner, 2), lax.div(inner, 2)


def distances(outer_count):
    return range(outer_count - 1, 0, -1)


def block_start(own, block, half):
    near, far = near_far()
    side = near if own else 1 - near
    top = lax.div(far, lax.axis_size("inner") // 4)
    return side * half + (1 - top if block else top) * (half // 2)


def columns(start, n):
    return pl.ds(pl.multiple_of(start + n * HEAD, HEAD), HEAD)


def slot_rows(s, count, depth):
    _, far = near_far()
    return pl.ds(pl.multiple_of(lax.rem(far ^ s, count) * depth, depth), depth)


def sums_of(tokens, start, out):
    for n in range(out.shape[1] // HEAD):
        q, k, v, d = (ref[:, columns(start, n)] for ref in tokens)
        out[0, n * HEAD : (n + 1) * HEAD] = dot(k, v, 0, 0).astype(BF16)
        out[1, n * HEAD : (n + 1) * HEAD] = dot(q, d, 0, 0).astype(BF16)


def load_kernel(*refs):
    tokens, held, (out, sems) = refs[:4], refs[4:8], refs[8:]
    copies = [
        pltpu.make_async_copy(ref, to, sems.at[i]) for i, (ref, to) in enumerate(zip(tokens, held))
    ]
    for copy in copies:
        copy.start()
    for copy in copies:
        copy.wait()
    sums_of(held, block_start(False, 0, held[0].shape[1] // 2), out)


def load(tokens):
    rows, width = tokens[0].shape
    *held, sums = pl.pallas_call(
        load_kernel,
        name="load",
        in_specs=[ANY] * 4,
        out_specs=[VMEM] * 5,
        out_shape=[pltpu.VMEM((rows, width), BF16)] * 4 + [pltpu.VMEM((2, width // 4, HEAD), BF16)],
        scratch_shapes=[pltpu.SemaphoreType.DMA((4,))],
        cost_estimate=pl.CostEstimate(
            flops=rows * width * HEAD, bytes_accessed=10 * rows * width, transcendentals=0
        ),
        compiler_params=SMALL,
    )(*(pltpu.with_memory_space_constraint(x, pltpu.HBM) for x in tokens))
    return tuple(held), sums


def sums_kernel(wanted, *refs):
    for (own, block), out in zip(wanted, refs[4:]):
        sums_of(refs[:4], block_start(own, block, refs[0].shape[1] // 2), out)


def sums(tokens, *wanted):
    rows, width = tokens[0].shape
    return pl.pallas_call(
        functools.partial(sums_kernel, wanted),
        name="sums",
        in_specs=[VMEM] * 4,
        out_specs=[VMEM] * len(wanted),
        out_shape=[jax.ShapeDtypeStruct((2, width // 4, HEAD), BF16)] * len(wanted),
        cost_estimate=pl.CostEstimate(
            flops=rows * width * HEAD * len(wanted),
            bytes_accessed=3 * rows * width * len(wanted),
            transcendentals=0,
        ),
        compiler_params=SMALL,
    )(*tokens)


def pair_kernel(keep_ref, got_ref, *slots):
    for s, slot in enumerate(slots):
        part = slot_rows(s, len(slots), slot.shape[1])
        for which in range(2):
            both = keep_ref[which, part].astype(F32) + got_ref[which, part].astype(F32)
            slot[which] = both.astype(BF16)


def pair_slots(keep, got, count):
    slot = jax.ShapeDtypeStruct((2, keep.shape[1] // count, HEAD), BF16)
    return pl.pallas_call(
        pair_kernel,
        name="pair",
        in_specs=[VMEM] * 2,
        out_specs=[VMEM] * count,
        out_shape=[slot] * count,
        compiler_params=SMALL,
    )(keep, got)


def totals_kernel(far_count, *refs):
    slots, sends = refs[:far_count], refs[far_count:]
    outer = lax.axis_index("outer")
    totals = []
    for which in range(2):
        total = slots[0][which].astype(F32)
        for slot in slots[1:]:
            total += slot[which].astype(F32)
        totals.append(total.astype(BF16))
    for s, send in zip(distances(len(sends) + 1), sends):
        upward = (outer ^ s) > outer
        send[...] = jnp.where(upward, totals[0], totals[1])


def group_sends(slots, outer_count):
    send = jax.ShapeDtypeStruct(slots[0].shape[1:], BF16)
    return pl.pallas_call(
        functools.partial(totals_kernel, len(slots)),
        name="totals",
        in_specs=[VMEM] * len(slots),
        out_specs=[VMEM] * (outer_count - 1),
        out_shape=[send] * (outer_count - 1),
        compiler_params=SMALL,
    )(*slots)


def scan_kernel(far_count, *refs):
    slots, others, outs = refs[:far_count], refs[far_count:-far_count], refs[-far_count:]
    outer = lax.axis_index("outer")
    _, far = near_far()
    for which in range(2):
        base = jnp.zeros(slots[0].shape[1:], F32)
        for s, other in zip(distances(len(others) + 1), others):
            below = (outer ^ s) < outer
            wanted = below if which == 0 else jnp.logical_not(below)
            base += jnp.where(wanted, other[...].astype(F32), 0.0)
        terms = [slot[which].astype(F32) for slot in slots]
        for s, out in enumerate(outs):
            total = base
            for t, term in enumerate(terms):
                if s != t:
                    below = (far ^ t) < (far ^ s)
                    wanted = below if which == 0 else jnp.logical_not(below)
                    total += jnp.where(wanted, term, 0.0)
            out[which] = total.astype(BF16)


def scan_slots(slots, others):
    far_count, slot = len(slots), jax.ShapeDtypeStruct(slots[0].shape, BF16)
    return pl.pallas_call(
        functools.partial(scan_kernel, far_count),
        name="scan",
        in_specs=[VMEM] * (far_count + len(others)),
        out_specs=[VMEM] * far_count,
        out_shape=[slot] * far_count,
        compiler_params=SMALL,
    )(*slots, *others)


def expand(slots, out, extras, extra_which):
    count, depth = len(slots) // 2, slots[0].shape[1]
    for n, slot in enumerate(slots):
        block, s = divmod(n, count)
        part = slot_rows(s, count, depth)
        into = slice(block * count * depth, (block + 1) * count * depth)
        target, extra = out.at[:, into], extras[block]
        for which in range(2):

            @pl.when(extra_which == which)
            def _():
                total = slot[which].astype(F32) + extra[which, part].astype(F32)
                target[which, part] = total.astype(BF16)

            @pl.when(extra_which != which)
            def _():
                target[which, part] = slot[which]


def theirs_kernel(*refs):
    slots, keep, out = refs[:-3], refs[-3:-1], refs[-1]
    near, _ = near_far()
    expand(slots, out, keep, near)


def state_for_neighbour(slots, keep):
    _, block, _ = keep[0].shape
    return pl.pallas_call(
        theirs_kernel,
        name="theirs",
        in_specs=[VMEM] * (len(slots) + 2),
        out_specs=VMEM,
        out_shape=jax.ShapeDtypeStruct((2, 2 * block, HEAD), BF16),
        compiler_params=SMALL,
    )(*slots, *keep)


def local_kernel(*refs):
    tokens, outs = refs[:4], refs[4:]
    rows, width = tokens[0].shape
    at = lax.broadcasted_iota(jnp.int32, (rows, rows), 0)
    to = lax.broadcasted_iota(jnp.int32, (rows, rows), 1)
    lower = at >= to

    def masked(a, b):
        return jnp.where(lower, dot(a, b, 1, 1), 0.0).astype(BF16)

    def second(cols, a, b):
        q, k, v, d = (ref[:, cols] for ref in tokens)
        att, gq, gk, gv = outs
        att[:, cols] = dot(a, v, 1, 0)
        gq[:, cols] = dot(b, k, 1, 0)
        gk[:, cols] = dot(b, q, 0, 0)
        gv[:, cols] = dot(a, d, 0, 0)

    last = None
    for h in range(width // HEAD):
        cols = slice(h * HEAD, (h + 1) * HEAD)
        q, k, v, d = (ref[:, cols] for ref in tokens)
        a, b = masked(q, k), masked(d, v)
        if last:
            second(*last)
        last = (cols, a, b)
    second(*last)


def local_part(tokens):
    rows, width = tokens[0].shape
    return pl.pallas_call(
        local_kernel,
        name="local",
        in_specs=[VMEM] * 4,
        out_specs=[VMEM] * 4,
        out_shape=[jax.ShapeDtypeStruct((rows, width), F32)] * 4,
        cost_estimate=pl.CostEstimate(
            flops=12 * rows * width * HEAD, bytes_accessed=24 * rows * width, transcendentals=0
        ),
        compiler_params=SMALL,
    )(*tokens)


def heads_of(own, p, half):
    piece = half // PIECES
    block, at = divmod(p, PIECES // 2)
    return block_start(own, block, half) + at * piece


def product_piece(scale, own, p, tokens, local, states, held):
    half = states.shape[1]
    piece = half // PIECES
    start = heads_of(own, p, half)
    for n in range(piece // HEAD):
        rows, cols = slice(p * piece + n * HEAD, p * piece + (n + 1) * HEAD), columns(start, n)
        q, k, v, d = (ref[:, cols] for ref in tokens)
        s, g = states[0, rows], states[1, rows]
        parts = (dot(q, s, 1, 0), dot(d, s, 1, 1), dot(v, g, 1, 1), dot(k, g, 1, 0))
        for i, part in enumerate(parts):
            out = (scale * (part + local[i][:, cols])).astype(BF16)
            held[i, :, n * HEAD : (n + 1) * HEAD] = out


def copies_out(own, p, held, outs, sems, half):
    there = pl.ds(pl.multiple_of(heads_of(own, p, half), half // PIECES), half // PIECES)
    return [
        pltpu.make_async_copy(held.at[i], out.at[:, there], sems.at[i, p])
        for i, out in enumerate(outs)
    ]


def finish_own_kernel(scale, slot_count, *refs):
    tokens, local, slots, refs = refs[:4], refs[4:8], refs[8 : 8 + slot_count], refs[8 + slot_count :]
    got, outs, (rest, states, held, sems) = refs[:2], refs[2:6], refs[6:]
    near, _ = near_far()
    expand(slots, states, got, 1 - near)
    half = states.shape[1]
    copies = []
    for p in range(PIECES):
        to = held.at[p] if p < PIECES - 1 else rest
        product_piece(scale, True, p, tokens, local, states, to)
        if p < PIECES - 1:
            copies += copies_out(True, p, to, outs, sems, half)
            for copy in copies[-4:]:
                copy.start()
    for copy in copies:
        copy.wait()


def finish_own(tokens, local, slots, got, scale):
    rows, width = tokens[0].shape
    half = width // 2
    out = jax.ShapeDtypeStruct((rows, width), BF16)
    piece = (4, rows, half // PIECES)
    *outs, rest = pl.pallas_call(
        functools.partial(finish_own_kernel, scale, len(slots)),
        name="finish_own",
        in_specs=[VMEM] * (10 + len(slots)),
        out_specs=[ANY] * 4 + [VMEM],
        out_shape=[out] * 4 + [pltpu.VMEM(piece, BF16)],
        scratch_shapes=[
            pltpu.VMEM((2, half, HEAD), BF16),
            pltpu.VMEM((PIECES - 1, *piece), BF16),
            pltpu.SemaphoreType.DMA((4, PIECES)),
        ],
        cost_estimate=pl.CostEstimate(
            flops=4 * rows * width * HEAD, bytes_accessed=17 * rows * width, transcendentals=0
        ),
        compiler_params=SMALL,
    )(*tokens, *local, *slots, *got)
    return outs, rest


def finish_other_kernel(scale, *refs):
    tokens, local, (states, rest), refs = refs[:4], refs[4:8], refs[8:10], refs[14:]
    outs, (held, sems, rest_sems) = refs[:4], refs[4:]
    half = states.shape[1]
    copies = copies_out(True, PIECES - 1, rest, outs, rest_sems, half)
    for copy in copies:
        copy.start()
    for p in range(PIECES):
        product_piece(scale, False, p, tokens, local, states, held.at[p])
        copies += copies_out(False, p, held.at[p], outs, sems, half)
        for copy in copies[-4:]:
            copy.start()
    for copy in copies:
        copy.wait()


def finish_other(tokens, local, states, rest, scale, before):
    rows, width = tokens[0].shape
    out = jax.ShapeDtypeStruct((rows, width), BF16)
    return pl.pallas_call(
        functools.partial(finish_other_kernel, scale),
        name="finish_other",
        in_specs=[VMEM] * 10 + [ANY] * 4,
        out_specs=[ANY] * 4,
        out_shape=[out] * 4,
        scratch_shapes=[
            pltpu.VMEM((PIECES, *rest.shape), BF16),
            pltpu.SemaphoreType.DMA((4, PIECES)),
            pltpu.SemaphoreType.DMA((4, PIECES)),
        ],
        input_output_aliases={10 + i: i for i in range(4)},
        cost_estimate=pl.CostEstimate(
            flops=4 * rows * width * HEAD, bytes_accessed=17 * rows * width, transcendentals=0
        ),
        compiler_params=SMALL,
    )(*tokens, *local, states, rest, *before)


def swap(x, axis, bits):
    return lax.ppermute(x, axis, [(i, i ^ bits) for i in range(lax.axis_size(axis))])


def swap_far(slots):
    return [slots[0]] + [swap(slots[s], "inner", 2 * s) for s in range(1, len(slots))]


def body(queries, keys, values, cotangent):
    far_count = lax.axis_size("inner") // 2
    outer_count = lax.axis_size("outer")
    scale = float(HEAD * queries.shape[0] * 2 * far_count * outer_count) ** (-0.5)
    tokens, give = load((queries, keys, values, cotangent))
    got = [swap(give, "inner", 1), swap(*sums(tokens, (False, 1)), "inner", 1)]
    keep = sums(tokens, (True, 0), (True, 1))
    slots = [slot for b in range(2) for slot in pair_slots(keep[b], got[b], far_count // 2)]
    slots, local = lax.optimization_barrier((swap_far(slots), local_part(tokens)))
    sends = group_sends(slots, outer_count)
    others = [swap(send, "outer", s) for s, send in zip(distances(outer_count), sends)]
    slots = swap_far(scan_slots(slots, others))
    arrived = swap(state_for_neighbour(slots, keep), "inner", 1)
    outs, rest = finish_own(tokens, local, slots, got, scale)
    return tuple(finish_other(tokens, local, arrived, rest, scale, outs))


def solution(mesh):
    spec = P(("outer", "inner"), None)
    return jax.shard_map(
        body, mesh=mesh, in_specs=(spec,) * 4, out_specs=(spec,) * 4, check_vma=False
    )
```

```python
import functools

import jax
import jax.numpy as jnp
from jax import lax
from jax.experimental import pallas as pl
from jax.experimental.pallas import tpu as pltpu
from jax.sharding import PartitionSpec as P

HEAD = 128
PIECES = 4
MIB = 1024 * 1024
ANY = pl.BlockSpec(memory_space=pl.ANY)
VMEM = pl.BlockSpec(memory_space=pltpu.VMEM)
BF16 = jnp.bfloat16
F32 = jnp.float32
SMALL = pltpu.CompilerParams(vmem_limit_bytes=4 * MIB)


def dot(a, b, over_a, over_b):
    return lax.dot_general(
        a, b, (((over_a,), (over_b,)), ((), ())), preferred_element_type=F32
    )


def near_far():
    inner = lax.axis_index("inner")
    return lax.rem(inner, 2), lax.div(inner, 2)


def distances(outer_count):
    return range(outer_count - 1, 0, -1)


def exchanged(bits):
    return bits ^ 3 if bits & 3 in (1, 2) and lax.axis_size("inner") > 4 else bits


def place_of(side):
    _, far = near_far()
    if lax.axis_size("inner") <= 4:
        return far
    low, high = lax.rem(far, 2), lax.rem(lax.div(far, 2), 2)
    other = far + low - high
    return jnp.where(side == 1, far, other)


def far_of(s):
    near, far = near_far()
    return jnp.where(near == 1, far ^ s, far ^ exchanged(s))


def slot_order(count):
    return [n ^ (n >> 1) for n in range(count)]


def block_start(own, block, half):
    near, _ = near_far()
    side = near if own else 1 - near
    top = lax.div(place_of(side), lax.axis_size("inner") // 4)
    return side * half + (1 - top if block else top) * (half // 2)


def columns(start, n):
    return pl.ds(pl.multiple_of(start + n * HEAD, HEAD), HEAD)


def slot_rows(s, count, depth):
    near, _ = near_far()
    return pl.ds(pl.multiple_of(lax.rem(place_of(near) ^ s, count) * depth, depth), depth)


def sums_of(tokens, start, out):
    for n in range(out.shape[1] // HEAD):
        q, k, v, d = (ref[:, columns(start, n)] for ref in tokens)
        out[0, n * HEAD : (n + 1) * HEAD] = dot(k, v, 0, 0).astype(BF16)
        out[1, n * HEAD : (n + 1) * HEAD] = dot(q, d, 0, 0).astype(BF16)


def load_kernel(*refs):
    tokens, held, (out, sems) = refs[:4], refs[4:8], refs[8:]
    copies = [
        pltpu.make_async_copy(ref, to, sems.at[i]) for i, (ref, to) in enumerate(zip(tokens, held))
    ]
    for copy in copies:
        copy.start()
    for copy in copies:
        copy.wait()
    sums_of(held, block_start(False, 0, held[0].shape[1] // 2), out)


def load(tokens):
    rows, width = tokens[0].shape
    *held, sums = pl.pallas_call(
        load_kernel,
        name="load",
        in_specs=[ANY] * 4,
        out_specs=[VMEM] * 5,
        out_shape=[pltpu.VMEM((rows, width), BF16)] * 4 + [pltpu.VMEM((2, width // 4, HEAD), BF16)],
        scratch_shapes=[pltpu.SemaphoreType.DMA((4,))],
        cost_estimate=pl.CostEstimate(
            flops=rows * width * HEAD, bytes_accessed=10 * rows * width, transcendentals=0
        ),
        compiler_params=SMALL,
    )(*(pltpu.with_memory_space_constraint(x, pltpu.HBM) for x in tokens))
    return tuple(held), sums


def sums_kernel(wanted, *refs):
    for (own, block), out in zip(wanted, refs[4:]):
        sums_of(refs[:4], block_start(own, block, refs[0].shape[1] // 2), out)


def sums(tokens, *wanted):
    rows, width = tokens[0].shape
    return pl.pallas_call(
        functools.partial(sums_kernel, wanted),
        name="sums",
        in_specs=[VMEM] * 4,
        out_specs=[VMEM] * len(wanted),
        out_shape=[jax.ShapeDtypeStruct((2, width // 4, HEAD), BF16)] * len(wanted),
        cost_estimate=pl.CostEstimate(
            flops=rows * width * HEAD * len(wanted),
            bytes_accessed=3 * rows * width * len(wanted),
            transcendentals=0,
        ),
        compiler_params=SMALL,
    )(*tokens)


def pair_kernel(block, keep_ref, got_ref, *slots):
    count = len(slots)
    for s, slot in zip(slot_order(2 * count)[block * count :], slots):
        part = slot_rows(s, len(slots), slot.shape[1])
        for which in range(2):
            both = keep_ref[which, part].astype(F32) + got_ref[which, part].astype(F32)
            slot[which] = both.astype(BF16)


def pair_slots(block, keep, got, count):
    slot = jax.ShapeDtypeStruct((2, keep.shape[1] // count, HEAD), BF16)
    return pl.pallas_call(
        functools.partial(pair_kernel, block),
        name="pair",
        in_specs=[VMEM] * 2,
        out_specs=[VMEM] * count,
        out_shape=[slot] * count,
        compiler_params=SMALL,
    )(keep, got)


def totals_kernel(far_count, *refs):
    slots, sends = refs[:far_count], refs[far_count:]
    outer = lax.axis_index("outer")
    totals = []
    for which in range(2):
        total = slots[0][which].astype(F32)
        for slot in slots[1:]:
            total += slot[which].astype(F32)
        totals.append(total.astype(BF16))
    for s, send in zip(distances(len(sends) + 1), sends):
        upward = (outer ^ s) > outer
        send[...] = jnp.where(upward, totals[0], totals[1])


def group_sends(slots, outer_count):
    send = jax.ShapeDtypeStruct(slots[0].shape[1:], BF16)
    return pl.pallas_call(
        functools.partial(totals_kernel, len(slots)),
        name="totals",
        in_specs=[VMEM] * len(slots),
        out_specs=[VMEM] * (outer_count - 1),
        out_shape=[send] * (outer_count - 1),
        compiler_params=SMALL,
    )(*slots)


def scan_kernel(far_count, *refs):
    slots, others, outs = refs[:far_count], refs[far_count:-far_count], refs[-far_count:]
    outer = lax.axis_index("outer")
    for which in range(2):
        base = jnp.zeros(slots[0].shape[1:], F32)
        for s, other in zip(distances(len(others) + 1), others):
            below = (outer ^ s) < outer
            wanted = below if which == 0 else jnp.logical_not(below)
            base += jnp.where(wanted, other[...].astype(F32), 0.0)
        terms = [slot[which].astype(F32) for slot in slots]
        fars = [far_of(s) for s in slot_order(far_count)]
        for s, out in enumerate(outs):
            total = base
            for t, term in enumerate(terms):
                if s != t:
                    below = fars[t] < fars[s]
                    wanted = below if which == 0 else jnp.logical_not(below)
                    total += jnp.where(wanted, term, 0.0)
            out[which] = total.astype(BF16)


def scan_slots(slots, others):
    far_count, slot = len(slots), jax.ShapeDtypeStruct(slots[0].shape, BF16)
    return pl.pallas_call(
        functools.partial(scan_kernel, far_count),
        name="scan",
        in_specs=[VMEM] * (far_count + len(others)),
        out_specs=[VMEM] * far_count,
        out_shape=[slot] * far_count,
        compiler_params=SMALL,
    )(*slots, *others)


def expand(slots, out, extras, extra_which):
    count, depth = len(slots) // 2, slots[0].shape[1]
    for n, (s, slot) in enumerate(zip(slot_order(2 * count), slots)):
        block = n // count
        part = slot_rows(s, count, depth)
        into = slice(block * count * depth, (block + 1) * count * depth)
        target, extra = out.at[:, into], extras[block]
        for which in range(2):

            @pl.when(extra_which == which)
            def _():
                total = slot[which].astype(F32) + extra[which, part].astype(F32)
                target[which, part] = total.astype(BF16)

            @pl.when(extra_which != which)
            def _():
                target[which, part] = slot[which]


def theirs_kernel(*refs):
    slots, keep, out = refs[:-3], refs[-3:-1], refs[-1]
    near, _ = near_far()
    expand(slots, out, keep, near)


def state_for_neighbour(slots, keep):
    _, block, _ = keep[0].shape
    return pl.pallas_call(
        theirs_kernel,
        name="theirs",
        in_specs=[VMEM] * (len(slots) + 2),
        out_specs=VMEM,
        out_shape=jax.ShapeDtypeStruct((2, 2 * block, HEAD), BF16),
        compiler_params=SMALL,
    )(*slots, *keep)


def local_kernel(*refs):
    tokens, outs = refs[:4], refs[4:]
    rows, width = tokens[0].shape
    at = lax.broadcasted_iota(jnp.int32, (rows, rows), 0)
    to = lax.broadcasted_iota(jnp.int32, (rows, rows), 1)
    lower = at >= to

    def masked(a, b):
        return jnp.where(lower, dot(a, b, 1, 1), 0.0).astype(BF16)

    def second(cols, a, b):
        q, k, v, d = (ref[:, cols] for ref in tokens)
        att, gq, gk, gv = outs
        att[:, cols] = dot(a, v, 1, 0)
        gq[:, cols] = dot(b, k, 1, 0)
        gk[:, cols] = dot(b, q, 0, 0)
        gv[:, cols] = dot(a, d, 0, 0)

    last = None
    for h in range(width // HEAD):
        cols = slice(h * HEAD, (h + 1) * HEAD)
        q, k, v, d = (ref[:, cols] for ref in tokens)
        a, b = masked(q, k), masked(d, v)
        if last:
            second(*last)
        last = (cols, a, b)
    second(*last)


def local_part(tokens):
    rows, width = tokens[0].shape
    return pl.pallas_call(
        local_kernel,
        name="local",
        in_specs=[VMEM] * 4,
        out_specs=[VMEM] * 4,
        out_shape=[jax.ShapeDtypeStruct((rows, width), F32)] * 4,
        cost_estimate=pl.CostEstimate(
            flops=12 * rows * width * HEAD, bytes_accessed=24 * rows * width, transcendentals=0
        ),
        compiler_params=SMALL,
    )(*tokens)


def heads_of(own, p, half):
    piece = half // PIECES
    block, at = divmod(p, PIECES // 2)
    return block_start(own, block, half) + at * piece


def product_piece(scale, own, p, tokens, local, states, held):
    half = states.shape[1]
    piece = half // PIECES
    start = heads_of(own, p, half)
    for n in range(piece // HEAD):
        rows, cols = slice(p * piece + n * HEAD, p * piece + (n + 1) * HEAD), columns(start, n)
        q, k, v, d = (ref[:, cols] for ref in tokens)
        s, g = states[0, rows], states[1, rows]
        parts = (dot(q, s, 1, 0), dot(d, s, 1, 1), dot(v, g, 1, 1), dot(k, g, 1, 0))
        for i, part in enumerate(parts):
            out = (scale * (part + local[i][:, cols])).astype(BF16)
            held[i, :, n * HEAD : (n + 1) * HEAD] = out


def copies_out(own, p, held, outs, sems, half):
    there = pl.ds(pl.multiple_of(heads_of(own, p, half), half // PIECES), half // PIECES)
    return [
        pltpu.make_async_copy(held.at[i], out.at[:, there], sems.at[i, p])
        for i, out in enumerate(outs)
    ]


def finish_own_kernel(scale, slot_count, *refs):
    tokens, local, slots, refs = refs[:4], refs[4:8], refs[8 : 8 + slot_count], refs[8 + slot_count :]
    got, outs, (rest, states, held, sems) = refs[:2], refs[2:6], refs[6:]
    near, _ = near_far()
    expand(slots, states, got, 1 - near)
    half = states.shape[1]
    copies = []
    for p in range(PIECES):
        to = held.at[p] if p < PIECES - 1 else rest
        product_piece(scale, True, p, tokens, local, states, to)
        if p < PIECES - 1:
            copies += copies_out(True, p, to, outs, sems, half)
            for copy in copies[-4:]:
                copy.start()
    for copy in copies:
        copy.wait()


def finish_own(tokens, local, slots, got, scale):
    rows, width = tokens[0].shape
    half = width // 2
    out = jax.ShapeDtypeStruct((rows, width), BF16)
    piece = (4, rows, half // PIECES)
    *outs, rest = pl.pallas_call(
        functools.partial(finish_own_kernel, scale, len(slots)),
        name="finish_own",
        in_specs=[VMEM] * (10 + len(slots)),
        out_specs=[ANY] * 4 + [VMEM],
        out_shape=[out] * 4 + [pltpu.VMEM(piece, BF16)],
        scratch_shapes=[
            pltpu.VMEM((2, half, HEAD), BF16),
            pltpu.VMEM((PIECES - 1, *piece), BF16),
            pltpu.SemaphoreType.DMA((4, PIECES)),
        ],
        cost_estimate=pl.CostEstimate(
            flops=4 * rows * width * HEAD, bytes_accessed=17 * rows * width, transcendentals=0
        ),
        compiler_params=SMALL,
    )(*tokens, *local, *slots, *got)
    return outs, rest


def finish_other_kernel(scale, *refs):
    tokens, local, (states, rest), refs = refs[:4], refs[4:8], refs[8:10], refs[14:]
    outs, (held, sems, rest_sems) = refs[:4], refs[4:]
    half = states.shape[1]
    copies = copies_out(True, PIECES - 1, rest, outs, rest_sems, half)
    for copy in copies:
        copy.start()
    for p in range(PIECES):
        product_piece(scale, False, p, tokens, local, states, held.at[p])
        copies += copies_out(False, p, held.at[p], outs, sems, half)
        for copy in copies[-4:]:
            copy.start()
    for copy in copies:
        copy.wait()


def finish_other(tokens, local, states, rest, scale, before):
    rows, width = tokens[0].shape
    out = jax.ShapeDtypeStruct((rows, width), BF16)
    return pl.pallas_call(
        functools.partial(finish_other_kernel, scale),
        name="finish_other",
        in_specs=[VMEM] * 10 + [ANY] * 4,
        out_specs=[ANY] * 4,
        out_shape=[out] * 4,
        scratch_shapes=[
            pltpu.VMEM((PIECES, *rest.shape), BF16),
            pltpu.SemaphoreType.DMA((4, PIECES)),
            pltpu.SemaphoreType.DMA((4, PIECES)),
        ],
        input_output_aliases={10 + i: i for i in range(4)},
        cost_estimate=pl.CostEstimate(
            flops=4 * rows * width * HEAD, bytes_accessed=17 * rows * width, transcendentals=0
        ),
        compiler_params=SMALL,
    )(*tokens, *local, states, rest, *before)


def swap(x, axis, bits):
    return lax.ppermute(x, axis, [(i, i ^ bits) for i in range(lax.axis_size(axis))])


def swap_far(slots):
    inner = range(lax.axis_size("inner"))
    pairs = [
        [(i, i ^ 2 * (s if i % 2 else exchanged(s))) for i in inner] for s in slot_order(len(slots))
    ]
    return [slots[0]] + [lax.ppermute(x, "inner", p) for x, p in zip(slots[1:], pairs[1:])]


def body(queries, keys, values, cotangent):
    far_count = lax.axis_size("inner") // 2
    outer_count = lax.axis_size("outer")
    scale = float(HEAD * queries.shape[0] * 2 * far_count * outer_count) ** (-0.5)
    tokens, give = load((queries, keys, values, cotangent))
    got = [swap(give, "inner", 1), swap(*sums(tokens, (False, 1)), "inner", 1)]
    keep = sums(tokens, (True, 0), (True, 1))
    slots = [slot for b in range(2) for slot in pair_slots(b, keep[b], got[b], far_count // 2)]
    slots, local = lax.optimization_barrier((swap_far(slots), local_part(tokens)))
    sends = group_sends(slots, outer_count)
    others = [swap(send, "outer", s) for s, send in zip(distances(outer_count), sends)]
    slots = swap_far(scan_slots(slots, others))
    arrived = swap(state_for_neighbour(slots, keep), "inner", 1)
    outs, rest = finish_own(tokens, local, slots, got, scale)
    return tuple(finish_other(tokens, local, arrived, rest, scale, outs))


def solution(mesh):
    spec = P(("outer", "inner"), None)
    return jax.shard_map(
        body, mesh=mesh, in_specs=(spec,) * 4, out_specs=(spec,) * 4, check_vma=False
    )
```

```python
import functools

import jax
import jax.numpy as jnp
from jax import lax
from jax.experimental import pallas as pl
from jax.experimental.pallas import tpu as pltpu
from jax.sharding import PartitionSpec as P

HEAD = 128
PIECE = 256
MIB = 1024 * 1024
ANY = pl.BlockSpec(memory_space=pl.ANY)
VMEM = pl.BlockSpec(memory_space=pltpu.VMEM)
BF16 = jnp.bfloat16
F32 = jnp.float32
SMALL = pltpu.CompilerParams(vmem_limit_bytes=4 * MIB)


def dot(a, b, over_a, over_b):
    return lax.dot_general(
        a, b, (((over_a,), (over_b,)), ((), ())), preferred_element_type=F32
    )


def near_far():
    inner = lax.axis_index("inner")
    return lax.rem(inner, 2), lax.div(inner, 2)


def block_start(block, width):
    _, far = near_far()
    top = lax.div(far, lax.axis_size("inner") // 4)
    return (1 - top if block else top) * (width // 2)


def rows_at(start, n, size):
    return pl.ds(pl.multiple_of(start + n * size, size), size)


def slot_rows(s, count, depth):
    _, far = near_far()
    return rows_at(lax.rem(far ^ s, count) * depth, 0, depth)


def by_core(odd, even):
    near, _ = near_far()
    pl.when(near == 1)(odd)
    pl.when(near == 0)(even)


def block_sums(own, block, tokens, out):
    q, k, v, d = tokens
    start = block_start(block, q.shape[1])

    def add(a, b):
        for n in range(out.shape[0] // HEAD):
            cols = rows_at(start, n, HEAD)
            out[n * HEAD : (n + 1) * HEAD] = dot(a[:, cols], b[:, cols], 0, 0).astype(BF16)

    kinds = [lambda: add(k, v), lambda: add(q, d)]
    by_core(*(kinds if own else kinds[::-1]))


def load_kernel(*refs):
    tokens, held, (out, sems) = refs[:4], refs[4:8], refs[8:]
    copies = [
        pltpu.make_async_copy(ref, to, sems.at[i]) for i, (ref, to) in enumerate(zip(tokens, held))
    ]
    for copy in copies:
        copy.start()
    for copy in copies:
        copy.wait()
    block_sums(False, 0, held, out)


def load(tokens):
    rows, width = tokens[0].shape
    *held, sums = pl.pallas_call(
        load_kernel,
        name="load",
        in_specs=[ANY] * 4,
        out_specs=[VMEM] * 5,
        out_shape=[pltpu.VMEM((rows, width), BF16)] * 4 + [pltpu.VMEM((width // 2, HEAD), BF16)],
        scratch_shapes=[pltpu.SemaphoreType.DMA((4,))],
        cost_estimate=pl.CostEstimate(
            flops=rows * width * HEAD, bytes_accessed=10 * rows * width, transcendentals=0
        ),
        compiler_params=SMALL,
    )(*(pltpu.with_memory_space_constraint(x, pltpu.HBM) for x in tokens))
    return tuple(held), sums


def sums_kernel(wanted, *refs):
    for (own, block), out in zip(wanted, refs[4:]):
        block_sums(own, block, refs[:4], out)


def sums(tokens, *wanted):
    rows, width = tokens[0].shape
    return pl.pallas_call(
        functools.partial(sums_kernel, wanted),
        name="sums",
        in_specs=[VMEM] * 4,
        out_specs=[VMEM] * len(wanted),
        out_shape=[jax.ShapeDtypeStruct((width // 2, HEAD), BF16)] * len(wanted),
        cost_estimate=pl.CostEstimate(
            flops=rows * width * HEAD * len(wanted),
            bytes_accessed=3 * rows * width * len(wanted),
            transcendentals=0,
        ),
        compiler_params=SMALL,
    )(*tokens)


def pair_kernel(keep_ref, got_ref, *slots):
    for s, slot in enumerate(slots):
        part = slot_rows(s, len(slots), slot.shape[0])
        slot[...] = (keep_ref[part].astype(F32) + got_ref[part].astype(F32)).astype(BF16)


def pair_slots(keep, got, count):
    slot = jax.ShapeDtypeStruct((keep.shape[0] // count, HEAD), BF16)
    return pl.pallas_call(
        pair_kernel,
        name="pair",
        in_specs=[VMEM] * 2,
        out_specs=[VMEM] * count,
        out_shape=[slot] * count,
        compiler_params=SMALL,
    )(keep, got)


def total_kernel(*refs):
    total = refs[0][...].astype(F32)
    for slot in refs[1:-1]:
        total += slot[...].astype(F32)
    refs[-1][...] = total.astype(BF16)


def total_of(slots):
    return pl.pallas_call(
        total_kernel,
        name="total",
        in_specs=[VMEM] * len(slots),
        out_specs=VMEM,
        out_shape=jax.ShapeDtypeStruct(slots[0].shape, BF16),
        compiler_params=SMALL,
    )(*slots)


def scan_kernel(count, *refs):
    slots, others, outs = refs[:count], refs[count:-count], refs[-count:]
    near, far = near_far()
    base = others[0][...].astype(F32)
    for other in others[1:]:
        base += other[...].astype(F32)
    terms = [slot[...].astype(F32) for slot in slots]
    for s, out in enumerate(outs):
        total = base
        for t, term in enumerate(terms):
            if s != t:
                below = (far ^ t) < (far ^ s)
                wanted = jnp.where(near == 1, below, jnp.logical_not(below))
                total += jnp.where(wanted, term, 0.0)
        out[...] = total.astype(BF16)


def scan_slots(slots, others):
    count, slot = len(slots), jax.ShapeDtypeStruct(slots[0].shape, BF16)
    return pl.pallas_call(
        functools.partial(scan_kernel, count),
        name="scan",
        in_specs=[VMEM] * (count + len(others)),
        out_specs=[VMEM] * count,
        out_shape=[slot] * count,
        compiler_params=SMALL,
    )(*slots, *others)


def local_kernel(*refs):
    tokens, outs = refs[:4], refs[4:]
    rows, width = tokens[0].shape
    at = lax.broadcasted_iota(jnp.int32, (rows, rows), 0)
    to = lax.broadcasted_iota(jnp.int32, (rows, rows), 1)
    lower = at >= to

    def masked(a, b):
        return jnp.where(lower, dot(a, b, 1, 1), 0.0).astype(BF16)

    def second(cols, a, b):
        q, k, v, d = (ref[:, cols] for ref in tokens)
        att, gq, gv, gk = outs
        att[:, cols] = dot(a, v, 1, 0)
        gq[:, cols] = dot(b, k, 1, 0)
        gv[:, cols] = dot(a, d, 0, 0)
        gk[:, cols] = dot(b, q, 0, 0)

    last = None
    for h in range(width // HEAD):
        cols = slice(h * HEAD, (h + 1) * HEAD)
        q, k, v, d = (ref[:, cols] for ref in tokens)
        a, b = masked(q, k), masked(d, v)
        if last:
            second(*last)
        last = (cols, a, b)
    second(*last)


def local_part(tokens):
    rows, width = tokens[0].shape
    return pl.pallas_call(
        local_kernel,
        name="local",
        in_specs=[VMEM] * 4,
        out_specs=[VMEM] * 4,
        out_shape=[jax.ShapeDtypeStruct((rows, width), F32)] * 4,
        cost_estimate=pl.CostEstimate(
            flops=12 * rows * width * HEAD, bytes_accessed=24 * rows * width, transcendentals=0
        ),
        compiler_params=SMALL,
    )(*tokens)


def results(scale, tokens, local, outs, held, sems, states):
    a_ref, b_ref = tokens
    depth = held.shape[2] // len(states)
    piece = min(depth, PIECE)
    _, far = near_far()
    for s, state in enumerate(states):
        for p in range(depth // piece):
            at = s * depth + p * piece
            there = rows_at((far ^ s) * depth, p, piece)
            for n in range(piece // HEAD):
                cols = rows_at((far ^ s) * depth + p * piece, n, HEAD)
                x = state(slice(p * piece + n * HEAD, p * piece + (n + 1) * HEAD))
                parts = dot(a_ref[:, cols], x, 1, 0), dot(b_ref[:, cols], x, 1, 1)
                for i, part in enumerate(parts):
                    out = (scale * (part + local[i][:, cols])).astype(BF16)
                    held[i, :, at + n * HEAD : at + (n + 1) * HEAD] = out
            yield [
                pltpu.make_async_copy(
                    held.at[i, :, pl.ds(at, piece)],
                    out.at[:, there],
                    sems.at[i, s * (depth // piece) + p],
                )
                for i, out in enumerate(outs)
            ]


def kinds(tokens, local, outs):
    q, k, v, d = tokens
    return ((q, d), local[:2], outs[:2]), ((k, v), local[2:], outs[2:])


def finish_kernel(scale, count, own, *refs):
    tokens, local, slots, refs = refs[:4], refs[4:8], refs[8 : 8 + count], refs[8 + count :]
    got = refs[:2] if own else ()
    outs, held, sems = refs[-6:-2], refs[-2], refs[-1]
    depth = slots[0].shape[0]

    def state(s):
        if not own:
            return lambda part: slots[s][part]

        def read(part):
            _, far = near_far()
            more = got[2 * s // count]
            there = rows_at(lax.rem(far ^ s, count // 2) * depth + part.start, 0, HEAD)
            return (slots[s][part].astype(F32) + more[there].astype(F32)).astype(BF16)

        return read

    def run(kind):
        started = []
        for copies in results(scale, *kind, held, sems, [state(s) for s in range(count)]):
            for copy in copies:
                copy.start()
            started += copies
        for copy in started:
            copy.wait()

    of_s, of_g = kinds(tokens, local, outs)
    both = [lambda: run(of_s), lambda: run(of_g)]
    by_core(*(both if own else both[::-1]))


def finish(tokens, local, slots, scale, got=(), before=()):
    rows, width = tokens[0].shape
    count, depth = len(slots), slots[0].shape[0]
    out = jax.ShapeDtypeStruct((rows, width), BF16)
    inputs = [*tokens, *local, *slots, *got]
    return pl.pallas_call(
        functools.partial(finish_kernel, scale, count, bool(got)),
        name="finish_own" if got else "finish_other",
        in_specs=[VMEM] * len(inputs) + [ANY] * len(before),
        out_specs=[ANY] * 4,
        out_shape=[out] * 4,
        scratch_shapes=[
            pltpu.VMEM((2, rows, width), BF16),
            pltpu.SemaphoreType.DMA((2, width // min(depth, PIECE))),
        ],
        input_output_aliases={len(inputs) + i: i for i in range(len(before))},
        cost_estimate=pl.CostEstimate(
            flops=4 * rows * width * HEAD, bytes_accessed=17 * rows * width, transcendentals=0
        ),
        compiler_params=SMALL,
    )(*inputs, *before)


def swap(x, bits):
    return lax.ppermute(x, "inner", [(i, i ^ bits) for i in range(lax.axis_size("inner"))])


def swap_far(slots):
    return [slots[0]] + [swap(slots[s], 2 * s) for s in range(1, len(slots))]


def from_groups(total):
    groups, count = lax.axis_size("outer"), lax.axis_size("inner")
    return [
        lax.ppermute(
            total,
            ("outer", "inner"),
            [
                (z * count + i, (z ^ s) * count + i)
                for z in range(groups)
                for i in range(count)
                if (z < z ^ s) == (i % 2 == 1)
            ],
        )
        for s in range(1, groups)
    ]


def body(queries, keys, values, cotangent):
    far_count = lax.axis_size("inner") // 2
    scale = float(HEAD * queries.shape[0] * 2 * far_count * lax.axis_size("outer")) ** (-0.5)
    tokens, give = load((queries, keys, values, cotangent))
    got = [swap(give, 1), swap(*sums(tokens, (False, 1)), 1)]
    keep = sums(tokens, (True, 0), (True, 1))
    slots = [slot for b in range(2) for slot in pair_slots(keep[b], got[b], far_count // 2)]
    slots, local = lax.optimization_barrier((swap_far(slots), local_part(tokens)))
    slots = swap_far(scan_slots(slots, from_groups(total_of(slots))))
    arrived = [swap(slot, 1) for slot in slots]
    outs = finish(tokens, local, slots, scale, got=got)
    att, gq, gv, gk = finish(tokens, local, arrived, scale, before=outs)
    return att, gq, gk, gv


def solution(mesh):
    spec = P(("outer", "inner"), None)
    return jax.shard_map(
        body, mesh=mesh, in_specs=(spec,) * 4, out_specs=(spec,) * 4, check_vma=False
    )
```

```python
import functools

import jax
import jax.numpy as jnp
from jax import lax
from jax.experimental import pallas as pl
from jax.experimental.pallas import tpu as pltpu
from jax.sharding import PartitionSpec as P

HEAD = 128
PIECES = 4
MIB = 1024 * 1024
ANY = pl.BlockSpec(memory_space=pl.ANY)
VMEM = pl.BlockSpec(memory_space=pltpu.VMEM)
BF16 = jnp.bfloat16
F32 = jnp.float32
SMALL = pltpu.CompilerParams(vmem_limit_bytes=4 * MIB)


def dot(a, b, over_a, over_b):
    return lax.dot_general(
        a, b, (((over_a,), (over_b,)), ((), ())), preferred_element_type=F32
    )


def near_far():
    inner = lax.axis_index("inner")
    return lax.rem(inner, 2), lax.div(inner, 2)


def distances(outer_count):
    return range(outer_count - 1, 0, -1)


def block_start(own, block, half):
    near, far = near_far()
    side = near if own else 1 - near
    top = lax.div(far, lax.axis_size("inner") // 4)
    return side * half + (1 - top if block else top) * (half // 2)


def columns(start, n):
    return pl.ds(pl.multiple_of(start + n * HEAD, HEAD), HEAD)


def slot_rows(s, count, depth):
    _, far = near_far()
    return pl.ds(pl.multiple_of(lax.rem(far ^ s, count) * depth, depth), depth)


def sums_of(tokens, start, out):
    for n in range(out.shape[1] // HEAD):
        q, k, v, d = (ref[:, columns(start, n)] for ref in tokens)
        out[0, n * HEAD : (n + 1) * HEAD] = dot(k, v, 0, 0).astype(BF16)
        out[1, n * HEAD : (n + 1) * HEAD] = dot(q, d, 0, 0).astype(BF16)


def load_kernel(*refs):
    tokens, held, (out, sems) = refs[:4], refs[4:8], refs[8:]
    copies = [
        pltpu.make_async_copy(ref, to, sems.at[i]) for i, (ref, to) in enumerate(zip(tokens, held))
    ]
    for copy in copies:
        copy.start()
    for copy in copies:
        copy.wait()
    sums_of(held, block_start(False, 0, held[0].shape[1] // 2), out)


def load(tokens):
    rows, width = tokens[0].shape
    *held, sums = pl.pallas_call(
        load_kernel,
        name="load",
        in_specs=[ANY] * 4,
        out_specs=[VMEM] * 5,
        out_shape=[pltpu.VMEM((rows, width), BF16)] * 4 + [pltpu.VMEM((2, width // 4, HEAD), BF16)],
        scratch_shapes=[pltpu.SemaphoreType.DMA((4,))],
        cost_estimate=pl.CostEstimate(
            flops=rows * width * HEAD, bytes_accessed=10 * rows * width, transcendentals=0
        ),
        compiler_params=SMALL,
    )(*(pltpu.with_memory_space_constraint(x, pltpu.HBM) for x in tokens))
    return tuple(held), sums


def sums_kernel(wanted, *refs):
    for (own, block), out in zip(wanted, refs[4:]):
        sums_of(refs[:4], block_start(own, block, refs[0].shape[1] // 2), out)


def sums(tokens, *wanted):
    rows, width = tokens[0].shape
    return pl.pallas_call(
        functools.partial(sums_kernel, wanted),
        name="sums",
        in_specs=[VMEM] * 4,
        out_specs=[VMEM] * len(wanted),
        out_shape=[jax.ShapeDtypeStruct((2, width // 4, HEAD), BF16)] * len(wanted),
        cost_estimate=pl.CostEstimate(
            flops=rows * width * HEAD * len(wanted),
            bytes_accessed=3 * rows * width * len(wanted),
            transcendentals=0,
        ),
        compiler_params=SMALL,
    )(*tokens)


def pair_kernel(keep_ref, got_ref, *slots):
    for s, slot in enumerate(slots):
        part = slot_rows(s, len(slots), slot.shape[1])
        for which in range(2):
            both = keep_ref[which, part].astype(F32) + got_ref[which, part].astype(F32)
            slot[which] = both.astype(BF16)


def pair_slots(keep, got, count):
    slot = jax.ShapeDtypeStruct((2, keep.shape[1] // count, HEAD), BF16)
    return pl.pallas_call(
        pair_kernel,
        name="pair",
        in_specs=[VMEM] * 2,
        out_specs=[VMEM] * count,
        out_shape=[slot] * count,
        compiler_params=SMALL,
    )(keep, got)


def totals_kernel(far_count, *refs):
    slots, sends = refs[:far_count], refs[far_count:]
    outer = lax.axis_index("outer")
    totals = []
    for which in range(2):
        total = slots[0][which].astype(F32)
        for slot in slots[1:]:
            total += slot[which].astype(F32)
        totals.append(total.astype(BF16))
    for s, send in zip(distances(len(sends) + 1), sends):
        upward = (outer ^ s) > outer
        send[...] = jnp.where(upward, totals[0], totals[1])


def group_sends(slots, outer_count):
    send = jax.ShapeDtypeStruct(slots[0].shape[1:], BF16)
    return pl.pallas_call(
        functools.partial(totals_kernel, len(slots)),
        name="totals",
        in_specs=[VMEM] * len(slots),
        out_specs=[VMEM] * (outer_count - 1),
        out_shape=[send] * (outer_count - 1),
        compiler_params=SMALL,
    )(*slots)


def scan_kernel(far_count, *refs):
    slots, others, outs = refs[:far_count], refs[far_count:-far_count], refs[-far_count:]
    outer = lax.axis_index("outer")
    _, far = near_far()
    for which in range(2):
        base = jnp.zeros(slots[0].shape[1:], F32)
        for s, other in zip(distances(len(others) + 1), others):
            below = (outer ^ s) < outer
            wanted = below if which == 0 else jnp.logical_not(below)
            base += jnp.where(wanted, other[...].astype(F32), 0.0)
        terms = [slot[which].astype(F32) for slot in slots]
        for s, out in enumerate(outs):
            total = base
            for t, term in enumerate(terms):
                if s != t:
                    below = (far ^ t) < (far ^ s)
                    wanted = below if which == 0 else jnp.logical_not(below)
                    total += jnp.where(wanted, term, 0.0)
            out[which] = total.astype(BF16)


def scan_slots(slots, others):
    far_count, slot = len(slots), jax.ShapeDtypeStruct(slots[0].shape, BF16)
    return pl.pallas_call(
        functools.partial(scan_kernel, far_count),
        name="scan",
        in_specs=[VMEM] * (far_count + len(others)),
        out_specs=[VMEM] * far_count,
        out_shape=[slot] * far_count,
        compiler_params=SMALL,
    )(*slots, *others)


def with_sums(slot, out, into, extra, part, extra_which):
    for which in range(2):

        @pl.when(extra_which == which)
        def _():
            total = slot[which].astype(F32) + extra[which, part].astype(F32)
            out[which, into] = total.astype(BF16)

        @pl.when(extra_which != which)
        def _():
            out[which, into] = slot[which]


def placed_rows(s, count, depth):
    _, far = near_far()
    start = s // count * count * depth + lax.rem(far ^ s, count) * depth
    return pl.ds(pl.multiple_of(start, depth), depth)


def theirs_kernel(s, count, slot, keep, out):
    depth = slot.shape[1]
    near, _ = near_far()
    with_sums(slot, out, pl.ds(0, depth), keep, slot_rows(s, count, depth), near)


def state_for_neighbour(s, count, slot, keep):
    return pl.pallas_call(
        functools.partial(theirs_kernel, s, count),
        name="theirs",
        in_specs=[VMEM] * 2,
        out_specs=VMEM,
        out_shape=jax.ShapeDtypeStruct(slot.shape, BF16),
        compiler_params=SMALL,
    )(slot, keep[s // count])


def local_kernel(*refs):
    tokens, outs = refs[:4], refs[4:]
    rows, width = tokens[0].shape
    at = lax.broadcasted_iota(jnp.int32, (rows, rows), 0)
    to = lax.broadcasted_iota(jnp.int32, (rows, rows), 1)
    lower = at >= to

    def masked(a, b):
        return jnp.where(lower, dot(a, b, 1, 1), 0.0).astype(BF16)

    def second(cols, a, b):
        q, k, v, d = (ref[:, cols] for ref in tokens)
        att, gq, gk, gv = outs
        att[:, cols] = dot(a, v, 1, 0)
        gq[:, cols] = dot(b, k, 1, 0)
        gk[:, cols] = dot(b, q, 0, 0)
        gv[:, cols] = dot(a, d, 0, 0)

    last = None
    for h in range(width // HEAD):
        cols = slice(h * HEAD, (h + 1) * HEAD)
        q, k, v, d = (ref[:, cols] for ref in tokens)
        a, b = masked(q, k), masked(d, v)
        if last:
            second(*last)
        last = (cols, a, b)
    second(*last)


def local_part(tokens):
    rows, width = tokens[0].shape
    return pl.pallas_call(
        local_kernel,
        name="local",
        in_specs=[VMEM] * 4,
        out_specs=[VMEM] * 4,
        out_shape=[jax.ShapeDtypeStruct((rows, width), F32)] * 4,
        cost_estimate=pl.CostEstimate(
            flops=12 * rows * width * HEAD, bytes_accessed=24 * rows * width, transcendentals=0
        ),
        compiler_params=SMALL,
    )(*tokens)


def heads_of(own, p, half):
    piece = half // PIECES
    block, at = divmod(p, PIECES // 2)
    return block_start(own, block, half) + at * piece


def product_piece(scale, own, p, tokens, local, states, held):
    half = states.shape[1]
    piece = half // PIECES
    start = heads_of(own, p, half)
    for n in range(piece // HEAD):
        rows, cols = slice(p * piece + n * HEAD, p * piece + (n + 1) * HEAD), columns(start, n)
        q, k, v, d = (ref[:, cols] for ref in tokens)
        s, g = states[0, rows], states[1, rows]
        parts = (dot(q, s, 1, 0), dot(d, s, 1, 1), dot(v, g, 1, 1), dot(k, g, 1, 0))
        for i, part in enumerate(parts):
            out = (scale * (part + local[i][:, cols])).astype(BF16)
            held[i, :, n * HEAD : (n + 1) * HEAD] = out


def copies_out(own, p, held, outs, sems, half):
    there = pl.ds(pl.multiple_of(heads_of(own, p, half), half // PIECES), half // PIECES)
    return [
        pltpu.make_async_copy(held.at[i], out.at[:, there], sems.at[i, p])
        for i, out in enumerate(outs)
    ]


def finish_own_kernel(scale, slot_count, *refs):
    tokens, local, slots, refs = refs[:4], refs[4:8], refs[8 : 8 + slot_count], refs[8 + slot_count :]
    got, outs, (rest, states, held, sems) = refs[:2], refs[2:6], refs[6:]
    near, _ = near_far()
    count, depth = slot_count // 2, slots[0].shape[1]
    for s, slot in enumerate(slots):
        into, part = placed_rows(s, count, depth), slot_rows(s, count, depth)
        with_sums(slot, states, into, got[s // count], part, 1 - near)
    half = states.shape[1]
    copies = []
    for p in range(PIECES):
        late = p - PIECES // 2
        to = held.at[p] if late < 0 else rest.at[late]
        product_piece(scale, True, p, tokens, local, states, to)
        if late < 0:
            copies += copies_out(True, p, to, outs, sems, half)
            for copy in copies[-4:]:
                copy.start()
    for copy in copies:
        copy.wait()


def finish_own(tokens, local, slots, got, scale):
    rows, width = tokens[0].shape
    half = width // 2
    out = jax.ShapeDtypeStruct((rows, width), BF16)
    pieces = (PIECES // 2, 4, rows, half // PIECES)
    *outs, rest = pl.pallas_call(
        functools.partial(finish_own_kernel, scale, len(slots)),
        name="finish_own",
        in_specs=[VMEM] * (10 + len(slots)),
        out_specs=[ANY] * 4 + [VMEM],
        out_shape=[out] * 4 + [pltpu.VMEM(pieces, BF16)],
        scratch_shapes=[
            pltpu.VMEM((2, half, HEAD), BF16),
            pltpu.VMEM(pieces, BF16),
            pltpu.SemaphoreType.DMA((4, PIECES)),
        ],
        cost_estimate=pl.CostEstimate(
            flops=4 * rows * width * HEAD, bytes_accessed=17 * rows * width, transcendentals=0
        ),
        compiler_params=SMALL,
    )(*tokens, *local, *slots, *got)
    return outs, rest


def finish_other_kernel(scale, slot_count, *refs):
    tokens, local, slots, refs = refs[:4], refs[4:8], refs[8 : 8 + slot_count], refs[8 + slot_count :]
    rest, outs, (states, held, sems, rest_sems) = refs[0], refs[5:9], refs[9:]
    half = states.shape[1]
    copies = []
    for late in range(PIECES // 2):
        copies += copies_out(True, PIECES // 2 + late, rest.at[late], outs, rest_sems, half)
    for copy in copies:
        copy.start()
    count, depth = slot_count // 2, slots[0].shape[1]
    for s, slot in enumerate(slots):
        into = placed_rows(s, count, depth)
        for which in range(2):
            states[which, into] = slot[which]
    for p in range(PIECES):
        product_piece(scale, False, p, tokens, local, states, held.at[p])
        copies += copies_out(False, p, held.at[p], outs, sems, half)
        for copy in copies[-4:]:
            copy.start()
    for copy in copies:
        copy.wait()


def finish_other(tokens, local, slots, rest, scale, before):
    rows, width = tokens[0].shape
    half = width // 2
    out = jax.ShapeDtypeStruct((rows, width), BF16)
    inputs = [*tokens, *local, *slots, rest]
    return pl.pallas_call(
        functools.partial(finish_other_kernel, scale, len(slots)),
        name="finish_other",
        in_specs=[VMEM] * len(inputs) + [ANY] * 4,
        out_specs=[ANY] * 4,
        out_shape=[out] * 4,
        scratch_shapes=[
            pltpu.VMEM((2, half, HEAD), BF16),
            pltpu.VMEM((PIECES, 4, rows, half // PIECES), BF16),
            pltpu.SemaphoreType.DMA((4, PIECES)),
            pltpu.SemaphoreType.DMA((4, PIECES)),
        ],
        input_output_aliases={len(inputs) + i: i for i in range(4)},
        cost_estimate=pl.CostEstimate(
            flops=4 * rows * width * HEAD, bytes_accessed=17 * rows * width, transcendentals=0
        ),
        compiler_params=SMALL,
    )(*inputs, *before)


def swap(x, axis, bits):
    return lax.ppermute(x, axis, [(i, i ^ bits) for i in range(lax.axis_size(axis))])


def swap_far(slots):
    return [slots[0]] + [swap(slots[s], "inner", 2 * s) for s in range(1, len(slots))]


def body(queries, keys, values, cotangent):
    far_count = lax.axis_size("inner") // 2
    outer_count = lax.axis_size("outer")
    scale = float(HEAD * queries.shape[0] * 2 * far_count * outer_count) ** (-0.5)
    tokens, give = load((queries, keys, values, cotangent))
    got = [swap(give, "inner", 1), swap(*sums(tokens, (False, 1)), "inner", 1)]
    keep = sums(tokens, (True, 0), (True, 1))
    slots = [slot for b in range(2) for slot in pair_slots(keep[b], got[b], far_count // 2)]
    slots, local = lax.optimization_barrier((swap_far(slots), local_part(tokens)))
    sends = group_sends(slots, outer_count)
    others = [swap(send, "outer", s) for s, send in zip(distances(outer_count), sends)]
    slots = swap_far(scan_slots(slots, others))
    theirs = [state_for_neighbour(s, far_count // 2, slot, keep) for s, slot in enumerate(slots)]
    arrived = [swap(x, "inner", 1) for x in theirs]
    outs, rest = finish_own(tokens, local, slots, got, scale)
    return tuple(finish_other(tokens, local, arrived, rest, scale, outs))


def solution(mesh):
    spec = P(("outer", "inner"), None)
    return jax.shard_map(
        body, mesh=mesh, in_specs=(spec,) * 4, out_specs=(spec,) * 4, check_vma=False
    )
```

```python
import functools

import jax
import jax.numpy as jnp
from jax import lax
from jax.experimental import pallas as pl
from jax.experimental.pallas import tpu as pltpu
from jax.sharding import PartitionSpec as P

HEAD = 128
PIECES = 2
MIB = 1024 * 1024
ANY = pl.BlockSpec(memory_space=pl.ANY)
VMEM = pl.BlockSpec(memory_space=pltpu.VMEM)
BF16 = jnp.bfloat16
F32 = jnp.float32
SMALL = pltpu.CompilerParams(vmem_limit_bytes=4 * MIB)


def dot(a, b, over_a, over_b):
    return lax.dot_general(
        a, b, (((over_a,), (over_b,)), ((), ())), preferred_element_type=F32
    )


def near_far():
    inner = lax.axis_index("inner")
    return lax.rem(inner, 2), lax.div(inner, 2)


def distances(outer_count):
    return range(outer_count - 1, 0, -1)


def block_start(own, block, half):
    near, far = near_far()
    side = near if own else 1 - near
    top = lax.div(far, lax.axis_size("inner") // 4)
    return side * half + (1 - top if block else top) * (half // 2)


def columns(start, n):
    return pl.ds(pl.multiple_of(start + n * HEAD, HEAD), HEAD)


def slot_rows(s, count, depth):
    _, far = near_far()
    return pl.ds(pl.multiple_of(lax.rem(far ^ s, count) * depth, depth), depth)


def sums_of(tokens, start, out):
    for n in range(out.shape[1] // HEAD):
        cols = columns(start, n) if not isinstance(start, int) else pl.ds(start + n * HEAD, HEAD)
        q, k, v, d = (ref[:, cols] for ref in tokens)
        out[0, n * HEAD : (n + 1) * HEAD] = dot(k, v, 0, 0).astype(BF16)
        out[1, n * HEAD : (n + 1) * HEAD] = dot(q, d, 0, 0).astype(BF16)


def load_kernel(*refs):
    tokens, held, (out, sems) = refs[:4], refs[4:8], refs[8:]
    copies = [
        pltpu.make_async_copy(ref, to, sems.at[i]) for i, (ref, to) in enumerate(zip(tokens, held))
    ]
    for copy in copies:
        copy.start()
    for copy in copies:
        copy.wait()
    width = held[0].shape[1]
    start = block_start(False, 0, width // 2)
    for n in range(4):
        pl.when(start == n * width // 4)(functools.partial(sums_of, held, n * width // 4, out))


def load(tokens):
    rows, width = tokens[0].shape
    *held, sums = pl.pallas_call(
        load_kernel,
        name="load",
        in_specs=[ANY] * 4,
        out_specs=[VMEM] * 5,
        out_shape=[pltpu.VMEM((rows, width), BF16)] * 4 + [pltpu.VMEM((2, width // 4, HEAD), BF16)],
        scratch_shapes=[pltpu.SemaphoreType.DMA((4,))],
        cost_estimate=pl.CostEstimate(
            flops=rows * width * HEAD, bytes_accessed=10 * rows * width, transcendentals=0
        ),
        compiler_params=SMALL,
    )(*(pltpu.with_memory_space_constraint(x, pltpu.HBM) for x in tokens))
    return tuple(held), sums


def sums_kernel(wanted, *refs):
    for (own, block), out in zip(wanted, refs[4:]):
        sums_of(refs[:4], block_start(own, block, refs[0].shape[1] // 2), out)


def sums(tokens, *wanted):
    rows, width = tokens[0].shape
    return pl.pallas_call(
        functools.partial(sums_kernel, wanted),
        name="sums",
        in_specs=[VMEM] * 4,
        out_specs=[VMEM] * len(wanted),
        out_shape=[jax.ShapeDtypeStruct((2, width // 4, HEAD), BF16)] * len(wanted),
        cost_estimate=pl.CostEstimate(
            flops=rows * width * HEAD * len(wanted),
            bytes_accessed=3 * rows * width * len(wanted),
            transcendentals=0,
        ),
        compiler_params=SMALL,
    )(*tokens)


def pair_kernel(keep_ref, got_ref, *slots):
    for s, slot in enumerate(slots):
        part = slot_rows(s, len(slots), slot.shape[1])
        for which in range(2):
            both = keep_ref[which, part].astype(F32) + got_ref[which, part].astype(F32)
            slot[which] = both.astype(BF16)


def pair_slots(keep, got, count):
    slot = jax.ShapeDtypeStruct((2, keep.shape[1] // count, HEAD), BF16)
    return pl.pallas_call(
        pair_kernel,
        name="pair",
        in_specs=[VMEM] * 2,
        out_specs=[VMEM] * count,
        out_shape=[slot] * count,
        compiler_params=SMALL,
    )(keep, got)


def totals_kernel(far_count, *refs):
    slots, sends = refs[:far_count], refs[far_count:]
    outer = lax.axis_index("outer")
    totals = []
    for which in range(2):
        total = slots[0][which].astype(F32)
        for slot in slots[1:]:
            total += slot[which].astype(F32)
        totals.append(total.astype(BF16))
    for s, send in zip(distances(len(sends) + 1), sends):
        upward = (outer ^ s) > outer
        send[...] = jnp.where(upward, totals[0], totals[1])


def group_sends(slots, outer_count):
    send = jax.ShapeDtypeStruct(slots[0].shape[1:], BF16)
    return pl.pallas_call(
        functools.partial(totals_kernel, len(slots)),
        name="totals",
        in_specs=[VMEM] * len(slots),
        out_specs=[VMEM] * (outer_count - 1),
        out_shape=[send] * (outer_count - 1),
        compiler_params=SMALL,
    )(*slots)


def scan_kernel(far_count, *refs):
    slots, others, refs = refs[:far_count], refs[far_count : -far_count - 2], refs[-far_count - 2 :]
    outs, (held, scanned) = refs[:far_count], refs[far_count:]
    outer = lax.axis_index("outer")
    _, far = near_far()
    for s, slot in enumerate(slots):
        held[far ^ s] = slot[...]
    for which in range(2):
        total = jnp.zeros(held.shape[2:], F32)
        for s, other in zip(distances(len(others) + 1), others):
            below = (outer ^ s) < outer
            wanted = below if which == 0 else jnp.logical_not(below)
            total += jnp.where(wanted, other[...].astype(F32), 0.0)
        for i in reversed(range(far_count)) if which else range(far_count):
            scanned[i, which] = total.astype(BF16)
            total += held[i, which].astype(F32)
    for s, out in enumerate(outs):
        out[...] = scanned[far ^ s]


def scan_slots(slots, others):
    far_count, slot = len(slots), jax.ShapeDtypeStruct(slots[0].shape, BF16)
    return pl.pallas_call(
        functools.partial(scan_kernel, far_count),
        name="scan",
        in_specs=[VMEM] * (far_count + len(others)),
        out_specs=[VMEM] * far_count,
        out_shape=[slot] * far_count,
        scratch_shapes=[pltpu.VMEM((far_count, *slot.shape), BF16)] * 2,
        compiler_params=SMALL,
    )(*slots, *others)


def with_sums(slot, which, extra, part):
    return (slot[which].astype(F32) + extra[which, part].astype(F32)).astype(BF16)


def half_rows(s, depth):
    _, far = near_far()
    return pl.ds(pl.multiple_of((far ^ s) * depth, depth), depth)


def by_core(run):
    near, _ = near_far()
    for core in range(2):
        pl.when(near == core)(functools.partial(run, core))


def theirs_kernel(s, count, slot, keep, out):
    part = slot_rows(s, count, slot.shape[1])

    def run(core):
        out[core] = with_sums(slot, core, keep, part)
        out[1 - core] = slot[1 - core]

    by_core(run)


def state_for_neighbour(s, count, slot, keep):
    return pl.pallas_call(
        functools.partial(theirs_kernel, s, count),
        name="theirs",
        in_specs=[VMEM] * 2,
        out_specs=VMEM,
        out_shape=jax.ShapeDtypeStruct(slot.shape, BF16),
        compiler_params=SMALL,
    )(slot, keep[s // count])


def local_kernel(*refs):
    tokens, outs = refs[:4], refs[4:]
    rows, width = tokens[0].shape
    at = lax.broadcasted_iota(jnp.int32, (rows, rows), 0)
    to = lax.broadcasted_iota(jnp.int32, (rows, rows), 1)
    lower = at >= to

    def masked(a, b):
        return jnp.where(lower, dot(a, b, 1, 1), 0.0).astype(BF16)

    def second(cols, a, b):
        q, k, v, d = (ref[:, cols] for ref in tokens)
        att, gq, gk, gv = outs
        att[:, cols] = dot(a, v, 1, 0)
        gq[:, cols] = dot(b, k, 1, 0)
        gk[:, cols] = dot(b, q, 0, 0)
        gv[:, cols] = dot(a, d, 0, 0)

    last = None
    for h in range(width // HEAD):
        cols = slice(h * HEAD, (h + 1) * HEAD)
        q, k, v, d = (ref[:, cols] for ref in tokens)
        a, b = masked(q, k), masked(d, v)
        if last:
            second(*last)
        last = (cols, a, b)
    second(*last)


def local_part(tokens):
    rows, width = tokens[0].shape
    return pl.pallas_call(
        local_kernel,
        name="local",
        in_specs=[VMEM] * 4,
        out_specs=[VMEM] * 4,
        out_shape=[jax.ShapeDtypeStruct((rows, width), F32)] * 4,
        cost_estimate=pl.CostEstimate(
            flops=12 * rows * width * HEAD, bytes_accessed=24 * rows * width, transcendentals=0
        ),
        compiler_params=SMALL,
    )(*tokens)


def product_piece(scale, side, p, tokens, local, states, held):
    half = states.shape[1]
    piece = half // PIECES
    for n in range(piece // HEAD):
        at = p * piece + n * HEAD
        rows, cols = slice(at, at + HEAD), slice(side * half + at, side * half + at + HEAD)
        q, k, v, d = (ref[:, cols] for ref in tokens)
        s, g = states[0, rows], states[1, rows]
        parts = (dot(q, s, 1, 0), dot(d, s, 1, 1), dot(v, g, 1, 1), dot(k, g, 1, 0))
        for i, part in enumerate(parts):
            out = (scale * (part + local[i][:, cols])).astype(BF16)
            held[i, :, n * HEAD : (n + 1) * HEAD] = out


def copies_out(side, p, held, outs, sems, half):
    there = pl.ds(side * half + p * half // PIECES, half // PIECES)
    return [
        pltpu.make_async_copy(held.at[i], out.at[:, there], sems.at[i, p])
        for i, out in enumerate(outs)
    ]


def finish_own_kernel(scale, slot_count, *refs):
    tokens, local, slots, refs = refs[:4], refs[4:8], refs[8 : 8 + slot_count], refs[8 + slot_count :]
    got, outs, (rest, states, held, sems) = refs[:2], refs[2:6], refs[6:]
    count, depth, half = slot_count // 2, slots[0].shape[1], states.shape[1]

    def run(core):
        for s, slot in enumerate(slots):
            into = half_rows(s, depth)
            states[core, into] = slot[core]
            part = slot_rows(s, count, depth)
            states[1 - core, into] = with_sums(slot, 1 - core, got[s // count], part)
        copies = []
        for p in range(PIECES):
            late = p - PIECES // 2
            to = held.at[p] if late < 0 else rest.at[late]
            product_piece(scale, core, p, tokens, local, states, to)
            if late < 0:
                copies += copies_out(core, p, to, outs, sems, half)
                for copy in copies[-4:]:
                    copy.start()
        for copy in copies:
            copy.wait()

    by_core(run)


def finish_own(tokens, local, slots, got, scale):
    rows, width = tokens[0].shape
    half = width // 2
    out = jax.ShapeDtypeStruct((rows, width), BF16)
    pieces = (PIECES // 2, 4, rows, half // PIECES)
    *outs, rest = pl.pallas_call(
        functools.partial(finish_own_kernel, scale, len(slots)),
        name="finish_own",
        in_specs=[VMEM] * (10 + len(slots)),
        out_specs=[ANY] * 4 + [VMEM],
        out_shape=[out] * 4 + [pltpu.VMEM(pieces, BF16)],
        scratch_shapes=[
            pltpu.VMEM((2, half, HEAD), BF16),
            pltpu.VMEM(pieces, BF16),
            pltpu.SemaphoreType.DMA((4, PIECES)),
        ],
        cost_estimate=pl.CostEstimate(
            flops=4 * rows * width * HEAD, bytes_accessed=17 * rows * width, transcendentals=0
        ),
        compiler_params=SMALL,
    )(*tokens, *local, *slots, *got)
    return outs, rest


def finish_other_kernel(scale, slot_count, *refs):
    tokens, local, slots, refs = refs[:4], refs[4:8], refs[8 : 8 + slot_count], refs[8 + slot_count :]
    rest, outs, (states, held, sems, rest_sems) = refs[0], refs[5:9], refs[9:]
    depth, half = slots[0].shape[1], states.shape[1]

    def run(core):
        copies = []
        for late in range(PIECES // 2):
            copies += copies_out(core, PIECES // 2 + late, rest.at[late], outs, rest_sems, half)
        for copy in copies:
            copy.start()
        for s, slot in enumerate(slots):
            states[:, half_rows(s, depth)] = slot[...]
        for p in range(PIECES):
            product_piece(scale, 1 - core, p, tokens, local, states, held.at[p])
            copies += copies_out(1 - core, p, held.at[p], outs, sems, half)
            for copy in copies[-4:]:
                copy.start()
        for copy in copies:
            copy.wait()

    by_core(run)


def finish_other(tokens, local, slots, rest, scale, before):
    rows, width = tokens[0].shape
    half = width // 2
    out = jax.ShapeDtypeStruct((rows, width), BF16)
    inputs = [*tokens, *local, *slots, rest]
    return pl.pallas_call(
        functools.partial(finish_other_kernel, scale, len(slots)),
        name="finish_other",
        in_specs=[VMEM] * len(inputs) + [ANY] * 4,
        out_specs=[ANY] * 4,
        out_shape=[out] * 4,
        scratch_shapes=[
            pltpu.VMEM((2, half, HEAD), BF16),
            pltpu.VMEM((PIECES, 4, rows, half // PIECES), BF16),
            pltpu.SemaphoreType.DMA((4, PIECES)),
            pltpu.SemaphoreType.DMA((4, PIECES)),
        ],
        input_output_aliases={len(inputs) + i: i for i in range(4)},
        cost_estimate=pl.CostEstimate(
            flops=4 * rows * width * HEAD, bytes_accessed=17 * rows * width, transcendentals=0
        ),
        compiler_params=SMALL,
    )(*inputs, *before)


def swap(x, axis, bits):
    return lax.ppermute(x, axis, [(i, i ^ bits) for i in range(lax.axis_size(axis))])


def swap_far(slots):
    return [slots[0]] + [swap(slots[s], "inner", 2 * s) for s in range(1, len(slots))]


def body(queries, keys, values, cotangent):
    far_count = lax.axis_size("inner") // 2
    outer_count = lax.axis_size("outer")
    scale = float(HEAD * queries.shape[0] * 2 * far_count * outer_count) ** (-0.5)
    tokens, give = load((queries, keys, values, cotangent))
    got = [swap(give, "inner", 1), swap(*sums(tokens, (False, 1)), "inner", 1)]
    keep = sums(tokens, (True, 0), (True, 1))
    slots = [slot for b in range(2) for slot in pair_slots(keep[b], got[b], far_count // 2)]
    slots, local = lax.optimization_barrier((swap_far(slots), local_part(tokens)))
    sends = group_sends(slots, outer_count)
    others = [swap(send, "outer", s) for s, send in zip(distances(outer_count), sends)]
    slots = swap_far(scan_slots(slots, others))
    theirs = [state_for_neighbour(s, far_count // 2, slot, keep) for s, slot in enumerate(slots)]
    arrived = [swap(x, "inner", 1) for x in theirs]
    outs, rest = finish_own(tokens, local, slots, got, scale)
    return tuple(finish_other(tokens, local, arrived, rest, scale, outs))


def solution(mesh):
    spec = P(("outer", "inner"), None)
    return jax.shard_map(
        body, mesh=mesh, in_specs=(spec,) * 4, out_specs=(spec,) * 4, check_vma=False
    )
```

```python
import functools

import jax
import jax.numpy as jnp
from jax import lax
from jax.experimental import pallas as pl
from jax.experimental.pallas import tpu as pltpu
from jax.sharding import PartitionSpec as P

HEAD = 128
PIECES = 4
MIB = 1024 * 1024
ANY = pl.BlockSpec(memory_space=pl.ANY)
VMEM = pl.BlockSpec(memory_space=pltpu.VMEM)
BF16 = jnp.bfloat16
F32 = jnp.float32
SMALL = pltpu.CompilerParams(vmem_limit_bytes=4 * MIB)


def dot(a, b, over_a, over_b):
    return lax.dot_general(
        a, b, (((over_a,), (over_b,)), ((), ())), preferred_element_type=F32
    )


def near_far():
    inner = lax.axis_index("inner")
    return lax.rem(inner, 2), lax.div(inner, 2)


def distances(outer_count):
    return range(outer_count - 1, 0, -1)


def block_start(own, block, half):
    near, far = near_far()
    side = near if own else 1 - near
    top = lax.div(far, lax.axis_size("inner") // 4)
    return side * half + (1 - top if block else top) * (half // 2)


def columns(start, n):
    return pl.ds(pl.multiple_of(start + n * HEAD, HEAD), HEAD)


def slot_rows(s, count, depth):
    _, far = near_far()
    return pl.ds(pl.multiple_of(lax.rem(far ^ s, count) * depth, depth), depth)


def one_ahead(products, use):
    last = None
    for key, product in products:
        if last:
            use(*last)
        last = key, product
    use(*last)


def sums_of(tokens, start, out):
    q, k, v, d = tokens

    def products():
        for n in range(out.shape[1] // HEAD):
            cols = pl.ds(start + n * HEAD, HEAD) if isinstance(start, int) else columns(start, n)
            for which, (a, b) in enumerate(((k, v), (q, d))):
                yield (which, n), dot(a[:, cols], b[:, cols], 0, 0)

    def use(key, product):
        which, n = key
        out[which, n * HEAD : (n + 1) * HEAD] = product.astype(BF16)

    one_ahead(products(), use)


def load_kernel(*refs):
    tokens, held, (out, sems) = refs[:4], refs[4:8], refs[8:]
    copies = [
        pltpu.make_async_copy(ref, to, sems.at[i]) for i, (ref, to) in enumerate(zip(tokens, held))
    ]
    for copy in copies:
        copy.start()
    for copy in copies:
        copy.wait()
    width = held[0].shape[1]
    start = block_start(False, 0, width // 2)
    for n in range(4):
        pl.when(start == n * width // 4)(functools.partial(sums_of, held, n * width // 4, out))


def load(tokens):
    rows, width = tokens[0].shape
    *held, sums = pl.pallas_call(
        load_kernel,
        name="load",
        in_specs=[ANY] * 4,
        out_specs=[VMEM] * 5,
        out_shape=[pltpu.VMEM((rows, width), BF16)] * 4 + [pltpu.VMEM((2, width // 4, HEAD), BF16)],
        scratch_shapes=[pltpu.SemaphoreType.DMA((4,))],
        cost_estimate=pl.CostEstimate(
            flops=rows * width * HEAD, bytes_accessed=10 * rows * width, transcendentals=0
        ),
        compiler_params=SMALL,
    )(*(pltpu.with_memory_space_constraint(x, pltpu.HBM) for x in tokens))
    return tuple(held), sums


def sums_kernel(wanted, *refs):
    for (own, block), out in zip(wanted, refs[4:]):
        sums_of(refs[:4], block_start(own, block, refs[0].shape[1] // 2), out)


def sums(tokens, *wanted):
    rows, width = tokens[0].shape
    return pl.pallas_call(
        functools.partial(sums_kernel, wanted),
        name="sums",
        in_specs=[VMEM] * 4,
        out_specs=[VMEM] * len(wanted),
        out_shape=[jax.ShapeDtypeStruct((2, width // 4, HEAD), BF16)] * len(wanted),
        cost_estimate=pl.CostEstimate(
            flops=rows * width * HEAD * len(wanted),
            bytes_accessed=3 * rows * width * len(wanted),
            transcendentals=0,
        ),
        compiler_params=SMALL,
    )(*tokens)


def pair_kernel(keep_ref, got_ref, *slots):
    for s, slot in enumerate(slots):
        part = slot_rows(s, len(slots), slot.shape[1])
        for which in range(2):
            both = keep_ref[which, part].astype(F32) + got_ref[which, part].astype(F32)
            slot[which] = both.astype(BF16)


def pair_slots(keep, got, count):
    slot = jax.ShapeDtypeStruct((2, keep.shape[1] // count, HEAD), BF16)
    return pl.pallas_call(
        pair_kernel,
        name="pair",
        in_specs=[VMEM] * 2,
        out_specs=[VMEM] * count,
        out_shape=[slot] * count,
        compiler_params=SMALL,
    )(keep, got)


def totals_kernel(far_count, *refs):
    slots, sends = refs[:far_count], refs[far_count:]
    outer = lax.axis_index("outer")
    totals = []
    for which in range(2):
        total = slots[0][which].astype(F32)
        for slot in slots[1:]:
            total += slot[which].astype(F32)
        totals.append(total.astype(BF16))
    for s, send in zip(distances(len(sends) + 1), sends):
        upward = (outer ^ s) > outer
        send[...] = jnp.where(upward, totals[0], totals[1])


def group_sends(slots, outer_count):
    send = jax.ShapeDtypeStruct(slots[0].shape[1:], BF16)
    return pl.pallas_call(
        functools.partial(totals_kernel, len(slots)),
        name="totals",
        in_specs=[VMEM] * len(slots),
        out_specs=[VMEM] * (outer_count - 1),
        out_shape=[send] * (outer_count - 1),
        compiler_params=SMALL,
    )(*slots)


def scan_kernel(far_count, *refs):
    slots, others, refs = refs[:far_count], refs[far_count : -far_count - 2], refs[-far_count - 2 :]
    outs, (held, scanned) = refs[:far_count], refs[far_count:]
    outer = lax.axis_index("outer")
    _, far = near_far()
    for s, slot in enumerate(slots):
        held[far ^ s] = slot[...]
    for which in range(2):
        total = jnp.zeros(held.shape[2:], F32)
        for s, other in zip(distances(len(others) + 1), others):
            below = (outer ^ s) < outer
            wanted = below if which == 0 else jnp.logical_not(below)
            total += jnp.where(wanted, other[...].astype(F32), 0.0)
        for i in reversed(range(far_count)) if which else range(far_count):
            scanned[i, which] = total.astype(BF16)
            total += held[i, which].astype(F32)
    for s, out in enumerate(outs):
        out[...] = scanned[far ^ s]


def scan_slots(slots, others):
    far_count, slot = len(slots), jax.ShapeDtypeStruct(slots[0].shape, BF16)
    return pl.pallas_call(
        functools.partial(scan_kernel, far_count),
        name="scan",
        in_specs=[VMEM] * (far_count + len(others)),
        out_specs=[VMEM] * far_count,
        out_shape=[slot] * far_count,
        scratch_shapes=[pltpu.VMEM((far_count, *slot.shape), BF16)] * 2,
        compiler_params=SMALL,
    )(*slots, *others)


def with_sums(slot, which, extra, part):
    return (slot[which].astype(F32) + extra[which, part].astype(F32)).astype(BF16)


def half_rows(s, depth):
    _, far = near_far()
    return pl.ds(pl.multiple_of((far ^ s) * depth, depth), depth)


def by_core(run):
    near, _ = near_far()
    for core in range(2):
        pl.when(near == core)(functools.partial(run, core))


def theirs_kernel(s, count, slot, keep, out):
    part = slot_rows(s, count, slot.shape[1])

    def run(core):
        out[core] = with_sums(slot, core, keep, part)
        out[1 - core] = slot[1 - core]

    by_core(run)


def state_for_neighbour(s, count, slot, keep):
    return pl.pallas_call(
        functools.partial(theirs_kernel, s, count),
        name="theirs",
        in_specs=[VMEM] * 2,
        out_specs=VMEM,
        out_shape=jax.ShapeDtypeStruct(slot.shape, BF16),
        compiler_params=SMALL,
    )(slot, keep[s // count])


def local_kernel(*refs):
    tokens, outs = refs[:4], refs[4:]
    rows, width = tokens[0].shape
    at = lax.broadcasted_iota(jnp.int32, (rows, rows), 0)
    to = lax.broadcasted_iota(jnp.int32, (rows, rows), 1)
    lower = at >= to

    def masked(a, b):
        return jnp.where(lower, dot(a, b, 1, 1), 0.0).astype(BF16)

    def second(cols, a, b):
        q, k, v, d = (ref[:, cols] for ref in tokens)
        att, gq, gk, gv = outs
        att[:, cols] = dot(a, v, 1, 0)
        gq[:, cols] = dot(b, k, 1, 0)
        gk[:, cols] = dot(b, q, 0, 0)
        gv[:, cols] = dot(a, d, 0, 0)

    last = None
    for h in range(width // HEAD):
        cols = slice(h * HEAD, (h + 1) * HEAD)
        q, k, v, d = (ref[:, cols] for ref in tokens)
        a, b = masked(q, k), masked(d, v)
        if last:
            second(*last)
        last = (cols, a, b)
    second(*last)


def local_part(tokens):
    rows, width = tokens[0].shape
    return pl.pallas_call(
        local_kernel,
        name="local",
        in_specs=[VMEM] * 4,
        out_specs=[VMEM] * 4,
        out_shape=[jax.ShapeDtypeStruct((rows, width), F32)] * 4,
        cost_estimate=pl.CostEstimate(
            flops=12 * rows * width * HEAD, bytes_accessed=24 * rows * width, transcendentals=0
        ),
        compiler_params=SMALL,
    )(*tokens)


def all_products(scale, side, tokens, local, states, store):
    half = states.shape[1]
    q, k, v, d = tokens

    def products():
        for h in range(half // HEAD):
            rows = slice(h * HEAD, (h + 1) * HEAD)
            cols = slice(side * half + h * HEAD, side * half + (h + 1) * HEAD)
            s, g = states[0, rows], states[1, rows]
            yield (h, 0, cols), dot(q[:, cols], s, 1, 0)
            yield (h, 1, cols), dot(d[:, cols], s, 1, 1)
            yield (h, 2, cols), dot(v[:, cols], g, 1, 1)
            yield (h, 3, cols), dot(k[:, cols], g, 1, 0)

    def use(key, product):
        h, i, cols = key
        store(h, i, (scale * (product + local[i][:, cols])).astype(BF16))

    one_ahead(products(), use)


def copies_out(side, p, held, outs, sems, half):
    there = pl.ds(side * half + p * half // PIECES, half // PIECES)
    return [
        pltpu.make_async_copy(held.at[i], out.at[:, there], sems.at[i, p])
        for i, out in enumerate(outs)
    ]


def finish_own_kernel(scale, slot_count, *refs):
    tokens, local, slots, refs = refs[:4], refs[4:8], refs[8 : 8 + slot_count], refs[8 + slot_count :]
    got, outs, (rest, states, held, sems) = refs[:2], refs[2:6], refs[6:]
    count, depth, half = slot_count // 2, slots[0].shape[1], states.shape[1]

    def run(core):
        for s, slot in enumerate(slots):
            into = half_rows(s, depth)
            states[core, into] = slot[core]
            part = slot_rows(s, count, depth)
            states[1 - core, into] = with_sums(slot, 1 - core, got[s // count], part)
        copies = []
        heads = half // PIECES // HEAD

        def store(h, i, out):
            p, n = divmod(h, heads)
            late = p - PIECES // 2
            to = held.at[p] if late < 0 else rest.at[late]
            to[i, :, n * HEAD : (n + 1) * HEAD] = out
            if late < 0 and n == heads - 1 and i == 3:
                copies.extend(copies_out(core, p, to, outs, sems, half))
                for copy in copies[-4:]:
                    copy.start()

        all_products(scale, core, tokens, local, states, store)
        for copy in copies:
            copy.wait()

    by_core(run)


def finish_own(tokens, local, slots, got, scale):
    rows, width = tokens[0].shape
    half = width // 2
    out = jax.ShapeDtypeStruct((rows, width), BF16)
    pieces = (PIECES // 2, 4, rows, half // PIECES)
    *outs, rest = pl.pallas_call(
        functools.partial(finish_own_kernel, scale, len(slots)),
        name="finish_own",
        in_specs=[VMEM] * (10 + len(slots)),
        out_specs=[ANY] * 4 + [VMEM],
        out_shape=[out] * 4 + [pltpu.VMEM(pieces, BF16)],
        scratch_shapes=[
            pltpu.VMEM((2, half, HEAD), BF16),
            pltpu.VMEM(pieces, BF16),
            pltpu.SemaphoreType.DMA((4, PIECES)),
        ],
        cost_estimate=pl.CostEstimate(
            flops=4 * rows * width * HEAD, bytes_accessed=17 * rows * width, transcendentals=0
        ),
        compiler_params=SMALL,
    )(*tokens, *local, *slots, *got)
    return outs, rest


def finish_other_kernel(scale, slot_count, *refs):
    tokens, local, slots, refs = refs[:4], refs[4:8], refs[8 : 8 + slot_count], refs[8 + slot_count :]
    rest, outs, (states, held, sems, rest_sems) = refs[0], refs[5:9], refs[9:]
    depth, half = slots[0].shape[1], states.shape[1]

    def run(core):
        copies = []
        for late in range(PIECES // 2):
            copies += copies_out(core, PIECES // 2 + late, rest.at[late], outs, rest_sems, half)
        for copy in copies:
            copy.start()
        for s, slot in enumerate(slots):
            states[:, half_rows(s, depth)] = slot[...]
        heads = half // PIECES // HEAD

        def store(h, i, out):
            p, n = divmod(h, heads)
            held[p, i, :, n * HEAD : (n + 1) * HEAD] = out
            if n == heads - 1 and i == 3:
                copies.extend(copies_out(1 - core, p, held.at[p], outs, sems, half))
                for copy in copies[-4:]:
                    copy.start()

        all_products(scale, 1 - core, tokens, local, states, store)
        for copy in copies:
            copy.wait()

    by_core(run)


def finish_other(tokens, local, slots, rest, scale, before):
    rows, width = tokens[0].shape
    half = width // 2
    out = jax.ShapeDtypeStruct((rows, width), BF16)
    inputs = [*tokens, *local, *slots, rest]
    return pl.pallas_call(
        functools.partial(finish_other_kernel, scale, len(slots)),
        name="finish_other",
        in_specs=[VMEM] * len(inputs) + [ANY] * 4,
        out_specs=[ANY] * 4,
        out_shape=[out] * 4,
        scratch_shapes=[
            pltpu.VMEM((2, half, HEAD), BF16),
            pltpu.VMEM((PIECES, 4, rows, half // PIECES), BF16),
            pltpu.SemaphoreType.DMA((4, PIECES)),
            pltpu.SemaphoreType.DMA((4, PIECES)),
        ],
        input_output_aliases={len(inputs) + i: i for i in range(4)},
        cost_estimate=pl.CostEstimate(
            flops=4 * rows * width * HEAD, bytes_accessed=17 * rows * width, transcendentals=0
        ),
        compiler_params=SMALL,
    )(*inputs, *before)


def swap(x, axis, bits):
    return lax.ppermute(x, axis, [(i, i ^ bits) for i in range(lax.axis_size(axis))])


def swap_far(slots):
    return [slots[0]] + [swap(slots[s], "inner", 2 * s) for s in range(1, len(slots))]


def body(queries, keys, values, cotangent):
    far_count = lax.axis_size("inner") // 2
    outer_count = lax.axis_size("outer")
    scale = float(HEAD * queries.shape[0] * 2 * far_count * outer_count) ** (-0.5)
    tokens, give = load((queries, keys, values, cotangent))
    got = [swap(give, "inner", 1), swap(*sums(tokens, (False, 1)), "inner", 1)]
    keep = sums(tokens, (True, 0), (True, 1))
    slots = [slot for b in range(2) for slot in pair_slots(keep[b], got[b], far_count // 2)]
    slots, local = lax.optimization_barrier((swap_far(slots), local_part(tokens)))
    sends = group_sends(slots, outer_count)
    others = [swap(send, "outer", s) for s, send in zip(distances(outer_count), sends)]
    slots = swap_far(scan_slots(slots, others))
    theirs = [state_for_neighbour(s, far_count // 2, slot, keep) for s, slot in enumerate(slots)]
    arrived = [swap(x, "inner", 1) for x in theirs]
    outs, rest = finish_own(tokens, local, slots, got, scale)
    return tuple(finish_other(tokens, local, arrived, rest, scale, outs))


def solution(mesh):
    spec = P(("outer", "inner"), None)
    return jax.shard_map(
        body, mesh=mesh, in_specs=(spec,) * 4, out_specs=(spec,) * 4, check_vma=False
    )
```

```python
import functools

import jax
import jax.numpy as jnp
from jax import lax
from jax.experimental import pallas as pl
from jax.experimental.pallas import tpu as pltpu
from jax.sharding import PartitionSpec as P

HEAD = 128
MIB = 1024 * 1024
ANY = pl.BlockSpec(memory_space=pl.ANY)
VMEM = pl.BlockSpec(memory_space=pltpu.VMEM)
BF16 = jnp.bfloat16
F32 = jnp.float32
SMALL = pltpu.CompilerParams(vmem_limit_bytes=4 * MIB)


def dot(a, b, over_a, over_b):
    return lax.dot_general(
        a, b, (((over_a,), (over_b,)), ((), ())), preferred_element_type=F32
    )


def near_far():
    inner = lax.axis_index("inner")
    return lax.rem(inner, 2), lax.div(inner, 2)


def distances(outer_count):
    return range(outer_count - 1, 0, -1)


def block_start(own, block, half):
    near, far = near_far()
    side = near if own else 1 - near
    top = lax.div(far, lax.axis_size("inner") // 4)
    return side * half + (1 - top if block else top) * (half // 2)


def columns(start, n):
    return pl.ds(pl.multiple_of(start + n * HEAD, HEAD), HEAD)


def slot_rows(s, count, depth):
    _, far = near_far()
    return pl.ds(pl.multiple_of(lax.rem(far ^ s, count) * depth, depth), depth)


def one_ahead(products, use):
    last = None
    for key, product in products:
        if last:
            use(*last)
        last = key, product
    use(*last)


def sums_of(tokens, start, out):
    q, k, v, d = tokens

    def products():
        for n in range(out.shape[1] // HEAD):
            cols = pl.ds(start + n * HEAD, HEAD) if isinstance(start, int) else columns(start, n)
            for which, (a, b) in enumerate(((k, v), (q, d))):
                yield (which, n), dot(a[:, cols], b[:, cols], 0, 0)

    def use(key, product):
        which, n = key
        out[which, n * HEAD : (n + 1) * HEAD] = product.astype(BF16)

    one_ahead(products(), use)


def load_kernel(*refs):
    tokens, held, (out, sems) = refs[:4], refs[4:8], refs[8:]
    copies = [
        pltpu.make_async_copy(ref, to, sems.at[i]) for i, (ref, to) in enumerate(zip(tokens, held))
    ]
    for copy in copies:
        copy.start()
    for copy in copies:
        copy.wait()
    width = held[0].shape[1]
    start = block_start(False, 0, width // 2)
    for n in range(4):
        pl.when(start == n * width // 4)(functools.partial(sums_of, held, n * width // 4, out))


def load(tokens):
    rows, width = tokens[0].shape
    *held, sums = pl.pallas_call(
        load_kernel,
        name="load",
        in_specs=[ANY] * 4,
        out_specs=[VMEM] * 5,
        out_shape=[pltpu.VMEM((rows, width), BF16)] * 4 + [pltpu.VMEM((2, width // 4, HEAD), BF16)],
        scratch_shapes=[pltpu.SemaphoreType.DMA((4,))],
        cost_estimate=pl.CostEstimate(
            flops=rows * width * HEAD, bytes_accessed=10 * rows * width, transcendentals=0
        ),
        compiler_params=SMALL,
    )(*(pltpu.with_memory_space_constraint(x, pltpu.HBM) for x in tokens))
    return tuple(held), sums


def sums_kernel(wanted, *refs):
    for (own, block), out in zip(wanted, refs[4:]):
        sums_of(refs[:4], block_start(own, block, refs[0].shape[1] // 2), out)


def sums(tokens, *wanted):
    rows, width = tokens[0].shape
    return pl.pallas_call(
        functools.partial(sums_kernel, wanted),
        name="sums",
        in_specs=[VMEM] * 4,
        out_specs=[VMEM] * len(wanted),
        out_shape=[jax.ShapeDtypeStruct((2, width // 4, HEAD), BF16)] * len(wanted),
        cost_estimate=pl.CostEstimate(
            flops=rows * width * HEAD * len(wanted),
            bytes_accessed=3 * rows * width * len(wanted),
            transcendentals=0,
        ),
        compiler_params=SMALL,
    )(*tokens)


def pair_kernel(keep_ref, got_ref, *slots):
    for s, slot in enumerate(slots):
        part = slot_rows(s, len(slots), slot.shape[1])
        for which in range(2):
            both = keep_ref[which, part].astype(F32) + got_ref[which, part].astype(F32)
            slot[which] = both.astype(BF16)


def pair_slots(keep, got, count):
    slot = jax.ShapeDtypeStruct((2, keep.shape[1] // count, HEAD), BF16)
    return pl.pallas_call(
        pair_kernel,
        name="pair",
        in_specs=[VMEM] * 2,
        out_specs=[VMEM] * count,
        out_shape=[slot] * count,
        compiler_params=SMALL,
    )(keep, got)


def totals_kernel(far_count, *refs):
    slots, sends = refs[:far_count], refs[far_count:]
    outer = lax.axis_index("outer")
    totals = []
    for which in range(2):
        total = slots[0][which].astype(F32)
        for slot in slots[1:]:
            total += slot[which].astype(F32)
        totals.append(total.astype(BF16))
    for s, send in zip(distances(len(sends) + 1), sends):
        upward = (outer ^ s) > outer
        send[...] = jnp.where(upward, totals[0], totals[1])


def group_sends(slots, outer_count):
    send = jax.ShapeDtypeStruct(slots[0].shape[1:], BF16)
    return pl.pallas_call(
        functools.partial(totals_kernel, len(slots)),
        name="totals",
        in_specs=[VMEM] * len(slots),
        out_specs=[VMEM] * (outer_count - 1),
        out_shape=[send] * (outer_count - 1),
        compiler_params=SMALL,
    )(*slots)


def scan_kernel(far_count, *refs):
    slots, others, refs = refs[:far_count], refs[far_count : -far_count - 2], refs[-far_count - 2 :]
    outs, (held, scanned) = refs[:far_count], refs[far_count:]
    outer = lax.axis_index("outer")
    _, far = near_far()
    for s, slot in enumerate(slots):
        held[far ^ s] = slot[...]
    for which in range(2):
        total = jnp.zeros(held.shape[2:], F32)
        for s, other in zip(distances(len(others) + 1), others):
            below = (outer ^ s) < outer
            wanted = below if which == 0 else jnp.logical_not(below)
            total += jnp.where(wanted, other[...].astype(F32), 0.0)
        for i in reversed(range(far_count)) if which else range(far_count):
            scanned[i, which] = total.astype(BF16)
            total += held[i, which].astype(F32)
    for s, out in enumerate(outs):
        out[...] = scanned[far ^ s]


def scan_slots(slots, others):
    far_count, slot = len(slots), jax.ShapeDtypeStruct(slots[0].shape, BF16)
    return pl.pallas_call(
        functools.partial(scan_kernel, far_count),
        name="scan",
        in_specs=[VMEM] * (far_count + len(others)),
        out_specs=[VMEM] * far_count,
        out_shape=[slot] * far_count,
        scratch_shapes=[pltpu.VMEM((far_count, *slot.shape), BF16)] * 2,
        compiler_params=SMALL,
    )(*slots, *others)


def with_sums(slot, which, extra, part):
    return (slot[which].astype(F32) + extra[which, part].astype(F32)).astype(BF16)


def by_core(run):
    near, _ = near_far()
    for core in range(2):
        pl.when(near == core)(functools.partial(run, core))


def theirs_kernel(s, count, slot, keep, out):
    part = slot_rows(s, count, slot.shape[1])

    def run(core):
        out[core] = with_sums(slot, core, keep, part)
        out[1 - core] = slot[1 - core]

    by_core(run)


def state_for_neighbour(s, count, slot, keep):
    return pl.pallas_call(
        functools.partial(theirs_kernel, s, count),
        name="theirs",
        in_specs=[VMEM] * 2,
        out_specs=VMEM,
        out_shape=jax.ShapeDtypeStruct(slot.shape, BF16),
        compiler_params=SMALL,
    )(slot, keep[s // count])


def local_kernel(*refs):
    tokens, outs = refs[:4], refs[4:]
    rows, width = tokens[0].shape
    at = lax.broadcasted_iota(jnp.int32, (rows, rows), 0)
    to = lax.broadcasted_iota(jnp.int32, (rows, rows), 1)
    lower = at >= to

    def masked(a, b):
        return jnp.where(lower, dot(a, b, 1, 1), 0.0).astype(BF16)

    def second(cols, a, b):
        q, k, v, d = (ref[:, cols] for ref in tokens)
        att, gq, gk, gv = outs
        att[:, cols] = dot(a, v, 1, 0)
        gq[:, cols] = dot(b, k, 1, 0)
        gk[:, cols] = dot(b, q, 0, 0)
        gv[:, cols] = dot(a, d, 0, 0)

    last = None
    for h in range(width // HEAD):
        cols = slice(h * HEAD, (h + 1) * HEAD)
        q, k, v, d = (ref[:, cols] for ref in tokens)
        a, b = masked(q, k), masked(d, v)
        if last:
            second(*last)
        last = (cols, a, b)
    second(*last)


def local_part(tokens):
    rows, width = tokens[0].shape
    return pl.pallas_call(
        local_kernel,
        name="local",
        in_specs=[VMEM] * 4,
        out_specs=[VMEM] * 4,
        out_shape=[jax.ShapeDtypeStruct((rows, width), F32)] * 4,
        cost_estimate=pl.CostEstimate(
            flops=12 * rows * width * HEAD, bytes_accessed=24 * rows * width, transcendentals=0
        ),
        compiler_params=SMALL,
    )(*tokens)


def all_products(scale, start, tokens, local, states, store):
    q, k, v, d = tokens

    def products():
        for n in range(states.shape[1] // HEAD):
            rows = slice(n * HEAD, (n + 1) * HEAD)
            cols = slice(start + n * HEAD, start + (n + 1) * HEAD)
            s, g = states[0, rows], states[1, rows]
            yield (rows, 0, cols), dot(q[:, cols], s, 1, 0)
            yield (rows, 1, cols), dot(d[:, cols], s, 1, 1)
            yield (rows, 2, cols), dot(v[:, cols], g, 1, 1)
            yield (rows, 3, cols), dot(k[:, cols], g, 1, 0)

    def use(key, product):
        rows, i, cols = key
        store(rows, i, (scale * (product + local[i][:, cols])).astype(BF16))

    one_ahead(products(), use)


def copies_out(own, block, held, outs, sems):
    size = held.shape[2]
    start = block_start(own, block, outs[0].shape[1] // 2)
    there = pl.ds(pl.multiple_of(start, size), size)
    return [
        pltpu.make_async_copy(held.at[i], out.at[:, there], sems.at[i])
        for i, out in enumerate(outs)
    ]


def finish_kernel(scale, own, block, count, rests, hold, *refs):
    tokens, local, slots, refs = refs[:4], refs[4:8], refs[8 : 8 + count], refs[8 + count :]
    got, refs = (refs[0], refs[1:]) if own else (None, refs)
    late, refs = refs[: len(rests)], refs[len(rests) :]
    if hold:
        held, states = refs
    else:
        outs, (states, held, sems) = refs[-7:-3], refs[-3:]
    width, depth = tokens[0].shape[1], slots[0].shape[1]
    copies = []
    for n, (rest, where) in enumerate(zip(late, rests)):
        copies += copies_out(*where, rest, outs, sems.at[n + 1])
    for copy in copies:
        copy.start()

    def store(rows, i, out):
        held[i, :, rows] = out

    def run(quarter):
        start = quarter * width // 4
        core = quarter // 2 if own else 1 - quarter // 2
        for s, slot in enumerate(slots):
            part = slot_rows(s, count, depth)
            if own:
                states[core, part] = slot[core]
                states[1 - core, part] = with_sums(slot, 1 - core, got, part)
            else:
                states[:, part] = slot[...]
        all_products(scale, start, tokens, local, states, store)

    start = block_start(own, block, width // 2)
    for quarter in range(4):
        pl.when(start == quarter * width // 4)(functools.partial(run, quarter))
    if not hold:
        last = copies_out(own, block, held, outs, sems.at[0])
        for copy in last:
            copy.start()
        for copy in copies + last:
            copy.wait()


def finish(own, block, tokens, local, slots, scale, got=(), rests=(), before=(), hold=False):
    rows, width = tokens[0].shape
    out = jax.ShapeDtypeStruct((rows, width), BF16)
    piece = pltpu.VMEM((4, rows, width // 4), BF16)
    inputs = [*tokens, *local, *slots, *got, *(x for _, x in rests)]
    states = pltpu.VMEM((2, width // 4, HEAD), BF16)
    wheres = [where for where, _ in rests]
    return pl.pallas_call(
        functools.partial(finish_kernel, scale, own, block, len(slots), wheres, hold),
        name="finish",
        in_specs=[VMEM] * len(inputs) + [ANY] * len(before),
        out_specs=VMEM if hold else [ANY] * 4,
        out_shape=piece if hold else [out] * 4,
        scratch_shapes=[states]
        + ([] if hold else [piece, pltpu.SemaphoreType.DMA((1 + len(rests), 4))]),
        input_output_aliases={len(inputs) + i: i for i in range(len(before))},
        cost_estimate=pl.CostEstimate(
            flops=2 * rows * width * HEAD, bytes_accessed=8 * rows * width, transcendentals=0
        ),
        compiler_params=SMALL,
    )(*inputs, *before)


def swap(x, axis, bits):
    return lax.ppermute(x, axis, [(i, i ^ bits) for i in range(lax.axis_size(axis))])


def swap_far(slots):
    return [slots[0]] + [swap(slots[s], "inner", 2 * s) for s in range(1, len(slots))]


def body(queries, keys, values, cotangent):
    far_count = lax.axis_size("inner") // 2
    outer_count = lax.axis_size("outer")
    scale = float(HEAD * queries.shape[0] * 2 * far_count * outer_count) ** (-0.5)
    tokens, give = load((queries, keys, values, cotangent))
    got = [swap(give, "inner", 1), swap(*sums(tokens, (False, 1)), "inner", 1)]
    keep = sums(tokens, (True, 0), (True, 1))
    slots = [slot for b in range(2) for slot in pair_slots(keep[b], got[b], far_count // 2)]
    slots, local = lax.optimization_barrier((swap_far(slots), local_part(tokens)))
    sends = group_sends(slots, outer_count)
    others = [swap(send, "outer", s) for s, send in zip(distances(outer_count), sends)]
    slots = swap_far(scan_slots(slots, others))
    half = far_count // 2
    arrived, outs, rests = [], (), []
    for block in range(2):
        part = slots[block * half : (block + 1) * half]
        if block:
            part, outs = lax.optimization_barrier((part, tuple(outs)))
        for s, slot in enumerate(part):
            theirs = state_for_neighbour(block * half + s, half, slot, keep)
            arrived.append(swap(theirs, "inner", 1))
        made = finish(True, block, tokens, local, part, scale, got=got[block : block + 1], hold=block)
        outs = outs or made
    rests.append(((True, 1), made))
    made = finish(False, 0, tokens, local, arrived[:half], scale, hold=True)
    rests.append(((False, 0), made))
    return tuple(finish(False, 1, tokens, local, arrived[half:], scale, rests=rests, before=outs))


def solution(mesh):
    spec = P(("outer", "inner"), None)
    return jax.shard_map(
        body, mesh=mesh, in_specs=(spec,) * 4, out_specs=(spec,) * 4, check_vma=False
    )
```

```python
import functools

import jax
import jax.numpy as jnp
from jax import lax
from jax.experimental import pallas as pl
from jax.experimental.pallas import tpu as pltpu
from jax.sharding import PartitionSpec as P

HEAD = 128
MIB = 1024 * 1024
ANY = pl.BlockSpec(memory_space=pl.ANY)
VMEM = pl.BlockSpec(memory_space=pltpu.VMEM)
BF16 = jnp.bfloat16
F32 = jnp.float32
SMALL = pltpu.CompilerParams(vmem_limit_bytes=4 * MIB)


def dot(a, b, over_a, over_b):
    return lax.dot_general(
        a, b, (((over_a,), (over_b,)), ((), ())), preferred_element_type=F32
    )


def near_far():
    inner = lax.axis_index("inner")
    return lax.rem(inner, 2), lax.div(inner, 2)


def distances(outer_count):
    return range(outer_count - 1, 0, -1)


def block_start(own, block, half):
    near, far = near_far()
    side = near if own else 1 - near
    top = lax.div(far, lax.axis_size("inner") // 4)
    return side * half + (1 - top if block else top) * (half // 2)


def columns(start, n):
    return pl.ds(pl.multiple_of(start + n * HEAD, HEAD), HEAD)


def slot_rows(s, count, depth):
    _, far = near_far()
    return pl.ds(pl.multiple_of(lax.rem(far ^ s, count) * depth, depth), depth)


def one_ahead(products, use):
    last = None
    for key, product in products:
        if last:
            use(*last)
        last = key, product
    use(*last)


def sums_of(tokens, start, out):
    q, k, v, d = tokens

    def products():
        for n in range(out.shape[1] // HEAD):
            cols = pl.ds(start + n * HEAD, HEAD) if isinstance(start, int) else columns(start, n)
            for which, (a, b) in enumerate(((k, v), (q, d))):
                yield (which, n), dot(a[:, cols], b[:, cols], 0, 0)

    def use(key, product):
        which, n = key
        out[which, n * HEAD : (n + 1) * HEAD] = product.astype(BF16)

    one_ahead(products(), use)


def load_kernel(*refs):
    tokens, held, (out, sems) = refs[:4], refs[4:8], refs[8:]
    copies = [
        pltpu.make_async_copy(ref, to, sems.at[i]) for i, (ref, to) in enumerate(zip(tokens, held))
    ]
    for copy in copies:
        copy.start()
    for copy in copies:
        copy.wait()
    width = held[0].shape[1]
    start = block_start(False, 0, width // 2)
    for n in range(4):
        pl.when(start == n * width // 4)(functools.partial(sums_of, held, n * width // 4, out))


def load(tokens):
    rows, width = tokens[0].shape
    *held, sums = pl.pallas_call(
        load_kernel,
        name="load",
        in_specs=[ANY] * 4,
        out_specs=[VMEM] * 5,
        out_shape=[pltpu.VMEM((rows, width), BF16)] * 4 + [pltpu.VMEM((2, width // 4, HEAD), BF16)],
        scratch_shapes=[pltpu.SemaphoreType.DMA((4,))],
        cost_estimate=pl.CostEstimate(
            flops=rows * width * HEAD, bytes_accessed=10 * rows * width, transcendentals=0
        ),
        compiler_params=SMALL,
    )(*(pltpu.with_memory_space_constraint(x, pltpu.HBM) for x in tokens))
    return tuple(held), sums


def sums_kernel(wanted, *refs):
    for (own, block), out in zip(wanted, refs[4:]):
        sums_of(refs[:4], block_start(own, block, refs[0].shape[1] // 2), out)


def sums(tokens, *wanted):
    rows, width = tokens[0].shape
    return pl.pallas_call(
        functools.partial(sums_kernel, wanted),
        name="sums",
        in_specs=[VMEM] * 4,
        out_specs=[VMEM] * len(wanted),
        out_shape=[jax.ShapeDtypeStruct((2, width // 4, HEAD), BF16)] * len(wanted),
        cost_estimate=pl.CostEstimate(
            flops=rows * width * HEAD * len(wanted),
            bytes_accessed=3 * rows * width * len(wanted),
            transcendentals=0,
        ),
        compiler_params=SMALL,
    )(*tokens)


def pair_kernel(keep_ref, got_ref, *slots):
    for s, slot in enumerate(slots):
        part = slot_rows(s, len(slots), slot.shape[1])
        for which in range(2):
            both = keep_ref[which, part].astype(F32) + got_ref[which, part].astype(F32)
            slot[which] = both.astype(BF16)


def pair_slots(keep, got, count):
    slot = jax.ShapeDtypeStruct((2, keep.shape[1] // count, HEAD), BF16)
    return pl.pallas_call(
        pair_kernel,
        name="pair",
        in_specs=[VMEM] * 2,
        out_specs=[VMEM] * count,
        out_shape=[slot] * count,
        compiler_params=SMALL,
    )(keep, got)


def totals_kernel(far_count, *refs):
    slots, sends = refs[:far_count], refs[far_count:]
    outer = lax.axis_index("outer")
    totals = []
    for which in range(2):
        total = slots[0][which].astype(F32)
        for slot in slots[1:]:
            total += slot[which].astype(F32)
        totals.append(total.astype(BF16))
    for s, send in zip(distances(len(sends) + 1), sends):
        upward = (outer ^ s) > outer
        send[...] = jnp.where(upward, totals[0], totals[1])


def group_sends(slots, outer_count):
    send = jax.ShapeDtypeStruct(slots[0].shape[1:], BF16)
    return pl.pallas_call(
        functools.partial(totals_kernel, len(slots)),
        name="totals",
        in_specs=[VMEM] * len(slots),
        out_specs=[VMEM] * (outer_count - 1),
        out_shape=[send] * (outer_count - 1),
        compiler_params=SMALL,
    )(*slots)


def scan_kernel(far_count, *refs):
    slots, others, refs = refs[:far_count], refs[far_count : -far_count - 2], refs[-far_count - 2 :]
    outs, (held, scanned) = refs[:far_count], refs[far_count:]
    outer = lax.axis_index("outer")
    _, far = near_far()
    for s, slot in enumerate(slots):
        held[far ^ s] = slot[...]
    for which in range(2):
        total = jnp.zeros(held.shape[2:], F32)
        for s, other in zip(distances(len(others) + 1), others):
            below = (outer ^ s) < outer
            wanted = below if which == 0 else jnp.logical_not(below)
            total += jnp.where(wanted, other[...].astype(F32), 0.0)
        for i in reversed(range(far_count)) if which else range(far_count):
            scanned[i, which] = total.astype(BF16)
            total += held[i, which].astype(F32)
    for s, out in enumerate(outs):
        out[...] = scanned[far ^ s]


def scan_slots(slots, others):
    far_count, slot = len(slots), jax.ShapeDtypeStruct(slots[0].shape, BF16)
    return pl.pallas_call(
        functools.partial(scan_kernel, far_count),
        name="scan",
        in_specs=[VMEM] * (far_count + len(others)),
        out_specs=[VMEM] * far_count,
        out_shape=[slot] * far_count,
        scratch_shapes=[pltpu.VMEM((far_count, *slot.shape), BF16)] * 2,
        compiler_params=SMALL,
    )(*slots, *others)


def with_sums(slot, which, extra, part):
    return (slot[which].astype(F32) + extra[which, part].astype(F32)).astype(BF16)


def by_core(run):
    near, _ = near_far()
    for core in range(2):
        pl.when(near == core)(functools.partial(run, core))


def theirs_kernel(*refs):
    slots, (keep, out) = refs[:-2], refs[-2:]

    def run(core):
        for s, slot in enumerate(slots):
            part = slot_rows(s, len(slots), slot.shape[1])
            out[core, part] = with_sums(slot, core, keep, part)
            out[1 - core, part] = slot[1 - core]

    by_core(run)


def states_for_neighbour(slots, keep):
    return pl.pallas_call(
        theirs_kernel,
        name="theirs",
        in_specs=[VMEM] * (len(slots) + 1),
        out_specs=VMEM,
        out_shape=jax.ShapeDtypeStruct(keep.shape, BF16),
        compiler_params=SMALL,
    )(*slots, keep)


def local_kernel(*refs):
    tokens, outs = refs[:4], refs[4:]
    rows, width = tokens[0].shape
    at = lax.broadcasted_iota(jnp.int32, (rows, rows), 0)
    to = lax.broadcasted_iota(jnp.int32, (rows, rows), 1)
    lower = at >= to

    def masked(a, b):
        return jnp.where(lower, dot(a, b, 1, 1), 0.0).astype(BF16)

    def second(cols, a, b):
        q, k, v, d = (ref[:, cols] for ref in tokens)
        att, gq, gk, gv = outs
        att[:, cols] = dot(a, v, 1, 0)
        gq[:, cols] = dot(b, k, 1, 0)
        gk[:, cols] = dot(b, q, 0, 0)
        gv[:, cols] = dot(a, d, 0, 0)

    last = None
    for h in range(width // HEAD):
        cols = slice(h * HEAD, (h + 1) * HEAD)
        q, k, v, d = (ref[:, cols] for ref in tokens)
        a, b = masked(q, k), masked(d, v)
        if last:
            second(*last)
        last = (cols, a, b)
    second(*last)


def local_part(tokens):
    rows, width = tokens[0].shape
    return pl.pallas_call(
        local_kernel,
        name="local",
        in_specs=[VMEM] * 4,
        out_specs=[VMEM] * 4,
        out_shape=[jax.ShapeDtypeStruct((rows, width), F32)] * 4,
        cost_estimate=pl.CostEstimate(
            flops=12 * rows * width * HEAD, bytes_accessed=24 * rows * width, transcendentals=0
        ),
        compiler_params=SMALL,
    )(*tokens)


def all_products(scale, start, tokens, local, states, store):
    q, k, v, d = tokens

    def products():
        for n in range(states.shape[1] // HEAD):
            rows = slice(n * HEAD, (n + 1) * HEAD)
            cols = slice(start + n * HEAD, start + (n + 1) * HEAD)
            s, g = states[0, rows], states[1, rows]
            yield (rows, 0, cols), dot(q[:, cols], s, 1, 0)
            yield (rows, 1, cols), dot(d[:, cols], s, 1, 1)
            yield (rows, 2, cols), dot(v[:, cols], g, 1, 1)
            yield (rows, 3, cols), dot(k[:, cols], g, 1, 0)

    def use(key, product):
        rows, i, cols = key
        store(rows, i, (scale * (product + local[i][:, cols])).astype(BF16))

    one_ahead(products(), use)


def copies_out(own, block, held, outs, sems, piece):
    first, size = (0, held.shape[2]) if piece is None else (piece * held.shape[2] // 2, held.shape[2] // 2)
    start = block_start(own, block, outs[0].shape[1] // 2) + first
    there = pl.ds(pl.multiple_of(start, size), size)
    return [
        pltpu.make_async_copy(held.at[i, :, pl.ds(first, size)], out.at[:, there], sems.at[i])
        for i, out in enumerate(outs)
    ]


def finish_kernel(scale, own, block, count, rests, hold, *refs):
    tokens, local, slots, refs = refs[:4], refs[4:8], refs[8 : 8 + count], refs[8 + count :]
    got, refs = (refs[0], refs[1:]) if own else (None, refs)
    late, refs = refs[: len(rests)], refs[len(rests) :]
    if own:
        refs, states = refs[:-1], refs[-1]
    else:
        states = slots[0]
    if hold:
        (held,) = refs
    else:
        outs, (held, sems) = refs[-6:-2], refs[-2:]
    width = tokens[0].shape[1]
    copies = []
    for n, (rest, where) in enumerate(zip(late, rests)):
        copies += copies_out(*where, rest, outs, sems.at[n + 2], None)
    for copy in copies:
        copy.start()

    def store(rows, i, out):
        held[i, :, rows] = out
        for piece in range(2):
            if not hold and i == 3 and rows.stop == (piece + 1) * states.shape[1] // 2:
                for copy in copies_out(own, block, held, outs, sems.at[piece], piece):
                    copy.start()

    def run(quarter):
        for s, slot in enumerate(slots if own else ()):
            core, part = quarter // 2, slot_rows(s, count, slot.shape[1])
            states[core, part] = slot[core]
            states[1 - core, part] = with_sums(slot, 1 - core, got, part)
        all_products(scale, quarter * width // 4, tokens, local, states, store)

    start = block_start(own, block, width // 2)
    for quarter in range(4):
        pl.when(start == quarter * width // 4)(functools.partial(run, quarter))
    if not hold:
        for piece in range(2):
            copies += copies_out(own, block, held, outs, sems.at[piece], piece)
    for copy in copies:
        copy.wait()


def finish(own, block, tokens, local, slots, scale, got=(), rests=(), before=(), hold=False):
    rows, width = tokens[0].shape
    out = jax.ShapeDtypeStruct((rows, width), BF16)
    piece = pltpu.VMEM((4, rows, width // 4), BF16)
    inputs = [*tokens, *local, *slots, *got, *(x for _, x in rests)]
    states = pltpu.VMEM((2, width // 4, HEAD), BF16)
    wheres = [where for where, _ in rests]
    return pl.pallas_call(
        functools.partial(finish_kernel, scale, own, block, len(slots), wheres, hold),
        name="finish",
        in_specs=[VMEM] * len(inputs) + [ANY] * len(before),
        out_specs=VMEM if hold else [ANY] * 4,
        out_shape=piece if hold else [out] * 4,
        scratch_shapes=([] if hold else [piece, pltpu.SemaphoreType.DMA((2 + len(rests), 4))])
        + ([states] if own else []),
        input_output_aliases={len(inputs) + i: i for i in range(len(before))},
        cost_estimate=pl.CostEstimate(
            flops=2 * rows * width * HEAD, bytes_accessed=8 * rows * width, transcendentals=0
        ),
        compiler_params=SMALL,
    )(*inputs, *before)


def swap(x, axis, bits):
    return lax.ppermute(x, axis, [(i, i ^ bits) for i in range(lax.axis_size(axis))])


def swap_far(slots):
    return [slots[0]] + [swap(slots[s], "inner", 2 * s) for s in range(1, len(slots))]


def body(queries, keys, values, cotangent):
    far_count = lax.axis_size("inner") // 2
    outer_count = lax.axis_size("outer")
    scale = float(HEAD * queries.shape[0] * 2 * far_count * outer_count) ** (-0.5)
    tokens, give = load((queries, keys, values, cotangent))
    got = [swap(give, "inner", 1), swap(*sums(tokens, (False, 1)), "inner", 1)]
    keep = sums(tokens, (True, 0), (True, 1))
    slots = [slot for b in range(2) for slot in pair_slots(keep[b], got[b], far_count // 2)]
    slots, local = lax.optimization_barrier((swap_far(slots), local_part(tokens)))
    sends = group_sends(slots, outer_count)
    others = [swap(send, "outer", s) for s, send in zip(distances(outer_count), sends)]
    slots = swap_far(scan_slots(slots, others))
    half = far_count // 2

    def near_swap(block, part):
        return swap(states_for_neighbour(part, keep[block]), "inner", 1)

    arrived = [near_swap(0, slots[:half])]
    outs = finish(True, 0, tokens, local, slots[:half], scale, got=got[:1])
    part, outs = lax.optimization_barrier((slots[half:], tuple(outs)))
    arrived.append(near_swap(1, part))
    rest = finish(False, 0, tokens, local, arrived[:1], scale, hold=True)
    rests = [((False, 0), rest)]
    outs = finish(True, 1, tokens, local, part, scale, got=got[1:], rests=rests, before=outs)
    return tuple(finish(False, 1, tokens, local, arrived[1:], scale, before=outs))


def solution(mesh):
    spec = P(("outer", "inner"), None)
    return jax.shard_map(
        body, mesh=mesh, in_specs=(spec,) * 4, out_specs=(spec,) * 4, check_vma=False
    )
```

```python
import functools

import jax
import jax.numpy as jnp
from jax import lax
from jax.experimental import pallas as pl
from jax.experimental.pallas import tpu as pltpu
from jax.sharding import PartitionSpec as P

HEAD = 128
LOADS = 4
MIB = 1024 * 1024
ANY = pl.BlockSpec(memory_space=pl.ANY)
VMEM = pl.BlockSpec(memory_space=pltpu.VMEM)
BF16 = jnp.bfloat16
F32 = jnp.float32
SMALL = pltpu.CompilerParams(vmem_limit_bytes=4 * MIB)


def dot(a, b, over_a, over_b):
    return lax.dot_general(
        a, b, (((over_a,), (over_b,)), ((), ())), preferred_element_type=F32
    )


def near_far():
    inner = lax.axis_index("inner")
    return lax.rem(inner, 2), lax.div(inner, 2)


def distances(outer_count):
    return range(outer_count - 1, 0, -1)


def block_start(own, block, half):
    near, far = near_far()
    side = near if own else 1 - near
    top = lax.div(far, lax.axis_size("inner") // 4)
    return side * half + (1 - top if block else top) * (half // 2)


def columns(start, n):
    return pl.ds(pl.multiple_of(start + n * HEAD, HEAD), HEAD)


def slot_rows(s, count, depth):
    _, far = near_far()
    return pl.ds(pl.multiple_of(lax.rem(far ^ s, count) * depth, depth), depth)


def one_ahead(products, use):
    last = None
    for key, product in products:
        if last:
            use(*last)
        last = key, product
    use(*last)


def sums_of(tokens, start, out):
    q, k, v, d = tokens

    def products():
        for n in range(out.shape[1] // HEAD):
            cols = pl.ds(start + n * HEAD, HEAD) if isinstance(start, int) else columns(start, n)
            for which, (a, b) in enumerate(((k, v), (q, d))):
                yield (which, n), dot(a[:, cols], b[:, cols], 0, 0)

    def use(key, product):
        which, n = key
        out[which, n * HEAD : (n + 1) * HEAD] = product.astype(BF16)

    one_ahead(products(), use)


def load_kernel(*refs):
    tokens, held, (out, sems) = refs[:4], refs[4:8], refs[8:]
    rows = tokens[0].shape[0] // LOADS
    copies = [
        pltpu.make_async_copy(ref.at[pl.ds(n * rows, rows)], to.at[pl.ds(n * rows, rows)], sems.at[i, n])
        for n in range(LOADS)
        for i, (ref, to) in enumerate(zip(tokens, held))
    ]
    for copy in copies:
        copy.start()
    for copy in copies:
        copy.wait()
    width = held[0].shape[1]
    start = block_start(False, 0, width // 2)
    for n in range(4):
        pl.when(start == n * width // 4)(functools.partial(sums_of, held, n * width // 4, out))


def load(tokens):
    rows, width = tokens[0].shape
    *held, sums = pl.pallas_call(
        load_kernel,
        name="load",
        in_specs=[ANY] * 4,
        out_specs=[VMEM] * 5,
        out_shape=[pltpu.VMEM((rows, width), BF16)] * 4 + [pltpu.VMEM((2, width // 4, HEAD), BF16)],
        scratch_shapes=[pltpu.SemaphoreType.DMA((4, LOADS))],
        cost_estimate=pl.CostEstimate(
            flops=rows * width * HEAD, bytes_accessed=10 * rows * width, transcendentals=0
        ),
        compiler_params=SMALL,
    )(*(pltpu.with_memory_space_constraint(x, pltpu.HBM) for x in tokens))
    return tuple(held), sums


def sums_kernel(wanted, *refs):
    for (own, block), out in zip(wanted, refs[4:]):
        sums_of(refs[:4], block_start(own, block, refs[0].shape[1] // 2), out)


def sums(tokens, *wanted):
    rows, width = tokens[0].shape
    return pl.pallas_call(
        functools.partial(sums_kernel, wanted),
        name="sums",
        in_specs=[VMEM] * 4,
        out_specs=[VMEM] * len(wanted),
        out_shape=[jax.ShapeDtypeStruct((2, width // 4, HEAD), BF16)] * len(wanted),
        cost_estimate=pl.CostEstimate(
            flops=rows * width * HEAD * len(wanted),
            bytes_accessed=3 * rows * width * len(wanted),
            transcendentals=0,
        ),
        compiler_params=SMALL,
    )(*tokens)


def pair_kernel(keep_ref, got_ref, *slots):
    for s, slot in enumerate(slots):
        part = slot_rows(s, len(slots), slot.shape[1])
        for which in range(2):
            both = keep_ref[which, part].astype(F32) + got_ref[which, part].astype(F32)
            slot[which] = both.astype(BF16)


def pair_slots(keep, got, count):
    slot = jax.ShapeDtypeStruct((2, keep.shape[1] // count, HEAD), BF16)
    return pl.pallas_call(
        pair_kernel,
        name="pair",
        in_specs=[VMEM] * 2,
        out_specs=[VMEM] * count,
        out_shape=[slot] * count,
        compiler_params=SMALL,
    )(keep, got)


def totals_kernel(far_count, *refs):
    slots, sends = refs[:far_count], refs[far_count:]
    outer = lax.axis_index("outer")
    totals = []
    for which in range(2):
        total = slots[0][which].astype(F32)
        for slot in slots[1:]:
            total += slot[which].astype(F32)
        totals.append(total.astype(BF16))
    for s, send in zip(distances(len(sends) + 1), sends):
        upward = (outer ^ s) > outer
        send[...] = jnp.where(upward, totals[0], totals[1])


def group_sends(slots, outer_count):
    send = jax.ShapeDtypeStruct(slots[0].shape[1:], BF16)
    return pl.pallas_call(
        functools.partial(totals_kernel, len(slots)),
        name="totals",
        in_specs=[VMEM] * len(slots),
        out_specs=[VMEM] * (outer_count - 1),
        out_shape=[send] * (outer_count - 1),
        compiler_params=SMALL,
    )(*slots)


def scan_kernel(far_count, *refs):
    slots, others, refs = refs[:far_count], refs[far_count : -far_count - 2], refs[-far_count - 2 :]
    outs, (held, scanned) = refs[:far_count], refs[far_count:]
    outer = lax.axis_index("outer")
    _, far = near_far()
    for s, slot in enumerate(slots):
        held[far ^ s] = slot[...]
    for which in range(2):
        total = jnp.zeros(held.shape[2:], F32)
        for s, other in zip(distances(len(others) + 1), others):
            below = (outer ^ s) < outer
            wanted = below if which == 0 else jnp.logical_not(below)
            total += jnp.where(wanted, other[...].astype(F32), 0.0)
        for i in reversed(range(far_count)) if which else range(far_count):
            scanned[i, which] = total.astype(BF16)
            total += held[i, which].astype(F32)
    for s, out in enumerate(outs):
        out[...] = scanned[far ^ s]


def scan_slots(slots, others):
    far_count, slot = len(slots), jax.ShapeDtypeStruct(slots[0].shape, BF16)
    return pl.pallas_call(
        functools.partial(scan_kernel, far_count),
        name="scan",
        in_specs=[VMEM] * (far_count + len(others)),
        out_specs=[VMEM] * far_count,
        out_shape=[slot] * far_count,
        scratch_shapes=[pltpu.VMEM((far_count, *slot.shape), BF16)] * 2,
        compiler_params=SMALL,
    )(*slots, *others)


def with_sums(slot, which, extra, part):
    return (slot[which].astype(F32) + extra[which, part].astype(F32)).astype(BF16)


def by_core(run):
    near, _ = near_far()
    for core in range(2):
        pl.when(near == core)(functools.partial(run, core))


def theirs_kernel(*refs):
    slots, (keep, out) = refs[:-2], refs[-2:]

    def run(core):
        for s, slot in enumerate(slots):
            part = slot_rows(s, len(slots), slot.shape[1])
            out[core, part] = with_sums(slot, core, keep, part)
            out[1 - core, part] = slot[1 - core]

    by_core(run)


def states_for_neighbour(slots, keep):
    return pl.pallas_call(
        theirs_kernel,
        name="theirs",
        in_specs=[VMEM] * (len(slots) + 1),
        out_specs=VMEM,
        out_shape=jax.ShapeDtypeStruct(keep.shape, BF16),
        compiler_params=SMALL,
    )(*slots, keep)


def local_kernel(*refs):
    tokens, outs = refs[:4], refs[4:]
    rows, width = tokens[0].shape
    at = lax.broadcasted_iota(jnp.int32, (rows, rows), 0)
    to = lax.broadcasted_iota(jnp.int32, (rows, rows), 1)
    lower = at >= to

    def masked(a, b):
        return jnp.where(lower, dot(a, b, 1, 1), 0.0).astype(BF16)

    def second(cols, a, b):
        q, k, v, d = (ref[:, cols] for ref in tokens)
        att, gq, gk, gv = outs
        att[:, cols] = dot(a, v, 1, 0)
        gq[:, cols] = dot(b, k, 1, 0)
        gk[:, cols] = dot(b, q, 0, 0)
        gv[:, cols] = dot(a, d, 0, 0)

    last = None
    for h in range(width // HEAD):
        cols = slice(h * HEAD, (h + 1) * HEAD)
        q, k, v, d = (ref[:, cols] for ref in tokens)
        a, b = masked(q, k), masked(d, v)
        if last:
            second(*last)
        last = (cols, a, b)
    second(*last)


def local_part(tokens):
    rows, width = tokens[0].shape
    return pl.pallas_call(
        local_kernel,
        name="local",
        in_specs=[VMEM] * 4,
        out_specs=[VMEM] * 4,
        out_shape=[jax.ShapeDtypeStruct((rows, width), F32)] * 4,
        cost_estimate=pl.CostEstimate(
            flops=12 * rows * width * HEAD, bytes_accessed=24 * rows * width, transcendentals=0
        ),
        compiler_params=SMALL,
    )(*tokens)


def all_products(scale, start, tokens, local, states, store):
    q, k, v, d = tokens

    def products():
        for n in range(states.shape[1] // HEAD):
            rows = slice(n * HEAD, (n + 1) * HEAD)
            cols = slice(start + n * HEAD, start + (n + 1) * HEAD)
            s, g = states[0, rows], states[1, rows]
            yield (rows, 0, cols), dot(q[:, cols], s, 1, 0)
            yield (rows, 1, cols), dot(d[:, cols], s, 1, 1)
            yield (rows, 2, cols), dot(v[:, cols], g, 1, 1)
            yield (rows, 3, cols), dot(k[:, cols], g, 1, 0)

    def use(key, product):
        rows, i, cols = key
        store(rows, i, (scale * (product + local[i][:, cols])).astype(BF16))

    one_ahead(products(), use)


def copies_out(own, block, held, outs, sems, piece):
    first, size = (0, held.shape[2]) if piece is None else (piece * held.shape[2] // 2, held.shape[2] // 2)
    start = block_start(own, block, outs[0].shape[1] // 2) + first
    there = pl.ds(pl.multiple_of(start, size), size)
    return [
        pltpu.make_async_copy(held.at[i, :, pl.ds(first, size)], out.at[:, there], sems.at[i])
        for i, out in enumerate(outs)
    ]


def finish_kernel(scale, own, block, count, rests, hold, *refs):
    tokens, local, slots, refs = refs[:4], refs[4:8], refs[8 : 8 + count], refs[8 + count :]
    got, refs = (refs[0], refs[1:]) if own else (None, refs)
    late, refs = refs[: len(rests)], refs[len(rests) :]
    if own:
        refs, states = refs[:-1], refs[-1]
    else:
        states = slots[0]
    if hold:
        (held,) = refs
    else:
        outs, (held, sems) = refs[-6:-2], refs[-2:]
    width = tokens[0].shape[1]
    copies = []
    for n, (rest, where) in enumerate(zip(late, rests)):
        copies += copies_out(*where, rest, outs, sems.at[n + 2], None)
    for copy in copies:
        copy.start()

    def store(rows, i, out):
        held[i, :, rows] = out
        for piece in range(2):
            if not hold and i == 3 and rows.stop == (piece + 1) * states.shape[1] // 2:
                for copy in copies_out(own, block, held, outs, sems.at[piece], piece):
                    copy.start()

    def run(quarter):
        for s, slot in enumerate(slots if own else ()):
            core, part = quarter // 2, slot_rows(s, count, slot.shape[1])
            states[core, part] = slot[core]
            states[1 - core, part] = with_sums(slot, 1 - core, got, part)
        all_products(scale, quarter * width // 4, tokens, local, states, store)

    start = block_start(own, block, width // 2)
    for quarter in range(4):
        pl.when(start == quarter * width // 4)(functools.partial(run, quarter))
    if not hold:
        for piece in range(2):
            copies += copies_out(own, block, held, outs, sems.at[piece], piece)
    for copy in copies:
        copy.wait()


def finish(own, block, tokens, local, slots, scale, got=(), rests=(), before=(), hold=False):
    rows, width = tokens[0].shape
    out = jax.ShapeDtypeStruct((rows, width), BF16)
    piece = pltpu.VMEM((4, rows, width // 4), BF16)
    inputs = [*tokens, *local, *slots, *got, *(x for _, x in rests)]
    states = pltpu.VMEM((2, width // 4, HEAD), BF16)
    wheres = [where for where, _ in rests]
    return pl.pallas_call(
        functools.partial(finish_kernel, scale, own, block, len(slots), wheres, hold),
        name="finish",
        in_specs=[VMEM] * len(inputs) + [ANY] * len(before),
        out_specs=VMEM if hold else [ANY] * 4,
        out_shape=piece if hold else [out] * 4,
        scratch_shapes=([] if hold else [piece, pltpu.SemaphoreType.DMA((2 + len(rests), 4))])
        + ([states] if own else []),
        input_output_aliases={len(inputs) + i: i for i in range(len(before))},
        cost_estimate=pl.CostEstimate(
            flops=2 * rows * width * HEAD, bytes_accessed=8 * rows * width, transcendentals=0
        ),
        compiler_params=SMALL,
    )(*inputs, *before)


def swap(x, axis, bits):
    return lax.ppermute(x, axis, [(i, i ^ bits) for i in range(lax.axis_size(axis))])


def swap_far(slots):
    return [slots[0]] + [swap(slots[s], "inner", 2 * s) for s in range(1, len(slots))]


def body(queries, keys, values, cotangent):
    far_count = lax.axis_size("inner") // 2
    outer_count = lax.axis_size("outer")
    scale = float(HEAD * queries.shape[0] * 2 * far_count * outer_count) ** (-0.5)
    tokens, give = load((queries, keys, values, cotangent))
    got = [swap(give, "inner", 1), swap(*sums(tokens, (False, 1)), "inner", 1)]
    keep = sums(tokens, (True, 0), (True, 1))
    slots = [slot for b in range(2) for slot in pair_slots(keep[b], got[b], far_count // 2)]
    slots, local = lax.optimization_barrier((swap_far(slots), local_part(tokens)))
    sends = group_sends(slots, outer_count)
    others = [swap(send, "outer", s) for s, send in zip(distances(outer_count), sends)]
    slots = swap_far(scan_slots(slots, others))
    half = far_count // 2

    def near_swap(block, part):
        return swap(states_for_neighbour(part, keep[block]), "inner", 1)

    arrived = [near_swap(0, slots[:half])]
    outs = finish(True, 0, tokens, local, slots[:half], scale, got=got[:1])
    part, outs = lax.optimization_barrier((slots[half:], tuple(outs)))
    arrived.append(near_swap(1, part))
    rests = [
        ((True, 1), finish(True, 1, tokens, local, part, scale, got=got[1:], hold=True)),
        ((False, 0), finish(False, 0, tokens, local, arrived[:1], scale, hold=True)),
    ]
    return tuple(finish(False, 1, tokens, local, arrived[1:], scale, rests=rests, before=outs))


def solution(mesh):
    spec = P(("outer", "inner"), None)
    return jax.shard_map(
        body, mesh=mesh, in_specs=(spec,) * 4, out_specs=(spec,) * 4, check_vma=False
    )
```

```python
import functools

import jax
import jax.numpy as jnp
from jax import lax
from jax.experimental import pallas as pl
from jax.experimental.pallas import tpu as pltpu
from jax.sharding import PartitionSpec as P

HEAD = 128
MIB = 1024 * 1024
ANY = pl.BlockSpec(memory_space=pl.ANY)
VMEM = pl.BlockSpec(memory_space=pltpu.VMEM)
BF16 = jnp.bfloat16
F32 = jnp.float32
SMALL = pltpu.CompilerParams(vmem_limit_bytes=4 * MIB)


def dot(a, b, over_a, over_b):
    return lax.dot_general(
        a, b, (((over_a,), (over_b,)), ((), ())), preferred_element_type=F32
    )


def near_far():
    inner = lax.axis_index("inner")
    return lax.rem(inner, 2), lax.div(inner, 2)


def distances(outer_count):
    return range(outer_count - 1, 0, -1)


def block_start(own, block, half):
    near, far = near_far()
    side = near if own else 1 - near
    top = lax.div(far, lax.axis_size("inner") // 4)
    return side * half + (1 - top if block else top) * (half // 2)


def columns(start, n):
    return pl.ds(pl.multiple_of(start + n * HEAD, HEAD), HEAD)


def slot_rows(s, count, depth):
    _, far = near_far()
    return pl.ds(pl.multiple_of(lax.rem(far ^ s, count) * depth, depth), depth)


def one_ahead(products, use):
    last = None
    for key, product in products:
        if last:
            use(*last)
        last = key, product
    use(*last)


def sums_of(tokens, start, out, kinds=(0, 1)):
    q, k, v, d = tokens

    def products():
        for n in range(out.shape[1] // HEAD):
            cols = pl.ds(start + n * HEAD, HEAD) if isinstance(start, int) else columns(start, n)
            for which in kinds:
                a, b = ((k, v), (q, d))[which]
                yield (which, n), dot(a[:, cols], b[:, cols], 0, 0)

    def use(key, product):
        which, n = key
        out[which, n * HEAD : (n + 1) * HEAD] = product.astype(BF16)

    one_ahead(products(), use)


def load_kernel(*refs):
    tokens, held, (out, sems) = refs[:4], refs[4:8], refs[8:]
    copies = [pltpu.make_async_copy(tokens[i], held[i], sems.at[i]) for i in range(4)]
    width = held[0].shape[1]
    start = block_start(False, 0, width // 2)
    pairs = ((1, 2), (0, 3))
    for i in pairs[0] + pairs[1]:
        copies[i].start()
    for kind, pair in enumerate(pairs):
        for i in pair:
            copies[i].wait()
        for n in range(4):
            at = n * width // 4
            pl.when(start == at)(functools.partial(sums_of, held, at, out, (kind,)))


def load(tokens):
    rows, width = tokens[0].shape
    *held, sums = pl.pallas_call(
        load_kernel,
        name="load",
        in_specs=[ANY] * 4,
        out_specs=[VMEM] * 5,
        out_shape=[pltpu.VMEM((rows, width), BF16)] * 4 + [pltpu.VMEM((2, width // 4, HEAD), BF16)],
        scratch_shapes=[pltpu.SemaphoreType.DMA((4,))],
        cost_estimate=pl.CostEstimate(
            flops=rows * width * HEAD, bytes_accessed=10 * rows * width, transcendentals=0
        ),
        compiler_params=SMALL,
    )(*(pltpu.with_memory_space_constraint(x, pltpu.HBM) for x in tokens))
    return tuple(held), sums


def sums_kernel(wanted, *refs):
    for (own, block), out in zip(wanted, refs[4:]):
        sums_of(refs[:4], block_start(own, block, refs[0].shape[1] // 2), out)


def sums(tokens, *wanted):
    rows, width = tokens[0].shape
    return pl.pallas_call(
        functools.partial(sums_kernel, wanted),
        name="sums",
        in_specs=[VMEM] * 4,
        out_specs=[VMEM] * len(wanted),
        out_shape=[jax.ShapeDtypeStruct((2, width // 4, HEAD), BF16)] * len(wanted),
        cost_estimate=pl.CostEstimate(
            flops=rows * width * HEAD * len(wanted),
            bytes_accessed=3 * rows * width * len(wanted),
            transcendentals=0,
        ),
        compiler_params=SMALL,
    )(*tokens)


def pair_kernel(keep_ref, got_ref, *slots):
    for s, slot in enumerate(slots):
        part = slot_rows(s, len(slots), slot.shape[1])
        for which in range(2):
            both = keep_ref[which, part].astype(F32) + got_ref[which, part].astype(F32)
            slot[which] = both.astype(BF16)


def pair_slots(keep, got, count):
    slot = jax.ShapeDtypeStruct((2, keep.shape[1] // count, HEAD), BF16)
    return pl.pallas_call(
        pair_kernel,
        name="pair",
        in_specs=[VMEM] * 2,
        out_specs=[VMEM] * count,
        out_shape=[slot] * count,
        compiler_params=SMALL,
    )(keep, got)


def totals_kernel(far_count, *refs):
    slots, sends = refs[:far_count], refs[far_count:]
    outer = lax.axis_index("outer")
    totals = []
    for which in range(2):
        total = slots[0][which].astype(F32)
        for slot in slots[1:]:
            total += slot[which].astype(F32)
        totals.append(total.astype(BF16))
    for s, send in zip(distances(len(sends) + 1), sends):
        upward = (outer ^ s) > outer
        send[...] = jnp.where(upward, totals[0], totals[1])


def group_sends(slots, outer_count):
    send = jax.ShapeDtypeStruct(slots[0].shape[1:], BF16)
    return pl.pallas_call(
        functools.partial(totals_kernel, len(slots)),
        name="totals",
        in_specs=[VMEM] * len(slots),
        out_specs=[VMEM] * (outer_count - 1),
        out_shape=[send] * (outer_count - 1),
        compiler_params=SMALL,
    )(*slots)


def scan_kernel(far_count, *refs):
    slots, others, refs = refs[:far_count], refs[far_count : -far_count - 2], refs[-far_count - 2 :]
    outs, (held, scanned) = refs[:far_count], refs[far_count:]
    outer = lax.axis_index("outer")
    _, far = near_far()
    for s, slot in enumerate(slots):
        held[far ^ s] = slot[...]
    for which in range(2):
        total = jnp.zeros(held.shape[2:], F32)
        for s, other in zip(distances(len(others) + 1), others):
            below = (outer ^ s) < outer
            wanted = below if which == 0 else jnp.logical_not(below)
            total += jnp.where(wanted, other[...].astype(F32), 0.0)
        for i in reversed(range(far_count)) if which else range(far_count):
            scanned[i, which] = total.astype(BF16)
            total += held[i, which].astype(F32)
    for s, out in enumerate(outs):
        out[...] = scanned[far ^ s]


def scan_slots(slots, others):
    far_count, slot = len(slots), jax.ShapeDtypeStruct(slots[0].shape, BF16)
    return pl.pallas_call(
        functools.partial(scan_kernel, far_count),
        name="scan",
        in_specs=[VMEM] * (far_count + len(others)),
        out_specs=[VMEM] * far_count,
        out_shape=[slot] * far_count,
        scratch_shapes=[pltpu.VMEM((far_count, *slot.shape), BF16)] * 2,
        compiler_params=SMALL,
    )(*slots, *others)


def with_sums(slot, which, extra, part):
    return (slot[which].astype(F32) + extra[which, part].astype(F32)).astype(BF16)


def by_core(run):
    near, _ = near_far()
    for core in range(2):
        pl.when(near == core)(functools.partial(run, core))


def theirs_kernel(s, count, slot, keep, out):
    part = slot_rows(s, count, slot.shape[1])

    def run(core):
        out[core] = with_sums(slot, core, keep, part)
        out[1 - core] = slot[1 - core]

    by_core(run)


def state_for_neighbour(s, count, slot, keep):
    return pl.pallas_call(
        functools.partial(theirs_kernel, s, count),
        name="theirs",
        in_specs=[VMEM] * 2,
        out_specs=VMEM,
        out_shape=jax.ShapeDtypeStruct(slot.shape, BF16),
        compiler_params=SMALL,
    )(slot, keep[s // count])


def local_kernel(*refs):
    tokens, outs = refs[:4], refs[4:]
    rows, width = tokens[0].shape
    at = lax.broadcasted_iota(jnp.int32, (rows, rows), 0)
    to = lax.broadcasted_iota(jnp.int32, (rows, rows), 1)
    lower = at >= to

    def masked(a, b):
        return jnp.where(lower, dot(a, b, 1, 1), 0.0).astype(BF16)

    def second(cols, a, b):
        q, k, v, d = (ref[:, cols] for ref in tokens)
        att, gq, gk, gv = outs
        att[:, cols] = dot(a, v, 1, 0)
        gq[:, cols] = dot(b, k, 1, 0)
        gk[:, cols] = dot(b, q, 0, 0)
        gv[:, cols] = dot(a, d, 0, 0)

    last = None
    for h in range(width // HEAD):
        cols = slice(h * HEAD, (h + 1) * HEAD)
        q, k, v, d = (ref[:, cols] for ref in tokens)
        a, b = masked(q, k), masked(d, v)
        if last:
            second(*last)
        last = (cols, a, b)
    second(*last)


def local_part(tokens):
    rows, width = tokens[0].shape
    return pl.pallas_call(
        local_kernel,
        name="local",
        in_specs=[VMEM] * 4,
        out_specs=[VMEM] * 4,
        out_shape=[jax.ShapeDtypeStruct((rows, width), F32)] * 4,
        cost_estimate=pl.CostEstimate(
            flops=12 * rows * width * HEAD, bytes_accessed=24 * rows * width, transcendentals=0
        ),
        compiler_params=SMALL,
    )(*tokens)


def all_products(scale, start, tokens, local, states, store):
    q, k, v, d = tokens

    def products():
        for n in range(states.shape[1] // HEAD):
            rows = slice(n * HEAD, (n + 1) * HEAD)
            cols = slice(start + n * HEAD, start + (n + 1) * HEAD)
            s, g = states[0, rows], states[1, rows]
            yield (rows, 0, cols), dot(q[:, cols], s, 1, 0)
            yield (rows, 1, cols), dot(d[:, cols], s, 1, 1)
            yield (rows, 2, cols), dot(v[:, cols], g, 1, 1)
            yield (rows, 3, cols), dot(k[:, cols], g, 1, 0)

    def use(key, product):
        rows, i, cols = key
        store(rows, i, (scale * (product + local[i][:, cols])).astype(BF16))

    one_ahead(products(), use)


def group_start(own, first, count, depth, half):
    near, far = near_far()
    side = near if own else 1 - near
    return side * half + lax.div(far ^ first, count) * (count * depth)


def copies_out(own, first, count, depth, held, outs, sems):
    start = group_start(own, first, count, depth, outs[0].shape[1] // 2)
    there = pl.ds(pl.multiple_of(start, count * depth), count * depth)
    return [
        pltpu.make_async_copy(held.at[i], out.at[:, there], sems.at[i])
        for i, out in enumerate(outs)
    ]


def finish_kernel(scale, own, first, count, rests, hold, *refs):
    tokens, local, slots, refs = refs[:4], refs[4:8], refs[8 : 8 + count], refs[8 + count :]
    got, refs = (refs[0], refs[1:]) if own else (None, refs)
    late, refs = refs[: len(rests)], refs[len(rests) :]
    if hold:
        held, states = refs
    else:
        outs, (states, held, sems) = refs[-7:-3], refs[-3:]
    width, depth = tokens[0].shape[1], slots[0].shape[1]
    copies = []
    for n, (rest, where) in enumerate(zip(late, rests)):
        copies += copies_out(*where, depth, rest, outs, sems.at[n + 1])
    for copy in copies:
        copy.start()

    def store(rows, i, out):
        held[i, :, rows] = out

    def run(start):
        core = start * 2 // width if own else 1 - start * 2 // width
        for s, slot in enumerate(slots, first):
            part = slot_rows(s, count, depth)
            if own:
                states[core, part] = slot[core]
                states[1 - core, part] = with_sums(slot, 1 - core, got, part)
            else:
                states[:, part] = slot[...]
        all_products(scale, start, tokens, local, states, store)

    start = group_start(own, first, count, depth, width // 2)
    for at in range(0, width, count * depth):
        pl.when(start == at)(functools.partial(run, at))
    if not hold:
        last = copies_out(own, first, count, depth, held, outs, sems.at[0])
        for copy in last:
            copy.start()
        for copy in copies + last:
            copy.wait()


def finish(own, first, tokens, local, slots, scale, got=(), rests=(), before=(), hold=False):
    rows, width = tokens[0].shape
    count, depth = len(slots), slots[0].shape[1]
    out = jax.ShapeDtypeStruct((rows, width), BF16)
    piece = pltpu.VMEM((4, rows, count * depth), BF16)
    inputs = [*tokens, *local, *slots, *got, *(x for _, x in rests)]
    states = pltpu.VMEM((2, count * depth, HEAD), BF16)
    wheres = [where for where, _ in rests]
    return pl.pallas_call(
        functools.partial(finish_kernel, scale, own, first, count, wheres, hold),
        name="finish",
        in_specs=[VMEM] * len(inputs) + [ANY] * len(before),
        out_specs=VMEM if hold else [ANY] * 4,
        out_shape=piece if hold else [out] * 4,
        scratch_shapes=[states]
        + ([] if hold else [piece, pltpu.SemaphoreType.DMA((1 + len(rests), 4))]),
        input_output_aliases={len(inputs) + i: i for i in range(len(before))},
        cost_estimate=pl.CostEstimate(
            flops=8 * rows * count * depth * HEAD,
            bytes_accessed=32 * rows * count * depth,
            transcendentals=0,
        ),
        compiler_params=SMALL,
    )(*inputs, *before)


def swap(x, axis, bits):
    return lax.ppermute(x, axis, [(i, i ^ bits) for i in range(lax.axis_size(axis))])


def swap_far(slots):
    return [slots[0]] + [swap(slots[s], "inner", 2 * s) for s in range(1, len(slots))]


def body(queries, keys, values, cotangent):
    far_count = lax.axis_size("inner") // 2
    outer_count = lax.axis_size("outer")
    scale = float(HEAD * queries.shape[0] * 2 * far_count * outer_count) ** (-0.5)
    tokens, give = load((queries, keys, values, cotangent))
    got = [swap(give, "inner", 1), swap(*sums(tokens, (False, 1)), "inner", 1)]
    keep = sums(tokens, (True, 0), (True, 1))
    slots = [slot for b in range(2) for slot in pair_slots(keep[b], got[b], far_count // 2)]
    slots, local = lax.optimization_barrier((swap_far(slots), local_part(tokens)))
    sends = group_sends(slots, outer_count)
    others = [swap(send, "outer", s) for s, send in zip(distances(outer_count), sends)]
    slots = swap_far(scan_slots(slots, others))
    half = far_count // 2
    arrived = []
    for s in range(far_count):
        if s == half:
            outs = finish(True, 0, tokens, local, slots[:half], scale, got=got[:1])
            slots[s], outs = lax.optimization_barrier((slots[s], tuple(outs)))
        elif s > half:
            slots[s], theirs = lax.optimization_barrier((slots[s], theirs))
        theirs = state_for_neighbour(s, half, slots[s], keep)
        arrived.append(swap(theirs, "inner", 1))
    held = finish(True, half, tokens, local, slots[half:], scale, got=got[1:], hold=True)
    rests = [((True, half, half), held)]
    first, count, least = 0, half, max(1, HEAD // slots[0].shape[1])
    while first + least < far_count:
        group = arrived[first : first + count]
        held = finish(False, first, tokens, local, group, scale, hold=True)
        rests.append(((False, first, count), held))
        first, count = first + count, max(count if first == 0 and half == least else count // 2, least)
    last = arrived[first:]
    return tuple(finish(False, first, tokens, local, last, scale, rests=rests, before=outs))


def solution(mesh):
    spec = P(("outer", "inner"), None)
    return jax.shard_map(
        body, mesh=mesh, in_specs=(spec,) * 4, out_specs=(spec,) * 4, check_vma=False
    )
```

```python
import functools

import jax
import jax.numpy as jnp
from jax import lax
from jax.experimental import pallas as pl
from jax.experimental.pallas import tpu as pltpu
from jax.sharding import PartitionSpec as P

HEAD = 128
MIB = 1024 * 1024
ANY = pl.BlockSpec(memory_space=pl.ANY)
VMEM = pl.BlockSpec(memory_space=pltpu.VMEM)
BF16 = jnp.bfloat16
F32 = jnp.float32
SMALL = pltpu.CompilerParams(vmem_limit_bytes=4 * MIB)


def dot(a, b, over_a, over_b):
    return lax.dot_general(
        a, b, (((over_a,), (over_b,)), ((), ())), preferred_element_type=F32
    )


def near_far():
    inner = lax.axis_index("inner")
    return lax.rem(inner, 2), lax.div(inner, 2)


def distances(outer_count):
    return range(outer_count - 1, 0, -1)


def block_start(own, block, half):
    near, far = near_far()
    side = near if own else 1 - near
    top = lax.div(far, lax.axis_size("inner") // 4)
    return side * half + (1 - top if block else top) * (half // 2)


def columns(start, n):
    return pl.ds(pl.multiple_of(start + n * HEAD, HEAD), HEAD)


def slot_rows(s, count, depth):
    _, far = near_far()
    return pl.ds(pl.multiple_of(lax.rem(far ^ s, count) * depth, depth), depth)


def one_ahead(products, use):
    last = None
    for key, product in products:
        if last:
            use(*last)
        last = key, product
    use(*last)


def sums_of(tokens, start, out, kinds=(0, 1)):
    q, k, v, d = tokens

    def products():
        for n in range(out.shape[1] // HEAD):
            cols = pl.ds(start + n * HEAD, HEAD) if isinstance(start, int) else columns(start, n)
            for which in kinds:
                a, b = ((k, v), (q, d))[which]
                yield (which, n), dot(a[:, cols], b[:, cols], 0, 0)

    def use(key, product):
        which, n = key
        out[which, n * HEAD : (n + 1) * HEAD] = product.astype(BF16)

    one_ahead(products(), use)


def load_kernel(*refs):
    tokens, held, (out, sems) = refs[:4], refs[4:8], refs[8:]
    copies = [pltpu.make_async_copy(tokens[i], held[i], sems.at[i]) for i in range(4)]
    width = held[0].shape[1]
    start = block_start(False, 0, width // 2)
    pairs = ((1, 2), (0, 3))
    for i in pairs[0] + pairs[1]:
        copies[i].start()
    for kind, pair in enumerate(pairs):
        for i in pair:
            copies[i].wait()
        for n in range(4):
            at = n * width // 4
            pl.when(start == at)(functools.partial(sums_of, held, at, out, (kind,)))


def load(tokens):
    rows, width = tokens[0].shape
    *held, sums = pl.pallas_call(
        load_kernel,
        name="load",
        in_specs=[ANY] * 4,
        out_specs=[VMEM] * 5,
        out_shape=[pltpu.VMEM((rows, width), BF16)] * 4 + [pltpu.VMEM((2, width // 4, HEAD), BF16)],
        scratch_shapes=[pltpu.SemaphoreType.DMA((4,))],
        cost_estimate=pl.CostEstimate(
            flops=rows * width * HEAD, bytes_accessed=10 * rows * width, transcendentals=0
        ),
        compiler_params=SMALL,
    )(*(pltpu.with_memory_space_constraint(x, pltpu.HBM) for x in tokens))
    return tuple(held), sums


def sums_kernel(wanted, *refs):
    for (own, block), out in zip(wanted, refs[4:]):
        sums_of(refs[:4], block_start(own, block, refs[0].shape[1] // 2), out)


def sums(tokens, *wanted):
    rows, width = tokens[0].shape
    return pl.pallas_call(
        functools.partial(sums_kernel, wanted),
        name="sums",
        in_specs=[VMEM] * 4,
        out_specs=[VMEM] * len(wanted),
        out_shape=[jax.ShapeDtypeStruct((2, width // 4, HEAD), BF16)] * len(wanted),
        cost_estimate=pl.CostEstimate(
            flops=rows * width * HEAD * len(wanted),
            bytes_accessed=3 * rows * width * len(wanted),
            transcendentals=0,
        ),
        compiler_params=SMALL,
    )(*tokens)


def pair_kernel(keep_ref, got_ref, *slots):
    for s, slot in enumerate(slots):
        part = slot_rows(s, len(slots), slot.shape[1])
        for which in range(2):
            both = keep_ref[which, part].astype(F32) + got_ref[which, part].astype(F32)
            slot[which] = both.astype(BF16)


def pair_slots(keep, got, count):
    slot = jax.ShapeDtypeStruct((2, keep.shape[1] // count, HEAD), BF16)
    return pl.pallas_call(
        pair_kernel,
        name="pair",
        in_specs=[VMEM] * 2,
        out_specs=[VMEM] * count,
        out_shape=[slot] * count,
        compiler_params=SMALL,
    )(keep, got)


def totals_kernel(far_count, *refs):
    slots, sends = refs[:far_count], refs[far_count:]
    outer = lax.axis_index("outer")
    totals = []
    for which in range(2):
        total = slots[0][which].astype(F32)
        for slot in slots[1:]:
            total += slot[which].astype(F32)
        totals.append(total.astype(BF16))
    for s, send in zip(distances(len(sends) + 1), sends):
        upward = (outer ^ s) > outer
        send[...] = jnp.where(upward, totals[0], totals[1])


def group_sends(slots, outer_count):
    send = jax.ShapeDtypeStruct(slots[0].shape[1:], BF16)
    return pl.pallas_call(
        functools.partial(totals_kernel, len(slots)),
        name="totals",
        in_specs=[VMEM] * len(slots),
        out_specs=[VMEM] * (outer_count - 1),
        out_shape=[send] * (outer_count - 1),
        compiler_params=SMALL,
    )(*slots)


def scan_kernel(far_count, *refs):
    slots, others, refs = refs[:far_count], refs[far_count : -far_count - 2], refs[-far_count - 2 :]
    outs, (held, scanned) = refs[:far_count], refs[far_count:]
    outer = lax.axis_index("outer")
    _, far = near_far()
    for s, slot in enumerate(slots):
        held[far ^ s] = slot[...]
    for which in range(2):
        total = jnp.zeros(held.shape[2:], F32)
        for s, other in zip(distances(len(others) + 1), others):
            below = (outer ^ s) < outer
            wanted = below if which == 0 else jnp.logical_not(below)
            total += jnp.where(wanted, other[...].astype(F32), 0.0)
        for i in reversed(range(far_count)) if which else range(far_count):
            scanned[i, which] = total.astype(BF16)
            total += held[i, which].astype(F32)
    for s, out in enumerate(outs):
        out[...] = scanned[far ^ s]


def scan_slots(slots, others):
    far_count, slot = len(slots), jax.ShapeDtypeStruct(slots[0].shape, BF16)
    return pl.pallas_call(
        functools.partial(scan_kernel, far_count),
        name="scan",
        in_specs=[VMEM] * (far_count + len(others)),
        out_specs=[VMEM] * far_count,
        out_shape=[slot] * far_count,
        scratch_shapes=[pltpu.VMEM((far_count, *slot.shape), BF16)] * 2,
        compiler_params=SMALL,
    )(*slots, *others)


def with_sums(slot, which, extra, part):
    return (slot[which].astype(F32) + extra[which, part].astype(F32)).astype(BF16)


def by_core(run):
    near, _ = near_far()
    for core in range(2):
        pl.when(near == core)(functools.partial(run, core))


def theirs_kernel(*refs):
    slots, (keep, out) = refs[:-2], refs[-2:]

    def run(core):
        for s, slot in enumerate(slots):
            part = slot_rows(s, len(slots), slot.shape[1])
            out[core, part] = with_sums(slot, core, keep, part)
            out[1 - core, part] = slot[1 - core]

    by_core(run)


def states_for_neighbour(slots, keep):
    return pl.pallas_call(
        theirs_kernel,
        name="theirs",
        in_specs=[VMEM] * (len(slots) + 1),
        out_specs=VMEM,
        out_shape=jax.ShapeDtypeStruct(keep.shape, BF16),
        compiler_params=SMALL,
    )(*slots, keep)


def local_kernel(*refs):
    tokens, outs = refs[:4], refs[4:]
    rows, width = tokens[0].shape
    at = lax.broadcasted_iota(jnp.int32, (rows, rows), 0)
    to = lax.broadcasted_iota(jnp.int32, (rows, rows), 1)
    lower = at >= to

    def masked(a, b):
        return jnp.where(lower, dot(a, b, 1, 1), 0.0).astype(BF16)

    def second(cols, a, b):
        q, k, v, d = (ref[:, cols] for ref in tokens)
        att, gq, gk, gv = outs
        att[:, cols] = dot(a, v, 1, 0)
        gq[:, cols] = dot(b, k, 1, 0)
        gk[:, cols] = dot(b, q, 0, 0)
        gv[:, cols] = dot(a, d, 0, 0)

    last = None
    for h in range(width // HEAD):
        cols = slice(h * HEAD, (h + 1) * HEAD)
        q, k, v, d = (ref[:, cols] for ref in tokens)
        a, b = masked(q, k), masked(d, v)
        if last:
            second(*last)
        last = (cols, a, b)
    second(*last)


def local_part(tokens):
    rows, width = tokens[0].shape
    return pl.pallas_call(
        local_kernel,
        name="local",
        in_specs=[VMEM] * 4,
        out_specs=[VMEM] * 4,
        out_shape=[jax.ShapeDtypeStruct((rows, width), F32)] * 4,
        cost_estimate=pl.CostEstimate(
            flops=12 * rows * width * HEAD, bytes_accessed=24 * rows * width, transcendentals=0
        ),
        compiler_params=SMALL,
    )(*tokens)


def all_products(scale, start, tokens, local, states, store):
    q, k, v, d = tokens

    def products():
        for n in range(states.shape[1] // HEAD):
            rows = slice(n * HEAD, (n + 1) * HEAD)
            cols = slice(start + n * HEAD, start + (n + 1) * HEAD)
            s, g = states[0, rows], states[1, rows]
            yield (rows, 0, cols), dot(q[:, cols], s, 1, 0)
            yield (rows, 1, cols), dot(d[:, cols], s, 1, 1)
            yield (rows, 2, cols), dot(v[:, cols], g, 1, 1)
            yield (rows, 3, cols), dot(k[:, cols], g, 1, 0)

    def use(key, product):
        rows, i, cols = key
        store(rows, i, (scale * (product + local[i][:, cols])).astype(BF16))

    one_ahead(products(), use)


def copies_out(own, block, held, outs, sems, piece):
    first, size = (0, held.shape[2]) if piece is None else (piece * held.shape[2] // 2, held.shape[2] // 2)
    start = block_start(own, block, outs[0].shape[1] // 2) + first
    there = pl.ds(pl.multiple_of(start, size), size)
    return [
        pltpu.make_async_copy(held.at[i, :, pl.ds(first, size)], out.at[:, there], sems.at[i])
        for i, out in enumerate(outs)
    ]


def finish_kernel(scale, own, block, count, rests, hold, *refs):
    tokens, local, slots, refs = refs[:4], refs[4:8], refs[8 : 8 + count], refs[8 + count :]
    got, refs = (refs[0], refs[1:]) if own else (None, refs)
    late, refs = refs[: len(rests)], refs[len(rests) :]
    if own:
        refs, states = refs[:-1], refs[-1]
    else:
        states = slots[0]
    if not hold or rests:
        *refs, sems = refs
    *refs, held = refs
    outs = refs[-4:]
    width = tokens[0].shape[1]
    copies = []
    for n, (rest, where) in enumerate(zip(late, rests)):
        copies += copies_out(*where, rest, outs, sems.at[n + 2], None)
    for copy in copies:
        copy.start()

    def store(rows, i, out):
        held[i, :, rows] = out
        for piece in range(2):
            if not hold and i == 3 and rows.stop == (piece + 1) * states.shape[1] // 2:
                for copy in copies_out(own, block, held, outs, sems.at[piece], piece):
                    copy.start()

    def run(quarter):
        for s, slot in enumerate(slots if own else ()):
            core, part = quarter // 2, slot_rows(s, count, slot.shape[1])
            states[core, part] = slot[core]
            states[1 - core, part] = with_sums(slot, 1 - core, got, part)
        all_products(scale, quarter * width // 4, tokens, local, states, store)

    start = block_start(own, block, width // 2)
    for quarter in range(4):
        pl.when(start == quarter * width // 4)(functools.partial(run, quarter))
    if not hold:
        for piece in range(2):
            copies += copies_out(own, block, held, outs, sems.at[piece], piece)
    for copy in copies:
        copy.wait()


def finish(own, block, tokens, local, slots, scale, got=(), rests=(), before=(), hold=False):
    rows, width = tokens[0].shape
    out = jax.ShapeDtypeStruct((rows, width), BF16)
    piece = pltpu.VMEM((4, rows, width // 4), BF16)
    inputs = [*tokens, *local, *slots, *got, *(x for _, x in rests)]
    states = pltpu.VMEM((2, width // 4, HEAD), BF16)
    wheres = [where for where, _ in rests]
    writes = not hold or bool(rests)
    return pl.pallas_call(
        functools.partial(finish_kernel, scale, own, block, len(slots), wheres, hold),
        name="finish",
        in_specs=[VMEM] * len(inputs) + [ANY] * len(before),
        out_specs=[ANY] * 4 * writes + [VMEM] * hold,
        out_shape=[out] * 4 * writes + [piece] * hold,
        scratch_shapes=[piece] * (not hold)
        + [pltpu.SemaphoreType.DMA((2 + len(rests), 4))] * writes
        + [states] * own,
        input_output_aliases={len(inputs) + i: i for i in range(len(before))},
        cost_estimate=pl.CostEstimate(
            flops=2 * rows * width * HEAD, bytes_accessed=8 * rows * width, transcendentals=0
        ),
        compiler_params=SMALL,
    )(*inputs, *before)


def swap(x, axis, bits):
    return lax.ppermute(x, axis, [(i, i ^ bits) for i in range(lax.axis_size(axis))])


def swap_far(slots):
    return [slots[0]] + [swap(slots[s], "inner", 2 * s) for s in range(1, len(slots))]


def body(queries, keys, values, cotangent):
    far_count = lax.axis_size("inner") // 2
    outer_count = lax.axis_size("outer")
    scale = float(HEAD * queries.shape[0] * 2 * far_count * outer_count) ** (-0.5)
    tokens, give = load((queries, keys, values, cotangent))
    got = [swap(give, "inner", 1), swap(*sums(tokens, (False, 1)), "inner", 1)]
    keep = sums(tokens, (True, 0), (True, 1))
    slots = [slot for b in range(2) for slot in pair_slots(keep[b], got[b], far_count // 2)]
    slots, local = lax.optimization_barrier((swap_far(slots), local_part(tokens)))
    sends = group_sends(slots, outer_count)
    others = [swap(send, "outer", s) for s, send in zip(distances(outer_count), sends)]
    slots = swap_far(scan_slots(slots, others))
    half = far_count // 2

    def near_swap(block, part):
        return swap(states_for_neighbour(part, keep[block]), "inner", 1)

    arrived = [near_swap(0, slots[:half])]
    outs = finish(True, 0, tokens, local, slots[:half], scale, got=got[:1])
    part, outs = lax.optimization_barrier((slots[half:], tuple(outs)))
    arrived.append(near_swap(1, part))
    (rest,) = finish(True, 1, tokens, local, part, scale, got=got[1:], hold=True)
    rests = [((True, 1), rest)]
    *outs, rest = finish(
        False, 0, tokens, local, arrived[:1], scale, rests=rests, before=outs, hold=True
    )
    rests = [((False, 0), rest)]
    return tuple(finish(False, 1, tokens, local, arrived[1:], scale, rests=rests, before=outs))


def solution(mesh):
    spec = P(("outer", "inner"), None)
    return jax.shard_map(
        body, mesh=mesh, in_specs=(spec,) * 4, out_specs=(spec,) * 4, check_vma=False
    )
```

```python
import functools

import jax
import jax.numpy as jnp
from jax import lax
from jax.experimental import pallas as pl
from jax.experimental.pallas import tpu as pltpu
from jax.sharding import PartitionSpec as P

HEAD = 128
MIB = 1024 * 1024
ANY = pl.BlockSpec(memory_space=pl.ANY)
VMEM = pl.BlockSpec(memory_space=pltpu.VMEM)
BF16 = jnp.bfloat16
F32 = jnp.float32
SMALL = pltpu.CompilerParams(vmem_limit_bytes=4 * MIB)


def dot(a, b, over_a, over_b):
    return lax.dot_general(
        a, b, (((over_a,), (over_b,)), ((), ())), preferred_element_type=F32
    )


def near_far():
    inner = lax.axis_index("inner")
    return lax.rem(inner, 2), lax.div(inner, 2)


def distances(outer_count):
    return range(outer_count - 1, 0, -1)


def exchanged(bits):
    return bits ^ 3 if bits & 3 in (1, 2) and lax.axis_size("inner") > 4 else bits


def place_of(side):
    _, far = near_far()
    if lax.axis_size("inner") <= 4:
        return far
    low, high = lax.rem(far, 2), lax.rem(lax.div(far, 2), 2)
    return jnp.where(side == 1, far, far + low - high)


def far_of(s):
    near, far = near_far()
    return jnp.where(near == 1, far ^ s, far ^ exchanged(s))


def block_start(own, block, half):
    near, _ = near_far()
    side = near if own else 1 - near
    top = lax.div(place_of(side), lax.axis_size("inner") // 4)
    return side * half + (1 - top if block else top) * (half // 2)


def columns(start, n):
    return pl.ds(pl.multiple_of(start + n * HEAD, HEAD), HEAD)


def slot_rows(s, count, depth):
    near, _ = near_far()
    return pl.ds(pl.multiple_of(lax.rem(place_of(near) ^ s, count) * depth, depth), depth)


def one_ahead(products, use):
    last = None
    for key, product in products:
        if last:
            use(*last)
        last = key, product
    use(*last)


def sums_of(tokens, start, out, kinds=(0, 1)):
    q, k, v, d = tokens

    def products():
        for n in range(out.shape[1] // HEAD):
            cols = pl.ds(start + n * HEAD, HEAD) if isinstance(start, int) else columns(start, n)
            for which in kinds:
                a, b = ((k, v), (q, d))[which]
                yield (which, n), dot(a[:, cols], b[:, cols], 0, 0)

    def use(key, product):
        which, n = key
        out[which, n * HEAD : (n + 1) * HEAD] = product.astype(BF16)

    one_ahead(products(), use)


def load_kernel(*refs):
    tokens, held, (out, sems) = refs[:4], refs[4:8], refs[8:]
    copies = [pltpu.make_async_copy(tokens[i], held[i], sems.at[i]) for i in range(4)]
    width = held[0].shape[1]
    start = block_start(False, 0, width // 2)
    pairs = ((1, 2), (0, 3))
    for i in pairs[0] + pairs[1]:
        copies[i].start()
    for kind, pair in enumerate(pairs):
        for i in pair:
            copies[i].wait()
        for n in range(4):
            at = n * width // 4
            pl.when(start == at)(functools.partial(sums_of, held, at, out, (kind,)))


def load(tokens):
    rows, width = tokens[0].shape
    *held, sums = pl.pallas_call(
        load_kernel,
        name="load",
        in_specs=[ANY] * 4,
        out_specs=[VMEM] * 5,
        out_shape=[pltpu.VMEM((rows, width), BF16)] * 4 + [pltpu.VMEM((2, width // 4, HEAD), BF16)],
        scratch_shapes=[pltpu.SemaphoreType.DMA((4,))],
        cost_estimate=pl.CostEstimate(
            flops=rows * width * HEAD, bytes_accessed=10 * rows * width, transcendentals=0
        ),
        compiler_params=SMALL,
    )(*(pltpu.with_memory_space_constraint(x, pltpu.HBM) for x in tokens))
    return tuple(held), sums


def sums_kernel(wanted, *refs):
    for (own, block), out in zip(wanted, refs[4:]):
        sums_of(refs[:4], block_start(own, block, refs[0].shape[1] // 2), out)


def sums(tokens, *wanted):
    rows, width = tokens[0].shape
    return pl.pallas_call(
        functools.partial(sums_kernel, wanted),
        name="sums",
        in_specs=[VMEM] * 4,
        out_specs=[VMEM] * len(wanted),
        out_shape=[jax.ShapeDtypeStruct((2, width // 4, HEAD), BF16)] * len(wanted),
        cost_estimate=pl.CostEstimate(
            flops=rows * width * HEAD * len(wanted),
            bytes_accessed=3 * rows * width * len(wanted),
            transcendentals=0,
        ),
        compiler_params=SMALL,
    )(*tokens)


def pair_kernel(keep_ref, got_ref, *slots):
    for s, slot in enumerate(slots):
        part = slot_rows(s, len(slots), slot.shape[1])
        for which in range(2):
            both = keep_ref[which, part].astype(F32) + got_ref[which, part].astype(F32)
            slot[which] = both.astype(BF16)


def pair_slots(keep, got, count):
    slot = jax.ShapeDtypeStruct((2, keep.shape[1] // count, HEAD), BF16)
    return pl.pallas_call(
        pair_kernel,
        name="pair",
        in_specs=[VMEM] * 2,
        out_specs=[VMEM] * count,
        out_shape=[slot] * count,
        compiler_params=SMALL,
    )(keep, got)


def totals_kernel(far_count, *refs):
    slots, sends = refs[:far_count], refs[far_count:]
    outer = lax.axis_index("outer")
    totals = []
    for which in range(2):
        total = slots[0][which].astype(F32)
        for slot in slots[1:]:
            total += slot[which].astype(F32)
        totals.append(total.astype(BF16))
    for s, send in zip(distances(len(sends) + 1), sends):
        upward = (outer ^ s) > outer
        send[...] = jnp.where(upward, totals[0], totals[1])


def group_sends(slots, outer_count):
    send = jax.ShapeDtypeStruct(slots[0].shape[1:], BF16)
    return pl.pallas_call(
        functools.partial(totals_kernel, len(slots)),
        name="totals",
        in_specs=[VMEM] * len(slots),
        out_specs=[VMEM] * (outer_count - 1),
        out_shape=[send] * (outer_count - 1),
        compiler_params=SMALL,
    )(*slots)


def scan_kernel(far_count, *refs):
    slots, others, refs = refs[:far_count], refs[far_count : -far_count - 2], refs[-far_count - 2 :]
    outs, (held, scanned) = refs[:far_count], refs[far_count:]
    outer = lax.axis_index("outer")
    for s, slot in enumerate(slots):
        held[far_of(s)] = slot[...]
    for which in range(2):
        total = jnp.zeros(held.shape[2:], F32)
        for s, other in zip(distances(len(others) + 1), others):
            below = (outer ^ s) < outer
            wanted = below if which == 0 else jnp.logical_not(below)
            total += jnp.where(wanted, other[...].astype(F32), 0.0)
        for i in reversed(range(far_count)) if which else range(far_count):
            scanned[i, which] = total.astype(BF16)
            total += held[i, which].astype(F32)
    for s, out in enumerate(outs):
        out[...] = scanned[far_of(s)]


def scan_slots(slots, others):
    far_count, slot = len(slots), jax.ShapeDtypeStruct(slots[0].shape, BF16)
    return pl.pallas_call(
        functools.partial(scan_kernel, far_count),
        name="scan",
        in_specs=[VMEM] * (far_count + len(others)),
        out_specs=[VMEM] * far_count,
        out_shape=[slot] * far_count,
        scratch_shapes=[pltpu.VMEM((far_count, *slot.shape), BF16)] * 2,
        compiler_params=SMALL,
    )(*slots, *others)


def with_sums(slot, which, extra, part):
    return (slot[which].astype(F32) + extra[which, part].astype(F32)).astype(BF16)


def by_core(run):
    near, _ = near_far()
    for core in range(2):
        pl.when(near == core)(functools.partial(run, core))


def theirs_kernel(*refs):
    slots, (keep, out) = refs[:-2], refs[-2:]

    def run(core):
        for s, slot in enumerate(slots):
            part = slot_rows(s, len(slots), slot.shape[1])
            out[core, part] = with_sums(slot, core, keep, part)
            out[1 - core, part] = slot[1 - core]

    by_core(run)


def states_for_neighbour(slots, keep):
    return pl.pallas_call(
        theirs_kernel,
        name="theirs",
        in_specs=[VMEM] * (len(slots) + 1),
        out_specs=VMEM,
        out_shape=jax.ShapeDtypeStruct(keep.shape, BF16),
        compiler_params=SMALL,
    )(*slots, keep)


def local_kernel(*refs):
    tokens, outs = refs[:4], refs[4:]
    rows, width = tokens[0].shape
    at = lax.broadcasted_iota(jnp.int32, (rows, rows), 0)
    to = lax.broadcasted_iota(jnp.int32, (rows, rows), 1)
    lower = at >= to

    def masked(a, b):
        return jnp.where(lower, dot(a, b, 1, 1), 0.0).astype(BF16)

    def second(cols, a, b):
        q, k, v, d = (ref[:, cols] for ref in tokens)
        att, gq, gk, gv = outs
        att[:, cols] = dot(a, v, 1, 0)
        gq[:, cols] = dot(b, k, 1, 0)
        gk[:, cols] = dot(b, q, 0, 0)
        gv[:, cols] = dot(a, d, 0, 0)

    last = None
    for h in range(width // HEAD):
        cols = slice(h * HEAD, (h + 1) * HEAD)
        q, k, v, d = (ref[:, cols] for ref in tokens)
        a, b = masked(q, k), masked(d, v)
        if last:
            second(*last)
        last = (cols, a, b)
    second(*last)


def local_part(tokens):
    rows, width = tokens[0].shape
    return pl.pallas_call(
        local_kernel,
        name="local",
        in_specs=[VMEM] * 4,
        out_specs=[VMEM] * 4,
        out_shape=[jax.ShapeDtypeStruct((rows, width), F32)] * 4,
        cost_estimate=pl.CostEstimate(
            flops=12 * rows * width * HEAD, bytes_accessed=24 * rows * width, transcendentals=0
        ),
        compiler_params=SMALL,
    )(*tokens)


def all_products(scale, start, tokens, local, states, store):
    q, k, v, d = tokens

    def products():
        for n in range(states.shape[1] // HEAD):
            rows = slice(n * HEAD, (n + 1) * HEAD)
            cols = slice(start + n * HEAD, start + (n + 1) * HEAD)
            s, g = states[0, rows], states[1, rows]
            yield (rows, 0, cols), dot(q[:, cols], s, 1, 0)
            yield (rows, 1, cols), dot(d[:, cols], s, 1, 1)
            yield (rows, 2, cols), dot(v[:, cols], g, 1, 1)
            yield (rows, 3, cols), dot(k[:, cols], g, 1, 0)

    def use(key, product):
        rows, i, cols = key
        store(rows, i, (scale * (product + local[i][:, cols])).astype(BF16))

    one_ahead(products(), use)


def copies_out(own, block, held, outs, sems, piece):
    first, size = (0, held.shape[2]) if piece is None else (piece * held.shape[2] // 2, held.shape[2] // 2)
    start = block_start(own, block, outs[0].shape[1] // 2) + first
    there = pl.ds(pl.multiple_of(start, size), size)
    return [
        pltpu.make_async_copy(held.at[i, :, pl.ds(first, size)], out.at[:, there], sems.at[i])
        for i, out in enumerate(outs)
    ]


def finish_kernel(scale, own, block, count, rests, hold, *refs):
    tokens, local, slots, refs = refs[:4], refs[4:8], refs[8 : 8 + count], refs[8 + count :]
    got, refs = (refs[0], refs[1:]) if own else (None, refs)
    late, refs = refs[: len(rests)], refs[len(rests) :]
    if own:
        refs, states = refs[:-1], refs[-1]
    else:
        states = slots[0]
    if not hold or rests:
        *refs, sems = refs
    *refs, held = refs
    outs = refs[-4:]
    width = tokens[0].shape[1]
    copies = []
    for n, (rest, where) in enumerate(zip(late, rests)):
        copies += copies_out(*where, rest, outs, sems.at[n + 2], None)
    for copy in copies:
        copy.start()

    def store(rows, i, out):
        held[i, :, rows] = out
        for piece in range(2):
            if not hold and i == 3 and rows.stop == (piece + 1) * states.shape[1] // 2:
                for copy in copies_out(own, block, held, outs, sems.at[piece], piece):
                    copy.start()

    def run(quarter):
        for s, slot in enumerate(slots if own else ()):
            core, part = quarter // 2, slot_rows(s, count, slot.shape[1])
            states[core, part] = slot[core]
            states[1 - core, part] = with_sums(slot, 1 - core, got, part)
        all_products(scale, quarter * width // 4, tokens, local, states, store)

    start = block_start(own, block, width // 2)
    for quarter in range(4):
        pl.when(start == quarter * width // 4)(functools.partial(run, quarter))
    if not hold:
        for piece in range(2):
            copies += copies_out(own, block, held, outs, sems.at[piece], piece)
    for copy in copies:
        copy.wait()


def finish(own, block, tokens, local, slots, scale, got=(), rests=(), before=(), hold=False):
    rows, width = tokens[0].shape
    out = jax.ShapeDtypeStruct((rows, width), BF16)
    piece = pltpu.VMEM((4, rows, width // 4), BF16)
    inputs = [*tokens, *local, *slots, *got, *(x for _, x in rests)]
    states = pltpu.VMEM((2, width // 4, HEAD), BF16)
    wheres = [where for where, _ in rests]
    writes = not hold or bool(rests)
    return pl.pallas_call(
        functools.partial(finish_kernel, scale, own, block, len(slots), wheres, hold),
        name="finish",
        in_specs=[VMEM] * len(inputs) + [ANY] * len(before),
        out_specs=[ANY] * 4 * writes + [VMEM] * hold,
        out_shape=[out] * 4 * writes + [piece] * hold,
        scratch_shapes=[piece] * (not hold)
        + [pltpu.SemaphoreType.DMA((2 + len(rests), 4))] * writes
        + [states] * own,
        input_output_aliases={len(inputs) + i: i for i in range(len(before))},
        cost_estimate=pl.CostEstimate(
            flops=2 * rows * width * HEAD, bytes_accessed=8 * rows * width, transcendentals=0
        ),
        compiler_params=SMALL,
    )(*inputs, *before)


def swap(x, axis, bits):
    return lax.ppermute(x, axis, [(i, i ^ bits) for i in range(lax.axis_size(axis))])


def swap_far(slots):
    inner = range(lax.axis_size("inner"))
    pairs = [[(i, i ^ 2 * (s if i % 2 else exchanged(s))) for i in inner] for s in range(len(slots))]
    return [slots[0]] + [lax.ppermute(x, "inner", p) for x, p in zip(slots[1:], pairs[1:])]


def body(queries, keys, values, cotangent):
    far_count = lax.axis_size("inner") // 2
    outer_count = lax.axis_size("outer")
    scale = float(HEAD * queries.shape[0] * 2 * far_count * outer_count) ** (-0.5)
    tokens, give = load((queries, keys, values, cotangent))
    got = [swap(give, "inner", 1), swap(*sums(tokens, (False, 1)), "inner", 1)]
    keep = sums(tokens, (True, 0), (True, 1))
    slots = [slot for b in range(2) for slot in pair_slots(keep[b], got[b], far_count // 2)]
    slots, local = lax.optimization_barrier((swap_far(slots), local_part(tokens)))
    sends = group_sends(slots, outer_count)
    others = [swap(send, "outer", s) for s, send in zip(distances(outer_count), sends)]
    slots = swap_far(scan_slots(slots, others))
    half = far_count // 2

    def near_swap(block, part):
        return swap(states_for_neighbour(part, keep[block]), "inner", 1)

    arrived = [near_swap(0, slots[:half])]
    outs = finish(True, 0, tokens, local, slots[:half], scale, got=got[:1])
    part, outs = lax.optimization_barrier((slots[half:], tuple(outs)))
    arrived.append(near_swap(1, part))
    (rest,) = finish(True, 1, tokens, local, part, scale, got=got[1:], hold=True)
    rests = [((True, 1), rest)]
    *outs, rest = finish(
        False, 0, tokens, local, arrived[:1], scale, rests=rests, before=outs, hold=True
    )
    rests = [((False, 0), rest)]
    return tuple(finish(False, 1, tokens, local, arrived[1:], scale, rests=rests, before=outs))


def solution(mesh):
    spec = P(("outer", "inner"), None)
    return jax.shard_map(
        body, mesh=mesh, in_specs=(spec,) * 4, out_specs=(spec,) * 4, check_vma=False
    )
```

```python
import functools

import jax
import jax.numpy as jnp
from jax import lax
from jax.experimental import pallas as pl
from jax.experimental.pallas import tpu as pltpu
from jax.sharding import PartitionSpec as P

HEAD = 128
MIB = 1024 * 1024
ANY = pl.BlockSpec(memory_space=pl.ANY)
VMEM = pl.BlockSpec(memory_space=pltpu.VMEM)
BF16 = jnp.bfloat16
F32 = jnp.float32
SMALL = pltpu.CompilerParams(vmem_limit_bytes=4 * MIB)


def dot(a, b, over_a, over_b):
    return lax.dot_general(
        a, b, (((over_a,), (over_b,)), ((), ())), preferred_element_type=F32
    )


def near_far():
    inner = lax.axis_index("inner")
    return lax.rem(inner, 2), lax.div(inner, 2)


def distances(outer_count):
    order = list(range(outer_count - 1, 0, -1))
    return order[1:2] + order[:1] + order[2:]


def block_start(own, block, half):
    near, far = near_far()
    side = near if own else 1 - near
    top = lax.div(far, lax.axis_size("inner") // 4)
    return side * half + (1 - top if block else top) * (half // 2)


def columns(start, n):
    return pl.ds(pl.multiple_of(start + n * HEAD, HEAD), HEAD)


def slot_rows(s, count, depth):
    _, far = near_far()
    return pl.ds(pl.multiple_of(lax.rem(far ^ s, count) * depth, depth), depth)


def one_ahead(products, use):
    last = None
    for key, product in products:
        if last:
            use(*last)
        last = key, product
    use(*last)


def sums_of(tokens, start, out, kinds=(0, 1)):
    q, k, v, d = tokens

    def products():
        for n in range(out.shape[1] // HEAD):
            cols = pl.ds(start + n * HEAD, HEAD) if isinstance(start, int) else columns(start, n)
            for which in kinds:
                a, b = ((k, v), (q, d))[which]
                yield (which, n), dot(a[:, cols], b[:, cols], 0, 0)

    def use(key, product):
        which, n = key
        out[which, n * HEAD : (n + 1) * HEAD] = product.astype(BF16)

    one_ahead(products(), use)


def load_kernel(*refs):
    tokens, held, (out, sems) = refs[:4], refs[4:8], refs[8:]
    copies = [pltpu.make_async_copy(tokens[i], held[i], sems.at[i]) for i in range(4)]
    width = held[0].shape[1]
    start = block_start(False, 0, width // 2)
    pairs = ((1, 2), (0, 3))
    for i in pairs[0] + pairs[1]:
        copies[i].start()
    for kind, pair in enumerate(pairs):
        for i in pair:
            copies[i].wait()
        for n in range(4):
            at = n * width // 4
            pl.when(start == at)(functools.partial(sums_of, held, at, out, (kind,)))


def load(tokens):
    rows, width = tokens[0].shape
    *held, sums = pl.pallas_call(
        load_kernel,
        name="load",
        in_specs=[ANY] * 4,
        out_specs=[VMEM] * 5,
        out_shape=[pltpu.VMEM((rows, width), BF16)] * 4 + [pltpu.VMEM((2, width // 4, HEAD), BF16)],
        scratch_shapes=[pltpu.SemaphoreType.DMA((4,))],
        cost_estimate=pl.CostEstimate(
            flops=rows * width * HEAD, bytes_accessed=10 * rows * width, transcendentals=0
        ),
        compiler_params=SMALL,
    )(*(pltpu.with_memory_space_constraint(x, pltpu.HBM) for x in tokens))
    return tuple(held), sums


def sums_kernel(wanted, *refs):
    for (own, block), out in zip(wanted, refs[4:]):
        sums_of(refs[:4], block_start(own, block, refs[0].shape[1] // 2), out)


def sums(tokens, *wanted):
    rows, width = tokens[0].shape
    return pl.pallas_call(
        functools.partial(sums_kernel, wanted),
        name="sums",
        in_specs=[VMEM] * 4,
        out_specs=[VMEM] * len(wanted),
        out_shape=[jax.ShapeDtypeStruct((2, width // 4, HEAD), BF16)] * len(wanted),
        cost_estimate=pl.CostEstimate(
            flops=rows * width * HEAD * len(wanted),
            bytes_accessed=3 * rows * width * len(wanted),
            transcendentals=0,
        ),
        compiler_params=SMALL,
    )(*tokens)


def pair_kernel(keep_ref, got_ref, *slots):
    for s, slot in enumerate(slots):
        part = slot_rows(s, len(slots), slot.shape[1])
        for which in range(2):
            both = keep_ref[which, part].astype(F32) + got_ref[which, part].astype(F32)
            slot[which] = both.astype(BF16)


def pair_slots(keep, got, count):
    slot = jax.ShapeDtypeStruct((2, keep.shape[1] // count, HEAD), BF16)
    return pl.pallas_call(
        pair_kernel,
        name="pair",
        in_specs=[VMEM] * 2,
        out_specs=[VMEM] * count,
        out_shape=[slot] * count,
        compiler_params=SMALL,
    )(keep, got)


def totals_kernel(far_count, *refs):
    slots, sends = refs[:far_count], refs[far_count:]
    outer = lax.axis_index("outer")
    totals = []
    for which in range(2):
        total = slots[0][which].astype(F32)
        for slot in slots[1:]:
            total += slot[which].astype(F32)
        totals.append(total.astype(BF16))
    for s, send in zip(distances(len(sends) + 1), sends):
        upward = (outer ^ s) > outer
        send[...] = jnp.where(upward, totals[0], totals[1])


def group_sends(slots, outer_count):
    send = jax.ShapeDtypeStruct(slots[0].shape[1:], BF16)
    return pl.pallas_call(
        functools.partial(totals_kernel, len(slots)),
        name="totals",
        in_specs=[VMEM] * len(slots),
        out_specs=[VMEM] * (outer_count - 1),
        out_shape=[send] * (outer_count - 1),
        compiler_params=SMALL,
    )(*slots)


def scan_kernel(far_count, *refs):
    slots, others, refs = refs[:far_count], refs[far_count : -far_count - 2], refs[-far_count - 2 :]
    outs, (held, scanned) = refs[:far_count], refs[far_count:]
    outer = lax.axis_index("outer")
    _, far = near_far()
    for s, slot in enumerate(slots):
        held[far ^ s] = slot[...]
    for which in range(2):
        total = jnp.zeros(held.shape[2:], F32)
        for s, other in zip(distances(len(others) + 1), others):
            below = (outer ^ s) < outer
            wanted = below if which == 0 else jnp.logical_not(below)
            total += jnp.where(wanted, other[...].astype(F32), 0.0)
        for i in reversed(range(far_count)) if which else range(far_count):
            scanned[i, which] = total.astype(BF16)
            total += held[i, which].astype(F32)
    for s, out in enumerate(outs):
        out[...] = scanned[far ^ s]


def scan_slots(slots, others):
    far_count, slot = len(slots), jax.ShapeDtypeStruct(slots[0].shape, BF16)
    return pl.pallas_call(
        functools.partial(scan_kernel, far_count),
        name="scan",
        in_specs=[VMEM] * (far_count + len(others)),
        out_specs=[VMEM] * far_count,
        out_shape=[slot] * far_count,
        scratch_shapes=[pltpu.VMEM((far_count, *slot.shape), BF16)] * 2,
        compiler_params=SMALL,
    )(*slots, *others)


def with_sums(slot, which, extra, part):
    return (slot[which].astype(F32) + extra[which, part].astype(F32)).astype(BF16)


def by_core(run):
    near, _ = near_far()
    for core in range(2):
        pl.when(near == core)(functools.partial(run, core))


def theirs_kernel(*refs):
    slots, (keep, out) = refs[:-2], refs[-2:]

    def run(core):
        for s, slot in enumerate(slots):
            part = slot_rows(s, len(slots), slot.shape[1])
            out[core, part] = with_sums(slot, core, keep, part)
            out[1 - core, part] = slot[1 - core]

    by_core(run)


def states_for_neighbour(slots, keep):
    return pl.pallas_call(
        theirs_kernel,
        name="theirs",
        in_specs=[VMEM] * (len(slots) + 1),
        out_specs=VMEM,
        out_shape=jax.ShapeDtypeStruct(keep.shape, BF16),
        compiler_params=SMALL,
    )(*slots, keep)


def local_kernel(*refs):
    tokens, outs = refs[:4], refs[4:]
    rows, width = tokens[0].shape
    at = lax.broadcasted_iota(jnp.int32, (rows, rows), 0)
    to = lax.broadcasted_iota(jnp.int32, (rows, rows), 1)
    lower = at >= to

    def masked(a, b):
        return jnp.where(lower, dot(a, b, 1, 1), 0.0).astype(BF16)

    def second(cols, a, b):
        q, k, v, d = (ref[:, cols] for ref in tokens)
        att, gq, gk, gv = outs
        att[:, cols] = dot(a, v, 1, 0)
        gq[:, cols] = dot(b, k, 1, 0)
        gk[:, cols] = dot(b, q, 0, 0)
        gv[:, cols] = dot(a, d, 0, 0)

    last = None
    for h in range(width // HEAD):
        cols = slice(h * HEAD, (h + 1) * HEAD)
        q, k, v, d = (ref[:, cols] for ref in tokens)
        a, b = masked(q, k), masked(d, v)
        if last:
            second(*last)
        last = (cols, a, b)
    second(*last)


def local_part(tokens):
    rows, width = tokens[0].shape
    return pl.pallas_call(
        local_kernel,
        name="local",
        in_specs=[VMEM] * 4,
        out_specs=[VMEM] * 4,
        out_shape=[jax.ShapeDtypeStruct((rows, width), F32)] * 4,
        cost_estimate=pl.CostEstimate(
            flops=12 * rows * width * HEAD, bytes_accessed=24 * rows * width, transcendentals=0
        ),
        compiler_params=SMALL,
    )(*tokens)


def all_products(scale, start, tokens, local, states, store):
    q, k, v, d = tokens

    def products():
        for n in range(states.shape[1] // HEAD):
            rows = slice(n * HEAD, (n + 1) * HEAD)
            cols = slice(start + n * HEAD, start + (n + 1) * HEAD)
            s, g = states[0, rows], states[1, rows]
            yield (rows, 0, cols), dot(q[:, cols], s, 1, 0)
            yield (rows, 1, cols), dot(d[:, cols], s, 1, 1)
            yield (rows, 2, cols), dot(v[:, cols], g, 1, 1)
            yield (rows, 3, cols), dot(k[:, cols], g, 1, 0)

    def use(key, product):
        rows, i, cols = key
        store(rows, i, (scale * (product + local[i][:, cols])).astype(BF16))

    one_ahead(products(), use)


def copies_out(own, block, held, outs, sems, piece):
    first, size = (0, held.shape[2]) if piece is None else (piece * held.shape[2] // 2, held.shape[2] // 2)
    start = block_start(own, block, outs[0].shape[1] // 2) + first
    there = pl.ds(pl.multiple_of(start, size), size)
    return [
        pltpu.make_async_copy(held.at[i, :, pl.ds(first, size)], out.at[:, there], sems.at[i])
        for i, out in enumerate(outs)
    ]


def finish_kernel(scale, own, block, count, rests, hold, *refs):
    tokens, local, slots, refs = refs[:4], refs[4:8], refs[8 : 8 + count], refs[8 + count :]
    got, refs = (refs[0], refs[1:]) if own else (None, refs)
    late, refs = refs[: len(rests)], refs[len(rests) :]
    if own:
        refs, states = refs[:-1], refs[-1]
    else:
        states = slots[0]
    if not hold or rests:
        *refs, sems = refs
    *refs, held = refs
    outs = refs[-4:]
    width = tokens[0].shape[1]
    copies = []
    for n, (rest, where) in enumerate(zip(late, rests)):
        copies += copies_out(*where, rest, outs, sems.at[n + 2], None)
    for copy in copies:
        copy.start()

    def store(rows, i, out):
        held[i, :, rows] = out
        for piece in range(2):
            if not hold and i == 3 and rows.stop == (piece + 1) * states.shape[1] // 2:
                for copy in copies_out(own, block, held, outs, sems.at[piece], piece):
                    copy.start()

    def run(quarter):
        for s, slot in enumerate(slots if own else ()):
            core, part = quarter // 2, slot_rows(s, count, slot.shape[1])
            states[core, part] = slot[core]
            states[1 - core, part] = with_sums(slot, 1 - core, got, part)
        all_products(scale, quarter * width // 4, tokens, local, states, store)

    start = block_start(own, block, width // 2)
    for quarter in range(4):
        pl.when(start == quarter * width // 4)(functools.partial(run, quarter))
    if not hold:
        for piece in range(2):
            copies += copies_out(own, block, held, outs, sems.at[piece], piece)
    for copy in copies:
        copy.wait()


def finish(own, block, tokens, local, slots, scale, got=(), rests=(), before=(), hold=False):
    rows, width = tokens[0].shape
    out = jax.ShapeDtypeStruct((rows, width), BF16)
    piece = pltpu.VMEM((4, rows, width // 4), BF16)
    inputs = [*tokens, *local, *slots, *got, *(x for _, x in rests)]
    states = pltpu.VMEM((2, width // 4, HEAD), BF16)
    wheres = [where for where, _ in rests]
    writes = not hold or bool(rests)
    return pl.pallas_call(
        functools.partial(finish_kernel, scale, own, block, len(slots), wheres, hold),
        name="finish",
        in_specs=[VMEM] * len(inputs) + [ANY] * len(before),
        out_specs=[ANY] * 4 * writes + [VMEM] * hold,
        out_shape=[out] * 4 * writes + [piece] * hold,
        scratch_shapes=[piece] * (not hold)
        + [pltpu.SemaphoreType.DMA((2 + len(rests), 4))] * writes
        + [states] * own,
        input_output_aliases={len(inputs) + i: i for i in range(len(before))},
        cost_estimate=pl.CostEstimate(
            flops=2 * rows * width * HEAD, bytes_accessed=8 * rows * width, transcendentals=0
        ),
        compiler_params=SMALL,
    )(*inputs, *before)


def swap(x, axis, bits):
    return lax.ppermute(x, axis, [(i, i ^ bits) for i in range(lax.axis_size(axis))])


def swap_far(slots):
    return [slots[0]] + [swap(slots[s], "inner", 2 * s) for s in range(1, len(slots))]


def body(queries, keys, values, cotangent):
    far_count = lax.axis_size("inner") // 2
    outer_count = lax.axis_size("outer")
    scale = float(HEAD * queries.shape[0] * 2 * far_count * outer_count) ** (-0.5)
    tokens, give = load((queries, keys, values, cotangent))
    got = [swap(give, "inner", 1), swap(*sums(tokens, (False, 1)), "inner", 1)]
    keep = sums(tokens, (True, 0), (True, 1))
    slots = [slot for b in range(2) for slot in pair_slots(keep[b], got[b], far_count // 2)]
    slots, local = lax.optimization_barrier((swap_far(slots), local_part(tokens)))
    sends = group_sends(slots, outer_count)
    others = [swap(send, "outer", s) for s, send in zip(distances(outer_count), sends)]
    slots = swap_far(scan_slots(slots, others))
    half = far_count // 2

    def near_swap(block, part):
        return swap(states_for_neighbour(part, keep[block]), "inner", 1)

    arrived = [near_swap(0, slots[:half])]
    outs = finish(True, 0, tokens, local, slots[:half], scale, got=got[:1])
    part, outs = lax.optimization_barrier((slots[half:], tuple(outs)))
    arrived.append(near_swap(1, part))
    (rest,) = finish(True, 1, tokens, local, part, scale, got=got[1:], hold=True)
    rests = [((True, 1), rest)]
    *outs, rest = finish(
        False, 0, tokens, local, arrived[:1], scale, rests=rests, before=outs, hold=True
    )
    rests = [((False, 0), rest)]
    return tuple(finish(False, 1, tokens, local, arrived[1:], scale, rests=rests, before=outs))


def solution(mesh):
    spec = P(("outer", "inner"), None)
    return jax.shard_map(
        body, mesh=mesh, in_specs=(spec,) * 4, out_specs=(spec,) * 4, check_vma=False
    )
```

```python
import functools

import jax
import jax.numpy as jnp
from jax import lax
from jax.experimental import pallas as pl
from jax.experimental.pallas import tpu as pltpu
from jax.sharding import PartitionSpec as P

HEAD = 128
MIB = 1024 * 1024
ANY = pl.BlockSpec(memory_space=pl.ANY)
VMEM = pl.BlockSpec(memory_space=pltpu.VMEM)
BF16 = jnp.bfloat16
F32 = jnp.float32
SMALL = pltpu.CompilerParams(vmem_limit_bytes=4 * MIB)


def dot(a, b, over_a, over_b):
    return lax.dot_general(
        a, b, (((over_a,), (over_b,)), ((), ())), preferred_element_type=F32
    )


def near_far():
    inner = lax.axis_index("inner")
    return lax.rem(inner, 2), lax.div(inner, 2)


def distances(outer_count):
    return range(outer_count - 1, 0, -1)


def block_start(own, block, half):
    near, far = near_far()
    side = near if own else 1 - near
    top = lax.div(far, lax.axis_size("inner") // 4)
    return side * half + (1 - top if block else top) * (half // 2)


def columns(start, n):
    return pl.ds(pl.multiple_of(start + n * HEAD, HEAD), HEAD)


def slot_rows(s, count, depth):
    _, far = near_far()
    return pl.ds(pl.multiple_of(lax.rem(far ^ s, count) * depth, depth), depth)


def one_ahead(products, use):
    last = None
    for key, product in products:
        if last:
            use(*last)
        last = key, product
    use(*last)


def sums_of(tokens, start, out, kinds=(0, 1)):
    q, k, v, d = tokens

    def products():
        for n in range(out.shape[1] // HEAD):
            cols = pl.ds(start + n * HEAD, HEAD) if isinstance(start, int) else columns(start, n)
            for which in kinds:
                a, b = ((k, v), (q, d))[which]
                yield (which, n), dot(a[:, cols], b[:, cols], 0, 0)

    def use(key, product):
        which, n = key
        out[which, n * HEAD : (n + 1) * HEAD] = product.astype(BF16)

    one_ahead(products(), use)


def give_kernel(*refs):
    tokens, (out, held, sems) = refs[:4], refs[4:]
    width = tokens[0].shape[1]
    start = pl.multiple_of(block_start(False, 0, width // 2), width // 4)
    pairs = ((1, 2), (0, 3))
    copies = [
        pltpu.make_async_copy(ref.at[:, pl.ds(start, width // 4)], held.at[i], sems.at[i])
        for i, ref in enumerate(tokens)
    ]
    for i in pairs[0] + pairs[1]:
        copies[i].start()
    for kind, pair in enumerate(pairs):
        for i in pair:
            copies[i].wait()
        sums_of([held.at[i] for i in range(4)], 0, out, (kind,))


def first_sums(tokens):
    rows, width = tokens[0].shape
    return pl.pallas_call(
        give_kernel,
        name="first_sums",
        in_specs=[ANY] * 4,
        out_specs=VMEM,
        out_shape=pltpu.VMEM((2, width // 4, HEAD), BF16),
        scratch_shapes=[pltpu.VMEM((4, rows, width // 4), BF16), pltpu.SemaphoreType.DMA((4,))],
        cost_estimate=pl.CostEstimate(
            flops=rows * width * HEAD, bytes_accessed=3 * rows * width, transcendentals=0
        ),
        compiler_params=SMALL,
    )(*(pltpu.with_memory_space_constraint(x, pltpu.HBM) for x in tokens))


def sums_kernel(wanted, *refs):
    for (own, block), out in zip(wanted, refs[4:]):
        sums_of(refs[:4], block_start(own, block, refs[0].shape[1] // 2), out)


def sums(tokens, *wanted):
    rows, width = tokens[0].shape
    return pl.pallas_call(
        functools.partial(sums_kernel, wanted),
        name="sums",
        in_specs=[VMEM] * 4,
        out_specs=[VMEM] * len(wanted),
        out_shape=[jax.ShapeDtypeStruct((2, width // 4, HEAD), BF16)] * len(wanted),
        cost_estimate=pl.CostEstimate(
            flops=rows * width * HEAD * len(wanted),
            bytes_accessed=3 * rows * width * len(wanted),
            transcendentals=0,
        ),
        compiler_params=SMALL,
    )(*tokens)


def pair_kernel(keep_ref, got_ref, *slots):
    for s, slot in enumerate(slots):
        part = slot_rows(s, len(slots), slot.shape[1])
        for which in range(2):
            both = keep_ref[which, part].astype(F32) + got_ref[which, part].astype(F32)
            slot[which] = both.astype(BF16)


def pair_slots(keep, got, count):
    slot = jax.ShapeDtypeStruct((2, keep.shape[1] // count, HEAD), BF16)
    return pl.pallas_call(
        pair_kernel,
        name="pair",
        in_specs=[VMEM] * 2,
        out_specs=[VMEM] * count,
        out_shape=[slot] * count,
        compiler_params=SMALL,
    )(keep, got)


def totals_kernel(far_count, *refs):
    slots, sends = refs[:far_count], refs[far_count:]
    outer = lax.axis_index("outer")
    totals = []
    for which in range(2):
        total = slots[0][which].astype(F32)
        for slot in slots[1:]:
            total += slot[which].astype(F32)
        totals.append(total.astype(BF16))
    for s, send in zip(distances(len(sends) + 1), sends):
        upward = (outer ^ s) > outer
        send[...] = jnp.where(upward, totals[0], totals[1])


def group_sends(slots, outer_count):
    send = jax.ShapeDtypeStruct(slots[0].shape[1:], BF16)
    return pl.pallas_call(
        functools.partial(totals_kernel, len(slots)),
        name="totals",
        in_specs=[VMEM] * len(slots),
        out_specs=[VMEM] * (outer_count - 1),
        out_shape=[send] * (outer_count - 1),
        compiler_params=SMALL,
    )(*slots)


def scan_kernel(far_count, *refs):
    slots, others, refs = refs[:far_count], refs[far_count : -far_count - 2], refs[-far_count - 2 :]
    outs, (held, scanned) = refs[:far_count], refs[far_count:]
    outer = lax.axis_index("outer")
    _, far = near_far()
    for s, slot in enumerate(slots):
        held[far ^ s] = slot[...]
    for which in range(2):
        total = jnp.zeros(held.shape[2:], F32)
        for s, other in zip(distances(len(others) + 1), others):
            below = (outer ^ s) < outer
            wanted = below if which == 0 else jnp.logical_not(below)
            total += jnp.where(wanted, other[...].astype(F32), 0.0)
        for i in reversed(range(far_count)) if which else range(far_count):
            scanned[i, which] = total.astype(BF16)
            total += held[i, which].astype(F32)
    for s, out in enumerate(outs):
        out[...] = scanned[far ^ s]


def scan_slots(slots, others):
    far_count, slot = len(slots), jax.ShapeDtypeStruct(slots[0].shape, BF16)
    return pl.pallas_call(
        functools.partial(scan_kernel, far_count),
        name="scan",
        in_specs=[VMEM] * (far_count + len(others)),
        out_specs=[VMEM] * far_count,
        out_shape=[slot] * far_count,
        scratch_shapes=[pltpu.VMEM((far_count, *slot.shape), BF16)] * 2,
        compiler_params=SMALL,
    )(*slots, *others)


def with_sums(slot, which, extra, part):
    return (slot[which].astype(F32) + extra[which, part].astype(F32)).astype(BF16)


def by_core(run):
    near, _ = near_far()
    for core in range(2):
        pl.when(near == core)(functools.partial(run, core))


def theirs_kernel(*refs):
    slots, (keep, out) = refs[:-2], refs[-2:]

    def run(core):
        for s, slot in enumerate(slots):
            part = slot_rows(s, len(slots), slot.shape[1])
            out[core, part] = with_sums(slot, core, keep, part)
            out[1 - core, part] = slot[1 - core]

    by_core(run)


def states_for_neighbour(slots, keep):
    return pl.pallas_call(
        theirs_kernel,
        name="theirs",
        in_specs=[VMEM] * (len(slots) + 1),
        out_specs=VMEM,
        out_shape=jax.ShapeDtypeStruct(keep.shape, BF16),
        compiler_params=SMALL,
    )(*slots, keep)


def local_kernel(*refs):
    tokens, outs = refs[:4], refs[4:]
    rows, width = tokens[0].shape
    at = lax.broadcasted_iota(jnp.int32, (rows, rows), 0)
    to = lax.broadcasted_iota(jnp.int32, (rows, rows), 1)
    lower = at >= to

    def masked(a, b):
        return jnp.where(lower, dot(a, b, 1, 1), 0.0).astype(BF16)

    def second(cols, a, b):
        q, k, v, d = (ref[:, cols] for ref in tokens)
        att, gq, gk, gv = outs
        att[:, cols] = dot(a, v, 1, 0)
        gq[:, cols] = dot(b, k, 1, 0)
        gk[:, cols] = dot(b, q, 0, 0)
        gv[:, cols] = dot(a, d, 0, 0)

    last = None
    for h in range(width // HEAD):
        cols = slice(h * HEAD, (h + 1) * HEAD)
        q, k, v, d = (ref[:, cols] for ref in tokens)
        a, b = masked(q, k), masked(d, v)
        if last:
            second(*last)
        last = (cols, a, b)
    second(*last)


def local_part(tokens):
    rows, width = tokens[0].shape
    return pl.pallas_call(
        local_kernel,
        name="local",
        in_specs=[VMEM] * 4,
        out_specs=[VMEM] * 4,
        out_shape=[jax.ShapeDtypeStruct((rows, width), F32)] * 4,
        cost_estimate=pl.CostEstimate(
            flops=12 * rows * width * HEAD, bytes_accessed=24 * rows * width, transcendentals=0
        ),
        compiler_params=SMALL,
    )(*tokens)


def all_products(scale, start, tokens, local, states, store):
    q, k, v, d = tokens

    def products():
        for n in range(states.shape[1] // HEAD):
            rows = slice(n * HEAD, (n + 1) * HEAD)
            cols = slice(start + n * HEAD, start + (n + 1) * HEAD)
            s, g = states[0, rows], states[1, rows]
            yield (rows, 0, cols), dot(q[:, cols], s, 1, 0)
            yield (rows, 1, cols), dot(d[:, cols], s, 1, 1)
            yield (rows, 2, cols), dot(v[:, cols], g, 1, 1)
            yield (rows, 3, cols), dot(k[:, cols], g, 1, 0)

    def use(key, product):
        rows, i, cols = key
        store(rows, i, (scale * (product + local[i][:, cols])).astype(BF16))

    one_ahead(products(), use)


def copies_out(own, block, held, outs, sems, piece):
    first, size = (0, held.shape[2]) if piece is None else (piece * held.shape[2] // 2, held.shape[2] // 2)
    start = block_start(own, block, outs[0].shape[1] // 2) + first
    there = pl.ds(pl.multiple_of(start, size), size)
    return [
        pltpu.make_async_copy(held.at[i, :, pl.ds(first, size)], out.at[:, there], sems.at[i])
        for i, out in enumerate(outs)
    ]


def finish_kernel(scale, own, block, count, rests, hold, *refs):
    tokens, local, slots, refs = refs[:4], refs[4:8], refs[8 : 8 + count], refs[8 + count :]
    got, refs = (refs[0], refs[1:]) if own else (None, refs)
    late, refs = refs[: len(rests)], refs[len(rests) :]
    if own:
        refs, states = refs[:-1], refs[-1]
    else:
        states = slots[0]
    if not hold or rests:
        *refs, sems = refs
    *refs, held = refs
    outs = refs[-4:]
    width = tokens[0].shape[1]
    copies = []
    for n, (rest, where) in enumerate(zip(late, rests)):
        copies += copies_out(*where, rest, outs, sems.at[n + 2], None)
    for copy in copies:
        copy.start()

    def store(rows, i, out):
        held[i, :, rows] = out
        for piece in range(2):
            if not hold and i == 3 and rows.stop == (piece + 1) * states.shape[1] // 2:
                for copy in copies_out(own, block, held, outs, sems.at[piece], piece):
                    copy.start()

    def run(quarter):
        for s, slot in enumerate(slots if own else ()):
            core, part = quarter // 2, slot_rows(s, count, slot.shape[1])
            states[core, part] = slot[core]
            states[1 - core, part] = with_sums(slot, 1 - core, got, part)
        all_products(scale, quarter * width // 4, tokens, local, states, store)

    start = block_start(own, block, width // 2)
    for quarter in range(4):
        pl.when(start == quarter * width // 4)(functools.partial(run, quarter))
    if not hold:
        for piece in range(2):
            copies += copies_out(own, block, held, outs, sems.at[piece], piece)
    for copy in copies:
        copy.wait()


def finish(own, block, tokens, local, slots, scale, got=(), rests=(), before=(), hold=False):
    rows, width = tokens[0].shape
    out = jax.ShapeDtypeStruct((rows, width), BF16)
    piece = pltpu.VMEM((4, rows, width // 4), BF16)
    inputs = [*tokens, *local, *slots, *got, *(x for _, x in rests)]
    states = pltpu.VMEM((2, width // 4, HEAD), BF16)
    wheres = [where for where, _ in rests]
    writes = not hold or bool(rests)
    return pl.pallas_call(
        functools.partial(finish_kernel, scale, own, block, len(slots), wheres, hold),
        name="finish",
        in_specs=[VMEM] * len(inputs) + [ANY] * len(before),
        out_specs=[ANY] * 4 * writes + [VMEM] * hold,
        out_shape=[out] * 4 * writes + [piece] * hold,
        scratch_shapes=[piece] * (not hold)
        + [pltpu.SemaphoreType.DMA((2 + len(rests), 4))] * writes
        + [states] * own,
        input_output_aliases={len(inputs) + i: i for i in range(len(before))},
        cost_estimate=pl.CostEstimate(
            flops=2 * rows * width * HEAD, bytes_accessed=8 * rows * width, transcendentals=0
        ),
        compiler_params=SMALL,
    )(*inputs, *before)


def swap(x, axis, bits):
    return lax.ppermute(x, axis, [(i, i ^ bits) for i in range(lax.axis_size(axis))])


def swap_far(slots):
    return [slots[0]] + [swap(slots[s], "inner", 2 * s) for s in range(1, len(slots))]


def body(queries, keys, values, cotangent):
    far_count = lax.axis_size("inner") // 2
    outer_count = lax.axis_size("outer")
    scale = float(HEAD * queries.shape[0] * 2 * far_count * outer_count) ** (-0.5)
    tokens = (queries, keys, values, cotangent)
    give = first_sums(tokens)
    got = [swap(give, "inner", 1), swap(*sums(tokens, (False, 1)), "inner", 1)]
    keep = sums(tokens, (True, 0), (True, 1))
    slots = [slot for b in range(2) for slot in pair_slots(keep[b], got[b], far_count // 2)]
    slots, local = lax.optimization_barrier((swap_far(slots), local_part(tokens)))
    sends = group_sends(slots, outer_count)
    others = [swap(send, "outer", s) for s, send in zip(distances(outer_count), sends)]
    slots = swap_far(scan_slots(slots, others))
    half = far_count // 2

    def near_swap(block, part):
        return swap(states_for_neighbour(part, keep[block]), "inner", 1)

    arrived = [near_swap(0, slots[:half])]
    outs = finish(True, 0, tokens, local, slots[:half], scale, got=got[:1])
    part, outs = lax.optimization_barrier((slots[half:], tuple(outs)))
    arrived.append(near_swap(1, part))
    (rest,) = finish(True, 1, tokens, local, part, scale, got=got[1:], hold=True)
    rests = [((True, 1), rest)]
    *outs, rest = finish(
        False, 0, tokens, local, arrived[:1], scale, rests=rests, before=outs, hold=True
    )
    rests = [((False, 0), rest)]
    return tuple(finish(False, 1, tokens, local, arrived[1:], scale, rests=rests, before=outs))


def solution(mesh):
    spec = P(("outer", "inner"), None)
    return jax.shard_map(
        body, mesh=mesh, in_specs=(spec,) * 4, out_specs=(spec,) * 4, check_vma=False
    )
```

```python
import functools

import jax
import jax.numpy as jnp
from jax import lax
from jax.experimental import pallas as pl
from jax.experimental.pallas import tpu as pltpu
from jax.sharding import PartitionSpec as P

HEAD = 128
MIB = 1024 * 1024
ANY = pl.BlockSpec(memory_space=pl.ANY)
VMEM = pl.BlockSpec(memory_space=pltpu.VMEM)
BF16 = jnp.bfloat16
F32 = jnp.float32
SMALL = pltpu.CompilerParams(vmem_limit_bytes=4 * MIB)


def dot(a, b, over_a, over_b):
    return lax.dot_general(
        a, b, (((over_a,), (over_b,)), ((), ())), preferred_element_type=F32
    )


def near_far():
    inner = lax.axis_index("inner")
    return lax.rem(inner, 2), lax.div(inner, 2)


def distances(outer_count):
    return range(outer_count - 1, 0, -1)


def block_start(own, block, half):
    near, far = near_far()
    side = near if own else 1 - near
    top = lax.div(far, lax.axis_size("inner") // 4)
    return side * half + (1 - top if block else top) * (half // 2)


def columns(start, n):
    return pl.ds(pl.multiple_of(start + n * HEAD, HEAD), HEAD)


def slot_rows(s, count, depth):
    _, far = near_far()
    return pl.ds(pl.multiple_of(lax.rem(far ^ s, count) * depth, depth), depth)


def one_ahead(products, use):
    last = None
    for key, product in products:
        if last:
            use(*last)
        last = key, product
    use(*last)


def sums_of(tokens, start, out, kinds=(0, 1)):
    q, k, v, d = tokens

    def products():
        for n in range(out.shape[1] // HEAD):
            cols = pl.ds(start + n * HEAD, HEAD) if isinstance(start, int) else columns(start, n)
            for which in kinds:
                a, b = ((k, v), (q, d))[which]
                yield (which, n), dot(a[:, cols], b[:, cols], 0, 0)

    def use(key, product):
        which, n = key
        out[which, n * HEAD : (n + 1) * HEAD] = product.astype(BF16)

    one_ahead(products(), use)


def load_kernel(*refs):
    tokens, held, (out, sems) = refs[:4], refs[4:8], refs[8:]
    copies = [pltpu.make_async_copy(tokens[i], held[i], sems.at[i]) for i in range(4)]
    width = held[0].shape[1]
    start = block_start(False, 0, width // 2)
    pairs = ((1, 2), (0, 3))
    for i in pairs[0] + pairs[1]:
        copies[i].start()
    for kind, pair in enumerate(pairs):
        for i in pair:
            copies[i].wait()
        for n in range(4):
            at = n * width // 4
            pl.when(start == at)(functools.partial(sums_of, held, at, out, (kind,)))


def load(tokens):
    rows, width = tokens[0].shape
    *held, sums = pl.pallas_call(
        load_kernel,
        name="load",
        in_specs=[ANY] * 4,
        out_specs=[VMEM] * 5,
        out_shape=[pltpu.VMEM((rows, width), BF16)] * 4 + [pltpu.VMEM((2, width // 4, HEAD), BF16)],
        scratch_shapes=[pltpu.SemaphoreType.DMA((4,))],
        cost_estimate=pl.CostEstimate(
            flops=rows * width * HEAD, bytes_accessed=10 * rows * width, transcendentals=0
        ),
        compiler_params=SMALL,
    )(*(pltpu.with_memory_space_constraint(x, pltpu.HBM) for x in tokens))
    return tuple(held), sums


def sums_kernel(wanted, *refs):
    for (own, block), out in zip(wanted, refs[4:]):
        sums_of(refs[:4], block_start(own, block, refs[0].shape[1] // 2), out)


def sums(tokens, *wanted):
    rows, width = tokens[0].shape
    return pl.pallas_call(
        functools.partial(sums_kernel, wanted),
        name="sums",
        in_specs=[VMEM] * 4,
        out_specs=[VMEM] * len(wanted),
        out_shape=[jax.ShapeDtypeStruct((2, width // 4, HEAD), BF16)] * len(wanted),
        cost_estimate=pl.CostEstimate(
            flops=rows * width * HEAD * len(wanted),
            bytes_accessed=3 * rows * width * len(wanted),
            transcendentals=0,
        ),
        compiler_params=SMALL,
    )(*tokens)


def pair_kernel(keep_ref, got_ref, _, *slots):
    for s, slot in enumerate(slots):
        part = slot_rows(s, len(slots), slot.shape[1])
        for which in range(2):
            both = keep_ref[which, part].astype(F32) + got_ref[which, part].astype(F32)
            slot[which] = both.astype(BF16)


def pair_slots(keep, got, count, after):
    slot = jax.ShapeDtypeStruct((2, keep.shape[1] // count, HEAD), BF16)
    return pl.pallas_call(
        pair_kernel,
        name="pair",
        in_specs=[VMEM] * 2 + [ANY],
        out_specs=[VMEM] * count,
        out_shape=[slot] * count,
        compiler_params=SMALL,
    )(keep, got, after)


def totals_kernel(far_count, *refs):
    slots, sends = refs[:far_count], refs[far_count:]
    outer = lax.axis_index("outer")
    totals = []
    for which in range(2):
        total = slots[0][which].astype(F32)
        for slot in slots[1:]:
            total += slot[which].astype(F32)
        totals.append(total.astype(BF16))
    for s, send in zip(distances(len(sends) + 1), sends):
        upward = (outer ^ s) > outer
        send[...] = jnp.where(upward, totals[0], totals[1])


def group_sends(slots, outer_count):
    send = jax.ShapeDtypeStruct(slots[0].shape[1:], BF16)
    return pl.pallas_call(
        functools.partial(totals_kernel, len(slots)),
        name="totals",
        in_specs=[VMEM] * len(slots),
        out_specs=[VMEM] * (outer_count - 1),
        out_shape=[send] * (outer_count - 1),
        compiler_params=SMALL,
    )(*slots)


def scan_kernel(far_count, *refs):
    slots, others, refs = refs[:far_count], refs[far_count : -far_count - 2], refs[-far_count - 2 :]
    outs, (held, scanned) = refs[:far_count], refs[far_count:]
    outer = lax.axis_index("outer")
    _, far = near_far()
    for s, slot in enumerate(slots):
        held[far ^ s] = slot[...]
    for which in range(2):
        total = jnp.zeros(held.shape[2:], F32)
        for s, other in zip(distances(len(others) + 1), others):
            below = (outer ^ s) < outer
            wanted = below if which == 0 else jnp.logical_not(below)
            total += jnp.where(wanted, other[...].astype(F32), 0.0)
        for i in reversed(range(far_count)) if which else range(far_count):
            scanned[i, which] = total.astype(BF16)
            total += held[i, which].astype(F32)
    for s, out in enumerate(outs):
        out[...] = scanned[far ^ s]


def scan_slots(slots, others):
    far_count, slot = len(slots), jax.ShapeDtypeStruct(slots[0].shape, BF16)
    return pl.pallas_call(
        functools.partial(scan_kernel, far_count),
        name="scan",
        in_specs=[VMEM] * (far_count + len(others)),
        out_specs=[VMEM] * far_count,
        out_shape=[slot] * far_count,
        scratch_shapes=[pltpu.VMEM((far_count, *slot.shape), BF16)] * 2,
        compiler_params=SMALL,
    )(*slots, *others)


def with_sums(slot, which, extra, part):
    return (slot[which].astype(F32) + extra[which, part].astype(F32)).astype(BF16)


def by_core(run):
    near, _ = near_far()
    for core in range(2):
        pl.when(near == core)(functools.partial(run, core))


def theirs_kernel(*refs):
    slots, (keep, out) = refs[:-2], refs[-2:]

    def run(core):
        for s, slot in enumerate(slots):
            part = slot_rows(s, len(slots), slot.shape[1])
            out[core, part] = with_sums(slot, core, keep, part)
            out[1 - core, part] = slot[1 - core]

    by_core(run)


def states_for_neighbour(slots, keep):
    return pl.pallas_call(
        theirs_kernel,
        name="theirs",
        in_specs=[VMEM] * (len(slots) + 1),
        out_specs=VMEM,
        out_shape=jax.ShapeDtypeStruct(keep.shape, BF16),
        compiler_params=SMALL,
    )(*slots, keep)


def local_kernel(core, *refs):
    near, _ = near_far()
    pl.when(near == core)(functools.partial(local_products, refs[:4], refs[-4:]))


def local_products(tokens, outs):
    rows, width = tokens[0].shape
    at = lax.broadcasted_iota(jnp.int32, (rows, rows), 0)
    to = lax.broadcasted_iota(jnp.int32, (rows, rows), 1)
    lower = at >= to

    def masked(a, b):
        return jnp.where(lower, dot(a, b, 1, 1), 0.0).astype(BF16)

    def second(cols, a, b):
        q, k, v, d = (ref[:, cols] for ref in tokens)
        att, gq, gk, gv = outs
        att[:, cols] = dot(a, v, 1, 0)
        gq[:, cols] = dot(b, k, 1, 0)
        gk[:, cols] = dot(b, q, 0, 0)
        gv[:, cols] = dot(a, d, 0, 0)

    last = None
    for h in range(width // HEAD):
        cols = slice(h * HEAD, (h + 1) * HEAD)
        q, k, v, d = (ref[:, cols] for ref in tokens)
        a, b = masked(q, k), masked(d, v)
        if last:
            second(*last)
        last = (cols, a, b)
    second(*last)


def local_part(core, tokens, after):
    rows, width = tokens[0].shape
    return pl.pallas_call(
        functools.partial(local_kernel, core),
        name="local",
        in_specs=[VMEM] * 4 + [ANY],
        out_specs=[VMEM] * 4,
        out_shape=[jax.ShapeDtypeStruct((rows, width), F32)] * 4,
        cost_estimate=pl.CostEstimate(flops=0, bytes_accessed=0, transcendentals=0),
        compiler_params=SMALL,
    )(*tokens, after)


def all_products(scale, start, tokens, local, states, store):
    q, k, v, d = tokens

    def products():
        for n in range(states.shape[1] // HEAD):
            rows = slice(n * HEAD, (n + 1) * HEAD)
            cols = slice(start + n * HEAD, start + (n + 1) * HEAD)
            s, g = states[0, rows], states[1, rows]
            yield (rows, 0, cols), dot(q[:, cols], s, 1, 0)
            yield (rows, 1, cols), dot(d[:, cols], s, 1, 1)
            yield (rows, 2, cols), dot(v[:, cols], g, 1, 1)
            yield (rows, 3, cols), dot(k[:, cols], g, 1, 0)

    def use(key, product):
        rows, i, cols = key
        store(rows, i, (scale * (product + local[i][:, cols])).astype(BF16))

    one_ahead(products(), use)


def copies_out(own, block, held, outs, sems, piece):
    first, size = (0, held.shape[2]) if piece is None else (piece * held.shape[2] // 2, held.shape[2] // 2)
    start = block_start(own, block, outs[0].shape[1] // 2) + first
    there = pl.ds(pl.multiple_of(start, size), size)
    return [
        pltpu.make_async_copy(held.at[i, :, pl.ds(first, size)], out.at[:, there], sems.at[i])
        for i, out in enumerate(outs)
    ]


def finish_kernel(scale, own, block, count, rests, hold, *refs):
    tokens, locals_, slots, refs = refs[:4], refs[4:12], refs[12 : 12 + count], refs[12 + count :]
    got, refs = (refs[0], refs[1:]) if own else (None, refs)
    late, refs = refs[: len(rests)], refs[len(rests) :]
    if own:
        refs, states = refs[:-1], refs[-1]
    else:
        states = slots[0]
    if not hold or rests:
        *refs, sems = refs
    *refs, held = refs
    outs = refs[-4:]
    width = tokens[0].shape[1]
    copies = []
    for n, (rest, where) in enumerate(zip(late, rests)):
        copies += copies_out(*where, rest, outs, sems.at[n + 2], None)
    for copy in copies:
        copy.start()

    def store(rows, i, out):
        held[i, :, rows] = out
        for piece in range(2):
            if not hold and i == 3 and rows.stop == (piece + 1) * states.shape[1] // 2:
                for copy in copies_out(own, block, held, outs, sems.at[piece], piece):
                    copy.start()

    def run(quarter):
        core = quarter // 2 if own else 1 - quarter // 2
        local = locals_[4 * core : 4 * core + 4]
        for s, slot in enumerate(slots if own else ()):
            part = slot_rows(s, count, slot.shape[1])
            states[core, part] = slot[core]
            states[1 - core, part] = with_sums(slot, 1 - core, got, part)
        all_products(scale, quarter * width // 4, tokens, local, states, store)

    start = block_start(own, block, width // 2)
    for quarter in range(4):
        pl.when(start == quarter * width // 4)(functools.partial(run, quarter))
    if not hold:
        for piece in range(2):
            copies += copies_out(own, block, held, outs, sems.at[piece], piece)
    for copy in copies:
        copy.wait()


def finish(own, block, tokens, local, slots, scale, got=(), rests=(), before=(), hold=False):
    rows, width = tokens[0].shape
    out = jax.ShapeDtypeStruct((rows, width), BF16)
    piece = pltpu.VMEM((4, rows, width // 4), BF16)
    inputs = [*tokens, *local, *slots, *got, *(x for _, x in rests)]
    states = pltpu.VMEM((2, width // 4, HEAD), BF16)
    wheres = [where for where, _ in rests]
    writes = not hold or bool(rests)
    return pl.pallas_call(
        functools.partial(finish_kernel, scale, own, block, len(slots), wheres, hold),
        name="finish",
        in_specs=[VMEM] * len(inputs) + [ANY] * len(before),
        out_specs=[ANY] * 4 * writes + [VMEM] * hold,
        out_shape=[out] * 4 * writes + [piece] * hold,
        scratch_shapes=[piece] * (not hold)
        + [pltpu.SemaphoreType.DMA((2 + len(rests), 4))] * writes
        + [states] * own,
        input_output_aliases={len(inputs) + i: i for i in range(len(before))},
        cost_estimate=pl.CostEstimate(
            flops=2 * rows * width * HEAD, bytes_accessed=8 * rows * width, transcendentals=0
        ),
        compiler_params=SMALL,
    )(*inputs, *before)


def swap(x, axis, bits):
    return lax.ppermute(x, axis, [(i, i ^ bits) for i in range(lax.axis_size(axis))])


def swap_far(slots):
    return [slots[0]] + [swap(slots[s], "inner", 2 * s) for s in range(1, len(slots))]


def body(queries, keys, values, cotangent):
    far_count = lax.axis_size("inner") // 2
    outer_count = lax.axis_size("outer")
    scale = float(HEAD * queries.shape[0] * 2 * far_count * outer_count) ** (-0.5)
    tokens, give = load((queries, keys, values, cotangent))
    got = [swap(give, "inner", 1), swap(*sums(tokens, (False, 1)), "inner", 1)]
    keep = sums(tokens, (True, 0), (True, 1))
    early = local_part(0, tokens, keep[1])
    slots = []
    for b in range(2):
        slots += pair_slots(keep[b], got[b], far_count // 2, slots[0] if slots else early[0])
    slots, late = lax.optimization_barrier((swap_far(slots), local_part(1, tokens, slots[-1])))
    local = [*early, *late]
    sends = group_sends(slots, outer_count)
    others = [swap(send, "outer", s) for s, send in zip(distances(outer_count), sends)]
    slots = swap_far(scan_slots(slots, others))
    half = far_count // 2

    def near_swap(block, part):
        return swap(states_for_neighbour(part, keep[block]), "inner", 1)

    arrived = [near_swap(0, slots[:half])]
    outs = finish(True, 0, tokens, local, slots[:half], scale, got=got[:1])
    part, outs = lax.optimization_barrier((slots[half:], tuple(outs)))
    arrived.append(near_swap(1, part))
    (rest,) = finish(True, 1, tokens, local, part, scale, got=got[1:], hold=True)
    rests = [((True, 1), rest)]
    *outs, rest = finish(
        False, 0, tokens, local, arrived[:1], scale, rests=rests, before=outs, hold=True
    )
    rests = [((False, 0), rest)]
    return tuple(finish(False, 1, tokens, local, arrived[1:], scale, rests=rests, before=outs))


def solution(mesh):
    spec = P(("outer", "inner"), None)
    return jax.shard_map(
        body, mesh=mesh, in_specs=(spec,) * 4, out_specs=(spec,) * 4, check_vma=False
    )
```

```python
import functools

import jax
import jax.numpy as jnp
from jax import lax
from jax.experimental import pallas as pl
from jax.experimental.pallas import tpu as pltpu
from jax.sharding import PartitionSpec as P

HEAD = 128
MIB = 1024 * 1024
ANY = pl.BlockSpec(memory_space=pl.ANY)
VMEM = pl.BlockSpec(memory_space=pltpu.VMEM)
BF16 = jnp.bfloat16
F32 = jnp.float32
SMALL = pltpu.CompilerParams(vmem_limit_bytes=4 * MIB)


def dot(a, b, over_a, over_b):
    return lax.dot_general(
        a, b, (((over_a,), (over_b,)), ((), ())), preferred_element_type=F32
    )


def near_far():
    inner = lax.axis_index("inner")
    return lax.rem(inner, 2), lax.div(inner, 2)


def distances(outer_count):
    return range(outer_count - 1, 0, -1)


def block_start(own, block, half):
    near, far = near_far()
    side = near if own else 1 - near
    top = lax.div(far, lax.axis_size("inner") // 4)
    return side * half + (1 - top if block else top) * (half // 2)


def columns(start, n):
    return pl.ds(pl.multiple_of(start + n * HEAD, HEAD), HEAD)


def slot_rows(s, count, depth):
    _, far = near_far()
    return pl.ds(pl.multiple_of(lax.rem(far ^ s, count) * depth, depth), depth)


def one_ahead(products, use):
    last = None
    for key, product in products:
        if last:
            use(*last)
        last = key, product
    use(*last)


def sums_of(tokens, start, out, kinds=(0, 1)):
    q, k, v, d = tokens

    def products():
        for n in range(out.shape[1] // HEAD):
            cols = pl.ds(start + n * HEAD, HEAD) if isinstance(start, int) else columns(start, n)
            for which in kinds:
                a, b = ((k, v), (q, d))[which]
                yield (which, n), dot(a[:, cols], b[:, cols], 0, 0)

    def use(key, product):
        which, n = key
        out[which, n * HEAD : (n + 1) * HEAD] = product.astype(BF16)

    one_ahead(products(), use)


def load_kernel(*refs):
    tokens, held, (out, sems) = refs[:4], refs[4:8], refs[8:]
    copies = [pltpu.make_async_copy(tokens[i], held[i], sems.at[i]) for i in range(4)]
    width = held[0].shape[1]
    start = block_start(False, 0, width // 2)
    pairs = ((1, 2), (0, 3))
    for i in pairs[0] + pairs[1]:
        copies[i].start()
    for kind, pair in enumerate(pairs):
        for i in pair:
            copies[i].wait()
        for n in range(4):
            at = n * width // 4
            pl.when(start == at)(functools.partial(sums_of, held, at, out, (kind,)))


def load(tokens):
    rows, width = tokens[0].shape
    *held, sums = pl.pallas_call(
        load_kernel,
        name="load",
        in_specs=[ANY] * 4,
        out_specs=[VMEM] * 5,
        out_shape=[pltpu.VMEM((rows, width), BF16)] * 4 + [pltpu.VMEM((2, width // 4, HEAD), BF16)],
        scratch_shapes=[pltpu.SemaphoreType.DMA((4,))],
        cost_estimate=pl.CostEstimate(
            flops=rows * width * HEAD, bytes_accessed=10 * rows * width, transcendentals=0
        ),
        compiler_params=SMALL,
    )(*(pltpu.with_memory_space_constraint(x, pltpu.HBM) for x in tokens))
    return tuple(held), sums


def sums_kernel(wanted, *refs):
    for (own, block), out in zip(wanted, refs[4:]):
        sums_of(refs[:4], block_start(own, block, refs[0].shape[1] // 2), out)


def sums(tokens, *wanted):
    rows, width = tokens[0].shape
    return pl.pallas_call(
        functools.partial(sums_kernel, wanted),
        name="sums",
        in_specs=[VMEM] * 4,
        out_specs=[VMEM] * len(wanted),
        out_shape=[jax.ShapeDtypeStruct((2, width // 4, HEAD), BF16)] * len(wanted),
        cost_estimate=pl.CostEstimate(
            flops=rows * width * HEAD * len(wanted),
            bytes_accessed=3 * rows * width * len(wanted),
            transcendentals=0,
        ),
        compiler_params=SMALL,
    )(*tokens)


def pair_kernel(keep_ref, got_ref, _, *slots):
    for s, slot in enumerate(slots):
        part = slot_rows(s, len(slots), slot.shape[1])
        for which in range(2):
            both = keep_ref[which, part].astype(F32) + got_ref[which, part].astype(F32)
            slot[which] = both.astype(BF16)


def pair_slots(keep, got, count, after):
    slot = jax.ShapeDtypeStruct((2, keep.shape[1] // count, HEAD), BF16)
    return pl.pallas_call(
        pair_kernel,
        name="pair",
        in_specs=[VMEM] * 2 + [ANY],
        out_specs=[VMEM] * count,
        out_shape=[slot] * count,
        compiler_params=SMALL,
    )(keep, got, after)


def totals_kernel(far_count, *refs):
    slots, sends = refs[:far_count], refs[far_count:]
    outer = lax.axis_index("outer")
    totals = []
    for which in range(2):
        total = slots[0][which].astype(F32)
        for slot in slots[1:]:
            total += slot[which].astype(F32)
        totals.append(total.astype(BF16))
    for s, send in zip(distances(len(sends) + 1), sends):
        upward = (outer ^ s) > outer
        send[...] = jnp.where(upward, totals[0], totals[1])


def group_sends(slots, outer_count):
    send = jax.ShapeDtypeStruct(slots[0].shape[1:], BF16)
    return pl.pallas_call(
        functools.partial(totals_kernel, len(slots)),
        name="totals",
        in_specs=[VMEM] * len(slots),
        out_specs=[VMEM] * (outer_count - 1),
        out_shape=[send] * (outer_count - 1),
        compiler_params=SMALL,
    )(*slots)


def scan_kernel(far_count, *refs):
    slots, others, refs = refs[:far_count], refs[far_count : -far_count - 2], refs[-far_count - 2 :]
    outs, (held, scanned) = refs[:far_count], refs[far_count:]
    outer = lax.axis_index("outer")
    _, far = near_far()
    for s, slot in enumerate(slots):
        held[far ^ s] = slot[...]
    for which in range(2):
        total = jnp.zeros(held.shape[2:], F32)
        for s, other in zip(distances(len(others) + 1), others):
            below = (outer ^ s) < outer
            wanted = below if which == 0 else jnp.logical_not(below)
            total += jnp.where(wanted, other[...].astype(F32), 0.0)
        for i in reversed(range(far_count)) if which else range(far_count):
            scanned[i, which] = total.astype(BF16)
            total += held[i, which].astype(F32)
    for s, out in enumerate(outs):
        out[...] = scanned[far ^ s]


def scan_slots(slots, others):
    far_count, slot = len(slots), jax.ShapeDtypeStruct(slots[0].shape, BF16)
    return pl.pallas_call(
        functools.partial(scan_kernel, far_count),
        name="scan",
        in_specs=[VMEM] * (far_count + len(others)),
        out_specs=[VMEM] * far_count,
        out_shape=[slot] * far_count,
        scratch_shapes=[pltpu.VMEM((far_count, *slot.shape), BF16)] * 2,
        compiler_params=SMALL,
    )(*slots, *others)


def with_sums(slot, which, extra, part):
    return (slot[which].astype(F32) + extra[which, part].astype(F32)).astype(BF16)


def by_core(run):
    near, _ = near_far()
    for core in range(2):
        pl.when(near == core)(functools.partial(run, core))


def theirs_kernel(*refs):
    slots, (keep, out) = refs[:-2], refs[-2:]

    def run(core):
        for s, slot in enumerate(slots):
            part = slot_rows(s, len(slots), slot.shape[1])
            out[core, part] = with_sums(slot, core, keep, part)
            out[1 - core, part] = slot[1 - core]

    by_core(run)


def states_for_neighbour(slots, keep):
    return pl.pallas_call(
        theirs_kernel,
        name="theirs",
        in_specs=[VMEM] * (len(slots) + 1),
        out_specs=VMEM,
        out_shape=jax.ShapeDtypeStruct(keep.shape, BF16),
        compiler_params=SMALL,
    )(*slots, keep)


def local_kernel(core, *refs):
    near, _ = near_far()
    pl.when(near == core)(functools.partial(local_products, refs[:4], refs[-4:]))


def local_products(tokens, outs):
    rows, width = tokens[0].shape
    at = lax.broadcasted_iota(jnp.int32, (rows, rows), 0)
    to = lax.broadcasted_iota(jnp.int32, (rows, rows), 1)
    lower = at >= to

    def masked(a, b):
        return jnp.where(lower, dot(a, b, 1, 1), 0.0).astype(BF16)

    def second(cols, a, b):
        q, k, v, d = (ref[:, cols] for ref in tokens)
        att, gq, gk, gv = outs
        att[:, cols] = dot(a, v, 1, 0)
        gq[:, cols] = dot(b, k, 1, 0)
        gk[:, cols] = dot(b, q, 0, 0)
        gv[:, cols] = dot(a, d, 0, 0)

    last = None
    for h in range(width // HEAD):
        cols = slice(h * HEAD, (h + 1) * HEAD)
        q, k, v, d = (ref[:, cols] for ref in tokens)
        a, b = masked(q, k), masked(d, v)
        if last:
            second(*last)
        last = (cols, a, b)
    second(*last)


def local_part(core, tokens, after):
    rows, width = tokens[0].shape
    return pl.pallas_call(
        functools.partial(local_kernel, core),
        name="local",
        in_specs=[VMEM] * 4 + [ANY],
        out_specs=[VMEM] * 4,
        out_shape=[jax.ShapeDtypeStruct((rows, width), F32)] * 4,
        cost_estimate=pl.CostEstimate(flops=0, bytes_accessed=0, transcendentals=0),
        compiler_params=SMALL,
    )(*tokens, after)


def all_products(scale, start, tokens, local, states, store):
    q, k, v, d = tokens

    def products():
        for n in range(states.shape[1] // HEAD):
            rows = slice(n * HEAD, (n + 1) * HEAD)
            cols = slice(start + n * HEAD, start + (n + 1) * HEAD)
            s, g = states[0, rows], states[1, rows]
            yield (rows, 0, cols), dot(q[:, cols], s, 1, 0)
            yield (rows, 1, cols), dot(d[:, cols], s, 1, 1)
            yield (rows, 2, cols), dot(v[:, cols], g, 1, 1)
            yield (rows, 3, cols), dot(k[:, cols], g, 1, 0)

    def use(key, product):
        rows, i, cols = key
        store(rows, i, (scale * (product + local[i][:, cols])).astype(BF16))

    one_ahead(products(), use)


def copies_out(own, block, held, outs, sems, piece):
    first, size = (0, held.shape[2]) if piece is None else (piece * held.shape[2] // 2, held.shape[2] // 2)
    start = block_start(own, block, outs[0].shape[1] // 2) + first
    there = pl.ds(pl.multiple_of(start, size), size)
    return [
        pltpu.make_async_copy(held.at[i, :, pl.ds(first, size)], out.at[:, there], sems.at[i])
        for i, out in enumerate(outs)
    ]


def finish_kernel(scale, own, block, count, rests, hold, *refs):
    tokens, locals_, slots, refs = refs[:4], refs[4:12], refs[12 : 12 + count], refs[12 + count :]
    got, refs = (refs[0], refs[1:]) if own else (None, refs)
    late, refs = refs[: len(rests)], refs[len(rests) :]
    if own:
        refs, states = refs[:-1], refs[-1]
    else:
        states = slots[0]
    if not hold or rests:
        *refs, sems = refs
    *refs, held = refs
    outs = refs[-4:]
    width = tokens[0].shape[1]
    copies = []
    for n, (rest, where) in enumerate(zip(late, rests)):
        copies += copies_out(*where, rest, outs, sems.at[n + 2], None)
    for copy in copies:
        copy.start()

    def store(rows, i, out):
        held[i, :, rows] = out
        for piece in range(2):
            if not hold and i == 3 and rows.stop == (piece + 1) * states.shape[1] // 2:
                for copy in copies_out(own, block, held, outs, sems.at[piece], piece):
                    copy.start()

    def run(quarter):
        core = quarter // 2 if own else 1 - quarter // 2
        local = locals_[4 * core : 4 * core + 4]
        for s, slot in enumerate(slots if own else ()):
            part = slot_rows(s, count, slot.shape[1])
            states[core, part] = slot[core]
            states[1 - core, part] = with_sums(slot, 1 - core, got, part)
        all_products(scale, quarter * width // 4, tokens, local, states, store)

    start = block_start(own, block, width // 2)
    for quarter in range(4):
        pl.when(start == quarter * width // 4)(functools.partial(run, quarter))
    if not hold:
        for piece in range(2):
            copies += copies_out(own, block, held, outs, sems.at[piece], piece)
    for copy in copies:
        copy.wait()


def finish(own, block, tokens, local, slots, scale, got=(), rests=(), before=(), hold=False):
    rows, width = tokens[0].shape
    out = jax.ShapeDtypeStruct((rows, width), BF16)
    piece = pltpu.VMEM((4, rows, width // 4), BF16)
    inputs = [*tokens, *local, *slots, *got, *(x for _, x in rests)]
    states = pltpu.VMEM((2, width // 4, HEAD), BF16)
    wheres = [where for where, _ in rests]
    writes = not hold or bool(rests)
    return pl.pallas_call(
        functools.partial(finish_kernel, scale, own, block, len(slots), wheres, hold),
        name="finish",
        in_specs=[VMEM] * len(inputs) + [ANY] * len(before),
        out_specs=[ANY] * 4 * writes + [VMEM] * hold,
        out_shape=[out] * 4 * writes + [piece] * hold,
        scratch_shapes=[piece] * (not hold)
        + [pltpu.SemaphoreType.DMA((2 + len(rests), 4))] * writes
        + [states] * own,
        input_output_aliases={len(inputs) + i: i for i in range(len(before))},
        cost_estimate=pl.CostEstimate(
            flops=2 * rows * width * HEAD, bytes_accessed=8 * rows * width, transcendentals=0
        ),
        compiler_params=SMALL,
    )(*inputs, *before)


def swap(x, axis, bits):
    return lax.ppermute(x, axis, [(i, i ^ bits) for i in range(lax.axis_size(axis))])


def swap_far(slots):
    return [slots[0]] + [swap(slots[s], "inner", 2 * s) for s in range(1, len(slots))]


def body(queries, keys, values, cotangent):
    far_count = lax.axis_size("inner") // 2
    outer_count = lax.axis_size("outer")
    scale = float(HEAD * queries.shape[0] * 2 * far_count * outer_count) ** (-0.5)
    tokens, give = load((queries, keys, values, cotangent))
    got = [swap(give, "inner", 1), swap(*sums(tokens, (False, 1)), "inner", 1)]
    keep = sums(tokens, (True, 0), (True, 1))
    early = local_part(1, tokens, keep[1])
    slots = []
    for b in range(2):
        slots += pair_slots(keep[b], got[b], far_count // 2, slots[0] if slots else early[0])
    slots, late = lax.optimization_barrier((swap_far(slots), local_part(0, tokens, slots[-1])))
    local = [*late, *early]
    sends = group_sends(slots, outer_count)
    others = [swap(send, "outer", s) for s, send in zip(distances(outer_count), sends)]
    slots = swap_far(scan_slots(slots, others))
    half = far_count // 2

    def near_swap(block, part):
        return swap(states_for_neighbour(part, keep[block]), "inner", 1)

    arrived = [near_swap(0, slots[:half])]
    outs = finish(True, 0, tokens, local, slots[:half], scale, got=got[:1])
    part, outs = lax.optimization_barrier((slots[half:], tuple(outs)))
    arrived.append(near_swap(1, part))
    (rest,) = finish(True, 1, tokens, local, part, scale, got=got[1:], hold=True)
    rests = [((True, 1), rest)]
    *outs, rest = finish(
        False, 0, tokens, local, arrived[:1], scale, rests=rests, before=outs, hold=True
    )
    rests = [((False, 0), rest)]
    return tuple(finish(False, 1, tokens, local, arrived[1:], scale, rests=rests, before=outs))


def solution(mesh):
    spec = P(("outer", "inner"), None)
    return jax.shard_map(
        body, mesh=mesh, in_specs=(spec,) * 4, out_specs=(spec,) * 4, check_vma=False
    )
```

```python
import functools

import jax
import jax.numpy as jnp
from jax import lax
from jax.experimental import pallas as pl
from jax.experimental.pallas import tpu as pltpu
from jax.sharding import PartitionSpec as P

HEAD = 128
MIB = 1024 * 1024
ANY = pl.BlockSpec(memory_space=pl.ANY)
VMEM = pl.BlockSpec(memory_space=pltpu.VMEM)
BF16 = jnp.bfloat16
F32 = jnp.float32
SMALL = pltpu.CompilerParams(vmem_limit_bytes=4 * MIB)


def dot(a, b, over_a, over_b):
    return lax.dot_general(
        a, b, (((over_a,), (over_b,)), ((), ())), preferred_element_type=F32
    )


def near_far():
    inner = lax.axis_index("inner")
    return lax.rem(inner, 2), lax.div(inner, 2)


def distances(outer_count):
    return range(outer_count - 1, 0, -1)


def block_start(own, block, half):
    near, far = near_far()
    side = near if own else 1 - near
    top = lax.div(far, lax.axis_size("inner") // 4)
    return side * half + (1 - top if block else top) * (half // 2)


def slot_order(count):
    return [n ^ (n >> 1) for n in range(count)]


def block_slots(block, count):
    return slot_order(2 * count)[block * count : (block + 1) * count]


def columns(start, n):
    return pl.ds(pl.multiple_of(start + n * HEAD, HEAD), HEAD)


def slot_rows(s, count, depth):
    _, far = near_far()
    return pl.ds(pl.multiple_of(lax.rem(far ^ s, count) * depth, depth), depth)


def one_ahead(products, use):
    last = None
    for key, product in products:
        if last:
            use(*last)
        last = key, product
    use(*last)


def sums_of(tokens, start, out, kinds=(0, 1)):
    q, k, v, d = tokens

    def products():
        for n in range(out.shape[1] // HEAD):
            cols = pl.ds(start + n * HEAD, HEAD) if isinstance(start, int) else columns(start, n)
            for which in kinds:
                a, b = ((k, v), (q, d))[which]
                yield (which, n), dot(a[:, cols], b[:, cols], 0, 0)

    def use(key, product):
        which, n = key
        out[which, n * HEAD : (n + 1) * HEAD] = product.astype(BF16)

    one_ahead(products(), use)


def load_kernel(*refs):
    tokens, held, (out, sems) = refs[:4], refs[4:8], refs[8:]
    copies = [pltpu.make_async_copy(tokens[i], held[i], sems.at[i]) for i in range(4)]
    width = held[0].shape[1]
    start = block_start(False, 0, width // 2)
    pairs = ((1, 2), (0, 3))
    for i in pairs[0] + pairs[1]:
        copies[i].start()
    for kind, pair in enumerate(pairs):
        for i in pair:
            copies[i].wait()
        for n in range(4):
            at = n * width // 4
            pl.when(start == at)(functools.partial(sums_of, held, at, out, (kind,)))


def load(tokens):
    rows, width = tokens[0].shape
    *held, sums = pl.pallas_call(
        load_kernel,
        name="load",
        in_specs=[ANY] * 4,
        out_specs=[VMEM] * 5,
        out_shape=[pltpu.VMEM((rows, width), BF16)] * 4 + [pltpu.VMEM((2, width // 4, HEAD), BF16)],
        scratch_shapes=[pltpu.SemaphoreType.DMA((4,))],
        cost_estimate=pl.CostEstimate(
            flops=rows * width * HEAD, bytes_accessed=10 * rows * width, transcendentals=0
        ),
        compiler_params=SMALL,
    )(*(pltpu.with_memory_space_constraint(x, pltpu.HBM) for x in tokens))
    return tuple(held), sums


def sums_kernel(wanted, *refs):
    for (own, block), out in zip(wanted, refs[4:]):
        sums_of(refs[:4], block_start(own, block, refs[0].shape[1] // 2), out)


def sums(tokens, *wanted):
    rows, width = tokens[0].shape
    return pl.pallas_call(
        functools.partial(sums_kernel, wanted),
        name="sums",
        in_specs=[VMEM] * 4,
        out_specs=[VMEM] * len(wanted),
        out_shape=[jax.ShapeDtypeStruct((2, width // 4, HEAD), BF16)] * len(wanted),
        cost_estimate=pl.CostEstimate(
            flops=rows * width * HEAD * len(wanted),
            bytes_accessed=3 * rows * width * len(wanted),
            transcendentals=0,
        ),
        compiler_params=SMALL,
    )(*tokens)


def pair_kernel(block, keep_ref, got_ref, *slots):
    for s, slot in zip(block_slots(block, len(slots)), slots):
        part = slot_rows(s, len(slots), slot.shape[1])
        for which in range(2):
            both = keep_ref[which, part].astype(F32) + got_ref[which, part].astype(F32)
            slot[which] = both.astype(BF16)


def pair_slots(block, keep, got, count):
    slot = jax.ShapeDtypeStruct((2, keep.shape[1] // count, HEAD), BF16)
    return pl.pallas_call(
        functools.partial(pair_kernel, block),
        name="pair",
        in_specs=[VMEM] * 2,
        out_specs=[VMEM] * count,
        out_shape=[slot] * count,
        compiler_params=SMALL,
    )(keep, got)


def totals_kernel(far_count, *refs):
    slots, sends = refs[:far_count], refs[far_count:]
    outer = lax.axis_index("outer")
    totals = []
    for which in range(2):
        total = slots[0][which].astype(F32)
        for slot in slots[1:]:
            total += slot[which].astype(F32)
        totals.append(total.astype(BF16))
    for s, send in zip(distances(len(sends) + 1), sends):
        upward = (outer ^ s) > outer
        send[...] = jnp.where(upward, totals[0], totals[1])


def group_sends(slots, outer_count):
    send = jax.ShapeDtypeStruct(slots[0].shape[1:], BF16)
    return pl.pallas_call(
        functools.partial(totals_kernel, len(slots)),
        name="totals",
        in_specs=[VMEM] * len(slots),
        out_specs=[VMEM] * (outer_count - 1),
        out_shape=[send] * (outer_count - 1),
        compiler_params=SMALL,
    )(*slots)


def scan_kernel(far_count, *refs):
    slots, others, refs = refs[:far_count], refs[far_count : -far_count - 2], refs[-far_count - 2 :]
    outs, (held, scanned) = refs[:far_count], refs[far_count:]
    outer = lax.axis_index("outer")
    _, far = near_far()
    for s, slot in zip(slot_order(far_count), slots):
        held[far ^ s] = slot[...]
    for which in range(2):
        total = jnp.zeros(held.shape[2:], F32)
        for s, other in zip(distances(len(others) + 1), others):
            below = (outer ^ s) < outer
            wanted = below if which == 0 else jnp.logical_not(below)
            total += jnp.where(wanted, other[...].astype(F32), 0.0)
        for i in reversed(range(far_count)) if which else range(far_count):
            scanned[i, which] = total.astype(BF16)
            total += held[i, which].astype(F32)
    for s, out in zip(slot_order(far_count), outs):
        out[...] = scanned[far ^ s]


def scan_slots(slots, others):
    far_count, slot = len(slots), jax.ShapeDtypeStruct(slots[0].shape, BF16)
    return pl.pallas_call(
        functools.partial(scan_kernel, far_count),
        name="scan",
        in_specs=[VMEM] * (far_count + len(others)),
        out_specs=[VMEM] * far_count,
        out_shape=[slot] * far_count,
        scratch_shapes=[pltpu.VMEM((far_count, *slot.shape), BF16)] * 2,
        compiler_params=SMALL,
    )(*slots, *others)


def with_sums(slot, which, extra, part):
    return (slot[which].astype(F32) + extra[which, part].astype(F32)).astype(BF16)


def by_core(run):
    near, _ = near_far()
    for core in range(2):
        pl.when(near == core)(functools.partial(run, core))


def theirs_kernel(block, *refs):
    slots, (keep, out) = refs[:-2], refs[-2:]

    def run(core):
        for s, slot in zip(block_slots(block, len(slots)), slots):
            part = slot_rows(s, len(slots), slot.shape[1])
            out[core, part] = with_sums(slot, core, keep, part)
            out[1 - core, part] = slot[1 - core]

    by_core(run)


def states_for_neighbour(block, slots, keep):
    return pl.pallas_call(
        functools.partial(theirs_kernel, block),
        name="theirs",
        in_specs=[VMEM] * (len(slots) + 1),
        out_specs=VMEM,
        out_shape=jax.ShapeDtypeStruct(keep.shape, BF16),
        compiler_params=SMALL,
    )(*slots, keep)


def local_kernel(*refs):
    tokens, outs = refs[:4], refs[4:]
    rows, width = tokens[0].shape
    at = lax.broadcasted_iota(jnp.int32, (rows, rows), 0)
    to = lax.broadcasted_iota(jnp.int32, (rows, rows), 1)
    lower = at >= to

    def masked(a, b):
        return jnp.where(lower, dot(a, b, 1, 1), 0.0).astype(BF16)

    def second(cols, a, b):
        q, k, v, d = (ref[:, cols] for ref in tokens)
        att, gq, gk, gv = outs
        att[:, cols] = dot(a, v, 1, 0)
        gq[:, cols] = dot(b, k, 1, 0)
        gk[:, cols] = dot(b, q, 0, 0)
        gv[:, cols] = dot(a, d, 0, 0)

    last = None
    for h in range(width // HEAD):
        cols = slice(h * HEAD, (h + 1) * HEAD)
        q, k, v, d = (ref[:, cols] for ref in tokens)
        a, b = masked(q, k), masked(d, v)
        if last:
            second(*last)
        last = (cols, a, b)
    second(*last)


def local_part(tokens):
    rows, width = tokens[0].shape
    return pl.pallas_call(
        local_kernel,
        name="local",
        in_specs=[VMEM] * 4,
        out_specs=[VMEM] * 4,
        out_shape=[jax.ShapeDtypeStruct((rows, width), F32)] * 4,
        cost_estimate=pl.CostEstimate(
            flops=12 * rows * width * HEAD, bytes_accessed=24 * rows * width, transcendentals=0
        ),
        compiler_params=SMALL,
    )(*tokens)


def all_products(scale, start, tokens, local, states, store):
    q, k, v, d = tokens

    def products():
        for n in range(states.shape[1] // HEAD):
            rows = slice(n * HEAD, (n + 1) * HEAD)
            cols = slice(start + n * HEAD, start + (n + 1) * HEAD)
            s, g = states[0, rows], states[1, rows]
            yield (rows, 0, cols), dot(q[:, cols], s, 1, 0)
            yield (rows, 1, cols), dot(d[:, cols], s, 1, 1)
            yield (rows, 2, cols), dot(v[:, cols], g, 1, 1)
            yield (rows, 3, cols), dot(k[:, cols], g, 1, 0)

    def use(key, product):
        rows, i, cols = key
        store(rows, i, (scale * (product + local[i][:, cols])).astype(BF16))

    one_ahead(products(), use)


def copies_out(own, block, held, outs, sems, piece):
    first, size = (0, held.shape[2]) if piece is None else (piece * held.shape[2] // 2, held.shape[2] // 2)
    start = block_start(own, block, outs[0].shape[1] // 2) + first
    there = pl.ds(pl.multiple_of(start, size), size)
    return [
        pltpu.make_async_copy(held.at[i, :, pl.ds(first, size)], out.at[:, there], sems.at[i])
        for i, out in enumerate(outs)
    ]


def finish_kernel(scale, own, block, count, rests, hold, *refs):
    tokens, local, slots, refs = refs[:4], refs[4:8], refs[8 : 8 + count], refs[8 + count :]
    got, refs = (refs[0], refs[1:]) if own else (None, refs)
    late, refs = refs[: len(rests)], refs[len(rests) :]
    if own:
        refs, states = refs[:-1], refs[-1]
    else:
        states = slots[0]
    if not hold or rests:
        *refs, sems = refs
    *refs, held = refs
    outs = refs[-4:]
    width = tokens[0].shape[1]
    copies = []
    for n, (rest, where) in enumerate(zip(late, rests)):
        copies += copies_out(*where, rest, outs, sems.at[n + 2], None)
    for copy in copies:
        copy.start()

    def store(rows, i, out):
        held[i, :, rows] = out
        for piece in range(2):
            if not hold and i == 3 and rows.stop == (piece + 1) * states.shape[1] // 2:
                for copy in copies_out(own, block, held, outs, sems.at[piece], piece):
                    copy.start()

    def run(quarter):
        for s, slot in zip(block_slots(block, count), slots if own else ()):
            core, part = quarter // 2, slot_rows(s, count, slot.shape[1])
            states[core, part] = slot[core]
            states[1 - core, part] = with_sums(slot, 1 - core, got, part)
        all_products(scale, quarter * width // 4, tokens, local, states, store)

    start = block_start(own, block, width // 2)
    for quarter in range(4):
        pl.when(start == quarter * width // 4)(functools.partial(run, quarter))
    if not hold:
        for piece in range(2):
            copies += copies_out(own, block, held, outs, sems.at[piece], piece)
    for copy in copies:
        copy.wait()


def finish(own, block, tokens, local, slots, scale, got=(), rests=(), before=(), hold=False):
    rows, width = tokens[0].shape
    out = jax.ShapeDtypeStruct((rows, width), BF16)
    piece = pltpu.VMEM((4, rows, width // 4), BF16)
    inputs = [*tokens, *local, *slots, *got, *(x for _, x in rests)]
    states = pltpu.VMEM((2, width // 4, HEAD), BF16)
    wheres = [where for where, _ in rests]
    writes = not hold or bool(rests)
    return pl.pallas_call(
        functools.partial(finish_kernel, scale, own, block, len(slots), wheres, hold),
        name="finish",
        in_specs=[VMEM] * len(inputs) + [ANY] * len(before),
        out_specs=[ANY] * 4 * writes + [VMEM] * hold,
        out_shape=[out] * 4 * writes + [piece] * hold,
        scratch_shapes=[piece] * (not hold)
        + [pltpu.SemaphoreType.DMA((2 + len(rests), 4))] * writes
        + [states] * own,
        input_output_aliases={len(inputs) + i: i for i in range(len(before))},
        cost_estimate=pl.CostEstimate(
            flops=2 * rows * width * HEAD, bytes_accessed=8 * rows * width, transcendentals=0
        ),
        compiler_params=SMALL,
    )(*inputs, *before)


def swap(x, axis, bits):
    return lax.ppermute(x, axis, [(i, i ^ bits) for i in range(lax.axis_size(axis))])


def swap_far(slots):
    order = slot_order(len(slots))
    return [slots[0]] + [swap(slots[n], "inner", 2 * order[n]) for n in range(1, len(slots))]


def body(queries, keys, values, cotangent):
    far_count = lax.axis_size("inner") // 2
    outer_count = lax.axis_size("outer")
    scale = float(HEAD * queries.shape[0] * 2 * far_count * outer_count) ** (-0.5)
    tokens, give = load((queries, keys, values, cotangent))
    got = [swap(give, "inner", 1), swap(*sums(tokens, (False, 1)), "inner", 1)]
    keep = sums(tokens, (True, 0), (True, 1))
    slots = [slot for b in range(2) for slot in pair_slots(b, keep[b], got[b], far_count // 2)]
    slots, local = lax.optimization_barrier((swap_far(slots), local_part(tokens)))
    sends = group_sends(slots, outer_count)
    others = [swap(send, "outer", s) for s, send in zip(distances(outer_count), sends)]
    slots = swap_far(scan_slots(slots, others))
    half = far_count // 2

    def near_swap(block, part):
        return swap(states_for_neighbour(block, part, keep[block]), "inner", 1)

    arrived = [near_swap(0, slots[:half])]
    outs = finish(True, 0, tokens, local, slots[:half], scale, got=got[:1])
    part, outs = lax.optimization_barrier((slots[half:], tuple(outs)))
    arrived.append(near_swap(1, part))
    (rest,) = finish(True, 1, tokens, local, part, scale, got=got[1:], hold=True)
    rests = [((True, 1), rest)]
    *outs, rest = finish(
        False, 0, tokens, local, arrived[:1], scale, rests=rests, before=outs, hold=True
    )
    rests = [((False, 0), rest)]
    return tuple(finish(False, 1, tokens, local, arrived[1:], scale, rests=rests, before=outs))


def solution(mesh):
    spec = P(("outer", "inner"), None)
    return jax.shard_map(
        body, mesh=mesh, in_specs=(spec,) * 4, out_specs=(spec,) * 4, check_vma=False
    )
```

```python
import functools

import jax
import jax.numpy as jnp
from jax import lax
from jax.experimental import pallas as pl
from jax.experimental.pallas import tpu as pltpu
from jax.sharding import PartitionSpec as P

HEAD = 128
MIB = 1024 * 1024
ANY = pl.BlockSpec(memory_space=pl.ANY)
VMEM = pl.BlockSpec(memory_space=pltpu.VMEM)
BF16 = jnp.bfloat16
F32 = jnp.float32
SMALL = pltpu.CompilerParams(vmem_limit_bytes=4 * MIB)


def dot(a, b, over_a, over_b):
    return lax.dot_general(
        a, b, (((over_a,), (over_b,)), ((), ())), preferred_element_type=F32
    )


def near_far():
    inner = lax.axis_index("inner")
    return lax.rem(inner, 2), lax.div(inner, 2)


def distances(outer_count):
    return [outer_count - 1, *range(1, outer_count - 1)]


def block_start(own, block, half):
    near, far = near_far()
    side = near if own else 1 - near
    top = lax.div(far, lax.axis_size("inner") // 4)
    return side * half + (1 - top if block else top) * (half // 2)


def columns(start, n):
    return pl.ds(pl.multiple_of(start + n * HEAD, HEAD), HEAD)


def slot_rows(s, count, depth):
    _, far = near_far()
    return pl.ds(pl.multiple_of(lax.rem(far ^ s, count) * depth, depth), depth)


def one_ahead(products, use):
    last = None
    for key, product in products:
        if last:
            use(*last)
        last = key, product
    use(*last)


def sums_of(tokens, start, out, kinds=(0, 1)):
    q, k, v, d = tokens

    def products():
        for n in range(out.shape[1] // HEAD):
            cols = pl.ds(start + n * HEAD, HEAD) if isinstance(start, int) else columns(start, n)
            for which in kinds:
                a, b = ((k, v), (q, d))[which]
                yield (which, n), dot(a[:, cols], b[:, cols], 0, 0)

    def use(key, product):
        which, n = key
        out[which, n * HEAD : (n + 1) * HEAD] = product.astype(BF16)

    one_ahead(products(), use)


def load_kernel(*refs):
    tokens, held, (out, sems) = refs[:4], refs[4:8], refs[8:]
    copies = [pltpu.make_async_copy(tokens[i], held[i], sems.at[i]) for i in range(4)]
    width = held[0].shape[1]
    start = block_start(False, 0, width // 2)
    pairs = ((1, 2), (0, 3))
    for i in pairs[0] + pairs[1]:
        copies[i].start()
    for kind, pair in enumerate(pairs):
        for i in pair:
            copies[i].wait()
        for n in range(4):
            at = n * width // 4
            pl.when(start == at)(functools.partial(sums_of, held, at, out, (kind,)))


def load(tokens):
    rows, width = tokens[0].shape
    *held, sums = pl.pallas_call(
        load_kernel,
        name="load",
        in_specs=[ANY] * 4,
        out_specs=[VMEM] * 5,
        out_shape=[pltpu.VMEM((rows, width), BF16)] * 4 + [pltpu.VMEM((2, width // 4, HEAD), BF16)],
        scratch_shapes=[pltpu.SemaphoreType.DMA((4,))],
        cost_estimate=pl.CostEstimate(
            flops=rows * width * HEAD, bytes_accessed=10 * rows * width, transcendentals=0
        ),
        compiler_params=SMALL,
    )(*(pltpu.with_memory_space_constraint(x, pltpu.HBM) for x in tokens))
    return tuple(held), sums


def sums_kernel(wanted, *refs):
    for (own, block), out in zip(wanted, refs[4:]):
        sums_of(refs[:4], block_start(own, block, refs[0].shape[1] // 2), out)


def sums(tokens, *wanted):
    rows, width = tokens[0].shape
    return pl.pallas_call(
        functools.partial(sums_kernel, wanted),
        name="sums",
        in_specs=[VMEM] * 4,
        out_specs=[VMEM] * len(wanted),
        out_shape=[jax.ShapeDtypeStruct((2, width // 4, HEAD), BF16)] * len(wanted),
        cost_estimate=pl.CostEstimate(
            flops=rows * width * HEAD * len(wanted),
            bytes_accessed=3 * rows * width * len(wanted),
            transcendentals=0,
        ),
        compiler_params=SMALL,
    )(*tokens)


def pair_kernel(keep_ref, got_ref, *slots):
    for s, slot in enumerate(slots):
        part = slot_rows(s, len(slots), slot.shape[1])
        for which in range(2):
            both = keep_ref[which, part].astype(F32) + got_ref[which, part].astype(F32)
            slot[which] = both.astype(BF16)


def pair_slots(keep, got, count):
    slot = jax.ShapeDtypeStruct((2, keep.shape[1] // count, HEAD), BF16)
    return pl.pallas_call(
        pair_kernel,
        name="pair",
        in_specs=[VMEM] * 2,
        out_specs=[VMEM] * count,
        out_shape=[slot] * count,
        compiler_params=SMALL,
    )(keep, got)


def totals_kernel(far_count, *refs):
    slots, sends = refs[:far_count], refs[far_count:]
    outer = lax.axis_index("outer")
    totals = []
    for which in range(2):
        total = slots[0][which].astype(F32)
        for slot in slots[1:]:
            total += slot[which].astype(F32)
        totals.append(total.astype(BF16))
    for s, send in zip(distances(len(sends) + 1), sends):
        upward = (outer ^ s) > outer
        send[...] = jnp.where(upward, totals[0], totals[1])


def group_sends(slots, outer_count):
    send = jax.ShapeDtypeStruct(slots[0].shape[1:], BF16)
    return pl.pallas_call(
        functools.partial(totals_kernel, len(slots)),
        name="totals",
        in_specs=[VMEM] * len(slots),
        out_specs=[VMEM] * (outer_count - 1),
        out_shape=[send] * (outer_count - 1),
        compiler_params=SMALL,
    )(*slots)


def scan_kernel(far_count, *refs):
    slots, others, refs = refs[:far_count], refs[far_count : -far_count - 2], refs[-far_count - 2 :]
    outs, (held, scanned) = refs[:far_count], refs[far_count:]
    outer = lax.axis_index("outer")
    _, far = near_far()
    for s, slot in enumerate(slots):
        held[far ^ s] = slot[...]
    for which in range(2):
        total = jnp.zeros(held.shape[2:], F32)
        for s, other in zip(distances(len(others) + 1), others):
            below = (outer ^ s) < outer
            wanted = below if which == 0 else jnp.logical_not(below)
            total += jnp.where(wanted, other[...].astype(F32), 0.0)
        for i in reversed(range(far_count)) if which else range(far_count):
            scanned[i, which] = total.astype(BF16)
            total += held[i, which].astype(F32)
    for s, out in enumerate(outs):
        out[...] = scanned[far ^ s]


def scan_slots(slots, others):
    far_count, slot = len(slots), jax.ShapeDtypeStruct(slots[0].shape, BF16)
    return pl.pallas_call(
        functools.partial(scan_kernel, far_count),
        name="scan",
        in_specs=[VMEM] * (far_count + len(others)),
        out_specs=[VMEM] * far_count,
        out_shape=[slot] * far_count,
        scratch_shapes=[pltpu.VMEM((far_count, *slot.shape), BF16)] * 2,
        compiler_params=SMALL,
    )(*slots, *others)


def with_sums(slot, which, extra, part):
    return (slot[which].astype(F32) + extra[which, part].astype(F32)).astype(BF16)


def by_core(run):
    near, _ = near_far()
    for core in range(2):
        pl.when(near == core)(functools.partial(run, core))


def theirs_kernel(*refs):
    slots, (keep, out) = refs[:-2], refs[-2:]

    def run(core):
        for s, slot in enumerate(slots):
            part = slot_rows(s, len(slots), slot.shape[1])
            out[core, part] = with_sums(slot, core, keep, part)
            out[1 - core, part] = slot[1 - core]

    by_core(run)


def states_for_neighbour(slots, keep):
    return pl.pallas_call(
        theirs_kernel,
        name="theirs",
        in_specs=[VMEM] * (len(slots) + 1),
        out_specs=VMEM,
        out_shape=jax.ShapeDtypeStruct(keep.shape, BF16),
        compiler_params=SMALL,
    )(*slots, keep)


def local_kernel(*refs):
    tokens, outs = refs[:4], refs[4:]
    rows, width = tokens[0].shape
    at = lax.broadcasted_iota(jnp.int32, (rows, rows), 0)
    to = lax.broadcasted_iota(jnp.int32, (rows, rows), 1)
    lower = at >= to

    def masked(a, b):
        return jnp.where(lower, dot(a, b, 1, 1), 0.0).astype(BF16)

    def second(cols, a, b):
        q, k, v, d = (ref[:, cols] for ref in tokens)
        att, gq, gk, gv = outs
        att[:, cols] = dot(a, v, 1, 0)
        gq[:, cols] = dot(b, k, 1, 0)
        gk[:, cols] = dot(b, q, 0, 0)
        gv[:, cols] = dot(a, d, 0, 0)

    last = None
    for h in range(width // HEAD):
        cols = slice(h * HEAD, (h + 1) * HEAD)
        q, k, v, d = (ref[:, cols] for ref in tokens)
        a, b = masked(q, k), masked(d, v)
        if last:
            second(*last)
        last = (cols, a, b)
    second(*last)


def local_part(tokens):
    rows, width = tokens[0].shape
    return pl.pallas_call(
        local_kernel,
        name="local",
        in_specs=[VMEM] * 4,
        out_specs=[VMEM] * 4,
        out_shape=[jax.ShapeDtypeStruct((rows, width), F32)] * 4,
        cost_estimate=pl.CostEstimate(
            flops=12 * rows * width * HEAD, bytes_accessed=24 * rows * width, transcendentals=0
        ),
        compiler_params=SMALL,
    )(*tokens)


def all_products(scale, start, tokens, local, states, store):
    q, k, v, d = tokens

    def products():
        for n in range(states.shape[1] // HEAD):
            rows = slice(n * HEAD, (n + 1) * HEAD)
            cols = slice(start + n * HEAD, start + (n + 1) * HEAD)
            s, g = states[0, rows], states[1, rows]
            yield (rows, 0, cols), dot(q[:, cols], s, 1, 0)
            yield (rows, 1, cols), dot(d[:, cols], s, 1, 1)
            yield (rows, 2, cols), dot(v[:, cols], g, 1, 1)
            yield (rows, 3, cols), dot(k[:, cols], g, 1, 0)

    def use(key, product):
        rows, i, cols = key
        store(rows, i, (scale * (product + local[i][:, cols])).astype(BF16))

    one_ahead(products(), use)


def copies_out(own, block, held, outs, sems, piece):
    first, size = (0, held.shape[2]) if piece is None else (piece * held.shape[2] // 2, held.shape[2] // 2)
    start = block_start(own, block, outs[0].shape[1] // 2) + first
    there = pl.ds(pl.multiple_of(start, size), size)
    return [
        pltpu.make_async_copy(held.at[i, :, pl.ds(first, size)], out.at[:, there], sems.at[i])
        for i, out in enumerate(outs)
    ]


def finish_kernel(scale, own, block, count, rests, hold, *refs):
    tokens, local, slots, refs = refs[:4], refs[4:8], refs[8 : 8 + count], refs[8 + count :]
    got, refs = (refs[0], refs[1:]) if own else (None, refs)
    late, refs = refs[: len(rests)], refs[len(rests) :]
    if own:
        refs, states = refs[:-1], refs[-1]
    else:
        states = slots[0]
    if not hold or rests:
        *refs, sems = refs
    *refs, held = refs
    outs = refs[-4:]
    width = tokens[0].shape[1]
    copies = []
    for n, (rest, where) in enumerate(zip(late, rests)):
        copies += copies_out(*where, rest, outs, sems.at[n + 2], None)
    for copy in copies:
        copy.start()

    def store(rows, i, out):
        held[i, :, rows] = out
        for piece in range(2):
            if not hold and i == 3 and rows.stop == (piece + 1) * states.shape[1] // 2:
                for copy in copies_out(own, block, held, outs, sems.at[piece], piece):
                    copy.start()

    def run(quarter):
        for s, slot in enumerate(slots if own else ()):
            core, part = quarter // 2, slot_rows(s, count, slot.shape[1])
            states[core, part] = slot[core]
            states[1 - core, part] = with_sums(slot, 1 - core, got, part)
        all_products(scale, quarter * width // 4, tokens, local, states, store)

    start = block_start(own, block, width // 2)
    for quarter in range(4):
        pl.when(start == quarter * width // 4)(functools.partial(run, quarter))
    if not hold:
        for piece in range(2):
            copies += copies_out(own, block, held, outs, sems.at[piece], piece)
    for copy in copies:
        copy.wait()


def finish(own, block, tokens, local, slots, scale, got=(), rests=(), before=(), hold=False):
    rows, width = tokens[0].shape
    out = jax.ShapeDtypeStruct((rows, width), BF16)
    piece = pltpu.VMEM((4, rows, width // 4), BF16)
    inputs = [*tokens, *local, *slots, *got, *(x for _, x in rests)]
    states = pltpu.VMEM((2, width // 4, HEAD), BF16)
    wheres = [where for where, _ in rests]
    writes = not hold or bool(rests)
    return pl.pallas_call(
        functools.partial(finish_kernel, scale, own, block, len(slots), wheres, hold),
        name="finish",
        in_specs=[VMEM] * len(inputs) + [ANY] * len(before),
        out_specs=[ANY] * 4 * writes + [VMEM] * hold,
        out_shape=[out] * 4 * writes + [piece] * hold,
        scratch_shapes=[piece] * (not hold)
        + [pltpu.SemaphoreType.DMA((2 + len(rests), 4))] * writes
        + [states] * own,
        input_output_aliases={len(inputs) + i: i for i in range(len(before))},
        cost_estimate=pl.CostEstimate(
            flops=2 * rows * width * HEAD, bytes_accessed=8 * rows * width, transcendentals=0
        ),
        compiler_params=SMALL,
    )(*inputs, *before)


def swap(x, axis, bits):
    return lax.ppermute(x, axis, [(i, i ^ bits) for i in range(lax.axis_size(axis))])


def swap_far(slots):
    return [slots[0]] + [swap(slots[s], "inner", 2 * s) for s in range(1, len(slots))]


def body(queries, keys, values, cotangent):
    far_count = lax.axis_size("inner") // 2
    outer_count = lax.axis_size("outer")
    scale = float(HEAD * queries.shape[0] * 2 * far_count * outer_count) ** (-0.5)
    tokens, give = load((queries, keys, values, cotangent))
    got = [swap(give, "inner", 1), swap(*sums(tokens, (False, 1)), "inner", 1)]
    keep = sums(tokens, (True, 0), (True, 1))
    slots = [slot for b in range(2) for slot in pair_slots(keep[b], got[b], far_count // 2)]
    slots, local = lax.optimization_barrier((swap_far(slots), local_part(tokens)))
    sends = group_sends(slots, outer_count)
    others = [swap(send, "outer", s) for s, send in zip(distances(outer_count), sends)]
    slots = swap_far(scan_slots(slots, others))
    half = far_count // 2

    def near_swap(block, part):
        return swap(states_for_neighbour(part, keep[block]), "inner", 1)

    arrived = [near_swap(0, slots[:half])]
    outs = finish(True, 0, tokens, local, slots[:half], scale, got=got[:1])
    part, outs = lax.optimization_barrier((slots[half:], tuple(outs)))
    arrived.append(near_swap(1, part))
    (rest,) = finish(True, 1, tokens, local, part, scale, got=got[1:], hold=True)
    rests = [((True, 1), rest)]
    *outs, rest = finish(
        False, 0, tokens, local, arrived[:1], scale, rests=rests, before=outs, hold=True
    )
    rests = [((False, 0), rest)]
    return tuple(finish(False, 1, tokens, local, arrived[1:], scale, rests=rests, before=outs))


def solution(mesh):
    spec = P(("outer", "inner"), None)
    return jax.shard_map(
        body, mesh=mesh, in_specs=(spec,) * 4, out_specs=(spec,) * 4, check_vma=False
    )
```

```python
import functools

import jax
import jax.numpy as jnp
from jax import lax
from jax.experimental import pallas as pl
from jax.experimental.pallas import tpu as pltpu
from jax.sharding import PartitionSpec as P

HEAD = 128
MIB = 1024 * 1024
ANY = pl.BlockSpec(memory_space=pl.ANY)
VMEM = pl.BlockSpec(memory_space=pltpu.VMEM)
BF16 = jnp.bfloat16
F32 = jnp.float32
SMALL = pltpu.CompilerParams(vmem_limit_bytes=4 * MIB)


def dot(a, b, over_a, over_b):
    return lax.dot_general(
        a, b, (((over_a,), (over_b,)), ((), ())), preferred_element_type=F32
    )


def near_far():
    inner = lax.axis_index("inner")
    return lax.rem(inner, 2), lax.div(inner, 2)


def distances(outer_count):
    return range(outer_count - 1, 0, -1)


def block_start(own, block, half):
    near, far = near_far()
    side = near if own else 1 - near
    top = lax.div(far, lax.axis_size("inner") // 4)
    return side * half + (1 - top if block else top) * (half // 2)


def columns(start, n):
    return pl.ds(pl.multiple_of(start + n * HEAD, HEAD), HEAD)


def slot_rows(s, count, depth):
    _, far = near_far()
    return pl.ds(pl.multiple_of(lax.rem(far ^ s, count) * depth, depth), depth)


def one_ahead(products, use):
    last = None
    for key, product in products:
        if last:
            use(*last)
        last = key, product
    use(*last)


def sums_of(tokens, start, out, kinds=(0, 1)):
    q, k, v, d = tokens

    def products():
        for n in range(out.shape[1] // HEAD):
            cols = pl.ds(start + n * HEAD, HEAD) if isinstance(start, int) else columns(start, n)
            for which in kinds:
                a, b = ((k, v), (q, d))[which]
                yield (which, n), dot(a[:, cols], b[:, cols], 0, 0)

    def use(key, product):
        which, n = key
        out[which, n * HEAD : (n + 1) * HEAD] = product.astype(BF16)

    one_ahead(products(), use)


def load_kernel(*refs):
    tokens, held, (out, sems) = refs[:4], refs[4:8], refs[8:]
    copies = [pltpu.make_async_copy(tokens[i], held[i], sems.at[i]) for i in range(4)]
    width = held[0].shape[1]
    start = block_start(False, 0, width // 2)
    pairs = ((1, 2), (0, 3))
    for i in pairs[0] + pairs[1]:
        copies[i].start()
    for kind, pair in enumerate(pairs):
        for i in pair:
            copies[i].wait()
        for n in range(4):
            at = n * width // 4
            pl.when(start == at)(functools.partial(sums_of, held, at, out, (kind,)))


def load(tokens):
    rows, width = tokens[0].shape
    *held, sums = pl.pallas_call(
        load_kernel,
        name="load",
        in_specs=[ANY] * 4,
        out_specs=[VMEM] * 5,
        out_shape=[pltpu.VMEM((rows, width), BF16)] * 4 + [pltpu.VMEM((2, width // 4, HEAD), BF16)],
        scratch_shapes=[pltpu.SemaphoreType.DMA((4,))],
        cost_estimate=pl.CostEstimate(
            flops=rows * width * HEAD, bytes_accessed=10 * rows * width, transcendentals=0
        ),
        compiler_params=SMALL,
    )(*(pltpu.with_memory_space_constraint(x, pltpu.HBM) for x in tokens))
    return tuple(held), sums


def sums_kernel(wanted, *refs):
    for (own, block), out in zip(wanted, refs[4:]):
        sums_of(refs[:4], block_start(own, block, refs[0].shape[1] // 2), out)


def sums(tokens, *wanted):
    rows, width = tokens[0].shape
    return pl.pallas_call(
        functools.partial(sums_kernel, wanted),
        name="sums",
        in_specs=[VMEM] * 4,
        out_specs=[VMEM] * len(wanted),
        out_shape=[jax.ShapeDtypeStruct((2, width // 4, HEAD), BF16)] * len(wanted),
        cost_estimate=pl.CostEstimate(
            flops=rows * width * HEAD * len(wanted),
            bytes_accessed=3 * rows * width * len(wanted),
            transcendentals=0,
        ),
        compiler_params=SMALL,
    )(*tokens)


def pair_kernel(keep_ref, got_ref, _, *slots):
    for s, slot in enumerate(slots):
        part = slot_rows(s, len(slots), slot.shape[1])
        for which in range(2):
            both = keep_ref[which, part].astype(F32) + got_ref[which, part].astype(F32)
            slot[which] = both.astype(BF16)


def pair_slots(keep, got, count, after):
    slot = jax.ShapeDtypeStruct((2, keep.shape[1] // count, HEAD), BF16)
    return pl.pallas_call(
        pair_kernel,
        name="pair",
        in_specs=[VMEM] * 2 + [ANY],
        out_specs=[VMEM] * count,
        out_shape=[slot] * count,
        compiler_params=SMALL,
    )(keep, got, after)


def totals_kernel(far_count, *refs):
    slots, sends = refs[:far_count], refs[far_count:]
    outer = lax.axis_index("outer")
    totals = []
    for which in range(2):
        total = slots[0][which].astype(F32)
        for slot in slots[1:]:
            total += slot[which].astype(F32)
        totals.append(total.astype(BF16))
    for s, send in zip(distances(len(sends) + 1), sends):
        upward = (outer ^ s) > outer
        send[...] = jnp.where(upward, totals[0], totals[1])


def group_sends(slots, outer_count):
    send = jax.ShapeDtypeStruct(slots[0].shape[1:], BF16)
    return pl.pallas_call(
        functools.partial(totals_kernel, len(slots)),
        name="totals",
        in_specs=[VMEM] * len(slots),
        out_specs=[VMEM] * (outer_count - 1),
        out_shape=[send] * (outer_count - 1),
        compiler_params=SMALL,
    )(*slots)


def scan_kernel(far_count, *refs):
    slots, others, refs = refs[:far_count], refs[far_count : -far_count - 2], refs[-far_count - 2 :]
    outs, (held, scanned) = refs[:far_count], refs[far_count:]
    outer = lax.axis_index("outer")
    _, far = near_far()
    for s, slot in enumerate(slots):
        held[far ^ s] = slot[...]
    for which in range(2):
        total = jnp.zeros(held.shape[2:], F32)
        for s, other in zip(distances(len(others) + 1), others):
            below = (outer ^ s) < outer
            wanted = below if which == 0 else jnp.logical_not(below)
            total += jnp.where(wanted, other[...].astype(F32), 0.0)
        for i in reversed(range(far_count)) if which else range(far_count):
            scanned[i, which] = total.astype(BF16)
            total += held[i, which].astype(F32)
    for s, out in enumerate(outs):
        out[...] = scanned[far ^ s]


def scan_slots(slots, others):
    far_count, slot = len(slots), jax.ShapeDtypeStruct(slots[0].shape, BF16)
    return pl.pallas_call(
        functools.partial(scan_kernel, far_count),
        name="scan",
        in_specs=[VMEM] * (far_count + len(others)),
        out_specs=[VMEM] * far_count,
        out_shape=[slot] * far_count,
        scratch_shapes=[pltpu.VMEM((far_count, *slot.shape), BF16)] * 2,
        compiler_params=SMALL,
    )(*slots, *others)


def with_sums(slot, which, extra, part):
    return (slot[which].astype(F32) + extra[which, part].astype(F32)).astype(BF16)


def by_core(run):
    near, _ = near_far()
    for core in range(2):
        pl.when(near == core)(functools.partial(run, core))


def theirs_kernel(*refs):
    slots, (keep, out) = refs[:-2], refs[-2:]

    def run(core):
        for s, slot in enumerate(slots):
            part = slot_rows(s, len(slots), slot.shape[1])
            out[core, part] = with_sums(slot, core, keep, part)
            out[1 - core, part] = slot[1 - core]

    by_core(run)


def states_for_neighbour(slots, keep):
    return pl.pallas_call(
        theirs_kernel,
        name="theirs",
        in_specs=[VMEM] * (len(slots) + 1),
        out_specs=VMEM,
        out_shape=jax.ShapeDtypeStruct(keep.shape, BF16),
        compiler_params=SMALL,
    )(*slots, keep)


def local_kernel(early, *refs):
    near, _ = near_far()
    tokens, outs = refs[:4], refs[-4:]
    heads = tokens[0].shape[1] // HEAD
    even = range(heads // 2) if early else range(heads // 2, heads)
    pl.when(near == 0)(functools.partial(local_products, tokens, outs, even))
    if not early:
        pl.when(near == 1)(functools.partial(local_products, tokens, outs, range(heads)))


def local_products(tokens, outs, heads):
    rows = tokens[0].shape[0]
    at = lax.broadcasted_iota(jnp.int32, (rows, rows), 0)
    to = lax.broadcasted_iota(jnp.int32, (rows, rows), 1)
    lower = at >= to

    def masked(a, b):
        return jnp.where(lower, dot(a, b, 1, 1), 0.0).astype(BF16)

    def second(cols, a, b):
        q, k, v, d = (ref[:, cols] for ref in tokens)
        att, gq, gk, gv = outs
        att[:, cols] = dot(a, v, 1, 0)
        gq[:, cols] = dot(b, k, 1, 0)
        gk[:, cols] = dot(b, q, 0, 0)
        gv[:, cols] = dot(a, d, 0, 0)

    last = None
    for h in heads:
        cols = slice(h * HEAD, (h + 1) * HEAD)
        q, k, v, d = (ref[:, cols] for ref in tokens)
        a, b = masked(q, k), masked(d, v)
        if last:
            second(*last)
        last = (cols, a, b)
    second(*last)


def local_part(early, tokens, after):
    rows, width = tokens[0].shape
    out = jax.ShapeDtypeStruct((rows, width // 2 if early else width), F32)
    return pl.pallas_call(
        functools.partial(local_kernel, early),
        name="local",
        in_specs=[VMEM] * 4 + [ANY],
        out_specs=[VMEM] * 4,
        out_shape=[out] * 4,
        cost_estimate=pl.CostEstimate(flops=0, bytes_accessed=0, transcendentals=0),
        compiler_params=SMALL,
    )(*tokens, after)


def all_products(scale, start, tokens, local, states, store):
    q, k, v, d = tokens

    def products():
        for n in range(states.shape[1] // HEAD):
            rows = slice(n * HEAD, (n + 1) * HEAD)
            cols = slice(start + n * HEAD, start + (n + 1) * HEAD)
            s, g = states[0, rows], states[1, rows]
            yield (rows, 0, cols), dot(q[:, cols], s, 1, 0)
            yield (rows, 1, cols), dot(d[:, cols], s, 1, 1)
            yield (rows, 2, cols), dot(v[:, cols], g, 1, 1)
            yield (rows, 3, cols), dot(k[:, cols], g, 1, 0)

    def use(key, product):
        rows, i, cols = key
        store(rows, i, (scale * (product + local[i][:, cols])).astype(BF16))

    one_ahead(products(), use)


def copies_out(own, block, held, outs, sems, piece):
    first, size = (0, held.shape[2]) if piece is None else (piece * held.shape[2] // 2, held.shape[2] // 2)
    start = block_start(own, block, outs[0].shape[1] // 2) + first
    there = pl.ds(pl.multiple_of(start, size), size)
    return [
        pltpu.make_async_copy(held.at[i, :, pl.ds(first, size)], out.at[:, there], sems.at[i])
        for i, out in enumerate(outs)
    ]


def finish_kernel(scale, own, block, count, rests, hold, *refs):
    tokens, locals_, slots, refs = refs[:4], refs[4:12], refs[12 : 12 + count], refs[12 + count :]
    got, refs = (refs[0], refs[1:]) if own else (None, refs)
    late, refs = refs[: len(rests)], refs[len(rests) :]
    if own:
        refs, states = refs[:-1], refs[-1]
    else:
        states = slots[0]
    if not hold or rests:
        *refs, sems = refs
    *refs, held = refs
    outs = refs[-4:]
    width = tokens[0].shape[1]
    copies = []
    for n, (rest, where) in enumerate(zip(late, rests)):
        copies += copies_out(*where, rest, outs, sems.at[n + 2], None)
    for copy in copies:
        copy.start()

    def store(rows, i, out):
        held[i, :, rows] = out
        for piece in range(2):
            if not hold and i == 3 and rows.stop == (piece + 1) * states.shape[1] // 2:
                for copy in copies_out(own, block, held, outs, sems.at[piece], piece):
                    copy.start()

    def run(quarter):
        core = quarter // 2 if own else 1 - quarter // 2
        local = locals_[:4] if core == quarter // 2 == 0 else locals_[4:]
        for s, slot in enumerate(slots if own else ()):
            part = slot_rows(s, count, slot.shape[1])
            states[core, part] = slot[core]
            states[1 - core, part] = with_sums(slot, 1 - core, got, part)
        all_products(scale, quarter * width // 4, tokens, local, states, store)

    start = block_start(own, block, width // 2)
    for quarter in range(4):
        pl.when(start == quarter * width // 4)(functools.partial(run, quarter))
    if not hold:
        for piece in range(2):
            copies += copies_out(own, block, held, outs, sems.at[piece], piece)
    for copy in copies:
        copy.wait()


def finish(own, block, tokens, local, slots, scale, got=(), rests=(), before=(), hold=False):
    rows, width = tokens[0].shape
    out = jax.ShapeDtypeStruct((rows, width), BF16)
    piece = pltpu.VMEM((4, rows, width // 4), BF16)
    inputs = [*tokens, *local, *slots, *got, *(x for _, x in rests)]
    states = pltpu.VMEM((2, width // 4, HEAD), BF16)
    wheres = [where for where, _ in rests]
    writes = not hold or bool(rests)
    return pl.pallas_call(
        functools.partial(finish_kernel, scale, own, block, len(slots), wheres, hold),
        name="finish",
        in_specs=[VMEM] * len(inputs) + [ANY] * len(before),
        out_specs=[ANY] * 4 * writes + [VMEM] * hold,
        out_shape=[out] * 4 * writes + [piece] * hold,
        scratch_shapes=[piece] * (not hold)
        + [pltpu.SemaphoreType.DMA((2 + len(rests), 4))] * writes
        + [states] * own,
        input_output_aliases={len(inputs) + i: i for i in range(len(before))},
        cost_estimate=pl.CostEstimate(
            flops=2 * rows * width * HEAD, bytes_accessed=8 * rows * width, transcendentals=0
        ),
        compiler_params=SMALL,
    )(*inputs, *before)


def swap(x, axis, bits):
    return lax.ppermute(x, axis, [(i, i ^ bits) for i in range(lax.axis_size(axis))])


def swap_far(slots):
    return [slots[0]] + [swap(slots[s], "inner", 2 * s) for s in range(1, len(slots))]


def body(queries, keys, values, cotangent):
    far_count = lax.axis_size("inner") // 2
    outer_count = lax.axis_size("outer")
    scale = float(HEAD * queries.shape[0] * 2 * far_count * outer_count) ** (-0.5)
    tokens, give = load((queries, keys, values, cotangent))
    got = [swap(give, "inner", 1), swap(*sums(tokens, (False, 1)), "inner", 1)]
    keep = sums(tokens, (True, 0), (True, 1))
    early = local_part(True, tokens, keep[1])
    slots = []
    for b in range(2):
        slots += pair_slots(keep[b], got[b], far_count // 2, slots[0] if slots else early[0])
    slots, late = lax.optimization_barrier((swap_far(slots), local_part(False, tokens, slots[-1])))
    local = [*early, *late]
    sends = group_sends(slots, outer_count)
    others = [swap(send, "outer", s) for s, send in zip(distances(outer_count), sends)]
    slots = swap_far(scan_slots(slots, others))
    half = far_count // 2

    def near_swap(block, part):
        return swap(states_for_neighbour(part, keep[block]), "inner", 1)

    arrived = [near_swap(0, slots[:half])]
    outs = finish(True, 0, tokens, local, slots[:half], scale, got=got[:1])
    part, outs = lax.optimization_barrier((slots[half:], tuple(outs)))
    arrived.append(near_swap(1, part))
    (rest,) = finish(True, 1, tokens, local, part, scale, got=got[1:], hold=True)
    rests = [((True, 1), rest)]
    *outs, rest = finish(
        False, 0, tokens, local, arrived[:1], scale, rests=rests, before=outs, hold=True
    )
    rests = [((False, 0), rest)]
    return tuple(finish(False, 1, tokens, local, arrived[1:], scale, rests=rests, before=outs))


def solution(mesh):
    spec = P(("outer", "inner"), None)
    return jax.shard_map(
        body, mesh=mesh, in_specs=(spec,) * 4, out_specs=(spec,) * 4, check_vma=False
    )
```

```python
import functools

import jax
import jax.numpy as jnp
from jax import lax
from jax.experimental import pallas as pl
from jax.experimental.pallas import tpu as pltpu
from jax.sharding import PartitionSpec as P

HEAD = 128
MIB = 1024 * 1024
ANY = pl.BlockSpec(memory_space=pl.ANY)
VMEM = pl.BlockSpec(memory_space=pltpu.VMEM)
BF16 = jnp.bfloat16
F32 = jnp.float32
SMALL = pltpu.CompilerParams(vmem_limit_bytes=4 * MIB)


def dot(a, b, over_a, over_b):
    return lax.dot_general(
        a, b, (((over_a,), (over_b,)), ((), ())), preferred_element_type=F32
    )


def near_far():
    inner = lax.axis_index("inner")
    return lax.rem(inner, 2), lax.div(inner, 2)


def distances(outer_count):
    return [outer_count - 1, *range(1, outer_count - 1)]


def block_start(own, block, half):
    near, far = near_far()
    side = near if own else 1 - near
    top = lax.div(far, lax.axis_size("inner") // 4)
    return side * half + (1 - top if block else top) * (half // 2)


def columns(start, n):
    return pl.ds(pl.multiple_of(start + n * HEAD, HEAD), HEAD)


def slot_rows(s, count, depth):
    _, far = near_far()
    return pl.ds(pl.multiple_of(lax.rem(far ^ s, count) * depth, depth), depth)


def one_ahead(products, use):
    last = None
    for key, product in products:
        if last:
            use(*last)
        last = key, product
    use(*last)


def sums_of(tokens, start, out, kinds=(0, 1)):
    q, k, v, d = tokens

    def products():
        for n in range(out.shape[1] // HEAD):
            cols = pl.ds(start + n * HEAD, HEAD) if isinstance(start, int) else columns(start, n)
            for which in kinds:
                a, b = ((k, v), (q, d))[which]
                yield (which, n), dot(a[:, cols], b[:, cols], 0, 0)

    def use(key, product):
        which, n = key
        out[which, n * HEAD : (n + 1) * HEAD] = product.astype(BF16)

    one_ahead(products(), use)


def give_kernel(*refs):
    tokens, (out, held, sems) = refs[:4], refs[4:]
    width = tokens[0].shape[1]
    start = pl.multiple_of(block_start(False, 0, width // 2), width // 4)
    pairs = ((1, 2), (0, 3))
    copies = [
        pltpu.make_async_copy(ref.at[:, pl.ds(start, width // 4)], held.at[i], sems.at[i])
        for i, ref in enumerate(tokens)
    ]
    for i in pairs[0] + pairs[1]:
        copies[i].start()
    for kind, pair in enumerate(pairs):
        for i in pair:
            copies[i].wait()
        sums_of([held.at[i] for i in range(4)], 0, out, (kind,))


def first_sums(tokens):
    rows, width = tokens[0].shape
    return pl.pallas_call(
        give_kernel,
        name="first_sums",
        in_specs=[ANY] * 4,
        out_specs=VMEM,
        out_shape=pltpu.VMEM((2, width // 4, HEAD), BF16),
        scratch_shapes=[pltpu.VMEM((4, rows, width // 4), BF16), pltpu.SemaphoreType.DMA((4,))],
        cost_estimate=pl.CostEstimate(
            flops=rows * width * HEAD, bytes_accessed=3 * rows * width, transcendentals=0
        ),
        compiler_params=SMALL,
    )(*(pltpu.with_memory_space_constraint(x, pltpu.HBM) for x in tokens))


def sums_kernel(wanted, *refs):
    for (own, block), out in zip(wanted, refs[4:]):
        sums_of(refs[:4], block_start(own, block, refs[0].shape[1] // 2), out)


def sums(tokens, *wanted):
    rows, width = tokens[0].shape
    return pl.pallas_call(
        functools.partial(sums_kernel, wanted),
        name="sums",
        in_specs=[VMEM] * 4,
        out_specs=[VMEM] * len(wanted),
        out_shape=[jax.ShapeDtypeStruct((2, width // 4, HEAD), BF16)] * len(wanted),
        cost_estimate=pl.CostEstimate(
            flops=rows * width * HEAD * len(wanted),
            bytes_accessed=3 * rows * width * len(wanted),
            transcendentals=0,
        ),
        compiler_params=SMALL,
    )(*tokens)


def pair_kernel(keep_ref, got_ref, *slots):
    for s, slot in enumerate(slots):
        part = slot_rows(s, len(slots), slot.shape[1])
        for which in range(2):
            both = keep_ref[which, part].astype(F32) + got_ref[which, part].astype(F32)
            slot[which] = both.astype(BF16)


def pair_slots(keep, got, count):
    slot = jax.ShapeDtypeStruct((2, keep.shape[1] // count, HEAD), BF16)
    return pl.pallas_call(
        pair_kernel,
        name="pair",
        in_specs=[VMEM] * 2,
        out_specs=[VMEM] * count,
        out_shape=[slot] * count,
        compiler_params=SMALL,
    )(keep, got)


def totals_kernel(far_count, *refs):
    slots, sends = refs[:far_count], refs[far_count:]
    outer = lax.axis_index("outer")
    totals = []
    for which in range(2):
        total = slots[0][which].astype(F32)
        for slot in slots[1:]:
            total += slot[which].astype(F32)
        totals.append(total.astype(BF16))
    for s, send in zip(distances(len(sends) + 1), sends):
        upward = (outer ^ s) > outer
        send[...] = jnp.where(upward, totals[0], totals[1])


def group_sends(slots, outer_count):
    send = jax.ShapeDtypeStruct(slots[0].shape[1:], BF16)
    return pl.pallas_call(
        functools.partial(totals_kernel, len(slots)),
        name="totals",
        in_specs=[VMEM] * len(slots),
        out_specs=[VMEM] * (outer_count - 1),
        out_shape=[send] * (outer_count - 1),
        compiler_params=SMALL,
    )(*slots)


def scan_kernel(far_count, *refs):
    slots, others, refs = refs[:far_count], refs[far_count : -far_count - 2], refs[-far_count - 2 :]
    outs, (held, scanned) = refs[:far_count], refs[far_count:]
    outer = lax.axis_index("outer")
    _, far = near_far()
    for s, slot in enumerate(slots):
        held[far ^ s] = slot[...]
    for which in range(2):
        total = jnp.zeros(held.shape[2:], F32)
        for s, other in zip(distances(len(others) + 1), others):
            below = (outer ^ s) < outer
            wanted = below if which == 0 else jnp.logical_not(below)
            total += jnp.where(wanted, other[...].astype(F32), 0.0)
        for i in reversed(range(far_count)) if which else range(far_count):
            scanned[i, which] = total.astype(BF16)
            total += held[i, which].astype(F32)
    for s, out in enumerate(outs):
        out[...] = scanned[far ^ s]


def scan_slots(slots, others):
    far_count, slot = len(slots), jax.ShapeDtypeStruct(slots[0].shape, BF16)
    return pl.pallas_call(
        functools.partial(scan_kernel, far_count),
        name="scan",
        in_specs=[VMEM] * (far_count + len(others)),
        out_specs=[VMEM] * far_count,
        out_shape=[slot] * far_count,
        scratch_shapes=[pltpu.VMEM((far_count, *slot.shape), BF16)] * 2,
        compiler_params=SMALL,
    )(*slots, *others)


def with_sums(slot, which, extra, part):
    return (slot[which].astype(F32) + extra[which, part].astype(F32)).astype(BF16)


def by_core(run):
    near, _ = near_far()
    for core in range(2):
        pl.when(near == core)(functools.partial(run, core))


def theirs_kernel(*refs):
    slots, (keep, out) = refs[:-2], refs[-2:]

    def run(core):
        for s, slot in enumerate(slots):
            part = slot_rows(s, len(slots), slot.shape[1])
            out[core, part] = with_sums(slot, core, keep, part)
            out[1 - core, part] = slot[1 - core]

    by_core(run)


def states_for_neighbour(slots, keep):
    return pl.pallas_call(
        theirs_kernel,
        name="theirs",
        in_specs=[VMEM] * (len(slots) + 1),
        out_specs=VMEM,
        out_shape=jax.ShapeDtypeStruct(keep.shape, BF16),
        compiler_params=SMALL,
    )(*slots, keep)


def local_kernel(*refs):
    tokens, outs = refs[:4], refs[4:]
    rows, width = tokens[0].shape
    at = lax.broadcasted_iota(jnp.int32, (rows, rows), 0)
    to = lax.broadcasted_iota(jnp.int32, (rows, rows), 1)
    lower = at >= to

    def masked(a, b):
        return jnp.where(lower, dot(a, b, 1, 1), 0.0).astype(BF16)

    def second(cols, a, b):
        q, k, v, d = (ref[:, cols] for ref in tokens)
        att, gq, gk, gv = outs
        att[:, cols] = dot(a, v, 1, 0)
        gq[:, cols] = dot(b, k, 1, 0)
        gk[:, cols] = dot(b, q, 0, 0)
        gv[:, cols] = dot(a, d, 0, 0)

    last = None
    for h in range(width // HEAD):
        cols = slice(h * HEAD, (h + 1) * HEAD)
        q, k, v, d = (ref[:, cols] for ref in tokens)
        a, b = masked(q, k), masked(d, v)
        if last:
            second(*last)
        last = (cols, a, b)
    second(*last)


def local_part(tokens):
    rows, width = tokens[0].shape
    return pl.pallas_call(
        local_kernel,
        name="local",
        in_specs=[VMEM] * 4,
        out_specs=[VMEM] * 4,
        out_shape=[jax.ShapeDtypeStruct((rows, width), F32)] * 4,
        cost_estimate=pl.CostEstimate(
            flops=12 * rows * width * HEAD, bytes_accessed=24 * rows * width, transcendentals=0
        ),
        compiler_params=SMALL,
    )(*tokens)


def all_products(scale, start, tokens, local, states, store):
    q, k, v, d = tokens

    def products():
        for n in range(states.shape[1] // HEAD):
            rows = slice(n * HEAD, (n + 1) * HEAD)
            cols = slice(start + n * HEAD, start + (n + 1) * HEAD)
            s, g = states[0, rows], states[1, rows]
            yield (rows, 0, cols), dot(q[:, cols], s, 1, 0)
            yield (rows, 1, cols), dot(d[:, cols], s, 1, 1)
            yield (rows, 2, cols), dot(v[:, cols], g, 1, 1)
            yield (rows, 3, cols), dot(k[:, cols], g, 1, 0)

    def use(key, product):
        rows, i, cols = key
        store(rows, i, (scale * (product + local[i][:, cols])).astype(BF16))

    one_ahead(products(), use)


def copies_out(own, block, held, outs, sems, piece):
    first, size = (0, held.shape[2]) if piece is None else (piece * held.shape[2] // 2, held.shape[2] // 2)
    start = block_start(own, block, outs[0].shape[1] // 2) + first
    there = pl.ds(pl.multiple_of(start, size), size)
    return [
        pltpu.make_async_copy(held.at[i, :, pl.ds(first, size)], out.at[:, there], sems.at[i])
        for i, out in enumerate(outs)
    ]


def finish_kernel(scale, own, block, count, rests, hold, *refs):
    tokens, local, slots, refs = refs[:4], refs[4:8], refs[8 : 8 + count], refs[8 + count :]
    got, refs = (refs[0], refs[1:]) if own else (None, refs)
    late, refs = refs[: len(rests)], refs[len(rests) :]
    if own:
        refs, states = refs[:-1], refs[-1]
    else:
        states = slots[0]
    if not hold or rests:
        *refs, sems = refs
    *refs, held = refs
    outs = refs[-4:]
    width = tokens[0].shape[1]
    copies = []
    for n, (rest, where) in enumerate(zip(late, rests)):
        copies += copies_out(*where, rest, outs, sems.at[n + 2], None)
    for copy in copies:
        copy.start()

    def store(rows, i, out):
        held[i, :, rows] = out
        for piece in range(2):
            if not hold and i == 3 and rows.stop == (piece + 1) * states.shape[1] // 2:
                for copy in copies_out(own, block, held, outs, sems.at[piece], piece):
                    copy.start()

    def run(quarter):
        for s, slot in enumerate(slots if own else ()):
            core, part = quarter // 2, slot_rows(s, count, slot.shape[1])
            states[core, part] = slot[core]
            states[1 - core, part] = with_sums(slot, 1 - core, got, part)
        all_products(scale, quarter * width // 4, tokens, local, states, store)

    start = block_start(own, block, width // 2)
    for quarter in range(4):
        pl.when(start == quarter * width // 4)(functools.partial(run, quarter))
    if not hold:
        for piece in range(2):
            copies += copies_out(own, block, held, outs, sems.at[piece], piece)
    for copy in copies:
        copy.wait()


def finish(own, block, tokens, local, slots, scale, got=(), rests=(), before=(), hold=False):
    rows, width = tokens[0].shape
    out = jax.ShapeDtypeStruct((rows, width), BF16)
    piece = pltpu.VMEM((4, rows, width // 4), BF16)
    inputs = [*tokens, *local, *slots, *got, *(x for _, x in rests)]
    states = pltpu.VMEM((2, width // 4, HEAD), BF16)
    wheres = [where for where, _ in rests]
    writes = not hold or bool(rests)
    return pl.pallas_call(
        functools.partial(finish_kernel, scale, own, block, len(slots), wheres, hold),
        name="finish",
        in_specs=[VMEM] * len(inputs) + [ANY] * len(before),
        out_specs=[ANY] * 4 * writes + [VMEM] * hold,
        out_shape=[out] * 4 * writes + [piece] * hold,
        scratch_shapes=[piece] * (not hold)
        + [pltpu.SemaphoreType.DMA((2 + len(rests), 4))] * writes
        + [states] * own,
        input_output_aliases={len(inputs) + i: i for i in range(len(before))},
        cost_estimate=pl.CostEstimate(
            flops=2 * rows * width * HEAD, bytes_accessed=8 * rows * width, transcendentals=0
        ),
        compiler_params=SMALL,
    )(*inputs, *before)


def swap(x, axis, bits):
    return lax.ppermute(x, axis, [(i, i ^ bits) for i in range(lax.axis_size(axis))])


def swap_far(slots):
    return [slots[0]] + [swap(slots[s], "inner", 2 * s) for s in range(1, len(slots))]


def body(queries, keys, values, cotangent):
    far_count = lax.axis_size("inner") // 2
    outer_count = lax.axis_size("outer")
    scale = float(HEAD * queries.shape[0] * 2 * far_count * outer_count) ** (-0.5)
    tokens = (queries, keys, values, cotangent)
    give = first_sums(tokens)
    got = [swap(give, "inner", 1), swap(*sums(tokens, (False, 1)), "inner", 1)]
    keep = sums(tokens, (True, 0), (True, 1))
    slots = [slot for b in range(2) for slot in pair_slots(keep[b], got[b], far_count // 2)]
    slots, local = lax.optimization_barrier((swap_far(slots), local_part(tokens)))
    sends = group_sends(slots, outer_count)
    others = [swap(send, "outer", s) for s, send in zip(distances(outer_count), sends)]
    slots = swap_far(scan_slots(slots, others))
    half = far_count // 2

    def near_swap(block, part):
        return swap(states_for_neighbour(part, keep[block]), "inner", 1)

    arrived = [near_swap(0, slots[:half])]
    outs = finish(True, 0, tokens, local, slots[:half], scale, got=got[:1])
    part, outs = lax.optimization_barrier((slots[half:], tuple(outs)))
    arrived.append(near_swap(1, part))
    (rest,) = finish(True, 1, tokens, local, part, scale, got=got[1:], hold=True)
    rests = [((True, 1), rest)]
    *outs, rest = finish(
        False, 0, tokens, local, arrived[:1], scale, rests=rests, before=outs, hold=True
    )
    rests = [((False, 0), rest)]
    return tuple(finish(False, 1, tokens, local, arrived[1:], scale, rests=rests, before=outs))


def solution(mesh):
    spec = P(("outer", "inner"), None)
    return jax.shard_map(
        body, mesh=mesh, in_specs=(spec,) * 4, out_specs=(spec,) * 4, check_vma=False
    )
```

```python
import functools

import jax
import jax.numpy as jnp
from jax import lax
from jax.experimental import pallas as pl
from jax.experimental.pallas import tpu as pltpu
from jax.sharding import PartitionSpec as P

HEAD = 128
MIB = 1024 * 1024
ANY = pl.BlockSpec(memory_space=pl.ANY)
VMEM = pl.BlockSpec(memory_space=pltpu.VMEM)
BF16 = jnp.bfloat16
F32 = jnp.float32
SMALL = pltpu.CompilerParams(vmem_limit_bytes=4 * MIB)


def dot(a, b, over_a, over_b):
    return lax.dot_general(
        a, b, (((over_a,), (over_b,)), ((), ())), preferred_element_type=F32
    )


def near_far():
    inner = lax.axis_index("inner")
    return lax.rem(inner, 2), lax.div(inner, 2)


def distances(outer_count):
    return [outer_count - 1, *range(1, outer_count - 1)]


def exchanged(bits):
    return bits ^ 3 if bits & 3 in (1, 2) and lax.axis_size("inner") > 4 else bits


def place():
    _, far = near_far()
    if lax.axis_size("inner") <= 4:
        return far
    return far + lax.rem(far, 2) - lax.rem(lax.div(far, 2), 2)


def block_start(own, block, half):
    near, _ = near_far()
    side = near if own else 1 - near
    top = lax.div(place(), lax.axis_size("inner") // 4)
    return side * half + (1 - top if block else top) * (half // 2)


def columns(start, n):
    return pl.ds(pl.multiple_of(start + n * HEAD, HEAD), HEAD)


def slot_rows(s, count, depth):
    return pl.ds(pl.multiple_of(lax.rem(place() ^ s, count) * depth, depth), depth)


def one_ahead(products, use):
    last = None
    for key, product in products:
        if last:
            use(*last)
        last = key, product
    use(*last)


def sums_of(tokens, start, out, kinds=(0, 1)):
    q, k, v, d = tokens

    def products():
        for n in range(out.shape[1] // HEAD):
            cols = pl.ds(start + n * HEAD, HEAD) if isinstance(start, int) else columns(start, n)
            for which in kinds:
                a, b = ((k, v), (q, d))[which]
                yield (which, n), dot(a[:, cols], b[:, cols], 0, 0)

    def use(key, product):
        which, n = key
        out[which, n * HEAD : (n + 1) * HEAD] = product.astype(BF16)

    one_ahead(products(), use)


def give_kernel(*refs):
    tokens, (out, held, sems) = refs[:4], refs[4:]
    width = tokens[0].shape[1]
    start = pl.multiple_of(block_start(False, 0, width // 2), width // 4)
    pairs = ((1, 2), (0, 3))
    copies = [
        pltpu.make_async_copy(ref.at[:, pl.ds(start, width // 4)], held.at[i], sems.at[i])
        for i, ref in enumerate(tokens)
    ]
    for i in pairs[0] + pairs[1]:
        copies[i].start()
    for kind, pair in enumerate(pairs):
        for i in pair:
            copies[i].wait()
        sums_of([held.at[i] for i in range(4)], 0, out, (kind,))


def first_sums(tokens):
    rows, width = tokens[0].shape
    return pl.pallas_call(
        give_kernel,
        name="first_sums",
        in_specs=[ANY] * 4,
        out_specs=VMEM,
        out_shape=pltpu.VMEM((2, width // 4, HEAD), BF16),
        scratch_shapes=[pltpu.VMEM((4, rows, width // 4), BF16), pltpu.SemaphoreType.DMA((4,))],
        cost_estimate=pl.CostEstimate(
            flops=rows * width * HEAD, bytes_accessed=3 * rows * width, transcendentals=0
        ),
        compiler_params=SMALL,
    )(*(pltpu.with_memory_space_constraint(x, pltpu.HBM) for x in tokens))


def sums_kernel(wanted, *refs):
    for (own, block), out in zip(wanted, refs[4:]):
        sums_of(refs[:4], block_start(own, block, refs[0].shape[1] // 2), out)


def sums(tokens, *wanted):
    rows, width = tokens[0].shape
    return pl.pallas_call(
        functools.partial(sums_kernel, wanted),
        name="sums",
        in_specs=[VMEM] * 4,
        out_specs=[VMEM] * len(wanted),
        out_shape=[jax.ShapeDtypeStruct((2, width // 4, HEAD), BF16)] * len(wanted),
        cost_estimate=pl.CostEstimate(
            flops=rows * width * HEAD * len(wanted),
            bytes_accessed=3 * rows * width * len(wanted),
            transcendentals=0,
        ),
        compiler_params=SMALL,
    )(*tokens)


def pair_kernel(keep_ref, got_ref, *slots):
    for s, slot in enumerate(slots):
        part = slot_rows(s, len(slots), slot.shape[1])
        for which in range(2):
            both = keep_ref[which, part].astype(F32) + got_ref[which, part].astype(F32)
            slot[which] = both.astype(BF16)


def pair_slots(keep, got, count):
    slot = jax.ShapeDtypeStruct((2, keep.shape[1] // count, HEAD), BF16)
    return pl.pallas_call(
        pair_kernel,
        name="pair",
        in_specs=[VMEM] * 2,
        out_specs=[VMEM] * count,
        out_shape=[slot] * count,
        compiler_params=SMALL,
    )(keep, got)


def totals_kernel(far_count, *refs):
    slots, sends = refs[:far_count], refs[far_count:]
    outer = lax.axis_index("outer")
    totals = []
    for which in range(2):
        total = slots[0][which].astype(F32)
        for slot in slots[1:]:
            total += slot[which].astype(F32)
        totals.append(total.astype(BF16))
    for s, send in zip(distances(len(sends) + 1), sends):
        upward = (outer ^ s) > outer
        send[...] = jnp.where(upward, totals[0], totals[1])


def group_sends(slots, outer_count):
    send = jax.ShapeDtypeStruct(slots[0].shape[1:], BF16)
    return pl.pallas_call(
        functools.partial(totals_kernel, len(slots)),
        name="totals",
        in_specs=[VMEM] * len(slots),
        out_specs=[VMEM] * (outer_count - 1),
        out_shape=[send] * (outer_count - 1),
        compiler_params=SMALL,
    )(*slots)


def scan_kernel(far_count, *refs):
    slots, others, refs = refs[:far_count], refs[far_count : -far_count - 2], refs[-far_count - 2 :]
    outs, (held, scanned) = refs[:far_count], refs[far_count:]
    outer = lax.axis_index("outer")
    _, far = near_far()
    for s, slot in enumerate(slots):
        held[far ^ exchanged(s)] = slot[...]
    for which in range(2):
        total = jnp.zeros(held.shape[2:], F32)
        for s, other in zip(distances(len(others) + 1), others):
            below = (outer ^ s) < outer
            wanted = below if which == 0 else jnp.logical_not(below)
            total += jnp.where(wanted, other[...].astype(F32), 0.0)
        for i in reversed(range(far_count)) if which else range(far_count):
            scanned[i, which] = total.astype(BF16)
            total += held[i, which].astype(F32)
    for s, out in enumerate(outs):
        out[...] = scanned[far ^ exchanged(s)]


def scan_slots(slots, others):
    far_count, slot = len(slots), jax.ShapeDtypeStruct(slots[0].shape, BF16)
    return pl.pallas_call(
        functools.partial(scan_kernel, far_count),
        name="scan",
        in_specs=[VMEM] * (far_count + len(others)),
        out_specs=[VMEM] * far_count,
        out_shape=[slot] * far_count,
        scratch_shapes=[pltpu.VMEM((far_count, *slot.shape), BF16)] * 2,
        compiler_params=SMALL,
    )(*slots, *others)


def with_sums(slot, which, extra, part):
    return (slot[which].astype(F32) + extra[which, part].astype(F32)).astype(BF16)


def by_core(run):
    near, _ = near_far()
    for core in range(2):
        pl.when(near == core)(functools.partial(run, core))


def theirs_kernel(*refs):
    slots, (keep, out) = refs[:-2], refs[-2:]

    def run(core):
        for s, slot in enumerate(slots):
            part = slot_rows(s, len(slots), slot.shape[1])
            out[core, part] = with_sums(slot, core, keep, part)
            out[1 - core, part] = slot[1 - core]

    by_core(run)


def states_for_neighbour(slots, keep):
    return pl.pallas_call(
        theirs_kernel,
        name="theirs",
        in_specs=[VMEM] * (len(slots) + 1),
        out_specs=VMEM,
        out_shape=jax.ShapeDtypeStruct(keep.shape, BF16),
        compiler_params=SMALL,
    )(*slots, keep)


def local_kernel(*refs):
    tokens, outs = refs[:4], refs[4:]
    rows, width = tokens[0].shape
    at = lax.broadcasted_iota(jnp.int32, (rows, rows), 0)
    to = lax.broadcasted_iota(jnp.int32, (rows, rows), 1)
    lower = at >= to

    def masked(a, b):
        return jnp.where(lower, dot(a, b, 1, 1), 0.0).astype(BF16)

    def second(cols, a, b):
        q, k, v, d = (ref[:, cols] for ref in tokens)
        att, gq, gk, gv = outs
        att[:, cols] = dot(a, v, 1, 0)
        gq[:, cols] = dot(b, k, 1, 0)
        gk[:, cols] = dot(b, q, 0, 0)
        gv[:, cols] = dot(a, d, 0, 0)

    last = None
    for h in range(width // HEAD):
        cols = slice(h * HEAD, (h + 1) * HEAD)
        q, k, v, d = (ref[:, cols] for ref in tokens)
        a, b = masked(q, k), masked(d, v)
        if last:
            second(*last)
        last = (cols, a, b)
    second(*last)


def local_part(tokens):
    rows, width = tokens[0].shape
    return pl.pallas_call(
        local_kernel,
        name="local",
        in_specs=[VMEM] * 4,
        out_specs=[VMEM] * 4,
        out_shape=[jax.ShapeDtypeStruct((rows, width), F32)] * 4,
        cost_estimate=pl.CostEstimate(
            flops=12 * rows * width * HEAD, bytes_accessed=24 * rows * width, transcendentals=0
        ),
        compiler_params=SMALL,
    )(*tokens)


def all_products(scale, start, tokens, local, states, store):
    q, k, v, d = tokens

    def products():
        for n in range(states.shape[1] // HEAD):
            rows = slice(n * HEAD, (n + 1) * HEAD)
            cols = slice(start + n * HEAD, start + (n + 1) * HEAD)
            s, g = states[0, rows], states[1, rows]
            yield (rows, 0, cols), dot(q[:, cols], s, 1, 0)
            yield (rows, 1, cols), dot(d[:, cols], s, 1, 1)
            yield (rows, 2, cols), dot(v[:, cols], g, 1, 1)
            yield (rows, 3, cols), dot(k[:, cols], g, 1, 0)

    def use(key, product):
        rows, i, cols = key
        store(rows, i, (scale * (product + local[i][:, cols])).astype(BF16))

    one_ahead(products(), use)


def copies_out(own, block, held, outs, sems, piece):
    first, size = (0, held.shape[2]) if piece is None else (piece * held.shape[2] // 2, held.shape[2] // 2)
    start = block_start(own, block, outs[0].shape[1] // 2) + first
    there = pl.ds(pl.multiple_of(start, size), size)
    return [
        pltpu.make_async_copy(held.at[i, :, pl.ds(first, size)], out.at[:, there], sems.at[i])
        for i, out in enumerate(outs)
    ]


def finish_kernel(scale, own, block, count, rests, hold, *refs):
    tokens, local, slots, refs = refs[:4], refs[4:8], refs[8 : 8 + count], refs[8 + count :]
    got, refs = (refs[0], refs[1:]) if own else (None, refs)
    late, refs = refs[: len(rests)], refs[len(rests) :]
    if own:
        refs, states = refs[:-1], refs[-1]
    else:
        states = slots[0]
    if not hold or rests:
        *refs, sems = refs
    *refs, held = refs
    outs = refs[-4:]
    width = tokens[0].shape[1]
    copies = []
    for n, (rest, where) in enumerate(zip(late, rests)):
        copies += copies_out(*where, rest, outs, sems.at[n + 2], None)
    for copy in copies:
        copy.start()

    def store(rows, i, out):
        held[i, :, rows] = out
        for piece in range(2):
            if not hold and i == 3 and rows.stop == (piece + 1) * states.shape[1] // 2:
                for copy in copies_out(own, block, held, outs, sems.at[piece], piece):
                    copy.start()

    def run(quarter):
        for s, slot in enumerate(slots if own else ()):
            core, part = quarter // 2, slot_rows(s, count, slot.shape[1])
            states[core, part] = slot[core]
            states[1 - core, part] = with_sums(slot, 1 - core, got, part)
        all_products(scale, quarter * width // 4, tokens, local, states, store)

    start = block_start(own, block, width // 2)
    for quarter in range(4):
        pl.when(start == quarter * width // 4)(functools.partial(run, quarter))
    if not hold:
        for piece in range(2):
            copies += copies_out(own, block, held, outs, sems.at[piece], piece)
    for copy in copies:
        copy.wait()


def finish(own, block, tokens, local, slots, scale, got=(), rests=(), before=(), hold=False):
    rows, width = tokens[0].shape
    out = jax.ShapeDtypeStruct((rows, width), BF16)
    piece = pltpu.VMEM((4, rows, width // 4), BF16)
    inputs = [*tokens, *local, *slots, *got, *(x for _, x in rests)]
    states = pltpu.VMEM((2, width // 4, HEAD), BF16)
    wheres = [where for where, _ in rests]
    writes = not hold or bool(rests)
    return pl.pallas_call(
        functools.partial(finish_kernel, scale, own, block, len(slots), wheres, hold),
        name="finish",
        in_specs=[VMEM] * len(inputs) + [ANY] * len(before),
        out_specs=[ANY] * 4 * writes + [VMEM] * hold,
        out_shape=[out] * 4 * writes + [piece] * hold,
        scratch_shapes=[piece] * (not hold)
        + [pltpu.SemaphoreType.DMA((2 + len(rests), 4))] * writes
        + [states] * own,
        input_output_aliases={len(inputs) + i: i for i in range(len(before))},
        cost_estimate=pl.CostEstimate(
            flops=2 * rows * width * HEAD, bytes_accessed=8 * rows * width, transcendentals=0
        ),
        compiler_params=SMALL,
    )(*inputs, *before)


def swap(x, axis, bits):
    return lax.ppermute(x, axis, [(i, i ^ bits) for i in range(lax.axis_size(axis))])


def swap_far(slots):
    return [slots[0]] + [swap(slots[s], "inner", 2 * exchanged(s)) for s in range(1, len(slots))]


def body(queries, keys, values, cotangent):
    far_count = lax.axis_size("inner") // 2
    outer_count = lax.axis_size("outer")
    scale = float(HEAD * queries.shape[0] * 2 * far_count * outer_count) ** (-0.5)
    tokens = (queries, keys, values, cotangent)
    give = first_sums(tokens)
    got = [swap(give, "inner", 1), swap(*sums(tokens, (False, 1)), "inner", 1)]
    keep = sums(tokens, (True, 0), (True, 1))
    slots = [slot for b in range(2) for slot in pair_slots(keep[b], got[b], far_count // 2)]
    slots, local = lax.optimization_barrier((swap_far(slots), local_part(tokens)))
    sends = group_sends(slots, outer_count)
    others = [swap(send, "outer", s) for s, send in zip(distances(outer_count), sends)]
    slots = swap_far(scan_slots(slots, others))
    half = far_count // 2

    def near_swap(block, part):
        return swap(states_for_neighbour(part, keep[block]), "inner", 1)

    arrived = [near_swap(0, slots[:half])]
    outs = finish(True, 0, tokens, local, slots[:half], scale, got=got[:1])
    part, outs = lax.optimization_barrier((slots[half:], tuple(outs)))
    arrived.append(near_swap(1, part))
    (rest,) = finish(True, 1, tokens, local, part, scale, got=got[1:], hold=True)
    rests = [((True, 1), rest)]
    *outs, rest = finish(
        False, 0, tokens, local, arrived[:1], scale, rests=rests, before=outs, hold=True
    )
    rests = [((False, 0), rest)]
    return tuple(finish(False, 1, tokens, local, arrived[1:], scale, rests=rests, before=outs))


def solution(mesh):
    spec = P(("outer", "inner"), None)
    return jax.shard_map(
        body, mesh=mesh, in_specs=(spec,) * 4, out_specs=(spec,) * 4, check_vma=False
    )
```

```python
import functools

import jax
import jax.numpy as jnp
from jax import lax
from jax.experimental import pallas as pl
from jax.experimental.pallas import tpu as pltpu
from jax.sharding import PartitionSpec as P

HEAD = 128
MIB = 1024 * 1024
ANY = pl.BlockSpec(memory_space=pl.ANY)
VMEM = pl.BlockSpec(memory_space=pltpu.VMEM)
BF16 = jnp.bfloat16
F32 = jnp.float32
SMALL = pltpu.CompilerParams(vmem_limit_bytes=4 * MIB)


def dot(a, b, over_a, over_b):
    return lax.dot_general(
        a, b, (((over_a,), (over_b,)), ((), ())), preferred_element_type=F32
    )


def near_far():
    inner = lax.axis_index("inner")
    return lax.rem(inner, 2), lax.div(inner, 2)


def distances(outer_count):
    return [outer_count - 1, *range(1, outer_count - 1)]


def block_start(own, block, half):
    near, far = near_far()
    side = near if own else 1 - near
    top = lax.div(far, lax.axis_size("inner") // 4)
    return side * half + (1 - top if block else top) * (half // 2)


def columns(start, n):
    return pl.ds(pl.multiple_of(start + n * HEAD, HEAD), HEAD)


def slot_rows(s, count, depth):
    _, far = near_far()
    return pl.ds(pl.multiple_of(lax.rem(far ^ s, count) * depth, depth), depth)


def one_ahead(products, use):
    last = None
    for key, product in products:
        if last:
            use(*last)
        last = key, product
    use(*last)


def sums_of(tokens, start, out, kinds=(0, 1)):
    q, k, v, d = tokens

    def products():
        for n in range(out.shape[1] // HEAD):
            cols = pl.ds(start + n * HEAD, HEAD) if isinstance(start, int) else columns(start, n)
            for which in kinds:
                a, b = ((k, v), (q, d))[which]
                yield (which, n), dot(a[:, cols], b[:, cols], 0, 0)

    def use(key, product):
        which, n = key
        out[which, n * HEAD : (n + 1) * HEAD] = product.astype(BF16)

    one_ahead(products(), use)


def give_kernel(*refs):
    tokens, (out, held, sems) = refs[:4], refs[4:]
    width = tokens[0].shape[1]
    start = pl.multiple_of(block_start(False, 0, width // 2), width // 4)
    pairs = ((1, 2), (0, 3))
    copies = [
        pltpu.make_async_copy(ref.at[:, pl.ds(start, width // 4)], held.at[i], sems.at[i])
        for i, ref in enumerate(tokens)
    ]
    for i in pairs[0] + pairs[1]:
        copies[i].start()
    for kind, pair in enumerate(pairs):
        for i in pair:
            copies[i].wait()
        sums_of([held.at[i] for i in range(4)], 0, out, (kind,))


def first_sums(tokens):
    rows, width = tokens[0].shape
    return pl.pallas_call(
        give_kernel,
        name="first_sums",
        in_specs=[ANY] * 4,
        out_specs=VMEM,
        out_shape=pltpu.VMEM((2, width // 4, HEAD), BF16),
        scratch_shapes=[pltpu.VMEM((4, rows, width // 4), BF16), pltpu.SemaphoreType.DMA((4,))],
        cost_estimate=pl.CostEstimate(
            flops=rows * width * HEAD, bytes_accessed=3 * rows * width, transcendentals=0
        ),
        compiler_params=SMALL,
    )(*(pltpu.with_memory_space_constraint(x, pltpu.HBM) for x in tokens))


def sums_kernel(wanted, *refs):
    for (own, block), out in zip(wanted, refs[4:]):
        sums_of(refs[:4], block_start(own, block, refs[0].shape[1] // 2), out)


def sums(tokens, *wanted):
    rows, width = tokens[0].shape
    return pl.pallas_call(
        functools.partial(sums_kernel, wanted),
        name="sums",
        in_specs=[VMEM] * 4,
        out_specs=[VMEM] * len(wanted),
        out_shape=[jax.ShapeDtypeStruct((2, width // 4, HEAD), BF16)] * len(wanted),
        cost_estimate=pl.CostEstimate(
            flops=rows * width * HEAD * len(wanted),
            bytes_accessed=3 * rows * width * len(wanted),
            transcendentals=0,
        ),
        compiler_params=SMALL,
    )(*tokens)


def pair_kernel(keep_ref, got_ref, *slots):
    for s, slot in enumerate(slots):
        part = slot_rows(s, len(slots), slot.shape[1])
        for which in range(2):
            both = keep_ref[which, part].astype(F32) + got_ref[which, part].astype(F32)
            slot[which] = both.astype(BF16)


def pair_slots(keep, got, count):
    slot = jax.ShapeDtypeStruct((2, keep.shape[1] // count, HEAD), BF16)
    return pl.pallas_call(
        pair_kernel,
        name="pair",
        in_specs=[VMEM] * 2,
        out_specs=[VMEM] * count,
        out_shape=[slot] * count,
        compiler_params=SMALL,
    )(keep, got)


def totals_kernel(far_count, *refs):
    slots, sends = refs[:far_count], refs[far_count:]
    outer = lax.axis_index("outer")
    totals = []
    for which in range(2):
        total = slots[0][which].astype(F32)
        for slot in slots[1:]:
            total += slot[which].astype(F32)
        totals.append(total.astype(BF16))
    for s, send in zip(distances(len(sends) + 1), sends):
        upward = (outer ^ s) > outer
        send[...] = jnp.where(upward, totals[0], totals[1])


def group_sends(slots, outer_count):
    send = jax.ShapeDtypeStruct(slots[0].shape[1:], BF16)
    return pl.pallas_call(
        functools.partial(totals_kernel, len(slots)),
        name="totals",
        in_specs=[VMEM] * len(slots),
        out_specs=[VMEM] * (outer_count - 1),
        out_shape=[send] * (outer_count - 1),
        compiler_params=SMALL,
    )(*slots)


def scan_kernel(far_count, *refs):
    slots, others, refs = refs[:far_count], refs[far_count : -far_count - 2], refs[-far_count - 2 :]
    outs, (held, scanned) = refs[:far_count], refs[far_count:]
    outer = lax.axis_index("outer")
    _, far = near_far()
    for s, slot in enumerate(slots):
        held[far ^ s] = slot[...]
    for which in range(2):
        total = jnp.zeros(held.shape[2:], F32)
        for s, other in zip(distances(len(others) + 1), others):
            below = (outer ^ s) < outer
            wanted = below if which == 0 else jnp.logical_not(below)
            total += jnp.where(wanted, other[...].astype(F32), 0.0)
        for i in reversed(range(far_count)) if which else range(far_count):
            scanned[i, which] = total.astype(BF16)
            total += held[i, which].astype(F32)
    for s, out in enumerate(outs):
        out[...] = scanned[far ^ s]


def scan_slots(slots, others):
    far_count, slot = len(slots), jax.ShapeDtypeStruct(slots[0].shape, BF16)
    return pl.pallas_call(
        functools.partial(scan_kernel, far_count),
        name="scan",
        in_specs=[VMEM] * (far_count + len(others)),
        out_specs=[VMEM] * far_count,
        out_shape=[slot] * far_count,
        scratch_shapes=[pltpu.VMEM((far_count, *slot.shape), BF16)] * 2,
        compiler_params=SMALL,
    )(*slots, *others)


def with_sums(slot, which, extra, part):
    return (slot[which].astype(F32) + extra[which, part].astype(F32)).astype(BF16)


def by_core(run):
    near, _ = near_far()
    for core in range(2):
        pl.when(near == core)(functools.partial(run, core))


def theirs_kernel(*refs):
    slots, (keep, out) = refs[:-2], refs[-2:]

    def run(core):
        for s, slot in enumerate(slots):
            part = slot_rows(s, len(slots), slot.shape[1])
            out[core, part] = with_sums(slot, core, keep, part)
            out[1 - core, part] = slot[1 - core]

    by_core(run)


def states_for_neighbour(slots, keep):
    return pl.pallas_call(
        theirs_kernel,
        name="theirs",
        in_specs=[VMEM] * (len(slots) + 1),
        out_specs=VMEM,
        out_shape=jax.ShapeDtypeStruct(keep.shape, BF16),
        compiler_params=SMALL,
    )(*slots, keep)


def local_kernel(*refs):
    tokens, outs = refs[:4], refs[4:]
    rows, width = tokens[0].shape
    at = lax.broadcasted_iota(jnp.int32, (rows, rows), 0)
    to = lax.broadcasted_iota(jnp.int32, (rows, rows), 1)
    lower = at >= to

    def masked(a, b):
        return jnp.where(lower, dot(a, b, 1, 1), 0.0).astype(BF16)

    def second(cols, a, b):
        q, k, v, d = (ref[:, cols] for ref in tokens)
        att, gq, gk, gv = outs
        att[:, cols] = dot(a, v, 1, 0)
        gq[:, cols] = dot(b, k, 1, 0)
        gk[:, cols] = dot(b, q, 0, 0)
        gv[:, cols] = dot(a, d, 0, 0)

    last = None
    for h in range(width // HEAD):
        cols = slice(h * HEAD, (h + 1) * HEAD)
        q, k, v, d = (ref[:, cols] for ref in tokens)
        a, b = masked(q, k), masked(d, v)
        if last:
            second(*last)
        last = (cols, a, b)
    second(*last)


def local_part(tokens):
    rows, width = tokens[0].shape
    return pl.pallas_call(
        local_kernel,
        name="local",
        in_specs=[VMEM] * 4,
        out_specs=[VMEM] * 4,
        out_shape=[jax.ShapeDtypeStruct((rows, width), F32)] * 4,
        cost_estimate=pl.CostEstimate(
            flops=12 * rows * width * HEAD, bytes_accessed=24 * rows * width, transcendentals=0
        ),
        compiler_params=SMALL,
    )(*tokens)


def all_products(scale, start, tokens, local, states, store):
    q, k, v, d = tokens

    def products():
        for n in range(states.shape[1] // HEAD):
            rows = slice(n * HEAD, (n + 1) * HEAD)
            cols = slice(start + n * HEAD, start + (n + 1) * HEAD)
            s, g = states[0, rows], states[1, rows]
            yield (rows, 0, cols), dot(q[:, cols], s, 1, 0)
            yield (rows, 1, cols), dot(d[:, cols], s, 1, 1)
            yield (rows, 2, cols), dot(v[:, cols], g, 1, 1)
            yield (rows, 3, cols), dot(k[:, cols], g, 1, 0)

    def use(key, product):
        rows, i, cols = key
        store(rows, i, (scale * (product + local[i][:, cols])).astype(BF16))

    one_ahead(products(), use)


def piece_of(width, piece):
    last = width - HEAD
    return (0, width) if piece is None else ((0, last), (last, HEAD))[piece]


def copies_out(own, block, held, outs, sems, piece):
    first, size = piece_of(held.shape[2], piece)
    start = block_start(own, block, outs[0].shape[1] // 2) + first
    there = pl.ds(pl.multiple_of(start, HEAD), size)
    return [
        pltpu.make_async_copy(held.at[i, :, pl.ds(first, size)], out.at[:, there], sems.at[i])
        for i, out in enumerate(outs)
    ]


def finish_kernel(scale, own, block, count, rests, hold, *refs):
    tokens, local, slots, refs = refs[:4], refs[4:8], refs[8 : 8 + count], refs[8 + count :]
    got, refs = (refs[0], refs[1:]) if own else (None, refs)
    late, refs = refs[: len(rests)], refs[len(rests) :]
    if own:
        refs, states = refs[:-1], refs[-1]
    else:
        states = slots[0]
    if not hold or rests:
        *refs, sems = refs
    *refs, held = refs
    outs = refs[-4:]
    width = tokens[0].shape[1]
    copies = []
    for n, (rest, where) in enumerate(zip(late, rests)):
        copies += copies_out(*where, rest, outs, sems.at[n + 2], None)
    for copy in copies:
        copy.start()

    def store(rows, i, out):
        held[i, :, rows] = out
        for piece in range(2):
            if not hold and i == 3 and rows.stop == sum(piece_of(states.shape[1], piece)):
                for copy in copies_out(own, block, held, outs, sems.at[piece], piece):
                    copy.start()

    def run(quarter):
        for s, slot in enumerate(slots if own else ()):
            core, part = quarter // 2, slot_rows(s, count, slot.shape[1])
            states[core, part] = slot[core]
            states[1 - core, part] = with_sums(slot, 1 - core, got, part)
        all_products(scale, quarter * width // 4, tokens, local, states, store)

    start = block_start(own, block, width // 2)
    for quarter in range(4):
        pl.when(start == quarter * width // 4)(functools.partial(run, quarter))
    if not hold:
        for piece in range(2):
            copies += copies_out(own, block, held, outs, sems.at[piece], piece)
    for copy in copies:
        copy.wait()


def finish(own, block, tokens, local, slots, scale, got=(), rests=(), before=(), hold=False):
    rows, width = tokens[0].shape
    out = jax.ShapeDtypeStruct((rows, width), BF16)
    piece = pltpu.VMEM((4, rows, width // 4), BF16)
    inputs = [*tokens, *local, *slots, *got, *(x for _, x in rests)]
    states = pltpu.VMEM((2, width // 4, HEAD), BF16)
    wheres = [where for where, _ in rests]
    writes = not hold or bool(rests)
    return pl.pallas_call(
        functools.partial(finish_kernel, scale, own, block, len(slots), wheres, hold),
        name="finish",
        in_specs=[VMEM] * len(inputs) + [ANY] * len(before),
        out_specs=[ANY] * 4 * writes + [VMEM] * hold,
        out_shape=[out] * 4 * writes + [piece] * hold,
        scratch_shapes=[piece] * (not hold)
        + [pltpu.SemaphoreType.DMA((2 + len(rests), 4))] * writes
        + [states] * own,
        input_output_aliases={len(inputs) + i: i for i in range(len(before))},
        cost_estimate=pl.CostEstimate(
            flops=2 * rows * width * HEAD, bytes_accessed=8 * rows * width, transcendentals=0
        ),
        compiler_params=SMALL,
    )(*inputs, *before)


def swap(x, axis, bits):
    return lax.ppermute(x, axis, [(i, i ^ bits) for i in range(lax.axis_size(axis))])


def swap_far(slots):
    return [slots[0]] + [swap(slots[s], "inner", 2 * s) for s in range(1, len(slots))]


def body(queries, keys, values, cotangent):
    far_count = lax.axis_size("inner") // 2
    outer_count = lax.axis_size("outer")
    scale = float(HEAD * queries.shape[0] * 2 * far_count * outer_count) ** (-0.5)
    tokens = (queries, keys, values, cotangent)
    give = first_sums(tokens)
    got = [swap(give, "inner", 1), swap(*sums(tokens, (False, 1)), "inner", 1)]
    keep = sums(tokens, (True, 0), (True, 1))
    slots = [slot for b in range(2) for slot in pair_slots(keep[b], got[b], far_count // 2)]
    slots, local = lax.optimization_barrier((swap_far(slots), local_part(tokens)))
    sends = group_sends(slots, outer_count)
    others = [swap(send, "outer", s) for s, send in zip(distances(outer_count), sends)]
    slots = swap_far(scan_slots(slots, others))
    half = far_count // 2

    def near_swap(block, part):
        return swap(states_for_neighbour(part, keep[block]), "inner", 1)

    arrived = [near_swap(0, slots[:half])]
    outs = finish(True, 0, tokens, local, slots[:half], scale, got=got[:1])
    part, outs = lax.optimization_barrier((slots[half:], tuple(outs)))
    arrived.append(near_swap(1, part))
    (rest,) = finish(True, 1, tokens, local, part, scale, got=got[1:], hold=True)
    rests = [((True, 1), rest)]
    *outs, rest = finish(
        False, 0, tokens, local, arrived[:1], scale, rests=rests, before=outs, hold=True
    )
    rests = [((False, 0), rest)]
    return tuple(finish(False, 1, tokens, local, arrived[1:], scale, rests=rests, before=outs))


def solution(mesh):
    spec = P(("outer", "inner"), None)
    return jax.shard_map(
        body, mesh=mesh, in_specs=(spec,) * 4, out_specs=(spec,) * 4, check_vma=False
    )
```

```python
import functools

import jax
import jax.numpy as jnp
from jax import lax
from jax.experimental import pallas as pl
from jax.experimental.pallas import tpu as pltpu
from jax.sharding import PartitionSpec as P

HEAD = 128
MIB = 1024 * 1024
ANY = pl.BlockSpec(memory_space=pl.ANY)
VMEM = pl.BlockSpec(memory_space=pltpu.VMEM)
BF16 = jnp.bfloat16
F32 = jnp.float32
SMALL = pltpu.CompilerParams(vmem_limit_bytes=4 * MIB)


def dot(a, b, over_a, over_b):
    return lax.dot_general(
        a, b, (((over_a,), (over_b,)), ((), ())), preferred_element_type=F32
    )


def near_far():
    inner = lax.axis_index("inner")
    return lax.rem(inner, 2), lax.div(inner, 2)


def distances(outer_count):
    return [outer_count - 1, *range(1, outer_count - 1)]


def block_start(own, block, half):
    near, far = near_far()
    side = near if own else 1 - near
    top = lax.div(far, lax.axis_size("inner") // 4)
    return side * half + (1 - top if block else top) * (half // 2)


def columns(start, n):
    return pl.ds(pl.multiple_of(start + n * HEAD, HEAD), HEAD)


def slot_rows(s, count, depth):
    _, far = near_far()
    return pl.ds(pl.multiple_of(lax.rem(far ^ s, count) * depth, depth), depth)


def one_ahead(products, use):
    last = None
    for key, product in products:
        if last:
            use(*last)
        last = key, product
    use(*last)


def sums_of(tokens, start, out, kinds=(0, 1)):
    q, k, v, d = tokens

    def products():
        for n in range(out.shape[1] // HEAD):
            cols = pl.ds(start + n * HEAD, HEAD) if isinstance(start, int) else columns(start, n)
            for which in kinds:
                a, b = ((k, v), (q, d))[which]
                yield (which, n), dot(a[:, cols], b[:, cols], 0, 0)

    def use(key, product):
        which, n = key
        out[which, n * HEAD : (n + 1) * HEAD] = product.astype(BF16)

    one_ahead(products(), use)


def give_kernel(*refs):
    tokens, (out, held, sems) = refs[:4], refs[4:]
    width = tokens[0].shape[1]
    start = pl.multiple_of(block_start(False, 0, width // 2), width // 4)
    pairs = ((1, 2), (0, 3))
    copies = [
        pltpu.make_async_copy(ref.at[:, pl.ds(start, width // 4)], held.at[i], sems.at[i])
        for i, ref in enumerate(tokens)
    ]
    for i in pairs[0] + pairs[1]:
        copies[i].start()
    for kind, pair in enumerate(pairs):
        for i in pair:
            copies[i].wait()
        sums_of([held.at[i] for i in range(4)], 0, out, (kind,))


def first_sums(tokens):
    rows, width = tokens[0].shape
    return pl.pallas_call(
        give_kernel,
        name="first_sums",
        in_specs=[ANY] * 4,
        out_specs=VMEM,
        out_shape=pltpu.VMEM((2, width // 4, HEAD), BF16),
        scratch_shapes=[pltpu.VMEM((4, rows, width // 4), BF16), pltpu.SemaphoreType.DMA((4,))],
        cost_estimate=pl.CostEstimate(
            flops=rows * width * HEAD, bytes_accessed=3 * rows * width, transcendentals=0
        ),
        compiler_params=SMALL,
    )(*(pltpu.with_memory_space_constraint(x, pltpu.HBM) for x in tokens))


def sums_kernel(wanted, *refs):
    for (own, block), out in zip(wanted, refs[4:]):
        sums_of(refs[:4], block_start(own, block, refs[0].shape[1] // 2), out)


def sums(tokens, *wanted):
    rows, width = tokens[0].shape
    return pl.pallas_call(
        functools.partial(sums_kernel, wanted),
        name="sums",
        in_specs=[VMEM] * 4,
        out_specs=[VMEM] * len(wanted),
        out_shape=[jax.ShapeDtypeStruct((2, width // 4, HEAD), BF16)] * len(wanted),
        cost_estimate=pl.CostEstimate(
            flops=rows * width * HEAD * len(wanted),
            bytes_accessed=3 * rows * width * len(wanted),
            transcendentals=0,
        ),
        compiler_params=SMALL,
    )(*tokens)


def pair_kernel(keep_ref, got_ref, *slots):
    for s, slot in enumerate(slots):
        part = slot_rows(s, len(slots), slot.shape[1])
        for which in range(2):
            both = keep_ref[which, part].astype(F32) + got_ref[which, part].astype(F32)
            slot[which] = both.astype(BF16)


def pair_slots(keep, got, count):
    slot = jax.ShapeDtypeStruct((2, keep.shape[1] // count, HEAD), BF16)
    return pl.pallas_call(
        pair_kernel,
        name="pair",
        in_specs=[VMEM] * 2,
        out_specs=[VMEM] * count,
        out_shape=[slot] * count,
        compiler_params=SMALL,
    )(keep, got)


def totals_kernel(far_count, *refs):
    slots, sends = refs[:far_count], refs[far_count:]
    outer = lax.axis_index("outer")
    totals = []
    for which in range(2):
        total = slots[0][which].astype(F32)
        for slot in slots[1:]:
            total += slot[which].astype(F32)
        totals.append(total.astype(BF16))
    for s, send in zip(distances(len(sends) + 1), sends):
        upward = (outer ^ s) > outer
        send[...] = jnp.where(upward, totals[0], totals[1])


def group_sends(slots, outer_count):
    send = jax.ShapeDtypeStruct(slots[0].shape[1:], BF16)
    return pl.pallas_call(
        functools.partial(totals_kernel, len(slots)),
        name="totals",
        in_specs=[VMEM] * len(slots),
        out_specs=[VMEM] * (outer_count - 1),
        out_shape=[send] * (outer_count - 1),
        compiler_params=SMALL,
    )(*slots)


def scan_kernel(far_count, *refs):
    slots, others, refs = refs[:far_count], refs[far_count : -far_count - 2], refs[-far_count - 2 :]
    outs, (held, scanned) = refs[:far_count], refs[far_count:]
    outer = lax.axis_index("outer")
    _, far = near_far()
    for s, slot in enumerate(slots):
        held[far ^ s] = slot[...]
    for which in range(2):
        total = jnp.zeros(held.shape[2:], F32)
        for s, other in zip(distances(len(others) + 1), others):
            below = (outer ^ s) < outer
            wanted = below if which == 0 else jnp.logical_not(below)
            total += jnp.where(wanted, other[...].astype(F32), 0.0)
        for i in reversed(range(far_count)) if which else range(far_count):
            scanned[i, which] = total.astype(BF16)
            total += held[i, which].astype(F32)
    for s, out in enumerate(outs):
        out[...] = scanned[far ^ s]


def scan_slots(slots, others):
    far_count, slot = len(slots), jax.ShapeDtypeStruct(slots[0].shape, BF16)
    return pl.pallas_call(
        functools.partial(scan_kernel, far_count),
        name="scan",
        in_specs=[VMEM] * (far_count + len(others)),
        out_specs=[VMEM] * far_count,
        out_shape=[slot] * far_count,
        scratch_shapes=[pltpu.VMEM((far_count, *slot.shape), BF16)] * 2,
        compiler_params=SMALL,
    )(*slots, *others)


def with_sums(slot, which, extra, part):
    return (slot[which].astype(F32) + extra[which, part].astype(F32)).astype(BF16)


def by_core(run):
    near, _ = near_far()
    for core in range(2):
        pl.when(near == core)(functools.partial(run, core))


def theirs_kernel(*refs):
    slots, (keep, out) = refs[:-2], refs[-2:]

    def run(core):
        for s, slot in enumerate(slots):
            part = slot_rows(s, len(slots), slot.shape[1])
            out[core, part] = with_sums(slot, core, keep, part)
            out[1 - core, part] = slot[1 - core]

    by_core(run)


def states_for_neighbour(slots, keep):
    return pl.pallas_call(
        theirs_kernel,
        name="theirs",
        in_specs=[VMEM] * (len(slots) + 1),
        out_specs=VMEM,
        out_shape=jax.ShapeDtypeStruct(keep.shape, BF16),
        compiler_params=SMALL,
    )(*slots, keep)


def local_kernel(*refs):
    tokens, outs = refs[:4], refs[4:]
    rows, width = tokens[0].shape
    at = lax.broadcasted_iota(jnp.int32, (rows, rows), 0)
    to = lax.broadcasted_iota(jnp.int32, (rows, rows), 1)
    lower = at >= to

    def masked(a, b):
        return jnp.where(lower, dot(a, b, 1, 1), 0.0).astype(BF16)

    def second(cols, a, b):
        q, k, v, d = (ref[:, cols] for ref in tokens)
        att, gq, gk, gv = outs
        att[:, cols] = dot(a, v, 1, 0)
        gq[:, cols] = dot(b, k, 1, 0)
        gk[:, cols] = dot(b, q, 0, 0)
        gv[:, cols] = dot(a, d, 0, 0)

    last = None
    for h in range(width // HEAD):
        cols = slice(h * HEAD, (h + 1) * HEAD)
        q, k, v, d = (ref[:, cols] for ref in tokens)
        a, b = masked(q, k), masked(d, v)
        if last:
            second(*last)
        last = (cols, a, b)
    second(*last)


def local_part(tokens):
    rows, width = tokens[0].shape
    return pl.pallas_call(
        local_kernel,
        name="local",
        in_specs=[VMEM] * 4,
        out_specs=[VMEM] * 4,
        out_shape=[jax.ShapeDtypeStruct((rows, width), F32)] * 4,
        cost_estimate=pl.CostEstimate(
            flops=12 * rows * width * HEAD, bytes_accessed=24 * rows * width, transcendentals=0
        ),
        compiler_params=SMALL,
    )(*tokens)


def all_products(scale, start, tokens, local, states, store):
    q, k, v, d = tokens

    def products():
        for n in range(states.shape[1] // HEAD):
            rows = slice(n * HEAD, (n + 1) * HEAD)
            cols = slice(start + n * HEAD, start + (n + 1) * HEAD)
            s, g = states[0, rows], states[1, rows]
            yield (rows, 0, cols), dot(q[:, cols], s, 1, 0)
            yield (rows, 1, cols), dot(d[:, cols], s, 1, 1)
            yield (rows, 2, cols), dot(v[:, cols], g, 1, 1)
            yield (rows, 3, cols), dot(k[:, cols], g, 1, 0)

    def use(key, product):
        rows, i, cols = key
        store(rows, i, (scale * (product + local[i][:, cols])).astype(BF16))

    one_ahead(products(), use)


def copies_out(own, block, held, outs, sems, piece):
    first, size = (0, held.shape[2]) if piece is None else (piece * held.shape[2] // 2, held.shape[2] // 2)
    start = block_start(own, block, outs[0].shape[1] // 2) + first
    there = pl.ds(pl.multiple_of(start, size), size)
    return [
        pltpu.make_async_copy(held.at[i, :, pl.ds(first, size)], out.at[:, there], sems.at[i])
        for i, out in enumerate(outs)
    ]


def finish_kernel(scale, own, block, count, rests, hold, *refs):
    tokens, local, slots, refs = refs[:4], refs[4:8], refs[8 : 8 + count], refs[8 + count :]
    got, refs = (refs[0], refs[1:]) if own else (None, refs)
    late, refs = refs[: len(rests)], refs[len(rests) :]
    if own:
        refs, states = refs[:-1], refs[-1]
    else:
        states = slots[0]
    if not hold or rests:
        *refs, sems = refs
    *refs, held = refs
    outs = refs[-4:]
    width = tokens[0].shape[1]
    copies = []
    for n, (rest, where) in enumerate(zip(late, rests)):
        copies += copies_out(*where, rest, outs, sems.at[n + 2], None)
    for copy in copies:
        copy.start()

    def store(rows, i, out):
        held[i, :, rows] = out
        for piece in range(2):
            if not hold and i == 3 and rows.stop == (piece + 1) * states.shape[1] // 2:
                for copy in copies_out(own, block, held, outs, sems.at[piece], piece):
                    copy.start()

    def run(quarter):
        for s, slot in enumerate(slots if own else ()):
            core, part = quarter // 2, slot_rows(s, count, slot.shape[1])
            states[core, part] = slot[core]
            states[1 - core, part] = with_sums(slot, 1 - core, got, part)
        all_products(scale, quarter * width // 4, tokens, local, states, store)

    start = block_start(own, block, width // 2)
    for quarter in range(4):
        pl.when(start == quarter * width // 4)(functools.partial(run, quarter))
    if not hold:
        for piece in range(2):
            copies += copies_out(own, block, held, outs, sems.at[piece], piece)
    for copy in copies:
        copy.wait()


def finish(own, block, tokens, local, slots, scale, got=(), rests=(), before=(), hold=False):
    rows, width = tokens[0].shape
    out = jax.ShapeDtypeStruct((rows, width), BF16)
    piece = pltpu.VMEM((4, rows, width // 4), BF16)
    inputs = [*tokens, *local, *slots, *got, *(x for _, x in rests)]
    states = pltpu.VMEM((2, width // 4, HEAD), BF16)
    wheres = [where for where, _ in rests]
    writes = not hold or bool(rests)
    return pl.pallas_call(
        functools.partial(finish_kernel, scale, own, block, len(slots), wheres, hold),
        name="finish",
        in_specs=[VMEM] * len(inputs) + [ANY] * len(before),
        out_specs=[ANY] * 4 * writes + [VMEM] * hold,
        out_shape=[out] * 4 * writes + [piece] * hold,
        scratch_shapes=[piece] * (not hold)
        + [pltpu.SemaphoreType.DMA((2 + len(rests), 4))] * writes
        + [states] * own,
        input_output_aliases={len(inputs) + i: i for i in range(len(before))},
        cost_estimate=pl.CostEstimate(
            flops=2 * rows * width * HEAD, bytes_accessed=8 * rows * width, transcendentals=0
        ),
        compiler_params=SMALL,
    )(*inputs, *before)


def swap(x, axis, bits):
    return lax.ppermute(x, axis, [(i, i ^ bits) for i in range(lax.axis_size(axis))])


def swap_far(slots):
    return [slots[0]] + [swap(slots[s], "inner", 2 * s) for s in range(1, len(slots))]


def body(queries, keys, values, cotangent):
    far_count = lax.axis_size("inner") // 2
    outer_count = lax.axis_size("outer")
    scale = float(HEAD * queries.shape[0] * 2 * far_count * outer_count) ** (-0.5)
    tokens = (queries, keys, values, cotangent)
    give = first_sums(tokens)
    *keep, give_rest = sums(tokens, (True, 0), (True, 1), (False, 1))
    got = [swap(give, "inner", 1), swap(give_rest, "inner", 1)]
    slots = [slot for b in range(2) for slot in pair_slots(keep[b], got[b], far_count // 2)]
    slots, local = lax.optimization_barrier((swap_far(slots), local_part(tokens)))
    sends = group_sends(slots, outer_count)
    others = [swap(send, "outer", s) for s, send in zip(distances(outer_count), sends)]
    slots = swap_far(scan_slots(slots, others))
    half = far_count // 2

    def near_swap(block, part):
        return swap(states_for_neighbour(part, keep[block]), "inner", 1)

    arrived = [near_swap(0, slots[:half])]
    outs = finish(True, 0, tokens, local, slots[:half], scale, got=got[:1])
    part, outs = lax.optimization_barrier((slots[half:], tuple(outs)))
    arrived.append(near_swap(1, part))
    (rest,) = finish(True, 1, tokens, local, part, scale, got=got[1:], hold=True)
    rests = [((True, 1), rest)]
    *outs, rest = finish(
        False, 0, tokens, local, arrived[:1], scale, rests=rests, before=outs, hold=True
    )
    rests = [((False, 0), rest)]
    return tuple(finish(False, 1, tokens, local, arrived[1:], scale, rests=rests, before=outs))


def solution(mesh):
    spec = P(("outer", "inner"), None)
    return jax.shard_map(
        body, mesh=mesh, in_specs=(spec,) * 4, out_specs=(spec,) * 4, check_vma=False
    )
```

```python
import functools

import jax
import jax.numpy as jnp
from jax import lax
from jax.experimental import pallas as pl
from jax.experimental.pallas import tpu as pltpu
from jax.sharding import PartitionSpec as P

HEAD = 128
MIB = 1024 * 1024
ANY = pl.BlockSpec(memory_space=pl.ANY)
VMEM = pl.BlockSpec(memory_space=pltpu.VMEM)
BF16 = jnp.bfloat16
F32 = jnp.float32
SMALL = pltpu.CompilerParams(vmem_limit_bytes=4 * MIB)


def dot(a, b, over_a, over_b):
    return lax.dot_general(
        a, b, (((over_a,), (over_b,)), ((), ())), preferred_element_type=F32
    )


def near_far():
    inner = lax.axis_index("inner")
    return lax.rem(inner, 2), lax.div(inner, 2)


def distances(outer_count):
    return [outer_count - 1, *range(1, outer_count - 1)]


def block_start(own, block, half):
    near, far = near_far()
    side = near if own else 1 - near
    top = lax.div(far, lax.axis_size("inner") // 4)
    return side * half + (1 - top if block else top) * (half // 2)


def columns(start, n):
    return pl.ds(pl.multiple_of(start + n * HEAD, HEAD), HEAD)


def slot_rows(s, count, depth):
    _, far = near_far()
    return pl.ds(pl.multiple_of(lax.rem(far ^ s, count) * depth, depth), depth)


def one_ahead(products, use):
    last = None
    for key, product in products:
        if last:
            use(*last)
        last = key, product
    use(*last)


def sums_of(tokens, start, out, kinds=(0, 1)):
    q, k, v, d = tokens

    def products():
        for n in range(out.shape[1] // HEAD):
            cols = pl.ds(start + n * HEAD, HEAD) if isinstance(start, int) else columns(start, n)
            for which in kinds:
                a, b = ((k, v), (q, d))[which]
                yield (which, n), dot(a[:, cols], b[:, cols], 0, 0)

    def use(key, product):
        which, n = key
        out[which, n * HEAD : (n + 1) * HEAD] = product.astype(BF16)

    one_ahead(products(), use)


def give_kernel(*refs):
    tokens, (out, held, sems) = refs[:4], refs[4:]
    width = tokens[0].shape[1]
    start = pl.multiple_of(block_start(False, 0, width // 2), width // 4)
    pairs = ((1, 2), (0, 3))
    copies = [
        pltpu.make_async_copy(ref.at[:, pl.ds(start, width // 4)], held.at[i], sems.at[i])
        for i, ref in enumerate(tokens)
    ]
    for i in pairs[0] + pairs[1]:
        copies[i].start()
    for kind, pair in enumerate(pairs):
        for i in pair:
            copies[i].wait()
        sums_of([held.at[i] for i in range(4)], 0, out, (kind,))


def first_sums(tokens):
    rows, width = tokens[0].shape
    return pl.pallas_call(
        give_kernel,
        name="first_sums",
        in_specs=[ANY] * 4,
        out_specs=VMEM,
        out_shape=pltpu.VMEM((2, width // 4, HEAD), BF16),
        scratch_shapes=[pltpu.VMEM((4, rows, width // 4), BF16), pltpu.SemaphoreType.DMA((4,))],
        cost_estimate=pl.CostEstimate(
            flops=rows * width * HEAD, bytes_accessed=3 * rows * width, transcendentals=0
        ),
        compiler_params=SMALL,
    )(*(pltpu.with_memory_space_constraint(x, pltpu.HBM) for x in tokens))


def sums_kernel(wanted, *refs):
    width = refs[0].shape[1]
    for (own, block), out in zip(wanted, refs[4:]):
        start = block_start(own, block, width // 2)
        for n in range(4):
            at = n * width // 4
            pl.when(start == at)(functools.partial(sums_of, refs[:4], at, out))


def sums(tokens, *wanted):
    rows, width = tokens[0].shape
    return pl.pallas_call(
        functools.partial(sums_kernel, wanted),
        name="sums",
        in_specs=[VMEM] * 4,
        out_specs=[VMEM] * len(wanted),
        out_shape=[jax.ShapeDtypeStruct((2, width // 4, HEAD), BF16)] * len(wanted),
        cost_estimate=pl.CostEstimate(
            flops=rows * width * HEAD * len(wanted),
            bytes_accessed=3 * rows * width * len(wanted),
            transcendentals=0,
        ),
        compiler_params=SMALL,
    )(*tokens)


def pair_kernel(keep_ref, got_ref, *slots):
    for s, slot in enumerate(slots):
        part = slot_rows(s, len(slots), slot.shape[1])
        for which in range(2):
            both = keep_ref[which, part].astype(F32) + got_ref[which, part].astype(F32)
            slot[which] = both.astype(BF16)


def pair_slots(keep, got, count):
    slot = jax.ShapeDtypeStruct((2, keep.shape[1] // count, HEAD), BF16)
    return pl.pallas_call(
        pair_kernel,
        name="pair",
        in_specs=[VMEM] * 2,
        out_specs=[VMEM] * count,
        out_shape=[slot] * count,
        compiler_params=SMALL,
    )(keep, got)


def totals_kernel(far_count, *refs):
    slots, sends = refs[:far_count], refs[far_count:]
    outer = lax.axis_index("outer")
    totals = []
    for which in range(2):
        total = slots[0][which].astype(F32)
        for slot in slots[1:]:
            total += slot[which].astype(F32)
        totals.append(total.astype(BF16))
    for s, send in zip(distances(len(sends) + 1), sends):
        upward = (outer ^ s) > outer
        send[...] = jnp.where(upward, totals[0], totals[1])


def group_sends(slots, outer_count):
    send = jax.ShapeDtypeStruct(slots[0].shape[1:], BF16)
    return pl.pallas_call(
        functools.partial(totals_kernel, len(slots)),
        name="totals",
        in_specs=[VMEM] * len(slots),
        out_specs=[VMEM] * (outer_count - 1),
        out_shape=[send] * (outer_count - 1),
        compiler_params=SMALL,
    )(*slots)


def scan_kernel(far_count, *refs):
    slots, others, refs = refs[:far_count], refs[far_count : -far_count - 2], refs[-far_count - 2 :]
    outs, (held, scanned) = refs[:far_count], refs[far_count:]
    outer = lax.axis_index("outer")
    _, far = near_far()
    for s, slot in enumerate(slots):
        held[far ^ s] = slot[...]
    for which in range(2):
        total = jnp.zeros(held.shape[2:], F32)
        for s, other in zip(distances(len(others) + 1), others):
            below = (outer ^ s) < outer
            wanted = below if which == 0 else jnp.logical_not(below)
            total += jnp.where(wanted, other[...].astype(F32), 0.0)
        for i in reversed(range(far_count)) if which else range(far_count):
            scanned[i, which] = total.astype(BF16)
            total += held[i, which].astype(F32)
    for s, out in enumerate(outs):
        out[...] = scanned[far ^ s]


def scan_slots(slots, others):
    far_count, slot = len(slots), jax.ShapeDtypeStruct(slots[0].shape, BF16)
    return pl.pallas_call(
        functools.partial(scan_kernel, far_count),
        name="scan",
        in_specs=[VMEM] * (far_count + len(others)),
        out_specs=[VMEM] * far_count,
        out_shape=[slot] * far_count,
        scratch_shapes=[pltpu.VMEM((far_count, *slot.shape), BF16)] * 2,
        compiler_params=SMALL,
    )(*slots, *others)


def with_sums(slot, which, extra, part):
    return (slot[which].astype(F32) + extra[which, part].astype(F32)).astype(BF16)


def by_core(run):
    near, _ = near_far()
    for core in range(2):
        pl.when(near == core)(functools.partial(run, core))


def theirs_kernel(*refs):
    slots, (keep, out) = refs[:-2], refs[-2:]

    def run(core):
        for s, slot in enumerate(slots):
            part = slot_rows(s, len(slots), slot.shape[1])
            out[core, part] = with_sums(slot, core, keep, part)
            out[1 - core, part] = slot[1 - core]

    by_core(run)


def states_for_neighbour(slots, keep):
    return pl.pallas_call(
        theirs_kernel,
        name="theirs",
        in_specs=[VMEM] * (len(slots) + 1),
        out_specs=VMEM,
        out_shape=jax.ShapeDtypeStruct(keep.shape, BF16),
        compiler_params=SMALL,
    )(*slots, keep)


def local_kernel(*refs):
    tokens, outs = refs[:4], refs[4:]
    rows, width = tokens[0].shape
    at = lax.broadcasted_iota(jnp.int32, (rows, rows), 0)
    to = lax.broadcasted_iota(jnp.int32, (rows, rows), 1)
    lower = at >= to

    def masked(a, b):
        return jnp.where(lower, dot(a, b, 1, 1), 0.0).astype(BF16)

    def second(cols, a, b):
        q, k, v, d = (ref[:, cols] for ref in tokens)
        att, gq, gk, gv = outs
        att[:, cols] = dot(a, v, 1, 0)
        gq[:, cols] = dot(b, k, 1, 0)
        gk[:, cols] = dot(b, q, 0, 0)
        gv[:, cols] = dot(a, d, 0, 0)

    last = None
    for h in range(width // HEAD):
        cols = slice(h * HEAD, (h + 1) * HEAD)
        q, k, v, d = (ref[:, cols] for ref in tokens)
        a, b = masked(q, k), masked(d, v)
        if last:
            second(*last)
        last = (cols, a, b)
    second(*last)


def local_part(tokens):
    rows, width = tokens[0].shape
    return pl.pallas_call(
        local_kernel,
        name="local",
        in_specs=[VMEM] * 4,
        out_specs=[VMEM] * 4,
        out_shape=[jax.ShapeDtypeStruct((rows, width), F32)] * 4,
        cost_estimate=pl.CostEstimate(
            flops=12 * rows * width * HEAD, bytes_accessed=24 * rows * width, transcendentals=0
        ),
        compiler_params=SMALL,
    )(*tokens)


def all_products(scale, start, tokens, local, states, store):
    q, k, v, d = tokens

    def products():
        for n in range(states.shape[1] // HEAD):
            rows = slice(n * HEAD, (n + 1) * HEAD)
            cols = slice(start + n * HEAD, start + (n + 1) * HEAD)
            s, g = states[0, rows], states[1, rows]
            yield (rows, 0, cols), dot(q[:, cols], s, 1, 0)
            yield (rows, 1, cols), dot(d[:, cols], s, 1, 1)
            yield (rows, 2, cols), dot(v[:, cols], g, 1, 1)
            yield (rows, 3, cols), dot(k[:, cols], g, 1, 0)

    def use(key, product):
        rows, i, cols = key
        store(rows, i, (scale * (product + local[i][:, cols])).astype(BF16))

    one_ahead(products(), use)


def copies_out(own, block, held, outs, sems, piece):
    first, size = (0, held.shape[2]) if piece is None else (piece * held.shape[2] // 2, held.shape[2] // 2)
    start = block_start(own, block, outs[0].shape[1] // 2) + first
    there = pl.ds(pl.multiple_of(start, size), size)
    return [
        pltpu.make_async_copy(held.at[i, :, pl.ds(first, size)], out.at[:, there], sems.at[i])
        for i, out in enumerate(outs)
    ]


def finish_kernel(scale, own, block, count, rests, hold, *refs):
    tokens, local, slots, refs = refs[:4], refs[4:8], refs[8 : 8 + count], refs[8 + count :]
    got, refs = (refs[0], refs[1:]) if own else (None, refs)
    late, refs = refs[: len(rests)], refs[len(rests) :]
    if own:
        refs, states = refs[:-1], refs[-1]
    else:
        states = slots[0]
    if not hold or rests:
        *refs, sems = refs
    *refs, held = refs
    outs = refs[-4:]
    width = tokens[0].shape[1]
    copies = []
    for n, (rest, where) in enumerate(zip(late, rests)):
        copies += copies_out(*where, rest, outs, sems.at[n + 2], None)
    for copy in copies:
        copy.start()

    def store(rows, i, out):
        held[i, :, rows] = out
        for piece in range(2):
            if not hold and i == 3 and rows.stop == (piece + 1) * states.shape[1] // 2:
                for copy in copies_out(own, block, held, outs, sems.at[piece], piece):
                    copy.start()

    def run(quarter):
        for s, slot in enumerate(slots if own else ()):
            core, part = quarter // 2, slot_rows(s, count, slot.shape[1])
            states[core, part] = slot[core]
            states[1 - core, part] = with_sums(slot, 1 - core, got, part)
        all_products(scale, quarter * width // 4, tokens, local, states, store)

    start = block_start(own, block, width // 2)
    for quarter in range(4):
        pl.when(start == quarter * width // 4)(functools.partial(run, quarter))
    if not hold:
        for piece in range(2):
            copies += copies_out(own, block, held, outs, sems.at[piece], piece)
    for copy in copies:
        copy.wait()


def finish(own, block, tokens, local, slots, scale, got=(), rests=(), before=(), hold=False):
    rows, width = tokens[0].shape
    out = jax.ShapeDtypeStruct((rows, width), BF16)
    piece = pltpu.VMEM((4, rows, width // 4), BF16)
    inputs = [*tokens, *local, *slots, *got, *(x for _, x in rests)]
    states = pltpu.VMEM((2, width // 4, HEAD), BF16)
    wheres = [where for where, _ in rests]
    writes = not hold or bool(rests)
    return pl.pallas_call(
        functools.partial(finish_kernel, scale, own, block, len(slots), wheres, hold),
        name="finish",
        in_specs=[VMEM] * len(inputs) + [ANY] * len(before),
        out_specs=[ANY] * 4 * writes + [VMEM] * hold,
        out_shape=[out] * 4 * writes + [piece] * hold,
        scratch_shapes=[piece] * (not hold)
        + [pltpu.SemaphoreType.DMA((2 + len(rests), 4))] * writes
        + [states] * own,
        input_output_aliases={len(inputs) + i: i for i in range(len(before))},
        cost_estimate=pl.CostEstimate(
            flops=2 * rows * width * HEAD, bytes_accessed=8 * rows * width, transcendentals=0
        ),
        compiler_params=SMALL,
    )(*inputs, *before)


def swap(x, axis, bits):
    return lax.ppermute(x, axis, [(i, i ^ bits) for i in range(lax.axis_size(axis))])


def swap_far(slots):
    return [slots[0]] + [swap(slots[s], "inner", 2 * s) for s in range(1, len(slots))]


def body(queries, keys, values, cotangent):
    far_count = lax.axis_size("inner") // 2
    outer_count = lax.axis_size("outer")
    scale = float(HEAD * queries.shape[0] * 2 * far_count * outer_count) ** (-0.5)
    tokens = (queries, keys, values, cotangent)
    give = first_sums(tokens)
    got = [swap(give, "inner", 1), swap(*sums(tokens, (False, 1)), "inner", 1)]
    keep = sums(tokens, (True, 0), (True, 1))
    slots = [slot for b in range(2) for slot in pair_slots(keep[b], got[b], far_count // 2)]
    slots, local = lax.optimization_barrier((swap_far(slots), local_part(tokens)))
    sends = group_sends(slots, outer_count)
    others = [swap(send, "outer", s) for s, send in zip(distances(outer_count), sends)]
    slots = swap_far(scan_slots(slots, others))
    half = far_count // 2

    def near_swap(block, part):
        return swap(states_for_neighbour(part, keep[block]), "inner", 1)

    arrived = [near_swap(0, slots[:half])]
    outs = finish(True, 0, tokens, local, slots[:half], scale, got=got[:1])
    part, outs = lax.optimization_barrier((slots[half:], tuple(outs)))
    arrived.append(near_swap(1, part))
    (rest,) = finish(True, 1, tokens, local, part, scale, got=got[1:], hold=True)
    rests = [((True, 1), rest)]
    *outs, rest = finish(
        False, 0, tokens, local, arrived[:1], scale, rests=rests, before=outs, hold=True
    )
    rests = [((False, 0), rest)]
    return tuple(finish(False, 1, tokens, local, arrived[1:], scale, rests=rests, before=outs))


def solution(mesh):
    spec = P(("outer", "inner"), None)
    return jax.shard_map(
        body, mesh=mesh, in_specs=(spec,) * 4, out_specs=(spec,) * 4, check_vma=False
    )
```
